32 devices in a mesh: pre: 8 (over y, x, core), rsp: 4 (over z).
Axes of the slice: x: 2, y: 2, z: 4, core: 2. Of those that a mesh axis runs over, the one named last changes fastest.
Arguments:
- prompt_query: bfloat16 [1024, 2560], P(('pre', 'rsp')), may hold values from -100 to 100
- prompt_k: bfloat16 [1024, 512], P('pre'), may hold values from -5 to 5
- prompt_value: bfloat16 [1024, 512], P('pre'), may hold values from -6 to 6
- prompt_output: bfloat16 [1024, 2560], P(('pre', 'rsp')), may hold values from -6 to 6
- prompt_output_gradient: bfloat16 [1024, 2560], P(('pre', 'rsp')), may hold values from -24 to 24
- reply_query: bfloat16 [4, 2048, 2560], P('rsp', 'pre'), may hold values from -100 to 100
- reply_key: bfloat16 [4, 2048, 512], P('rsp', 'pre'), may hold values from -6 to 6
- reply_value: bfloat16 [4, 2048, 512], P('rsp', 'pre'), may hold values from -6 to 6
- reply_output: bfloat16 [4, 2048, 2560], P('rsp', 'pre'), may hold values from -6 to 6
- reply_output_gradient: bfloat16 [4, 2048, 2560], P('rsp', 'pre'), may hold values from -24 to 24
- reply_len: int32 [8], replicated, may hold values from 1 to 1024, 5120 in all
- reply_slot: int32 [8], replicated, may hold values from 0 to 7, each once
Outputs:
- prompt_dq: bfloat16 [1024, 2560], P(('pre', 'rsp'))
- prompt_dk: bfloat16 [1024, 512], P(('pre', 'rsp'))
- prompt_dv: bfloat16 [1024, 512], P(('pre', 'rsp'))
- reply_dq: bfloat16 [4, 2048, 2560], P('rsp', 'pre')
- reply_dk: bfloat16 [4, 2048, 512], P('rsp', 'pre')
- reply_dv: bfloat16 [4, 2048, 512], P('rsp', 'pre')
The draws below stay inside these ranges and needn't reach their ends.
Inputs may be any that keep to these rules, and one draw needn't show every extreme that they name: `reply_len`: one response is exactly 1024 long; the lengths sum to 5120, rounded down. `reply_slot`: every slot is taken by exactly one response.
All inputs are finite; a program needn't handle non-finite values.
Results may differ from the reference program's by a relative error of at most 0.012.
Values may be sent and summed in bfloat16 or wider, within the bound.
No kernel may reach another device: no remote copies, remote signals or barrier semaphores. Data moves between devices by JAX's collectives and lax.ppermute only.
A program may use at most 128 MiB of HBM per device.

```python
import math
import jax
import jax.numpy as jnp
import numpy as np
from jax import lax

QUERY_HEADS = 20
KEY_VALUE_HEADS = 4
HEAD_WIDTH = 128
PREFIX_TOKENS = 128
LMAX = 1024
RESP_DEV = 2
PROMPT_TOKENS = 1024
REPLY_TOKEN_ROWS = 2048
NRESP = 8
N_PRE = 8
N_RSP = 4


def drawn_keys(key):
    return jnp.clip(jax.random.normal(key, (PREFIX_TOKENS * N_PRE, KEY_VALUE_HEADS * HEAD_WIDTH), jnp.float32), -4.5, 4.5)


def draw_prompt_k(key, part):
    return drawn_keys(key).astype(jnp.bfloat16)


def draw_prompt_query(key, part):
    key = jax.random.fold_in(key, 2)
    return jax.random.normal(key, (PREFIX_TOKENS * N_PRE, QUERY_HEADS * HEAD_WIDTH), jnp.float32).astype(jnp.bfloat16)


def draw_reply_query(key, part):
    key = jax.random.fold_in(key, 3)
    return jax.random.normal(key, (N_RSP, RESP_DEV * LMAX, QUERY_HEADS * HEAD_WIDTH), jnp.float32).astype(jnp.bfloat16)


def block_scale(rng, dims, shards, smallest, top_value):
    def one(position, parts):
        draws = jax.random.uniform(jax.random.fold_in(jax.random.fold_in(rng, 6), position), (parts,), jnp.float32, smallest / len(shards), top_value / len(shards))
        return jnp.repeat(jnp.exp(draws), dims[position] // parts).reshape((-1,) + (1,) * (len(dims) - position - 1))

    loudness = one(*shards[0])
    for cut in shards[1:]:
        loudness = loudness * one(*cut)
    return loudness


def profile(amount, total, most, lean):
    portions = [(1 << 20) // math.isqrt(standing ** lean) + 1 for standing in range(2, amount + 1)]
    spare, given = total - most - (amount - 1), [1] * (amount - 1)
    while spare > 0:
        free = [i for i in range(amount - 1) if given[i] < most]
        mass, budget = sum([portions[i] for i in free]), spare
        for i in free:
            extra = min(most - given[i], max(1, budget * portions[i] // mass), spare)
            given[i] = given[i] + extra
            spare = spare - extra
    return np.array([most] + given)


def uneven(stream_key, count, total, most, slope):
    if count == 2:
        one = jax.random.randint(stream_key, (), max(1, total - most), min(most, total - 1) + 1)
        return jnp.stack([one, total - one])
    sizes = jnp.asarray(profile(count, total, most, slope), jnp.int32)
    couples = (count - 1) // 2
    donor, sink = sizes[1:1 + 2 * couples:2], sizes[2:2 + 2 * couples:2]
    slack = jnp.minimum(donor - 1, most - sink)
    moved = jax.random.randint(jax.random.fold_in(stream_key, 1), (couples,), 0, 1 << 20) % (slack + 1)
    sizes = sizes.at[1:1 + 2 * couples:2].set(donor - moved).at[2:2 + 2 * couples:2].set(sink + moved)
    return sizes[jax.random.permutation(jax.random.fold_in(stream_key, 2), count)]


def scatter_about(rng, dims, deviation, limit, shards=(), kind=jnp.bfloat16):
    factor_of = block_scale(rng, dims, shards, -0.22, 0.18) if shards else 1.0
    entries = jax.random.normal(rng, dims, jnp.float32) * deviation * factor_of
    return jnp.minimum(jnp.maximum(entries, -limit), limit).astype(kind)


def setup_inputs(seed: int = 0) -> dict:
    seeds = jax.random.split(jax.random.key(seed), 13)
    return {
        "prompt_query": draw_prompt_query(jax.random.fold_in(seeds[12], 71), 0),
        "prompt_k": draw_prompt_k(jax.random.fold_in(seeds[12], 71), 0),
        "prompt_value": scatter_about(seeds[2], (PROMPT_TOKENS, KEY_VALUE_HEADS * HEAD_WIDTH), 1.0, 6.0, ((0, 8),)),
        "prompt_output": scatter_about(seeds[3], (PROMPT_TOKENS, QUERY_HEADS * HEAD_WIDTH), 1.0, 6.0, ((0, 32),)),
        "prompt_output_gradient": scatter_about(seeds[4], (PROMPT_TOKENS, QUERY_HEADS * HEAD_WIDTH), 4.0, 24.0, ((0, 32),)),
        "reply_query": draw_reply_query(jax.random.fold_in(seeds[12], 71), 0),
        "reply_key": scatter_about(seeds[6], (N_RSP, REPLY_TOKEN_ROWS, KEY_VALUE_HEADS * HEAD_WIDTH), 1.0, 6.0, ((0, 4), (1, 8))),
        "reply_value": scatter_about(seeds[7], (N_RSP, REPLY_TOKEN_ROWS, KEY_VALUE_HEADS * HEAD_WIDTH), 1.0, 6.0, ((0, 4), (1, 8))),
        "reply_output": scatter_about(seeds[8], (N_RSP, REPLY_TOKEN_ROWS, QUERY_HEADS * HEAD_WIDTH), 1.0, 6.0, ((0, 4), (1, 8))),
        "reply_output_gradient": scatter_about(seeds[9], (N_RSP, REPLY_TOKEN_ROWS, QUERY_HEADS * HEAD_WIDTH), 4.0, 24.0, ((0, 4), (1, 8))),
        "reply_len": uneven(seeds[10], NRESP, NRESP * LMAX * 5 // 8, LMAX, 1).astype(jnp.int32),
        "reply_slot": jax.random.permutation(seeds[11], NRESP).astype(jnp.int32),
    }


NEGATIVE_FLOOR = -1.0e30


def attend(query_rows, upstream_gradient, forward_outputs, weight, prompt_limit, key_phase, key_upper, prompt_key_rows, prompt_value_rows, reply_own_keys, reply_own_values):
    group_member_count = QUERY_HEADS // KEY_VALUE_HEADS
    score_scaling = HEAD_WIDTH ** -0.5
    count_of_rows = query_rows.shape[0]
    prompt_count = prompt_key_rows.shape[0]
    key_head_rows = jnp.concatenate([prompt_key_rows, reply_own_keys], 0).astype(jnp.float32).reshape(-1, KEY_VALUE_HEADS, HEAD_WIDTH)
    value_head_rows = jnp.concatenate([prompt_value_rows, reply_own_values], 0).astype(jnp.float32).reshape(-1, KEY_VALUE_HEADS, HEAD_WIDTH)
    positions = jnp.arange(key_head_rows.shape[0], dtype=jnp.int32)
    own_positions = positions - prompt_count
    own_phase = jnp.mod(own_positions, RESP_DEV).astype(jnp.int32)
    visible = jnp.where(positions[None, :] < prompt_count, positions[None, :] < prompt_limit[:, None], (own_phase[None, :] == key_phase[:, None]) & (own_positions[None, :] >= 0) & (own_positions[None, :] < key_upper[:, None]))
    query_head_rows = query_rows.astype(jnp.float32).reshape(count_of_rows, KEY_VALUE_HEADS, group_member_count, HEAD_WIDTH)
    gradient_head_rows = upstream_gradient.astype(jnp.float32).reshape(count_of_rows, KEY_VALUE_HEADS, group_member_count, HEAD_WIDTH)
    output_head_rows = forward_outputs.astype(jnp.float32).reshape(count_of_rows, KEY_VALUE_HEADS, group_member_count, HEAD_WIDTH)
    scores = jnp.where(visible[None, None], jnp.einsum("rhgd,nhd->hgrn", query_head_rows, key_head_rows) * score_scaling, NEGATIVE_FLOOR)
    row_top = jnp.max(scores, axis=-1)
    row_mass = jnp.sum(jnp.where(visible[None, None], jnp.exp(scores - row_top[..., None]), 0.0), axis=-1)
    log_mass = row_top + jnp.log(row_mass)
    attn_prob = jnp.where(visible[None, None], jnp.exp(scores - log_mass[..., None]), 0.0) * weight[None, None, :, None]
    probability_half = lax.optimization_barrier(attn_prob.astype(jnp.bfloat16)).astype(jnp.float32)
    row_delta = jnp.einsum("rhgd,rhgd->hgr", gradient_head_rows, output_head_rows)
    prob_grad = jnp.einsum("rhgd,nhd->hgrn", gradient_head_rows, value_head_rows)
    score_gradient = lax.optimization_barrier((attn_prob * (prob_grad - row_delta[..., None])).astype(jnp.bfloat16)).astype(jnp.float32)
    query_grad = jnp.einsum("hgrn,nhd->rhgd", score_gradient, key_head_rows) * score_scaling
    key_gradient = (jnp.einsum("ctob,octx->bcx", score_gradient, query_head_rows) * score_scaling).reshape(-1, KEY_VALUE_HEADS * HEAD_WIDTH)
    value_gradient = jnp.einsum("ctob,octx->bcx", probability_half, gradient_head_rows).reshape(-1, KEY_VALUE_HEADS * HEAD_WIDTH)
    return query_grad.reshape(count_of_rows, -1), key_gradient[:prompt_count], value_gradient[:prompt_count], key_gradient[prompt_count:], value_gradient[prompt_count:]


def slice_rows(source, row_start, row_block):
    return lax.dynamic_slice_in_dim(source, row_start, row_block, 0)


def reference(prompt_query, prompt_k, prompt_value, prompt_output, prompt_output_gradient, reply_query, reply_key, reply_value, reply_output, reply_output_gradient, reply_len, reply_slot):
    prompt_total = prompt_query.shape[0]
    group_count = reply_query.shape[0]
    capacity = reply_query.shape[1]
    key_width = prompt_k.shape[1]
    prompt_block = min(256, prompt_total)
    reply_block = min(256, capacity)
    dummy_keys = jnp.zeros((1, key_width), prompt_k.dtype)

    def prompt_step(running, row_start):
        key_acc, value_acc = running
        row_ids = row_start + jnp.arange(prompt_block, dtype=jnp.int32)
        empty = jnp.zeros((prompt_block,), jnp.int32)
        results = attend(slice_rows(prompt_query, row_start, prompt_block), slice_rows(prompt_output_gradient, row_start, prompt_block), slice_rows(prompt_output, row_start, prompt_block), jnp.ones((prompt_block,), jnp.float32), row_ids + 1, empty, empty, prompt_k, prompt_value, dummy_keys, dummy_keys)
        return (key_acc + results[1], value_acc + results[2]), results[0]

    zero_prompt = jnp.zeros((prompt_total, key_width), jnp.float32)
    prompt_starts = jnp.arange(prompt_total // prompt_block, dtype=jnp.int32) * prompt_block
    (key_sum, value_sum), prompt_grads = lax.scan(prompt_step, (zero_prompt, zero_prompt), prompt_starts)

    def group_step(running, group_index):
        group_q = lax.dynamic_index_in_dim(reply_query, group_index, 0, keepdims=False)
        group_k = lax.dynamic_index_in_dim(reply_key, group_index, 0, keepdims=False)
        group_v = lax.dynamic_index_in_dim(reply_value, group_index, 0, keepdims=False)
        group_o = lax.dynamic_index_in_dim(reply_output, group_index, 0, keepdims=False)
        group_do = lax.dynamic_index_in_dim(reply_output_gradient, group_index, 0, keepdims=False)

        def rows_step(inner, row_start):
            key_acc, value_acc, own_key_acc, own_value_acc = inner
            row_ids = row_start + jnp.arange(reply_block, dtype=jnp.int32)
            row_phase = (row_ids % RESP_DEV).astype(jnp.int32)
            slot_ids = group_index * RESP_DEV + row_phase
            slot_length = jnp.sum(reply_len[None, :] * (reply_slot[None, :] == slot_ids[:, None]).astype(jnp.int32), axis=1)
            weight = ((row_ids // RESP_DEV) < slot_length).astype(jnp.float32)
            results = attend(slice_rows(group_q, row_start, reply_block), slice_rows(group_do, row_start, reply_block), slice_rows(group_o, row_start, reply_block), weight, jnp.full((reply_block,), prompt_total, jnp.int32), row_phase, row_ids + 1, prompt_k, prompt_value, group_k, group_v)
            return (key_acc + results[1], value_acc + results[2], own_key_acc + results[3], own_value_acc + results[4]), results[0]

        zero_own = jnp.zeros((capacity, key_width), jnp.float32)
        reply_starts = jnp.arange(capacity // reply_block, dtype=jnp.int32) * reply_block
        (key_acc, value_acc, own_key, own_value), query_blocks = lax.scan(rows_step, (running[0], running[1], zero_own, zero_own), reply_starts)
        outputs = (query_blocks.reshape(capacity, -1).astype(jnp.bfloat16), own_key.astype(jnp.bfloat16), own_value.astype(jnp.bfloat16))
        return (key_acc, value_acc), outputs

    (key_sum, value_sum), (reply_dq, reply_dk, reply_dv) = lax.scan(group_step, (key_sum, value_sum), jnp.arange(group_count, dtype=jnp.int32))
    prompt_dq = prompt_grads.reshape(prompt_total, -1).astype(jnp.bfloat16)
    return prompt_dq, key_sum.astype(jnp.bfloat16), value_sum.astype(jnp.bfloat16), reply_dq, reply_dk, reply_dv
```

```python
import functools
import math

import jax
import jax.numpy as jnp
from jax import lax
from jax.experimental import pallas as pl
from jax.experimental.pallas import tpu as pltpu
from jax.sharding import PartitionSpec as P

QUERY_HEADS = 20
KEY_VALUE_HEADS = 4
GROUP = QUERY_HEADS // KEY_VALUE_HEADS
HEAD_WIDTH = 128
RESP_DEV = 2
CORES = 2
LOCAL_HEADS = KEY_VALUE_HEADS // CORES
GROUP_WIDTH = GROUP * HEAD_WIDTH

SCALE = HEAD_WIDTH ** (-0.5)
SCALE_LOG2 = SCALE * math.log2(math.e)
NEGATIVE_FLOOR = -1e30
DEAD = 1e30
F32 = jnp.float32
BF16 = jnp.bfloat16
VMEM = pl.BlockSpec(memory_space=pltpu.VMEM)
SMEM = pl.BlockSpec(memory_space=pltpu.SMEM)


def params(mib):
    return pltpu.CompilerParams(vmem_limit_bytes=mib * 1024 * 1024)


def dot(a, b, over=(1, 0)):
    return lax.dot_general(
        a, b, (((over[0],), (over[1],)), ((), ())), preferred_element_type=F32
    )


def iota(shape, axis):
    return lax.broadcasted_iota(jnp.int32, shape, axis)


def sorting(rows):
    half = rows // RESP_DEV
    out = iota((rows, rows), 0)
    source = jnp.where(out < half, RESP_DEV * out, RESP_DEV * (out - half) + 1)
    return (iota((rows, rows), 1) == source).astype(BF16)


def unsorting(rows):
    half = rows // RESP_DEV
    out = iota((rows, rows), 1)
    source = jnp.where(out < half, RESP_DEV * out, RESP_DEV * (out - half) + 1)
    return (iota((rows, rows), 0) == source).astype(BF16)


def lanes(index, width):
    return pl.ds(pl.multiple_of(index * width, width), width)


def head_of(core, cross, local):
    owner = (1 - core) if cross else core
    return owner * LOCAL_HEADS + local


def prepare_keys(place, pk, pv, rk, rv, *outs):
    core = place[1]
    prompt = pk.shape[0]
    order = sorting(rk.shape[0])
    for local in range(LOCAL_HEADS):
        for cross in range(CORES):
            out = outs[local * CORES + cross]
            span = lanes(head_of(core, cross, local), HEAD_WIDTH)
            for part, (p, r) in enumerate(((pk, rk), (pv, rv))):
                to = slice(part * HEAD_WIDTH, (part + 1) * HEAD_WIDTH)
                out[:prompt, to] = p[:, span]
                out[prompt:, to] = dot(order, r[:, span]).astype(BF16)


def prepare_rows(place, pq, po, pg, rq, ro, rg, *outs):
    core = place[1]
    reply = rq.shape[0]
    order = sorting(reply)
    pick = (iota((8, GROUP_WIDTH), 1) // HEAD_WIDTH == iota((8, GROUP_WIDTH), 0)).astype(BF16)

    def delta(gradient, output):
        product = gradient.astype(F32) * output.astype(F32)
        high = product.astype(BF16)
        low = (product - high.astype(F32)).astype(BF16)
        return dot(pick, high, (1, 1)) + dot(pick, low, (1, 1))

    for local in range(LOCAL_HEADS):
        for cross in range(CORES):
            rows_out, delta_out = outs[2 * (local * CORES + cross) :][:2]
            span = lanes(head_of(core, cross, local), GROUP_WIDTH)
            rows_out[reply:, :GROUP_WIDTH] = pq[:, span]
            rows_out[reply:, GROUP_WIDTH:] = pg[:, span]
            rows_out[:reply, :GROUP_WIDTH] = dot(order, rq[:, span]).astype(BF16)
            gradient = dot(order, rg[:, span]).astype(BF16)
            rows_out[:reply, GROUP_WIDTH:] = gradient
            output = dot(order, ro[:, span]).astype(BF16)
            delta_out[:, :reply] = delta(gradient, output)
            delta_out[:, reply:] = delta(pg[:, span], po[:, span])


def attend(sizes, place, reply_len, reply_slot, *refs):
    chips, reply_own, prompt_own, prompt_rows, prompt_keys = sizes
    own_positions = reply_own // RESP_DEV
    positions = CORES * own_positions
    chip_prompt = CORES * prompt_keys
    block = positions
    per_chip = chip_prompt // block
    prompt_blocks = chips * per_chip
    rows_in, refs = refs[:2], refs[2:]
    delta_in, refs = refs[:2], refs[2:]
    keys_in, refs = refs[: chips * CORES], refs[chips * CORES :]
    query_out, refs = refs[:2], refs[2:]
    keys_out, refs = refs[: chips * CORES], refs[chips * CORES :]
    keys, keys_t, total, query, gradient, delta, scores, top, mass, prob, score_grad, query_grad = refs
    chip, core, group = place[0], place[1], place[2]

    for index in range(chips * CORES):
        away, other = index // CORES, index % CORES
        source = keys_in[index]
        at = away * chip_prompt + other * prompt_keys
        keys[at : at + prompt_keys] = source[:prompt_keys]
        for slot in range(RESP_DEV):
            at = prompt_blocks * block + (slot * chips + away) * positions + other * own_positions
            begin = prompt_keys + slot * own_positions
            keys[at : at + own_positions] = source[begin : begin + own_positions]
    total[...] = jnp.zeros_like(total)

    def transpose_block(index, carry):
        rows = pl.ds(pl.multiple_of(index * block, block), block)
        keys_t[index] = keys[rows, :HEAD_WIDTH].astype(F32).T.astype(BF16)
        return carry

    lax.fori_loop(0, keys_t.shape[0], transpose_block, 0)

    def score_block(region, place_in, width, chunks, hidden):
        rows = pl.ds(pl.multiple_of(region * block, block), block)
        key_rows = keys[rows, :HEAD_WIDTH]
        for chunk in range(chunks):
            span = slice(chunk * width, (chunk + 1) * width)
            value = dot(key_rows, query[span], (1, 1)) * SCALE_LOG2
            if hidden is not None:
                value = jnp.where(hidden, NEGATIVE_FLOOR, value)
            scores[place_in, :, span] = value
            split = value.reshape(block // 8, 8, width)
            before = top[:, span]
            now = jnp.maximum(before, jnp.max(split, axis=0))
            top[:, span] = now
            mass[:, span] = mass[:, span] * jnp.exp2(before - now) + jnp.sum(
                jnp.exp2(split - now[None]), axis=0
            )

    def grad_block(region, place_in, width, chunks, log_mass):
        rows = pl.ds(pl.multiple_of(region * block, block), block)
        value_rows = keys[rows, HEAD_WIDTH:]
        all_rows = width * chunks
        for chunk in range(chunks):
            span = slice(chunk * width, (chunk + 1) * width)
            p = jnp.exp2(scores[place_in, :, span] - log_mass[chunk])
            dp = dot(value_rows, gradient[span], (1, 1))
            prob[:, span] = p.astype(BF16)
            score_grad[:, span] = (p * (dp - delta[0:1, span])).astype(BF16)
        total[rows, HEAD_WIDTH:] += dot(prob[:, :all_rows], gradient[:all_rows])
        total[rows, :HEAD_WIDTH] += dot(score_grad[:, :all_rows], query[:all_rows])
        query_grad[:, :all_rows] += dot(keys_t[region], score_grad[:, :all_rows])

    def begin(all_rows):
        top[:, :all_rows] = jnp.full((8, all_rows), NEGATIVE_FLOOR, F32)
        mass[:, :all_rows] = jnp.zeros((8, all_rows), F32)
        query_grad[:, :all_rows] = jnp.zeros((HEAD_WIDTH, all_rows), F32)

    def log_masses(width, chunks, live):
        found = []
        for chunk in range(chunks):
            span = slice(chunk * width, (chunk + 1) * width)
            peak = jnp.max(top[:, span], axis=0, keepdims=True)
            summed = jnp.sum(mass[:, span] * jnp.exp2(top[:, span] - peak), axis=0, keepdims=True)
            found.append(jnp.where(live, peak + jnp.log2(summed), DEAD))
        return found

    def absolute(index, half):
        return index + jnp.where(index < half, core * half, -core * half)

    def reply_tile(slot, carry):
        length = jnp.int32(0)
        for response in range(reply_len.shape[0]):
            mine = reply_slot[response] == group * RESP_DEV + slot
            length = length + jnp.where(mine, reply_len[response], 0)
        first = chip * positions
        source = pl.ds(pl.multiple_of(slot * own_positions, own_positions), own_positions)

        @pl.when(length > first)
        def _():
            for head in range(GROUP):
                for other in range(CORES):
                    at = head * positions + other * own_positions
                    to = slice(at, at + own_positions)
                    left = slice(head * HEAD_WIDTH, (head + 1) * HEAD_WIDTH)
                    right = slice(GROUP_WIDTH + head * HEAD_WIDTH, GROUP_WIDTH + (head + 1) * HEAD_WIDTH)
                    query[to] = rows_in[other][source, left]
                    gradient[to] = rows_in[other][source, right]
                    for which in range(RESP_DEV):
                        @pl.when(slot == which)
                        def _():
                            delta[0:1, to] = delta_in[other][
                                head : head + 1, which * own_positions : (which + 1) * own_positions
                            ]
            begin(GROUP * positions)
            base = prompt_blocks + slot * chips
            past = prompt_blocks + chip

            def region_of(index):
                reply = base + ((index - prompt_blocks) ^ chip)
                return jnp.where(index < prompt_blocks, index, reply)

            def stats(index, carry):
                score_block(region_of(index), index, positions, GROUP, None)
                return carry

            lax.fori_loop(0, past, stats, 0)
            row_at = absolute(iota((1, positions), 1), own_positions)
            key_at = absolute(iota((block, 1), 0), own_positions)
            score_block(base, past, positions, GROUP, key_at > row_at)
            live = first + row_at < length
            log_mass = log_masses(positions, GROUP, live)

            def grads(index, carry):
                region = jnp.where(index == past, base, region_of(index))
                grad_block(region, index, positions, GROUP, log_mass)
                return carry

            lax.fori_loop(0, past + 1, grads, 0)
            for head in range(GROUP):
                turned = (query_grad[:, head * positions : (head + 1) * positions].T * SCALE).astype(BF16)
                for other in range(CORES):
                    query_out[other][source, head * HEAD_WIDTH : (head + 1) * HEAD_WIDTH] = turned[
                        other * own_positions : (other + 1) * own_positions
                    ]

        @pl.when(length <= first)
        def _():
            for other in range(CORES):
                query_out[other][source, :] = jnp.zeros((own_positions, GROUP_WIDTH), BF16)

        return carry

    lax.fori_loop(0, RESP_DEV, reply_tile, 0)

    head_rows = CORES * prompt_own
    used = GROUP * head_rows
    all_rows = -(-used // 128) * 128
    if all_rows > used:
        query[used:all_rows] = jnp.zeros((all_rows - used, HEAD_WIDTH), BF16)
        gradient[used:all_rows] = jnp.zeros((all_rows - used, HEAD_WIDTH), BF16)
    delta[0:1, :all_rows] = jnp.zeros((1, all_rows), F32)
    for head in range(GROUP):
        for other in range(CORES):
            at = head * head_rows + other * prompt_own
            to = slice(at, at + prompt_own)
            left = slice(head * HEAD_WIDTH, (head + 1) * HEAD_WIDTH)
            right = slice(GROUP_WIDTH + head * HEAD_WIDTH, GROUP_WIDTH + (head + 1) * HEAD_WIDTH)
            query[to] = rows_in[other][reply_own:, left]
            gradient[to] = rows_in[other][reply_own:, right]
            delta[0:1, to] = delta_in[other][head : head + 1, reply_own:]
    begin(all_rows)
    lane = iota((1, all_rows), 1)
    within = lane
    for head in range(1, GROUP):
        within = within - jnp.where(lane >= head * head_rows, head_rows, 0)
    offset = jnp.where(within < prompt_own, within, within - prompt_own)
    row_core = jnp.where(within < prompt_own, core, 1 - core)
    real = (lane < used) & (offset < prompt_rows)
    row_at = jnp.where(
        real, (chip * CORES + row_core) * prompt_keys + group * prompt_rows + offset, -1
    )
    seen = (chip + 1) * per_chip

    def prompt_region(index):
        return (index // per_chip ^ chip) * per_chip + index % per_chip

    def prompt_stats(index, carry):
        key_row = iota((block, 1), 0) + index % per_chip * block
        key_at = index // per_chip * chip_prompt + absolute(key_row, prompt_keys)
        score_block(prompt_region(index), index, all_rows, 1, key_at > row_at)
        return carry

    lax.fori_loop(0, seen, prompt_stats, 0)
    log_mass = log_masses(all_rows, 1, real)

    def prompt_grads(index, carry):
        grad_block(prompt_region(index), index, all_rows, 1, log_mass)
        return carry

    lax.fori_loop(0, seen, prompt_grads, 0)
    turned = (query_grad[:, :all_rows].T * SCALE).astype(BF16)
    for head in range(GROUP):
        for other in range(CORES):
            at = head * head_rows + other * prompt_own
            query_out[other][reply_own:, head * HEAD_WIDTH : (head + 1) * HEAD_WIDTH] = turned[
                at : at + prompt_own
            ]

    for index in range(chips * CORES):
        away, other = index // CORES, index % CORES
        out = keys_out[index]

        def put(to, at, count):
            out[to : to + count, :HEAD_WIDTH] = (total[at : at + count, :HEAD_WIDTH] * SCALE).astype(BF16)
            out[to : to + count, HEAD_WIDTH:] = total[at : at + count, HEAD_WIDTH:].astype(BF16)

        put(0, away * chip_prompt + other * prompt_keys, prompt_keys)
        for slot in range(RESP_DEV):
            at = prompt_blocks * block + (slot * chips + away) * positions + other * own_positions
            put(prompt_keys + slot * own_positions, at, own_positions)


def spread_prompt(chips, prompt_keys, place, *refs):
    parts, outs, summed = refs[: chips * CORES], refs[chips * CORES : -1], refs[-1]
    groups = len(outs)
    rows = prompt_keys // groups
    for other in range(CORES):
        value = parts[other][:prompt_keys].astype(F32)
        for away in range(1, chips):
            value = value + parts[away * CORES + other][:prompt_keys].astype(F32)
        summed[other] = value
    for shift in range(groups):
        target = lax.rem(place[2] + shift, groups)
        at = pl.ds(pl.multiple_of(target * rows, rows), rows)
        for other in range(CORES):
            outs[shift][other] = summed[other, at].astype(BF16)


def finish(chips, groups, prompt_keys, prompt_own, place, *refs):
    count = chips * CORES
    parts, refs = refs[: LOCAL_HEADS * count], refs[LOCAL_HEADS * count :]
    slices, refs = refs[: LOCAL_HEADS * groups], refs[LOCAL_HEADS * groups :]
    queries, refs = refs[: LOCAL_HEADS * CORES], refs[LOCAL_HEADS * CORES :]
    prompt_dq, prompt_dk, prompt_dv, reply_dq, reply_dk, reply_dv = refs
    core = place[1]
    reply = reply_dq.shape[0]
    order = unsorting(reply)
    for local in range(LOCAL_HEADS):
        for other in range(CORES):
            head = head_of(core, other, local)
            span = lanes(head, HEAD_WIDTH)
            value = slices[local * groups][other].astype(F32)
            for shift in range(1, groups):
                value = value + slices[local * groups + shift][other].astype(F32)
            prompt_dk[:, span] = value[:, :HEAD_WIDTH].astype(BF16)
            prompt_dv[:, span] = value[:, HEAD_WIDTH:].astype(BF16)
            value = parts[local * count + other][prompt_keys:].astype(F32)
            for away in range(1, chips):
                value = value + parts[local * count + away * CORES + other][prompt_keys:].astype(F32)
            value = dot(order, value.astype(BF16)).astype(BF16)
            reply_dk[:, span] = value[:, :HEAD_WIDTH]
            reply_dv[:, span] = value[:, HEAD_WIDTH:]
            span = lanes(head, GROUP_WIDTH)
            source = queries[local * CORES + other]
            reply_dq[:, span] = dot(order, source[:reply]).astype(BF16)
            prompt_dq[:, span] = source[reply:]


def on_device(
    prompt_query,
    prompt_k,
    prompt_value,
    prompt_output,
    prompt_output_gradient,
    reply_query,
    reply_key,
    reply_value,
    reply_output,
    reply_output_gradient,
    reply_len,
    reply_slot,
):
    devices = lax.axis_size("pre")
    groups = lax.axis_size("rsp")
    chips = devices // CORES
    prompt_rows = prompt_query.shape[0]
    prompt_own = -(-prompt_rows // 16) * 16
    prompt_keys = prompt_k.shape[0]
    reply_own = reply_query.shape[1]
    own_positions = reply_own // RESP_DEV
    positions = CORES * own_positions
    chip_prompt = CORES * prompt_keys
    assert chip_prompt % positions == 0 and chips & (chips - 1) == 0
    pre_index = lax.axis_index("pre")
    place = jnp.stack([pre_index // CORES, pre_index % CORES, lax.axis_index("rsp")]).astype(jnp.int32)

    def shape(*dims, dtype=BF16):
        return jax.ShapeDtypeStruct(dims, dtype)

    def move(array, away, cross):
        pairs = [
            (p, (p // CORES ^ away) * CORES + (p % CORES ^ cross)) for p in range(devices)
        ]
        return lax.ppermute(array, "pre", pairs)

    def exchange(same, cross):
        return [
            (same, cross)[other](away) if (away, other) == (0, 0)
            else move((same, cross)[other](away), away, other)
            for away in range(chips)
            for other in range(CORES)
        ]

    key_rows = prompt_keys + reply_own
    key_blocks = pl.pallas_call(
        prepare_keys,
        out_shape=[shape(key_rows, 2 * HEAD_WIDTH)] * KEY_VALUE_HEADS,
        in_specs=[SMEM] + [VMEM] * 4,
        out_specs=[VMEM] * KEY_VALUE_HEADS,
        compiler_params=params(32),
        name="prepare_keys",
    )(place, prompt_k, prompt_value, reply_key[0], reply_value[0])
    gathered = [
        exchange(
            lambda away: key_blocks[local * CORES], lambda away: key_blocks[local * CORES + 1]
        )
        for local in range(LOCAL_HEADS)
    ]
    if prompt_own > prompt_rows:
        room = ((0, prompt_own - prompt_rows), (0, 0))
        prompt_query, prompt_output, prompt_output_gradient = (
            jnp.pad(array, room)
            for array in (prompt_query, prompt_output, prompt_output_gradient)
        )
    own_rows = reply_own + prompt_own
    row_blocks = pl.pallas_call(
        prepare_rows,
        out_shape=[shape(own_rows, 2 * GROUP_WIDTH), shape(8, own_rows, dtype=F32)] * KEY_VALUE_HEADS,
        in_specs=[SMEM] + [VMEM] * 6,
        out_specs=[VMEM] * (2 * KEY_VALUE_HEADS),
        compiler_params=params(48),
        name="prepare_rows",
    )(
        place,
        prompt_query,
        prompt_output,
        prompt_output_gradient,
        reply_query[0],
        reply_output[0],
        reply_output_gradient[0],
    )

    blocks = chips * (chip_prompt // positions) + RESP_DEV * chips
    slots = chips * (chip_prompt // positions) + chips
    all_rows = max(GROUP * positions, -(-GROUP * CORES * prompt_own // 128) * 128)
    sizes = (chips, reply_own, prompt_own, prompt_rows, prompt_keys)
    score_count = GROUP * (positions * RESP_DEV * slots * positions)
    parts, queries, slices = [], [], []
    for local in range(LOCAL_HEADS):
        mine, mine_delta, theirs, theirs_delta = row_blocks[4 * local : 4 * local + 4]
        results = pl.pallas_call(
            functools.partial(attend, sizes),
            out_shape=[shape(own_rows, GROUP_WIDTH)] * CORES
            + [shape(key_rows, 2 * HEAD_WIDTH)] * devices,
            in_specs=[SMEM] * 3 + [VMEM] * (4 + devices),
            out_specs=[VMEM] * (CORES + devices),
            scratch_shapes=[
                pltpu.VMEM((blocks * positions, 2 * HEAD_WIDTH), BF16),
                pltpu.VMEM((blocks, HEAD_WIDTH, positions), BF16),
                pltpu.VMEM((blocks * positions, 2 * HEAD_WIDTH), F32),
                pltpu.VMEM((all_rows, HEAD_WIDTH), BF16),
                pltpu.VMEM((all_rows, HEAD_WIDTH), BF16),
                pltpu.VMEM((8, all_rows), F32),
                pltpu.VMEM((slots, positions, all_rows), F32),
                pltpu.VMEM((8, all_rows), F32),
                pltpu.VMEM((8, all_rows), F32),
                pltpu.VMEM((positions, all_rows), BF16),
                pltpu.VMEM((positions, all_rows), BF16),
                pltpu.VMEM((HEAD_WIDTH, all_rows), F32),
            ],
            compiler_params=params(48),
            cost_estimate=pl.CostEstimate(
                flops=score_count * 10 * HEAD_WIDTH,
                bytes_accessed=8 * 1024 * 1024,
                transcendentals=2 * score_count,
            ),
            name="attend",
        )(
            place,
            reply_len,
            reply_slot,
            mine,
            move(theirs, 0, 1),
            mine_delta,
            move(theirs_delta, 0, 1),
            *gathered[local],
        )
        queries += [results[0], move(results[1], 0, 1)]
        sums = results[CORES:]
        arrived = exchange(lambda away: sums[away * CORES], lambda away: sums[away * CORES + 1])
        parts += arrived
        cut = pl.pallas_call(
            functools.partial(spread_prompt, chips, prompt_keys),
            out_shape=[shape(CORES, prompt_keys // groups, 2 * HEAD_WIDTH)] * groups,
            in_specs=[SMEM] + [VMEM] * devices,
            out_specs=[VMEM] * groups,
            scratch_shapes=[pltpu.VMEM((CORES, prompt_keys, 2 * HEAD_WIDTH), F32)],
            compiler_params=params(32),
            name="spread_prompt",
        )(place, *arrived)
        slices += [cut[0]] + [
            lax.ppermute(cut[shift], "rsp", [(g, (g + shift) % groups) for g in range(groups)])
            for shift in range(1, groups)
        ]

    key_width = KEY_VALUE_HEADS * HEAD_WIDTH
    query_width = QUERY_HEADS * HEAD_WIDTH
    cut_rows = prompt_keys // groups
    prompt_dq, prompt_dk, prompt_dv, reply_dq, reply_dk, reply_dv = pl.pallas_call(
        functools.partial(finish, chips, groups, prompt_keys, prompt_own),
        out_shape=[
            shape(prompt_own, query_width),
            shape(cut_rows, key_width),
            shape(cut_rows, key_width),
            shape(reply_own, query_width),
            shape(reply_own, key_width),
            shape(reply_own, key_width),
        ],
        in_specs=[SMEM] + [VMEM] * (LOCAL_HEADS * (devices + groups + CORES)),
        out_specs=[VMEM] * 6,
        compiler_params=params(48),
        name="finish",
    )(place, *parts, *slices, *queries)
    return (
        prompt_dq[:prompt_rows],
        prompt_dk,
        prompt_dv,
        reply_dq[None],
        reply_dk[None],
        reply_dv[None],
    )


def solution(mesh):
    return jax.shard_map(
        on_device,
        mesh=mesh,
        in_specs=(
            P(("pre", "rsp"), None),
            P("pre", None),
            P("pre", None),
            P(("pre", "rsp"), None),
            P(("pre", "rsp"), None),
            P("rsp", "pre", None),
            P("rsp", "pre", None),
            P("rsp", "pre", None),
            P("rsp", "pre", None),
            P("rsp", "pre", None),
            P(),
            P(),
        ),
        out_specs=(
            P(("pre", "rsp"), None),
            P(("pre", "rsp"), None),
            P(("pre", "rsp"), None),
            P("rsp", "pre", None),
            P("rsp", "pre", None),
            P("rsp", "pre", None),
        ),
        check_vma=False,
    )
```

```python
import functools
import math

import jax
import jax.numpy as jnp
from jax import lax
from jax.experimental import pallas as pl
from jax.experimental.pallas import tpu as pltpu
from jax.sharding import PartitionSpec as P

QUERY_HEADS = 20
KEY_VALUE_HEADS = 4
GROUP = QUERY_HEADS // KEY_VALUE_HEADS
HEAD_WIDTH = 128
RESP_DEV = 2
CORES = 2
LOCAL_HEADS = KEY_VALUE_HEADS // CORES
GROUP_WIDTH = GROUP * HEAD_WIDTH

SCALE = HEAD_WIDTH ** (-0.5)
SCALE_LOG2 = SCALE * math.log2(math.e)
NEGATIVE_FLOOR = -1e30
DEAD = 1e30
F32 = jnp.float32
BF16 = jnp.bfloat16
VMEM = pl.BlockSpec(memory_space=pltpu.VMEM)
SMEM = pl.BlockSpec(memory_space=pltpu.SMEM)


VMEM_MIB = 48


def params(mib):
    return pltpu.CompilerParams(vmem_limit_bytes=mib * 1024 * 1024)


def dot(a, b, over=(1, 0)):
    return lax.dot_general(
        a, b, (((over[0],), (over[1],)), ((), ())), preferred_element_type=F32
    )


def iota(shape, axis):
    return lax.broadcasted_iota(jnp.int32, shape, axis)


def sorting(rows):
    half = rows // RESP_DEV
    out = iota((rows, rows), 0)
    source = jnp.where(out < half, RESP_DEV * out, RESP_DEV * (out - half) + 1)
    return (iota((rows, rows), 1) == source).astype(BF16)


def unsorting(rows):
    half = rows // RESP_DEV
    out = iota((rows, rows), 1)
    source = jnp.where(out < half, RESP_DEV * out, RESP_DEV * (out - half) + 1)
    return (iota((rows, rows), 0) == source).astype(BF16)


def lanes(index, width):
    return pl.ds(pl.multiple_of(index * width, width), width)


def head_of(core, cross, local):
    owner = (1 - core) if cross else core
    return owner * LOCAL_HEADS + local


def prepare_keys(place, pk, pv, rk, rv, *outs):
    prompt = pk.shape[0]
    order = sorting(rk.shape[0])
    for local in range(LOCAL_HEADS):
        out = outs[local]
        for target in range(CORES):
            head = target * LOCAL_HEADS + local
            span = slice(head * HEAD_WIDTH, (head + 1) * HEAD_WIDTH)
            for part, (p, r) in enumerate(((pk, rk), (pv, rv))):
                to = slice(part * HEAD_WIDTH, (part + 1) * HEAD_WIDTH)
                reply = dot(order, r[:, span]).astype(BF16)
                for device in range(target, out.shape[0], CORES):
                    out[device, :prompt, to] = p[:, span]
                    out[device, prompt:, to] = reply
    outs[LOCAL_HEADS][...] = jnp.zeros_like(outs[LOCAL_HEADS])


def prepare_rows(place, token, pq, po, pg, rq, ro, rg, own, other):
    reply = rq.shape[0]
    order = sorting(reply)
    column = iota((GROUP_WIDTH, HEAD_WIDTH), 1)
    pick = (column // 3 == iota((GROUP_WIDTH, HEAD_WIDTH), 0) // HEAD_WIDTH).astype(BF16)

    def delta(gradient, output):
        product = gradient.astype(F32) * output.astype(F32)
        high = product.astype(BF16)
        low = (product - high.astype(F32)).astype(BF16)
        value = dot(high, pick) + dot(low, pick)
        first = value.astype(BF16).astype(F32)
        second = (value - first).astype(BF16).astype(F32)
        part = iota(value.shape, 1) % 3
        return jnp.where(part == 0, first, jnp.where(part == 1, second, value - first - second)).astype(BF16)

    def write(out):
        out[0, reply:, :GROUP_WIDTH] = pq[...]
        out[0, reply:, GROUP_WIDTH : 2 * GROUP_WIDTH] = pg[...]
        out[0, reply:, 2 * GROUP_WIDTH :] = delta(pg[...], po[...])
        out[0, :reply, :GROUP_WIDTH] = dot(order, rq[...]).astype(BF16)
        gradient = dot(order, rg[...]).astype(BF16)
        out[0, :reply, GROUP_WIDTH : 2 * GROUP_WIDTH] = gradient
        out[0, :reply, 2 * GROUP_WIDTH :] = delta(gradient, dot(order, ro[...]).astype(BF16))

    mine = pl.program_id(0) >= LOCAL_HEADS

    @pl.when(mine)
    def _():
        write(own)

    @pl.when(jnp.logical_not(mine))
    def _():
        write(other)


def attend(sizes, place, reply_len, reply_slot, *refs):
    chips, reply_own, prompt_own, prompt_rows, prompt_keys = sizes
    own_positions = reply_own // RESP_DEV
    positions = CORES * own_positions
    chip_prompt = CORES * prompt_keys
    block = positions
    per_chip = chip_prompt // block
    prompt_blocks = chips * per_chip
    rows_in, keys_in, query_out, keys_out, refs = refs[:2], refs[2], refs[3:5], refs[5], refs[6:]
    keys, keys_t, total, query, gradient, deltas, delta, scores, top, mass, prob, score_grad, query_grad = refs
    chip, core, group = place[0], place[1], place[2]

    def device(away, other):
        return (chip ^ away) * CORES + (core ^ other)

    pick = (iota((8, HEAD_WIDTH), 1) // 3 == iota((8, HEAD_WIDTH), 0)).astype(BF16)
    for other in range(CORES):
        deltas[other] = dot(pick, rows_in[other][:, 2 * GROUP_WIDTH :], (1, 1))

    for index in range(chips * CORES):
        away, other = index // CORES, index % CORES
        source = device(away, other)
        at = away * chip_prompt + other * prompt_keys
        keys[at : at + prompt_keys] = keys_in[source, :prompt_keys]
        for slot in range(RESP_DEV):
            at = prompt_blocks * block + (slot * chips + away) * positions + other * own_positions
            begin = prompt_keys + slot * own_positions
            keys[at : at + own_positions] = keys_in[source, begin : begin + own_positions]
    total[...] = jnp.zeros_like(total)

    def transpose_block(index, carry):
        rows = pl.ds(pl.multiple_of(index * block, block), block)
        keys_t[index] = keys[rows, :HEAD_WIDTH].astype(F32).T.astype(BF16)
        return carry

    lax.fori_loop(0, keys_t.shape[0], transpose_block, 0)

    def score_block(region, place_in, width, chunks, hidden):
        rows = pl.ds(pl.multiple_of(region * block, block), block)
        key_rows = keys[rows, :HEAD_WIDTH]
        for chunk in range(chunks):
            span = slice(chunk * width, (chunk + 1) * width)
            value = dot(key_rows, query[span], (1, 1)) * SCALE_LOG2
            if hidden is not None:
                value = jnp.where(hidden, NEGATIVE_FLOOR, value)
            scores[place_in, :, span] = value
            split = value.reshape(block // 8, 8, width)
            before = top[:, span]
            now = jnp.maximum(before, jnp.max(split, axis=0))
            top[:, span] = now
            mass[:, span] = mass[:, span] * jnp.exp2(before - now) + jnp.sum(
                jnp.exp2(split - now[None]), axis=0
            )

    def grad_block(region, place_in, width, chunks, log_mass):
        rows = pl.ds(pl.multiple_of(region * block, block), block)
        value_rows = keys[rows, HEAD_WIDTH:]
        all_rows = width * chunks
        for chunk in range(chunks):
            span = slice(chunk * width, (chunk + 1) * width)
            p = jnp.exp2(scores[place_in, :, span] - log_mass[chunk])
            dp = dot(value_rows, gradient[span], (1, 1))
            prob[:, span] = p.astype(BF16)
            score_grad[:, span] = (p * (dp - delta[0:1, span])).astype(BF16)
        total[rows, HEAD_WIDTH:] += dot(prob[:, :all_rows], gradient[:all_rows])
        total[rows, :HEAD_WIDTH] += dot(score_grad[:, :all_rows], query[:all_rows])
        query_grad[:, :all_rows] += dot(keys_t[region], score_grad[:, :all_rows])

    def begin(all_rows):
        top[:, :all_rows] = jnp.full((8, all_rows), NEGATIVE_FLOOR, F32)
        mass[:, :all_rows] = jnp.zeros((8, all_rows), F32)
        query_grad[:, :all_rows] = jnp.zeros((HEAD_WIDTH, all_rows), F32)

    def log_masses(width, chunks, live):
        found = []
        for chunk in range(chunks):
            span = slice(chunk * width, (chunk + 1) * width)
            peak = jnp.max(top[:, span], axis=0, keepdims=True)
            summed = jnp.sum(mass[:, span] * jnp.exp2(top[:, span] - peak), axis=0, keepdims=True)
            found.append(jnp.where(live, peak + jnp.log2(summed), DEAD))
        return found

    def absolute(index, half):
        return index + jnp.where(index < half, core * half, -core * half)

    def reply_tile(slot, carry):
        length = jnp.int32(0)
        for response in range(reply_len.shape[0]):
            mine = reply_slot[response] == group * RESP_DEV + slot
            length = length + jnp.where(mine, reply_len[response], 0)
        first = chip * positions
        source = pl.ds(pl.multiple_of(slot * own_positions, own_positions), own_positions)

        @pl.when(length > first)
        def _():
            for head in range(GROUP):
                for other in range(CORES):
                    at = head * positions + other * own_positions
                    to = slice(at, at + own_positions)
                    left = slice(head * HEAD_WIDTH, (head + 1) * HEAD_WIDTH)
                    right = slice(GROUP_WIDTH + head * HEAD_WIDTH, GROUP_WIDTH + (head + 1) * HEAD_WIDTH)
                    query[to] = rows_in[other][source, left]
                    gradient[to] = rows_in[other][source, right]
                    for which in range(RESP_DEV):
                        @pl.when(slot == which)
                        def _():
                            delta[0:1, to] = deltas[
                                other, head : head + 1, which * own_positions : (which + 1) * own_positions
                            ]
            begin(GROUP * positions)
            base = prompt_blocks + slot * chips
            past = prompt_blocks + chip

            def region_of(index):
                reply = base + ((index - prompt_blocks) ^ chip)
                return jnp.where(index < prompt_blocks, index, reply)

            def stats(index, carry):
                score_block(region_of(index), index, positions, GROUP, None)
                return carry

            lax.fori_loop(0, past, stats, 0)
            row_at = absolute(iota((1, positions), 1), own_positions)
            key_at = absolute(iota((block, 1), 0), own_positions)
            score_block(base, past, positions, GROUP, key_at > row_at)
            live = first + row_at < length
            log_mass = log_masses(positions, GROUP, live)

            def grads(index, carry):
                region = jnp.where(index == past, base, region_of(index))
                grad_block(region, index, positions, GROUP, log_mass)
                return carry

            lax.fori_loop(0, past + 1, grads, 0)
            for head in range(GROUP):
                turned = (query_grad[:, head * positions : (head + 1) * positions].T * SCALE).astype(BF16)
                for other in range(CORES):
                    query_out[other][source, head * HEAD_WIDTH : (head + 1) * HEAD_WIDTH] = turned[
                        other * own_positions : (other + 1) * own_positions
                    ]

        @pl.when(length <= first)
        def _():
            for other in range(CORES):
                query_out[other][source, :] = jnp.zeros((own_positions, GROUP_WIDTH), BF16)

        return carry

    lax.fori_loop(0, RESP_DEV, reply_tile, 0)

    head_rows = CORES * prompt_own
    used = GROUP * head_rows
    all_rows = -(-used // 128) * 128
    if all_rows > used:
        query[used:all_rows] = jnp.zeros((all_rows - used, HEAD_WIDTH), BF16)
        gradient[used:all_rows] = jnp.zeros((all_rows - used, HEAD_WIDTH), BF16)
    delta[0:1, :all_rows] = jnp.zeros((1, all_rows), F32)
    for head in range(GROUP):
        for other in range(CORES):
            at = head * head_rows + other * prompt_own
            to = slice(at, at + prompt_own)
            left = slice(head * HEAD_WIDTH, (head + 1) * HEAD_WIDTH)
            right = slice(GROUP_WIDTH + head * HEAD_WIDTH, GROUP_WIDTH + (head + 1) * HEAD_WIDTH)
            query[to] = rows_in[other][reply_own:, left]
            gradient[to] = rows_in[other][reply_own:, right]
            delta[0:1, to] = deltas[other, head : head + 1, reply_own:]
    begin(all_rows)
    lane = iota((1, all_rows), 1)
    within = lane
    for head in range(1, GROUP):
        within = within - jnp.where(lane >= head * head_rows, head_rows, 0)
    offset = jnp.where(within < prompt_own, within, within - prompt_own)
    row_core = jnp.where(within < prompt_own, core, 1 - core)
    real = (lane < used) & (offset < prompt_rows)
    row_at = jnp.where(
        real, (chip * CORES + row_core) * prompt_keys + group * prompt_rows + offset, -1
    )
    seen = (chip + 1) * per_chip

    def prompt_region(index):
        return (index // per_chip ^ chip) * per_chip + index % per_chip

    def prompt_stats(index, carry):
        key_row = iota((block, 1), 0) + index % per_chip * block
        key_at = index // per_chip * chip_prompt + absolute(key_row, prompt_keys)
        score_block(prompt_region(index), index, all_rows, 1, key_at > row_at)
        return carry

    lax.fori_loop(0, seen, prompt_stats, 0)
    log_mass = log_masses(all_rows, 1, real)

    def prompt_grads(index, carry):
        grad_block(prompt_region(index), index, all_rows, 1, log_mass)
        return carry

    lax.fori_loop(0, seen, prompt_grads, 0)
    turned = (query_grad[:, :all_rows].T * SCALE).astype(BF16)
    for head in range(GROUP):
        for other in range(CORES):
            at = head * head_rows + other * prompt_own
            query_out[other][reply_own:, head * HEAD_WIDTH : (head + 1) * HEAD_WIDTH] = turned[
                at : at + prompt_own
            ]

    for index in range(chips * CORES):
        away, other = index // CORES, index % CORES
        out = device(away, other)

        def put(to, at, count):
            key_sum = (total[at : at + count, :HEAD_WIDTH] * SCALE).astype(BF16)
            keys_out[out, to : to + count, :HEAD_WIDTH] = key_sum
            keys_out[out, to : to + count, HEAD_WIDTH:] = total[at : at + count, HEAD_WIDTH:].astype(BF16)

        put(0, away * chip_prompt + other * prompt_keys, prompt_keys)
        for slot in range(RESP_DEV):
            at = prompt_blocks * block + (slot * chips + away) * positions + other * own_positions
            put(prompt_keys + slot * own_positions, at, own_positions)


def spread_prompt(place, parts, outs, summed):
    groups, rows = outs.shape[0], outs.shape[2]
    prompt_keys = groups * rows
    for other in range(CORES):
        source = place[1] ^ other
        value = parts[source, :prompt_keys].astype(F32)
        for chip in range(1, parts.shape[0] // CORES):
            value = value + parts[chip * CORES + source, :prompt_keys].astype(F32)
        summed[...] = value
        for target in range(groups):
            outs[target, other] = summed[target * rows : (target + 1) * rows].astype(BF16)


def finish(prompt_keys, place, *refs):
    parts, refs = refs[:LOCAL_HEADS], refs[LOCAL_HEADS:]
    slices, refs = refs[:LOCAL_HEADS], refs[LOCAL_HEADS:]
    queries, refs = refs[: LOCAL_HEADS * CORES], refs[LOCAL_HEADS * CORES :]
    prompt_dq, prompt_dk, prompt_dv, reply_dq, reply_dk, reply_dv = refs
    core = place[1]
    reply = reply_dq.shape[0]
    order = unsorting(reply)
    for local in range(LOCAL_HEADS):
        for other in range(CORES):
            head = head_of(core, other, local)
            span = lanes(head, HEAD_WIDTH)
            value = slices[local][0, other].astype(F32)
            for group in range(1, slices[local].shape[0]):
                value = value + slices[local][group, other].astype(F32)
            prompt_dk[:, span] = value[:, :HEAD_WIDTH].astype(BF16)
            prompt_dv[:, span] = value[:, HEAD_WIDTH:].astype(BF16)
            source = core ^ other
            value = parts[local][source, prompt_keys:].astype(F32)
            for chip in range(1, parts[local].shape[0] // CORES):
                value = value + parts[local][chip * CORES + source, prompt_keys:].astype(F32)
            value = dot(order, value.astype(BF16)).astype(BF16)
            reply_dk[:, span] = value[:, :HEAD_WIDTH]
            reply_dv[:, span] = value[:, HEAD_WIDTH:]
            span = lanes(head, GROUP_WIDTH)
            query = queries[local * CORES + other]
            reply_dq[:, span] = dot(order, query[:reply]).astype(BF16)
            prompt_dq[:, span] = query[reply:]


def on_device(
    prompt_query,
    prompt_k,
    prompt_value,
    prompt_output,
    prompt_output_gradient,
    reply_query,
    reply_key,
    reply_value,
    reply_output,
    reply_output_gradient,
    reply_len,
    reply_slot,
):
    devices = lax.axis_size("pre")
    groups = lax.axis_size("rsp")
    chips = devices // CORES
    prompt_rows = prompt_query.shape[0]
    prompt_own = -(-prompt_rows // 16) * 16
    prompt_keys = prompt_k.shape[0]
    reply_own = reply_query.shape[1]
    own_positions = reply_own // RESP_DEV
    positions = CORES * own_positions
    chip_prompt = CORES * prompt_keys
    assert chip_prompt % positions == 0 and chips & (chips - 1) == 0
    pre_index = lax.axis_index("pre")
    place = jnp.stack([pre_index // CORES, pre_index % CORES, lax.axis_index("rsp")]).astype(jnp.int32)

    def shape(*dims, dtype=BF16):
        return jax.ShapeDtypeStruct(dims, dtype)

    def swap(array):
        return lax.ppermute(array, "pre", [(p, p ^ 1) for p in range(devices)])

    def trade(array, axis):
        return lax.all_to_all(array, axis, 0, 0, tiled=True)

    key_rows = prompt_keys + reply_own
    *key_blocks, token = pl.pallas_call(
        prepare_keys,
        out_shape=[shape(devices, key_rows, 2 * HEAD_WIDTH)] * LOCAL_HEADS + [shape(8, 128, dtype=F32)],
        in_specs=[SMEM] + [VMEM] * 4,
        out_specs=[VMEM] * (LOCAL_HEADS + 1),
        compiler_params=params(VMEM_MIB),
        name="prepare_keys",
    )(place, prompt_k, prompt_value, reply_key[0], reply_value[0])
    gathered = [trade(block, "pre") for block in key_blocks]
    if prompt_own > prompt_rows:
        room = ((0, prompt_own - prompt_rows), (0, 0))
        prompt_query, prompt_output, prompt_output_gradient = (
            jnp.pad(array, room)
            for array in (prompt_query, prompt_output, prompt_output_gradient)
        )
    own_rows = reply_own + prompt_own
    row_width = 2 * GROUP_WIDTH + HEAD_WIDTH

    def row_head(step, place):
        core = place[1]
        owner = jnp.where(step < LOCAL_HEADS, 1 - core, core)
        return 0, owner * LOCAL_HEADS + step % LOCAL_HEADS

    mine, theirs = pl.pallas_call(
        prepare_rows,
        out_shape=[shape(LOCAL_HEADS, own_rows, row_width)] * CORES,
        grid_spec=pltpu.PrefetchScalarGridSpec(
            num_scalar_prefetch=1,
            grid=(KEY_VALUE_HEADS,),
            in_specs=[pl.BlockSpec(memory_space=pl.ANY)]
            + [pl.BlockSpec((prompt_own, GROUP_WIDTH), row_head)] * 3
            + [pl.BlockSpec((reply_own, GROUP_WIDTH), row_head)] * 3,
            out_specs=[
                pl.BlockSpec(
                    (1, own_rows, row_width),
                    lambda step, place: (jnp.maximum(step - LOCAL_HEADS, 0), 0, 0),
                ),
                pl.BlockSpec(
                    (1, own_rows, row_width),
                    lambda step, place: (jnp.minimum(step, LOCAL_HEADS - 1), 0, 0),
                ),
            ],
        ),
        compiler_params=params(VMEM_MIB),
        name="prepare_rows",
    )(
        place,
        token,
        prompt_query,
        prompt_output,
        prompt_output_gradient,
        reply_query[0],
        reply_output[0],
        reply_output_gradient[0],
    )
    theirs = swap(theirs)

    blocks = chips * (chip_prompt // positions) + RESP_DEV * chips
    slots = chips * (chip_prompt // positions) + chips
    all_rows = max(GROUP * positions, -(-GROUP * CORES * prompt_own // 128) * 128)
    sizes = (chips, reply_own, prompt_own, prompt_rows, prompt_keys)
    score_count = GROUP * (positions * RESP_DEV * slots * positions)
    parts, queries, slices = [], [], []
    for local in range(LOCAL_HEADS):
        rows_spec = pl.BlockSpec((pl.squeezed, own_rows, row_width), lambda step, local=local: (local, 0, 0))
        query_mine, query_theirs, sums = pl.pallas_call(
            functools.partial(attend, sizes),
            out_shape=[shape(own_rows, GROUP_WIDTH)] * CORES
            + [shape(devices, key_rows, 2 * HEAD_WIDTH)],
            grid=(1,),
            in_specs=[SMEM] * 3 + [rows_spec] * 2 + [VMEM],
            out_specs=[VMEM] * 3,
            scratch_shapes=[
                pltpu.VMEM((blocks * positions, 2 * HEAD_WIDTH), BF16),
                pltpu.VMEM((blocks, HEAD_WIDTH, positions), BF16),
                pltpu.VMEM((blocks * positions, 2 * HEAD_WIDTH), F32),
                pltpu.VMEM((all_rows, HEAD_WIDTH), BF16),
                pltpu.VMEM((all_rows, HEAD_WIDTH), BF16),
                pltpu.VMEM((CORES, 8, own_rows), F32),
                pltpu.VMEM((8, all_rows), F32),
                pltpu.VMEM((slots, positions, all_rows), F32),
                pltpu.VMEM((8, all_rows), F32),
                pltpu.VMEM((8, all_rows), F32),
                pltpu.VMEM((positions, all_rows), BF16),
                pltpu.VMEM((positions, all_rows), BF16),
                pltpu.VMEM((HEAD_WIDTH, all_rows), F32),
            ],
            compiler_params=params(VMEM_MIB),
            cost_estimate=pl.CostEstimate(
                flops=score_count * 10 * HEAD_WIDTH,
                bytes_accessed=8 * 1024 * 1024,
                transcendentals=2 * score_count,
            ),
            name="attend",
        )(place, reply_len, reply_slot, mine, theirs, gathered[local])
        queries += [query_mine, swap(query_theirs)]
        parts.append(trade(sums, "pre"))
        cut_shape = (groups, CORES, prompt_keys // groups, 2 * HEAD_WIDTH)
        cut = pl.pallas_call(
            spread_prompt,
            out_shape=shape(*cut_shape),
            in_specs=[SMEM, VMEM],
            out_specs=VMEM,
            scratch_shapes=[pltpu.VMEM((prompt_keys, 2 * HEAD_WIDTH), F32)],
            compiler_params=params(VMEM_MIB),
            name="spread_prompt",
        )(place, parts[-1])
        slices.append(trade(cut, "rsp"))

    key_width = KEY_VALUE_HEADS * HEAD_WIDTH
    query_width = QUERY_HEADS * HEAD_WIDTH
    cut_rows = prompt_keys // groups
    prompt_dq, prompt_dk, prompt_dv, reply_dq, reply_dk, reply_dv = pl.pallas_call(
        functools.partial(finish, prompt_keys),
        out_shape=[
            shape(prompt_own, query_width),
            shape(cut_rows, key_width),
            shape(cut_rows, key_width),
            shape(reply_own, query_width),
            shape(reply_own, key_width),
            shape(reply_own, key_width),
        ],
        in_specs=[SMEM] + [VMEM] * (LOCAL_HEADS * (2 + CORES)),
        out_specs=[VMEM] * 6,
        compiler_params=params(VMEM_MIB),
        name="finish",
    )(place, *parts, *slices, *queries)
    return (
        prompt_dq[:prompt_rows],
        prompt_dk,
        prompt_dv,
        reply_dq[None],
        reply_dk[None],
        reply_dv[None],
    )


def solution(mesh):
    return jax.shard_map(
        on_device,
        mesh=mesh,
        in_specs=(
            P(("pre", "rsp"), None),
            P("pre", None),
            P("pre", None),
            P(("pre", "rsp"), None),
            P(("pre", "rsp"), None),
            P("rsp", "pre", None),
            P("rsp", "pre", None),
            P("rsp", "pre", None),
            P("rsp", "pre", None),
            P("rsp", "pre", None),
            P(),
            P(),
        ),
        out_specs=(
            P(("pre", "rsp"), None),
            P(("pre", "rsp"), None),
            P(("pre", "rsp"), None),
            P("rsp", "pre", None),
            P("rsp", "pre", None),
            P("rsp", "pre", None),
        ),
        check_vma=False,
    )
```

```python
import functools
import math

import jax
import jax.numpy as jnp
from jax import lax
from jax.experimental import pallas as pl
from jax.experimental.pallas import tpu as pltpu
from jax.sharding import PartitionSpec as P

QUERY_HEADS = 20
KEY_VALUE_HEADS = 4
GROUP = QUERY_HEADS // KEY_VALUE_HEADS
HEAD_WIDTH = 128
RESP_DEV = 2
CORES = 2
LOCAL_HEADS = KEY_VALUE_HEADS // CORES
GROUP_WIDTH = GROUP * HEAD_WIDTH

SCALE = HEAD_WIDTH ** (-0.5)
SCALE_LOG2 = SCALE * math.log2(math.e)
NEGATIVE_FLOOR = -1e30
DEAD = 1e30
F32 = jnp.float32
BF16 = jnp.bfloat16
VMEM = pl.BlockSpec(memory_space=pltpu.VMEM)
SMEM = pl.BlockSpec(memory_space=pltpu.SMEM)


VMEM_MIB = 60


def params(mib):
    return pltpu.CompilerParams(vmem_limit_bytes=mib * 1024 * 1024)


def dot(a, b, over=(1, 0)):
    return lax.dot_general(
        a, b, (((over[0],), (over[1],)), ((), ())), preferred_element_type=F32
    )


def iota(shape, axis):
    return lax.broadcasted_iota(jnp.int32, shape, axis)


def sorting(rows):
    half = rows // RESP_DEV
    out = iota((rows, rows), 0)
    source = jnp.where(out < half, RESP_DEV * out, RESP_DEV * (out - half) + 1)
    return (iota((rows, rows), 1) == source).astype(BF16)


def unsorting(rows):
    half = rows // RESP_DEV
    out = iota((rows, rows), 1)
    source = jnp.where(out < half, RESP_DEV * out, RESP_DEV * (out - half) + 1)
    return (iota((rows, rows), 0) == source).astype(BF16)


def lanes(index, width):
    return pl.ds(pl.multiple_of(index * width, width), width)


def head_of(core, cross, local):
    owner = (1 - core) if cross else core
    return owner * LOCAL_HEADS + local


def prepare_keys(place, pk, pv, rk, rv, *outs):
    prompt = pk.shape[0]
    order = sorting(rk.shape[0])
    for local in range(LOCAL_HEADS):
        out = outs[local]
        for target in range(CORES):
            head = target * LOCAL_HEADS + local
            span = slice(head * HEAD_WIDTH, (head + 1) * HEAD_WIDTH)
            for part, (p, r) in enumerate(((pk, rk), (pv, rv))):
                to = slice(part * HEAD_WIDTH, (part + 1) * HEAD_WIDTH)
                reply = dot(order, r[:, span]).astype(BF16)
                for device in range(target, out.shape[0], CORES):
                    out[device, :prompt, to] = p[:, span]
                    out[device, prompt:, to] = reply
    outs[LOCAL_HEADS][...] = jnp.zeros_like(outs[LOCAL_HEADS])


def prepare_rows(place, token, pq, po, pg, rq, ro, rg, own, other):
    reply = rq.shape[0]
    order = sorting(reply)
    column = iota((GROUP_WIDTH, HEAD_WIDTH), 1)
    pick = (column // 3 == iota((GROUP_WIDTH, HEAD_WIDTH), 0) // HEAD_WIDTH).astype(BF16)

    def delta(gradient, output):
        product = gradient.astype(F32) * output.astype(F32)
        high = product.astype(BF16)
        low = (product - high.astype(F32)).astype(BF16)
        value = dot(high, pick) + dot(low, pick)
        first = value.astype(BF16).astype(F32)
        second = (value - first).astype(BF16).astype(F32)
        part = iota(value.shape, 1) % 3
        return jnp.where(part == 0, first, jnp.where(part == 1, second, value - first - second)).astype(BF16)

    def write(out):
        out[0, reply:, :GROUP_WIDTH] = pq[...]
        out[0, reply:, GROUP_WIDTH : 2 * GROUP_WIDTH] = pg[...]
        out[0, reply:, 2 * GROUP_WIDTH :] = delta(pg[...], po[...])
        out[0, :reply, :GROUP_WIDTH] = dot(order, rq[...]).astype(BF16)
        gradient = dot(order, rg[...]).astype(BF16)
        out[0, :reply, GROUP_WIDTH : 2 * GROUP_WIDTH] = gradient
        out[0, :reply, 2 * GROUP_WIDTH :] = delta(gradient, dot(order, ro[...]).astype(BF16))

    mine = pl.program_id(0) >= LOCAL_HEADS

    @pl.when(mine)
    def _():
        write(own)

    @pl.when(jnp.logical_not(mine))
    def _():
        write(other)


def attend(sizes, place, reply_len, reply_slot, *refs):
    chips, reply_own, prompt_own, prompt_rows, prompt_keys = sizes
    own_positions = reply_own // RESP_DEV
    positions = CORES * own_positions
    chip_prompt = CORES * prompt_keys
    block = positions
    per_chip = chip_prompt // block
    prompt_blocks = chips * per_chip
    rows_in, keys_in, query_out, reply_out, refs = refs[:2], refs[2], refs[3:5], refs[5], refs[6:]
    groups = prompt_keys // prompt_rows
    prompt_out, refs = refs[:groups], refs[groups:]
    keys, keys_t, total, query, gradient, deltas, delta, scores, top, mass, prob, score_grad, query_grad = refs
    chip, core, group = place[0], place[1], place[2]

    def device(away, other):
        return (chip ^ away) * CORES + (core ^ other)

    pick = (iota((8, HEAD_WIDTH), 1) // 3 == iota((8, HEAD_WIDTH), 0)).astype(BF16)
    for other in range(CORES):
        deltas[other] = dot(pick, rows_in[other][:, 2 * GROUP_WIDTH :], (1, 1))

    for index in range(chips * CORES):
        away, other = index // CORES, index % CORES
        source = device(away, other)
        at = away * chip_prompt + other * prompt_keys
        keys[at : at + prompt_keys] = keys_in[source, :prompt_keys]
        for slot in range(RESP_DEV):
            at = prompt_blocks * block + (slot * chips + away) * positions + other * own_positions
            begin = prompt_keys + slot * own_positions
            keys[at : at + own_positions] = keys_in[source, begin : begin + own_positions]
    total[...] = jnp.zeros_like(total)

    def transpose_block(index, carry):
        rows = pl.ds(pl.multiple_of(index * block, block), block)
        keys_t[index] = keys[rows, :HEAD_WIDTH].astype(F32).T.astype(BF16)
        return carry

    lax.fori_loop(0, keys_t.shape[0], transpose_block, 0)

    def score_block(region, place_in, width, chunks, hidden):
        rows = pl.ds(pl.multiple_of(region * block, block), block)
        key_rows = keys[rows, :HEAD_WIDTH]
        for chunk in range(chunks):
            span = slice(chunk * width, (chunk + 1) * width)
            value = dot(key_rows, query[span], (1, 1)) * SCALE_LOG2
            if hidden is not None:
                value = jnp.where(hidden, NEGATIVE_FLOOR, value)
            scores[place_in, :, span] = value
            split = value.reshape(block // 8, 8, width)
            before = top[:, span]
            now = jnp.maximum(before, jnp.max(split, axis=0))
            top[:, span] = now
            mass[:, span] = mass[:, span] * jnp.exp2(before - now) + jnp.sum(
                jnp.exp2(split - now[None]), axis=0
            )

    def grad_block(region, place_in, width, chunks, log_mass):
        rows = pl.ds(pl.multiple_of(region * block, block), block)
        value_rows = keys[rows, HEAD_WIDTH:]
        all_rows = width * chunks
        for chunk in range(chunks):
            span = slice(chunk * width, (chunk + 1) * width)
            p = jnp.exp2(scores[place_in, :, span] - log_mass[chunk])
            dp = dot(value_rows, gradient[span], (1, 1))
            prob[:, span] = p.astype(BF16)
            score_grad[:, span] = (p * (dp - delta[0:1, span])).astype(BF16)
        total[rows, HEAD_WIDTH:] += dot(prob[:, :all_rows], gradient[:all_rows])
        total[rows, :HEAD_WIDTH] += dot(score_grad[:, :all_rows], query[:all_rows])
        query_grad[:, :all_rows] += dot(keys_t[region], score_grad[:, :all_rows])

    def begin(all_rows):
        top[:, :all_rows] = jnp.full((8, all_rows), NEGATIVE_FLOOR, F32)
        mass[:, :all_rows] = jnp.zeros((8, all_rows), F32)
        query_grad[:, :all_rows] = jnp.zeros((HEAD_WIDTH, all_rows), F32)

    def log_masses(width, chunks, live):
        found = []
        for chunk in range(chunks):
            span = slice(chunk * width, (chunk + 1) * width)
            peak = jnp.max(top[:, span], axis=0, keepdims=True)
            summed = jnp.sum(mass[:, span] * jnp.exp2(top[:, span] - peak), axis=0, keepdims=True)
            found.append(jnp.where(live, peak + jnp.log2(summed), DEAD))
        return found

    def absolute(index, half):
        return index + jnp.where(index < half, core * half, -core * half)

    def reply_tile(slot, carry):
        length = jnp.int32(0)
        for response in range(reply_len.shape[0]):
            mine = reply_slot[response] == group * RESP_DEV + slot
            length = length + jnp.where(mine, reply_len[response], 0)
        first = chip * positions
        source = pl.ds(pl.multiple_of(slot * own_positions, own_positions), own_positions)

        @pl.when(length > first)
        def _():
            for head in range(GROUP):
                for other in range(CORES):
                    at = head * positions + other * own_positions
                    to = slice(at, at + own_positions)
                    left = slice(head * HEAD_WIDTH, (head + 1) * HEAD_WIDTH)
                    right = slice(GROUP_WIDTH + head * HEAD_WIDTH, GROUP_WIDTH + (head + 1) * HEAD_WIDTH)
                    query[to] = rows_in[other][source, left]
                    gradient[to] = rows_in[other][source, right]
                    for which in range(RESP_DEV):
                        @pl.when(slot == which)
                        def _():
                            delta[0:1, to] = deltas[
                                other, head : head + 1, which * own_positions : (which + 1) * own_positions
                            ]
            begin(GROUP * positions)
            base = prompt_blocks + slot * chips
            past = prompt_blocks + chip

            def region_of(index):
                reply = base + ((index - prompt_blocks) ^ chip)
                return jnp.where(index < prompt_blocks, index, reply)

            def stats(index, carry):
                score_block(region_of(index), index, positions, GROUP, None)
                return carry

            lax.fori_loop(0, past, stats, 0)
            row_at = absolute(iota((1, positions), 1), own_positions)
            key_at = absolute(iota((block, 1), 0), own_positions)
            score_block(base, past, positions, GROUP, key_at > row_at)
            live = first + row_at < length
            log_mass = log_masses(positions, GROUP, live)

            def grads(index, carry):
                region = jnp.where(index == past, base, region_of(index))
                grad_block(region, index, positions, GROUP, log_mass)
                return carry

            lax.fori_loop(0, past + 1, grads, 0)
            for head in range(GROUP):
                turned = (query_grad[:, head * positions : (head + 1) * positions].T * SCALE).astype(BF16)
                for other in range(CORES):
                    query_out[other][source, head * HEAD_WIDTH : (head + 1) * HEAD_WIDTH] = turned[
                        other * own_positions : (other + 1) * own_positions
                    ]

        @pl.when(length <= first)
        def _():
            for other in range(CORES):
                query_out[other][source, :] = jnp.zeros((own_positions, GROUP_WIDTH), BF16)

        return carry

    lax.fori_loop(0, RESP_DEV, reply_tile, 0)

    head_rows = CORES * prompt_own
    used = GROUP * head_rows
    all_rows = -(-used // 128) * 128
    if all_rows > used:
        query[used:all_rows] = jnp.zeros((all_rows - used, HEAD_WIDTH), BF16)
        gradient[used:all_rows] = jnp.zeros((all_rows - used, HEAD_WIDTH), BF16)
    delta[0:1, :all_rows] = jnp.zeros((1, all_rows), F32)
    for head in range(GROUP):
        for other in range(CORES):
            at = head * head_rows + other * prompt_own
            to = slice(at, at + prompt_own)
            left = slice(head * HEAD_WIDTH, (head + 1) * HEAD_WIDTH)
            right = slice(GROUP_WIDTH + head * HEAD_WIDTH, GROUP_WIDTH + (head + 1) * HEAD_WIDTH)
            query[to] = rows_in[other][reply_own:, left]
            gradient[to] = rows_in[other][reply_own:, right]
            delta[0:1, to] = deltas[other, head : head + 1, reply_own:]
    begin(all_rows)
    lane = iota((1, all_rows), 1)
    within = lane
    for head in range(1, GROUP):
        within = within - jnp.where(lane >= head * head_rows, head_rows, 0)
    offset = jnp.where(within < prompt_own, within, within - prompt_own)
    row_core = jnp.where(within < prompt_own, core, 1 - core)
    real = (lane < used) & (offset < prompt_rows)
    row_at = jnp.where(
        real, (chip * CORES + row_core) * prompt_keys + group * prompt_rows + offset, -1
    )
    seen = (chip + 1) * per_chip

    def prompt_region(index):
        return (index // per_chip ^ chip) * per_chip + index % per_chip

    def prompt_stats(index, carry):
        key_row = iota((block, 1), 0) + index % per_chip * block
        key_at = index // per_chip * chip_prompt + absolute(key_row, prompt_keys)
        score_block(prompt_region(index), index, all_rows, 1, key_at > row_at)
        return carry

    lax.fori_loop(0, seen, prompt_stats, 0)
    log_mass = log_masses(all_rows, 1, real)

    def prompt_grads(index, carry):
        grad_block(prompt_region(index), index, all_rows, 1, log_mass)
        return carry

    lax.fori_loop(0, seen, prompt_grads, 0)
    turned = (query_grad[:, :all_rows].T * SCALE).astype(BF16)
    for head in range(GROUP):
        for other in range(CORES):
            at = head * head_rows + other * prompt_own
            query_out[other][reply_own:, head * HEAD_WIDTH : (head + 1) * HEAD_WIDTH] = turned[
                at : at + prompt_own
            ]

    def put(out, at, count):
        out[:, :HEAD_WIDTH] = (total[pl.ds(at, count), :HEAD_WIDTH] * SCALE).astype(BF16)
        out[:, HEAD_WIDTH:] = total[pl.ds(at, count), HEAD_WIDTH:].astype(BF16)

    for index in range(chips * CORES):
        away, other = index // CORES, index % CORES
        to = device(away, other)
        for slot in range(RESP_DEV):
            at = prompt_blocks * block + (slot * chips + away) * positions + other * own_positions
            put(reply_out.at[to, slot * own_positions : (slot + 1) * own_positions], at, own_positions)
        for shift in range(groups):
            part = lax.rem(group + shift, groups) * prompt_rows
            at = pl.multiple_of(away * chip_prompt + other * prompt_keys + part, prompt_rows)
            put(prompt_out[shift].at[to], at, prompt_rows)


def add_groups(*refs):
    parts, out = refs[:-1], refs[-1]
    groups = len(parts) // LOCAL_HEADS
    for local in range(LOCAL_HEADS):
        value = parts[local * groups][...].astype(F32)
        for shift in range(1, groups):
            value = value + parts[local * groups + shift][...].astype(F32)
        out[:, local] = value.astype(BF16)


def finish(place, *refs):
    reply_sums, prompt_sums, refs = refs[:LOCAL_HEADS], refs[LOCAL_HEADS], refs[LOCAL_HEADS + 1 :]
    queries, refs = refs[: LOCAL_HEADS * CORES], refs[LOCAL_HEADS * CORES :]
    prompt_dq, prompt_dk, prompt_dv, reply_dq, reply_dk, reply_dv = refs
    core = place[1]
    reply = reply_dq.shape[0]
    order = unsorting(reply)

    def over_chips(parts, source):
        value = parts[source].astype(F32)
        for chip in range(1, parts.shape[0] // CORES):
            value = value + parts[chip * CORES + source].astype(F32)
        return value

    for local in range(LOCAL_HEADS):
        for other in range(CORES):
            head = head_of(core, other, local)
            span = lanes(head, HEAD_WIDTH)
            value = over_chips(prompt_sums.at[:, local], core ^ other)
            prompt_dk[:, span] = value[:, :HEAD_WIDTH].astype(BF16)
            prompt_dv[:, span] = value[:, HEAD_WIDTH:].astype(BF16)
            value = over_chips(reply_sums[local], core ^ other)
            value = dot(order, value.astype(BF16)).astype(BF16)
            reply_dk[:, span] = value[:, :HEAD_WIDTH]
            reply_dv[:, span] = value[:, HEAD_WIDTH:]
            span = lanes(head, GROUP_WIDTH)
            query = queries[local * CORES + other]
            reply_dq[:, span] = dot(order, query[:reply]).astype(BF16)
            prompt_dq[:, span] = query[reply:]


def on_device(
    prompt_query,
    prompt_k,
    prompt_value,
    prompt_output,
    prompt_output_gradient,
    reply_query,
    reply_key,
    reply_value,
    reply_output,
    reply_output_gradient,
    reply_len,
    reply_slot,
):
    devices = lax.axis_size("pre")
    groups = lax.axis_size("rsp")
    chips = devices // CORES
    prompt_rows = prompt_query.shape[0]
    prompt_own = -(-prompt_rows // 16) * 16
    prompt_keys = prompt_k.shape[0]
    reply_own = reply_query.shape[1]
    own_positions = reply_own // RESP_DEV
    positions = CORES * own_positions
    chip_prompt = CORES * prompt_keys
    assert chip_prompt % positions == 0 and chips & (chips - 1) == 0
    pre_index = lax.axis_index("pre")
    place = jnp.stack([lax.div(pre_index, CORES), lax.rem(pre_index, CORES), lax.axis_index("rsp")])

    def shape(*dims, dtype=BF16):
        return jax.ShapeDtypeStruct(dims, dtype)

    def swap(array):
        return lax.ppermute(array, "pre", [(p, p ^ 1) for p in range(devices)])

    def trade(array, axis):
        return lax.all_to_all(array, axis, 0, 0, tiled=True)

    key_rows = prompt_keys + reply_own
    *key_blocks, token = pl.pallas_call(
        prepare_keys,
        out_shape=[shape(devices, key_rows, 2 * HEAD_WIDTH)] * LOCAL_HEADS + [shape(8, 128, dtype=F32)],
        in_specs=[SMEM] + [VMEM] * 4,
        out_specs=[VMEM] * (LOCAL_HEADS + 1),
        compiler_params=params(VMEM_MIB),
        name="prepare_keys",
    )(place, prompt_k, prompt_value, reply_key[0], reply_value[0])
    gathered = [trade(block, "pre") for block in key_blocks]
    if prompt_own > prompt_rows:
        room = ((0, prompt_own - prompt_rows), (0, 0))
        prompt_query, prompt_output, prompt_output_gradient = (
            jnp.pad(array, room)
            for array in (prompt_query, prompt_output, prompt_output_gradient)
        )
    own_rows = reply_own + prompt_own
    row_width = 2 * GROUP_WIDTH + HEAD_WIDTH

    def row_head(step, place):
        core = place[1]
        owner = jnp.where(step < LOCAL_HEADS, 1 - core, core)
        return 0, owner * LOCAL_HEADS + step % LOCAL_HEADS

    mine, theirs = pl.pallas_call(
        prepare_rows,
        out_shape=[shape(LOCAL_HEADS, own_rows, row_width)] * CORES,
        grid_spec=pltpu.PrefetchScalarGridSpec(
            num_scalar_prefetch=1,
            grid=(KEY_VALUE_HEADS,),
            in_specs=[pl.BlockSpec(memory_space=pl.ANY)]
            + [pl.BlockSpec((prompt_own, GROUP_WIDTH), row_head)] * 3
            + [pl.BlockSpec((reply_own, GROUP_WIDTH), row_head)] * 3,
            out_specs=[
                pl.BlockSpec(
                    (1, own_rows, row_width),
                    lambda step, place: (jnp.maximum(step - LOCAL_HEADS, 0), 0, 0),
                ),
                pl.BlockSpec(
                    (1, own_rows, row_width),
                    lambda step, place: (jnp.minimum(step, LOCAL_HEADS - 1), 0, 0),
                ),
            ],
        ),
        compiler_params=params(VMEM_MIB),
        name="prepare_rows",
    )(
        place,
        token,
        prompt_query,
        prompt_output,
        prompt_output_gradient,
        reply_query[0],
        reply_output[0],
        reply_output_gradient[0],
    )
    theirs = swap(theirs)

    blocks = chips * (chip_prompt // positions) + RESP_DEV * chips
    slots = chips * (chip_prompt // positions) + chips
    all_rows = max(GROUP * positions, -(-GROUP * CORES * prompt_own // 128) * 128)
    sizes = (chips, reply_own, prompt_own, prompt_rows, prompt_keys)
    score_count = GROUP * (positions * RESP_DEV * slots * positions)
    cut_rows = prompt_keys // groups
    reply_sums, prompt_parts, queries = [], [], []
    for local in range(LOCAL_HEADS):
        rows_spec = pl.BlockSpec((pl.squeezed, own_rows, row_width), lambda step, local=local: (local, 0, 0))
        query_mine, query_theirs, sums, *cuts = pl.pallas_call(
            functools.partial(attend, sizes),
            out_shape=[shape(own_rows, GROUP_WIDTH)] * CORES
            + [shape(devices, reply_own, 2 * HEAD_WIDTH)]
            + [shape(devices, cut_rows, 2 * HEAD_WIDTH)] * groups,
            grid=(1,),
            in_specs=[SMEM] * 3 + [rows_spec] * 2 + [VMEM],
            out_specs=[VMEM] * (3 + groups),
            scratch_shapes=[
                pltpu.VMEM((blocks * positions, 2 * HEAD_WIDTH), BF16),
                pltpu.VMEM((blocks, HEAD_WIDTH, positions), BF16),
                pltpu.VMEM((blocks * positions, 2 * HEAD_WIDTH), F32),
                pltpu.VMEM((all_rows, HEAD_WIDTH), BF16),
                pltpu.VMEM((all_rows, HEAD_WIDTH), BF16),
                pltpu.VMEM((CORES, 8, own_rows), F32),
                pltpu.VMEM((8, all_rows), F32),
                pltpu.VMEM((slots, positions, all_rows), F32),
                pltpu.VMEM((8, all_rows), F32),
                pltpu.VMEM((8, all_rows), F32),
                pltpu.VMEM((positions, all_rows), BF16),
                pltpu.VMEM((positions, all_rows), BF16),
                pltpu.VMEM((HEAD_WIDTH, all_rows), F32),
            ],
            compiler_params=params(VMEM_MIB),
            cost_estimate=pl.CostEstimate(
                flops=score_count * 10 * HEAD_WIDTH,
                bytes_accessed=8 * 1024 * 1024,
                transcendentals=2 * score_count,
            ),
            name="attend",
        )(place, reply_len, reply_slot, mine, theirs, gathered[local])
        queries += [query_mine, swap(query_theirs)]
        reply_sums.append(trade(sums, "pre"))
        prompt_parts += [cuts[0]] + [
            lax.ppermute(cuts[shift], "rsp", [(g, (g + shift) % groups) for g in range(groups)])
            for shift in range(1, groups)
        ]
    prompt_sums = pl.pallas_call(
        add_groups,
        out_shape=shape(devices, LOCAL_HEADS, cut_rows, 2 * HEAD_WIDTH),
        in_specs=[VMEM] * len(prompt_parts),
        out_specs=VMEM,
        compiler_params=params(16),
        name="add_groups",
    )(*prompt_parts)
    prompt_sums = trade(prompt_sums, "pre")

    key_width = KEY_VALUE_HEADS * HEAD_WIDTH
    query_width = QUERY_HEADS * HEAD_WIDTH
    prompt_dq, prompt_dk, prompt_dv, reply_dq, reply_dk, reply_dv = pl.pallas_call(
        finish,
        out_shape=[
            shape(prompt_own, query_width),
            shape(cut_rows, key_width),
            shape(cut_rows, key_width),
            shape(reply_own, query_width),
            shape(reply_own, key_width),
            shape(reply_own, key_width),
        ],
        in_specs=[SMEM] + [VMEM] * (LOCAL_HEADS * (1 + CORES) + 1),
        out_specs=[VMEM] * 6,
        compiler_params=params(16),
        name="finish",
    )(place, *reply_sums, prompt_sums, *queries)
    return (
        prompt_dq[:prompt_rows],
        prompt_dk,
        prompt_dv,
        reply_dq[None],
        reply_dk[None],
        reply_dv[None],
    )


def solution(mesh):
    return jax.shard_map(
        on_device,
        mesh=mesh,
        in_specs=(
            P(("pre", "rsp"), None),
            P("pre", None),
            P("pre", None),
            P(("pre", "rsp"), None),
            P(("pre", "rsp"), None),
            P("rsp", "pre", None),
            P("rsp", "pre", None),
            P("rsp", "pre", None),
            P("rsp", "pre", None),
            P("rsp", "pre", None),
            P(),
            P(),
        ),
        out_specs=(
            P(("pre", "rsp"), None),
            P(("pre", "rsp"), None),
            P(("pre", "rsp"), None),
            P("rsp", "pre", None),
            P("rsp", "pre", None),
            P("rsp", "pre", None),
        ),
        check_vma=False,
    )
```

```python
import functools
import math

import jax
import jax.numpy as jnp
from jax import lax
from jax.experimental import pallas as pl
from jax.experimental.pallas import tpu as pltpu
from jax.sharding import PartitionSpec as P

QUERY_HEADS = 20
KEY_VALUE_HEADS = 4
GROUP = QUERY_HEADS // KEY_VALUE_HEADS
HEAD_WIDTH = 128
RESP_DEV = 2
CORES = 2
LOCAL_HEADS = KEY_VALUE_HEADS // CORES
GROUP_WIDTH = GROUP * HEAD_WIDTH

SCALE = HEAD_WIDTH ** (-0.5)
SCALE_LOG2 = SCALE * math.log2(math.e)
NEGATIVE_FLOOR = -1e30
DEAD = 1e30
F32 = jnp.float32
BF16 = jnp.bfloat16
VMEM = pl.BlockSpec(memory_space=pltpu.VMEM)
SMEM = pl.BlockSpec(memory_space=pltpu.SMEM)


VMEM_MIB = 40
SMALL_MIB = 24


def params(mib):
    return pltpu.CompilerParams(vmem_limit_bytes=mib * 1024 * 1024)


def dot(a, b, over=(1, 0)):
    return lax.dot_general(
        a, b, (((over[0],), (over[1],)), ((), ())), preferred_element_type=F32
    )


def iota(shape, axis):
    return lax.broadcasted_iota(jnp.int32, shape, axis)


def sorting(rows):
    half = rows // RESP_DEV
    out = iota((rows, rows), 0)
    source = jnp.where(out < half, RESP_DEV * out, RESP_DEV * (out - half) + 1)
    return (iota((rows, rows), 1) == source).astype(BF16)


def unsorting(rows):
    half = rows // RESP_DEV
    out = iota((rows, rows), 1)
    source = jnp.where(out < half, RESP_DEV * out, RESP_DEV * (out - half) + 1)
    return (iota((rows, rows), 0) == source).astype(BF16)


def lanes(index, width):
    return pl.ds(pl.multiple_of(index * width, width), width)


def head_of(core, cross, local):
    owner = (1 - core) if cross else core
    return owner * LOCAL_HEADS + local


def prepare_keys(place, pk, pv, rk, rv, mine0, theirs0, mine1, theirs, token):
    core = place[1]
    prompt = pk.shape[0]
    order = sorting(rk.shape[0])
    for local, outs in enumerate(((mine0, theirs.at[0]), (mine1, theirs.at[1]))):
        for cross, out in enumerate(outs):
            span = lanes(head_of(core, cross, local), HEAD_WIDTH)
            for part, (p, r) in enumerate(((pk, rk), (pv, rv))):
                to = slice(part * HEAD_WIDTH, (part + 1) * HEAD_WIDTH)
                out[:prompt, to] = p[:, span]
                out[prompt:, to] = dot(order, r[:, span]).astype(BF16)
    theirs0[...] = theirs[0]
    token[...] = jnp.zeros_like(token)


def prepare_rows(place, token, pq, po, pg, rq, ro, rg, *outs):
    reply = rq.shape[0]
    order = sorting(reply)
    column = iota((GROUP_WIDTH, HEAD_WIDTH), 1)
    pick = (column // 3 == iota((GROUP_WIDTH, HEAD_WIDTH), 0) // HEAD_WIDTH).astype(BF16)

    def delta(gradient, output):
        product = gradient.astype(F32) * output.astype(F32)
        high = product.astype(BF16)
        low = (product - high.astype(F32)).astype(BF16)
        value = dot(high, pick) + dot(low, pick)
        first = value.astype(BF16).astype(F32)
        second = (value - first).astype(BF16).astype(F32)
        part = iota(value.shape, 1) % 3
        return jnp.where(part == 0, first, jnp.where(part == 1, second, value - first - second)).astype(BF16)

    def write(out):
        out[reply:, :GROUP_WIDTH] = pq[...]
        out[reply:, GROUP_WIDTH : 2 * GROUP_WIDTH] = pg[...]
        out[reply:, 2 * GROUP_WIDTH :] = delta(pg[...], po[...])
        out[:reply, :GROUP_WIDTH] = dot(order, rq[...]).astype(BF16)
        gradient = dot(order, rg[...]).astype(BF16)
        out[:reply, GROUP_WIDTH : 2 * GROUP_WIDTH] = gradient
        out[:reply, 2 * GROUP_WIDTH :] = delta(gradient, dot(order, ro[...]).astype(BF16))

    for step, out in enumerate(outs):

        @pl.when(pl.program_id(0) == step)
        def _():
            write(out)


def attend(sizes, joint_keys, place, reply_len, reply_slot, *refs):
    chips, reply_own, prompt_own, prompt_rows, prompt_keys = sizes
    own_positions = reply_own // RESP_DEV
    positions = CORES * own_positions
    chip_prompt = CORES * prompt_keys
    block = positions
    per_chip = chip_prompt // block
    prompt_blocks = chips * per_chip
    rows_in, refs = refs[:2], refs[2:]
    count = chips if joint_keys else chips * CORES
    keys_in, refs = refs[:count], refs[count:]
    query_out, refs = refs[:2], refs[2:]
    count = chips * CORES if joint_keys else chips
    keys_out, refs = refs[:count], refs[count:]
    keys, keys_t, total, query, gradient, deltas, delta, scores, top, mass, prob, score_grad, query_grad = refs
    chip, core, group = place[0], place[1], place[2]

    pick = (iota((8, HEAD_WIDTH), 1) // 3 == iota((8, HEAD_WIDTH), 0)).astype(BF16)
    for other in range(CORES):
        deltas[other] = dot(pick, rows_in[other][:, 2 * GROUP_WIDTH :], (1, 1))

    for index in range(chips * CORES):
        away, other = index // CORES, index % CORES
        source = keys_in[away].at[other] if joint_keys else keys_in[index]
        source = source if len(source.shape) == 2 else source.at[0]
        at = away * chip_prompt + other * prompt_keys
        keys[at : at + prompt_keys] = source[:prompt_keys]
        for slot in range(RESP_DEV):
            at = prompt_blocks * block + (slot * chips + away) * positions + other * own_positions
            begin = prompt_keys + slot * own_positions
            keys[at : at + own_positions] = source[begin : begin + own_positions]
    total[...] = jnp.zeros_like(total)

    def transpose_block(index, carry):
        rows = pl.ds(pl.multiple_of(index * block, block), block)
        keys_t[index] = keys[rows, :HEAD_WIDTH].astype(F32).T.astype(BF16)
        return carry

    lax.fori_loop(0, keys_t.shape[0], transpose_block, 0)

    def score_block(region, place_in, width, chunks, hidden):
        rows = pl.ds(pl.multiple_of(region * block, block), block)
        key_rows = keys[rows, :HEAD_WIDTH]
        for chunk in range(chunks):
            span = slice(chunk * width, (chunk + 1) * width)
            value = dot(key_rows, query[span], (1, 1)) * SCALE_LOG2
            if hidden is not None:
                value = jnp.where(hidden, NEGATIVE_FLOOR, value)
            scores[place_in, :, span] = value
            split = value.reshape(block // 8, 8, width)
            before = top[:, span]
            now = jnp.maximum(before, jnp.max(split, axis=0))
            top[:, span] = now
            mass[:, span] = mass[:, span] * jnp.exp2(before - now) + jnp.sum(
                jnp.exp2(split - now[None]), axis=0
            )

    def grad_block(region, place_in, width, chunks, log_mass):
        rows = pl.ds(pl.multiple_of(region * block, block), block)
        value_rows = keys[rows, HEAD_WIDTH:]
        all_rows = width * chunks
        for chunk in range(chunks):
            span = slice(chunk * width, (chunk + 1) * width)
            p = jnp.exp2(scores[place_in, :, span] - log_mass[chunk])
            dp = dot(value_rows, gradient[span], (1, 1))
            prob[:, span] = p.astype(BF16)
            score_grad[:, span] = (p * (dp - delta[0:1, span])).astype(BF16)
        total[rows, HEAD_WIDTH:] += dot(prob[:, :all_rows], gradient[:all_rows])
        total[rows, :HEAD_WIDTH] += dot(score_grad[:, :all_rows], query[:all_rows])
        query_grad[:, :all_rows] += dot(keys_t[region], score_grad[:, :all_rows])

    def begin(all_rows):
        top[:, :all_rows] = jnp.full((8, all_rows), NEGATIVE_FLOOR, F32)
        mass[:, :all_rows] = jnp.zeros((8, all_rows), F32)
        query_grad[:, :all_rows] = jnp.zeros((HEAD_WIDTH, all_rows), F32)

    def log_masses(width, chunks, live):
        found = []
        for chunk in range(chunks):
            span = slice(chunk * width, (chunk + 1) * width)
            peak = jnp.max(top[:, span], axis=0, keepdims=True)
            summed = jnp.sum(mass[:, span] * jnp.exp2(top[:, span] - peak), axis=0, keepdims=True)
            found.append(jnp.where(live, peak + jnp.log2(summed), DEAD))
        return found

    def absolute(index, half):
        return index + jnp.where(index < half, core * half, -core * half)

    def reply_tile(slot, carry):
        length = jnp.int32(0)
        for response in range(reply_len.shape[0]):
            mine = reply_slot[response] == group * RESP_DEV + slot
            length = length + jnp.where(mine, reply_len[response], 0)
        first = chip * positions
        source = pl.ds(pl.multiple_of(slot * own_positions, own_positions), own_positions)

        @pl.when(length > first)
        def _():
            for head in range(GROUP):
                for other in range(CORES):
                    at = head * positions + other * own_positions
                    to = slice(at, at + own_positions)
                    left = slice(head * HEAD_WIDTH, (head + 1) * HEAD_WIDTH)
                    right = slice(GROUP_WIDTH + head * HEAD_WIDTH, GROUP_WIDTH + (head + 1) * HEAD_WIDTH)
                    query[to] = rows_in[other][source, left]
                    gradient[to] = rows_in[other][source, right]
                    for which in range(RESP_DEV):
                        @pl.when(slot == which)
                        def _():
                            delta[0:1, to] = deltas[
                                other, head : head + 1, which * own_positions : (which + 1) * own_positions
                            ]
            begin(GROUP * positions)
            base = prompt_blocks + slot * chips
            past = prompt_blocks + chip

            def region_of(index):
                reply = base + ((index - prompt_blocks) ^ chip)
                return jnp.where(index < prompt_blocks, index, reply)

            def stats(index, carry):
                score_block(region_of(index), index, positions, GROUP, None)
                return carry

            lax.fori_loop(0, past, stats, 0)
            row_at = absolute(iota((1, positions), 1), own_positions)
            key_at = absolute(iota((block, 1), 0), own_positions)
            score_block(base, past, positions, GROUP, key_at > row_at)
            live = first + row_at < length
            log_mass = log_masses(positions, GROUP, live)

            def grads(index, carry):
                region = jnp.where(index == past, base, region_of(index))
                grad_block(region, index, positions, GROUP, log_mass)
                return carry

            lax.fori_loop(0, past + 1, grads, 0)
            for head in range(GROUP):
                turned = (query_grad[:, head * positions : (head + 1) * positions].T * SCALE).astype(BF16)
                for other in range(CORES):
                    query_out[other][source, head * HEAD_WIDTH : (head + 1) * HEAD_WIDTH] = turned[
                        other * own_positions : (other + 1) * own_positions
                    ]

        @pl.when(length <= first)
        def _():
            for other in range(CORES):
                query_out[other][source, :] = jnp.zeros((own_positions, GROUP_WIDTH), BF16)

        return carry

    lax.fori_loop(0, RESP_DEV, reply_tile, 0)

    head_rows = CORES * prompt_own
    used = GROUP * head_rows
    all_rows = -(-used // 128) * 128
    if all_rows > used:
        query[used:all_rows] = jnp.zeros((all_rows - used, HEAD_WIDTH), BF16)
        gradient[used:all_rows] = jnp.zeros((all_rows - used, HEAD_WIDTH), BF16)
    delta[0:1, :all_rows] = jnp.zeros((1, all_rows), F32)
    for head in range(GROUP):
        for other in range(CORES):
            at = head * head_rows + other * prompt_own
            to = slice(at, at + prompt_own)
            left = slice(head * HEAD_WIDTH, (head + 1) * HEAD_WIDTH)
            right = slice(GROUP_WIDTH + head * HEAD_WIDTH, GROUP_WIDTH + (head + 1) * HEAD_WIDTH)
            query[to] = rows_in[other][reply_own:, left]
            gradient[to] = rows_in[other][reply_own:, right]
            delta[0:1, to] = deltas[other, head : head + 1, reply_own:]
    begin(all_rows)
    lane = iota((1, all_rows), 1)
    within = lane
    for head in range(1, GROUP):
        within = within - jnp.where(lane >= head * head_rows, head_rows, 0)
    offset = jnp.where(within < prompt_own, within, within - prompt_own)
    row_core = jnp.where(within < prompt_own, core, 1 - core)
    real = (lane < used) & (offset < prompt_rows)
    row_at = jnp.where(
        real, (chip * CORES + row_core) * prompt_keys + group * prompt_rows + offset, -1
    )
    seen = (chip + 1) * per_chip

    def prompt_region(index):
        return (index // per_chip ^ chip) * per_chip + index % per_chip

    def prompt_stats(index, carry):
        key_row = iota((block, 1), 0) + index % per_chip * block
        key_at = index // per_chip * chip_prompt + absolute(key_row, prompt_keys)
        score_block(prompt_region(index), index, all_rows, 1, key_at > row_at)
        return carry

    lax.fori_loop(0, seen, prompt_stats, 0)
    log_mass = log_masses(all_rows, 1, real)

    def prompt_grads(index, carry):
        grad_block(prompt_region(index), index, all_rows, 1, log_mass)
        return carry

    lax.fori_loop(0, seen, prompt_grads, 0)
    turned = (query_grad[:, :all_rows].T * SCALE).astype(BF16)
    for head in range(GROUP):
        for other in range(CORES):
            at = head * head_rows + other * prompt_own
            query_out[other][reply_own:, head * HEAD_WIDTH : (head + 1) * HEAD_WIDTH] = turned[
                at : at + prompt_own
            ]

    for index in range(chips * CORES):
        away, other = index // CORES, index % CORES
        out = keys_out[index] if joint_keys else keys_out[away].at[other]

        def put(to, at, count):
            out[to : to + count, :HEAD_WIDTH] = (total[at : at + count, :HEAD_WIDTH] * SCALE).astype(BF16)
            out[to : to + count, HEAD_WIDTH:] = total[at : at + count, HEAD_WIDTH:].astype(BF16)

        put(0, away * chip_prompt + other * prompt_keys, prompt_keys)
        for slot in range(RESP_DEV):
            at = prompt_blocks * block + (slot * chips + away) * positions + other * own_positions
            put(prompt_keys + slot * own_positions, at, own_positions)


def add(first, *rest):
    value = first.astype(F32)
    for part in rest:
        value = value + part.astype(F32)
    return value


def add_pairs(*refs):
    count = len(refs) // 3
    for index in range(count):
        refs[2 * count + index][...] = add(refs[index][...], refs[count + index][...]).astype(BF16)


def collect(*refs):
    parts, mine, theirs = refs[:-2], refs[-2], refs[-1]
    mine[...] = add(*(part[0] for part in parts))
    theirs[...] = add(*(part[1] for part in parts)).astype(BF16)


def spread_prompt(sizes, place, *refs):
    refs, outs, summed = refs[: sum(sizes)], refs[sum(sizes) : -1], refs[-1]
    groups, rows = len(outs), outs[0].shape[1]
    for index, size in enumerate(sizes):
        parts, refs = refs[:size], refs[size:]
        summed[index] = add(*(part[: groups * rows] for part in parts))
    for shift in range(groups):
        at = pl.ds(pl.multiple_of(lax.rem(place[2] + shift, groups) * rows, rows), rows)
        for index in range(len(sizes)):
            outs[shift][index] = summed[index, at].astype(BF16)


def finish_reply(sizes, place, *refs):
    parts_in, refs = refs[: sum(sizes)], refs[sum(sizes) :]
    queries, refs = refs[: len(sizes)], refs[len(sizes) :]
    prompt_dq, reply_dq, reply_dk, reply_dv = refs
    reply = reply_dq.shape[0]
    order = unsorting(reply)
    for index, size in enumerate(sizes):
        parts, parts_in = parts_in[:size], parts_in[size:]
        head = head_of(place[1], index % CORES, index // CORES)
        span = lanes(head, HEAD_WIDTH)
        value = add(*(part[part.shape[0] - reply :] for part in parts))
        value = dot(order, value.astype(BF16)).astype(BF16)
        reply_dk[:, span] = value[:, :HEAD_WIDTH]
        reply_dv[:, span] = value[:, HEAD_WIDTH:]
        span = lanes(head, GROUP_WIDTH)
        reply_dq[:, span] = dot(order, queries[index][:reply]).astype(BF16)
        prompt_dq[:, span] = queries[index][reply:]


def finish_prompt(place, *refs):
    parts, prompt_dk, prompt_dv = refs[:-2], refs[-2], refs[-1]
    for index in range(KEY_VALUE_HEADS):
        span = lanes(head_of(place[1], index % CORES, index // CORES), HEAD_WIDTH)
        value = add(*(part[index] for part in parts)).astype(BF16)
        prompt_dk[:, span] = value[:, :HEAD_WIDTH]
        prompt_dv[:, span] = value[:, HEAD_WIDTH:]


def on_device(
    prompt_query,
    prompt_k,
    prompt_value,
    prompt_output,
    prompt_output_gradient,
    reply_query,
    reply_key,
    reply_value,
    reply_output,
    reply_output_gradient,
    reply_len,
    reply_slot,
):
    devices = lax.axis_size("pre")
    groups = lax.axis_size("rsp")
    chips = devices // CORES
    prompt_rows = prompt_query.shape[0]
    prompt_own = -(-prompt_rows // 16) * 16
    prompt_keys = prompt_k.shape[0]
    reply_own = reply_query.shape[1]
    own_positions = reply_own // RESP_DEV
    positions = CORES * own_positions
    chip_prompt = CORES * prompt_keys
    assert chip_prompt % positions == 0 and chips & (chips - 1) == 0
    pre_index = lax.axis_index("pre")
    place = jnp.stack([lax.div(pre_index, CORES), lax.rem(pre_index, CORES), lax.axis_index("rsp")])

    def shape(*dims, dtype=BF16):
        return jax.ShapeDtypeStruct(dims, dtype)

    def move(array, away, cross=0):
        pairs = [(p, (p // CORES ^ away) * CORES + (p % CORES ^ cross)) for p in range(devices)]
        return lax.ppermute(array, "pre", pairs)

    def swap(array):
        return move(array, 0, 1)

    def call(kernel, name, mib, inputs, outs, scalars=1, **more):
        return pl.pallas_call(
            kernel,
            out_shape=outs,
            in_specs=[SMEM] * scalars + [VMEM] * (len(inputs) - scalars),
            out_specs=[VMEM] * len(outs),
            compiler_params=params(mib),
            name=name,
            **more,
        )(*inputs)

    relayed = chips == 4
    key_shape = (prompt_keys + reply_own, 2 * HEAD_WIDTH)
    mine0, theirs0, mine1, theirs, token = call(
        prepare_keys,
        "prepare_keys",
        VMEM_MIB,
        (place, prompt_k, prompt_value, reply_key[0], reply_value[0]),
        [shape(*key_shape)] * 3 + [shape(LOCAL_HEADS, *key_shape), shape(8, 128, dtype=F32)],
    )
    blocks0 = {(0, 0): mine0, (0, 1): swap(theirs)}
    for away in range(1, 3 if relayed else chips):
        blocks0[away, 0] = move(mine0, away)
        blocks0[away, 1] = move(theirs0, away, 1)
    if prompt_own > prompt_rows:
        room = ((0, prompt_own - prompt_rows), (0, 0))
        prompt_query, prompt_output, prompt_output_gradient = (
            jnp.pad(array, room)
            for array in (prompt_query, prompt_output, prompt_output_gradient)
        )
    own_rows = reply_own + prompt_own
    row_width = 2 * GROUP_WIDTH + HEAD_WIDTH

    def head_block(step, place):
        owner = jnp.where(step % CORES == 0, 1 - place[1], place[1])
        return 0, owner * LOCAL_HEADS + step // CORES

    rows = pl.pallas_call(
        prepare_rows,
        out_shape=[shape(own_rows, row_width)] * KEY_VALUE_HEADS,
        grid_spec=pltpu.PrefetchScalarGridSpec(
            num_scalar_prefetch=1,
            grid=(KEY_VALUE_HEADS,),
            in_specs=[pl.BlockSpec(memory_space=pl.ANY)]
            + [pl.BlockSpec((prompt_own, GROUP_WIDTH), head_block)] * 3
            + [pl.BlockSpec((reply_own, GROUP_WIDTH), head_block)] * 3,
            out_specs=[pl.BlockSpec((own_rows, row_width), lambda step, place: (0, 0))] * KEY_VALUE_HEADS,
        ),
        compiler_params=params(VMEM_MIB),
        cost_estimate=pl.CostEstimate(
            flops=6 * reply_own * reply_own * QUERY_HEADS * HEAD_WIDTH,
            bytes_accessed=20 * reply_own * QUERY_HEADS * HEAD_WIDTH,
            transcendentals=0,
        ),
        name="prepare_rows",
    )(
        place,
        token,
        prompt_query,
        prompt_output,
        prompt_output_gradient,
        reply_query[0],
        reply_output[0],
        reply_output_gradient[0],
    )

    blocks0, rows, mine1 = lax.optimization_barrier((blocks0, rows, mine1))
    if relayed:
        blocks0[3, 0] = move(blocks0[1, 0], 2)
        blocks0[3, 1] = move(blocks0[2, 1], 1)
    chip1 = jnp.stack([mine1, blocks0[0, 1][1]])
    blocks1 = [chip1] + [move(chip1, away) for away in range(1, chips)]

    blocks = chips * (chip_prompt // positions) + RESP_DEV * chips
    slots = chips * (chip_prompt // positions) + chips
    all_rows = max(GROUP * positions, -(-GROUP * CORES * prompt_own // 128) * 128)
    sizes = (chips, reply_own, prompt_own, prompt_rows, prompt_keys)
    score_count = GROUP * (positions * RESP_DEV * slots * positions)

    def run_attend(local, key_blocks):
        joint_keys = local == 1
        sums = [shape(*key_shape)] * devices if joint_keys else [shape(CORES, *key_shape)] * chips
        query_mine, query_theirs, *sums = call(
            functools.partial(attend, sizes, joint_keys),
            "attend",
            VMEM_MIB,
            (
                place,
                reply_len,
                reply_slot,
                rows[CORES * local + 1],
                swap(rows[CORES * local]),
                *key_blocks,
            ),
            [shape(own_rows, GROUP_WIDTH)] * CORES + sums,
            scalars=3,
            scratch_shapes=[
                pltpu.VMEM((blocks * positions, 2 * HEAD_WIDTH), BF16),
                pltpu.VMEM((blocks, HEAD_WIDTH, positions), BF16),
                pltpu.VMEM((blocks * positions, 2 * HEAD_WIDTH), F32),
                pltpu.VMEM((all_rows, HEAD_WIDTH), BF16),
                pltpu.VMEM((all_rows, HEAD_WIDTH), BF16),
                pltpu.VMEM((CORES, 8, own_rows), F32),
                pltpu.VMEM((8, all_rows), F32),
                pltpu.VMEM((slots, positions, all_rows), F32),
                pltpu.VMEM((8, all_rows), F32),
                pltpu.VMEM((8, all_rows), F32),
                pltpu.VMEM((positions, all_rows), BF16),
                pltpu.VMEM((positions, all_rows), BF16),
                pltpu.VMEM((HEAD_WIDTH, all_rows), F32),
            ],
            cost_estimate=pl.CostEstimate(
                flops=score_count * 10 * HEAD_WIDTH,
                bytes_accessed=8 * 1024 * 1024,
                transcendentals=2 * score_count,
            ),
        )
        return query_mine, query_theirs, sums

    query_mine0, query_theirs0, sums0 = run_attend(
        0, [blocks0[away, other] for away in range(chips) for other in range(CORES)]
    )
    arrived0 = [sums0[0]] + [move(sums0[away], away) for away in range(1, chips)]
    query_theirs0 = swap(query_theirs0)
    query_mine1, query_theirs1, sums1 = run_attend(1, blocks1)
    arrived0, query_theirs0, query_theirs1, sums1 = lax.optimization_barrier(
        (arrived0, query_theirs0, query_theirs1, sums1)
    )
    sums1 = [sums1[CORES * away : CORES * away + CORES] for away in range(chips)]
    if relayed:
        through_y, through_x = move(sums1[3][0], 2), move(sums1[3][1], 1)
        for_x, for_y = call(
            add_pairs,
            "add_pairs",
            SMALL_MIB,
            (sums1[1][0], sums1[2][1], through_y, through_x),
            [shape(*key_shape)] * 2,
            scalars=0,
        )
        near = [sums1[0][0], move(sums1[1][1], 1, 1), move(sums1[2][0], 2)]
        for_x, for_y, sums1[0][1], query_theirs1 = lax.optimization_barrier(
            (for_x, for_y, sums1[0][1], query_theirs1)
        )
        lists1 = [[near[0], move(for_x, 1), near[2]], [swap(sums1[0][1]), near[1], move(for_y, 2, 1)]]
    else:
        lists1 = [
            [move(pair[other], away, other) if away or other else pair[other] for away, pair in enumerate(sums1)]
            for other in range(CORES)
        ]
    mine0, theirs0 = call(
        collect,
        "collect",
        SMALL_MIB,
        arrived0,
        [shape(*key_shape, dtype=F32), shape(*key_shape)],
        scalars=0,
    )
    lists = [[mine0], [swap(theirs0)]] + lists1
    queries = [query_mine0, query_theirs0, query_mine1, swap(query_theirs1)]
    counts = [len(parts) for parts in lists]
    parts = [part for one in lists for part in one]
    cut_rows = prompt_keys // groups
    cuts = call(
        functools.partial(spread_prompt, counts),
        "spread_prompt",
        SMALL_MIB,
        (place, *parts),
        [shape(KEY_VALUE_HEADS, cut_rows, 2 * HEAD_WIDTH)] * groups,
        scratch_shapes=[pltpu.VMEM((KEY_VALUE_HEADS, prompt_keys, 2 * HEAD_WIDTH), F32)],
    )
    slices = [cuts[0]] + [
        lax.ppermute(cuts[shift], "rsp", [(g, (g + shift) % groups) for g in range(groups)])
        for shift in range(1, groups)
    ]
    key_width = KEY_VALUE_HEADS * HEAD_WIDTH
    query_width = QUERY_HEADS * HEAD_WIDTH
    prompt_dq, reply_dq, reply_dk, reply_dv = call(
        functools.partial(finish_reply, counts),
        "finish_reply",
        SMALL_MIB,
        (place, *parts, *queries),
        [
            shape(prompt_own, query_width),
            shape(reply_own, query_width),
            shape(reply_own, key_width),
            shape(reply_own, key_width),
        ],
        cost_estimate=pl.CostEstimate(
            flops=2 * reply_own * reply_own * (query_width + 2 * key_width),
            bytes_accessed=16 * reply_own * query_width,
            transcendentals=0,
        ),
    )
    slices, prompt_dq = lax.optimization_barrier((slices, prompt_dq))
    prompt_dk, prompt_dv = call(
        finish_prompt,
        "finish_prompt",
        SMALL_MIB,
        (place, *slices),
        [shape(cut_rows, key_width)] * 2,
    )
    return (
        prompt_dq[:prompt_rows],
        prompt_dk,
        prompt_dv,
        reply_dq[None],
        reply_dk[None],
        reply_dv[None],
    )


def solution(mesh):
    return jax.shard_map(
        on_device,
        mesh=mesh,
        in_specs=(
            P(("pre", "rsp"), None),
            P("pre", None),
            P("pre", None),
            P(("pre", "rsp"), None),
            P(("pre", "rsp"), None),
            P("rsp", "pre", None),
            P("rsp", "pre", None),
            P("rsp", "pre", None),
            P("rsp", "pre", None),
            P("rsp", "pre", None),
            P(),
            P(),
        ),
        out_specs=(
            P(("pre", "rsp"), None),
            P(("pre", "rsp"), None),
            P(("pre", "rsp"), None),
            P("rsp", "pre", None),
            P("rsp", "pre", None),
            P("rsp", "pre", None),
        ),
        check_vma=False,
    )
```

```python
import functools
import math

import jax
import jax.numpy as jnp
from jax import lax
from jax.experimental import pallas as pl
from jax.experimental.pallas import tpu as pltpu
from jax.sharding import PartitionSpec as P

QUERY_HEADS = 20
KEY_VALUE_HEADS = 4
GROUP = QUERY_HEADS // KEY_VALUE_HEADS
HEAD_WIDTH = 128
RESP_DEV = 2
CORES = 2
LOCAL_HEADS = KEY_VALUE_HEADS // CORES
GROUP_WIDTH = GROUP * HEAD_WIDTH

SCALE = HEAD_WIDTH ** (-0.5)
SCALE_LOG2 = SCALE * math.log2(math.e)
NEGATIVE_FLOOR = -1e30
DEAD = 1e30
F32 = jnp.float32
BF16 = jnp.bfloat16
VMEM = pl.BlockSpec(memory_space=pltpu.VMEM)
SMEM = pl.BlockSpec(memory_space=pltpu.SMEM)
HBM = pl.BlockSpec(memory_space=pltpu.HBM)


VMEM_MIB = 40
SMALL_MIB = 24
LARGE_MIB = 58


def params(mib):
    return pltpu.CompilerParams(vmem_limit_bytes=mib * 1024 * 1024)


def dot(a, b, over=(1, 0)):
    return lax.dot_general(
        a, b, (((over[0],), (over[1],)), ((), ())), preferred_element_type=F32
    )


def iota(shape, axis):
    return lax.broadcasted_iota(jnp.int32, shape, axis)


def sorting(rows):
    half = rows // RESP_DEV
    out = iota((rows, rows), 0)
    source = jnp.where(out < half, RESP_DEV * out, RESP_DEV * (out - half) + 1)
    return (iota((rows, rows), 1) == source).astype(BF16)


def unsorting(rows):
    half = rows // RESP_DEV
    out = iota((rows, rows), 1)
    source = jnp.where(out < half, RESP_DEV * out, RESP_DEV * (out - half) + 1)
    return (iota((rows, rows), 0) == source).astype(BF16)


def lanes(index, width):
    return pl.ds(pl.multiple_of(index * width, width), width)


def head_of(core, cross, local):
    owner = (1 - core) if cross else core
    return owner * LOCAL_HEADS + local


def fetch(pairs, sems):
    copies = [pltpu.make_async_copy(src, dst, sems.at[i]) for i, (src, dst) in enumerate(pairs)]
    for copy in copies:
        copy.start()
    return copies


def prepare_keys(place, pk, pv, rk, rv, mine0, theirs0, mine1, theirs, token, *scratch):
    core = place[1]
    bufs, sems = scratch[:-1], scratch[-1]
    copies = fetch(zip((pk, pv, rk, rv), bufs), sems)
    prompt = pk.shape[0]
    order = sorting(rk.shape[0])
    for copy in copies:
        copy.wait()
    pk, pv, rk, rv = bufs
    for local, outs in enumerate(((mine0, theirs.at[0]), (mine1, theirs.at[1]))):
        for cross, out in enumerate(outs):
            span = lanes(head_of(core, cross, local), HEAD_WIDTH)
            for part, (p, r) in enumerate(((pk, rk), (pv, rv))):
                to = slice(part * HEAD_WIDTH, (part + 1) * HEAD_WIDTH)
                out[:prompt, to] = p[:, span]
                out[prompt:, to] = dot(order, r[:, span]).astype(BF16)
    theirs0[...] = theirs[0]
    token[...] = jnp.zeros_like(token)


def prepare_rows(place, token, pq, po, pg, rq, ro, rg, *refs):
    outs, bufs, sems = refs[:KEY_VALUE_HEADS], refs[KEY_VALUE_HEADS:-1], refs[-1]
    core = place[1]
    reply = rq.shape[0]
    sources = (pq, po, pg, rq, ro, rg)
    pairs = []
    for step in range(KEY_VALUE_HEADS):
        span = lanes(head_of(core, 1 - step % CORES, step // CORES), GROUP_WIDTH)
        pairs += [(source.at[:, span], buf.at[step]) for source, buf in zip(sources, bufs)]
    copies = fetch(pairs, sems)
    order = sorting(reply)
    column = iota((GROUP_WIDTH, HEAD_WIDTH), 1)
    pick = (column // 3 == iota((GROUP_WIDTH, HEAD_WIDTH), 0) // HEAD_WIDTH).astype(BF16)

    def delta(gradient, output):
        product = gradient.astype(F32) * output.astype(F32)
        high = product.astype(BF16)
        low = (product - high.astype(F32)).astype(BF16)
        value = dot(high, pick) + dot(low, pick)
        first = value.astype(BF16).astype(F32)
        second = (value - first).astype(BF16).astype(F32)
        part = iota(value.shape, 1) % 3
        return jnp.where(part == 0, first, jnp.where(part == 1, second, value - first - second)).astype(BF16)

    for step, out in enumerate(outs):
        for copy in copies[step * len(sources) : (step + 1) * len(sources)]:
            copy.wait()
        pq, po, pg, rq, ro, rg = (buf[step] for buf in bufs)
        out[reply:, :GROUP_WIDTH] = pq
        out[reply:, GROUP_WIDTH : 2 * GROUP_WIDTH] = pg
        out[reply:, 2 * GROUP_WIDTH :] = delta(pg, po)
        out[:reply, :GROUP_WIDTH] = dot(order, rq).astype(BF16)
        gradient = dot(order, rg).astype(BF16)
        out[:reply, GROUP_WIDTH : 2 * GROUP_WIDTH] = gradient
        out[:reply, 2 * GROUP_WIDTH :] = delta(gradient, dot(order, ro).astype(BF16))


def attend(sizes, joint_keys, place, reply_len, reply_slot, *refs):
    chips, reply_own, prompt_own, prompt_rows, prompt_keys = sizes
    own_positions = reply_own // RESP_DEV
    positions = CORES * own_positions
    chip_prompt = CORES * prompt_keys
    block = positions
    per_chip = chip_prompt // block
    prompt_blocks = chips * per_chip
    rows_in, refs = refs[:2], refs[2:]
    count = chips if joint_keys else chips * CORES
    keys_in, refs = refs[:count], refs[count:]
    query_out, refs = refs[:2], refs[2:]
    count = chips * CORES if joint_keys else chips
    keys_out, refs = refs[:count], refs[count:]
    keys, keys_t, total, query, gradient, deltas, delta, scores, top, mass, query_grad = refs
    chip, core, group = place[0], place[1], place[2]

    pick = (iota((8, HEAD_WIDTH), 1) // 3 == iota((8, HEAD_WIDTH), 0)).astype(BF16)
    for other in range(CORES):
        deltas[other] = dot(pick, rows_in[other][:, 2 * GROUP_WIDTH :], (1, 1))

    for index in range(chips * CORES):
        away, other = index // CORES, index % CORES
        source = keys_in[away].at[other] if joint_keys else keys_in[index]
        source = source if len(source.shape) == 2 else source.at[0]
        at = away * chip_prompt + other * prompt_keys
        keys[at : at + prompt_keys] = source[:prompt_keys]
        for slot in range(RESP_DEV):
            at = prompt_blocks * block + (slot * chips + away) * positions + other * own_positions
            begin = prompt_keys + slot * own_positions
            keys[at : at + own_positions] = source[begin : begin + own_positions]
    total[...] = jnp.zeros_like(total)

    unit = (iota((HEAD_WIDTH, HEAD_WIDTH), 0) == iota((HEAD_WIDTH, HEAD_WIDTH), 1)).astype(BF16)

    def transpose_block(index, carry):
        rows = pl.ds(pl.multiple_of(index * block, block), block)
        keys_t[index] = dot(unit, keys[rows, :HEAD_WIDTH], (1, 1)).astype(BF16)
        return carry

    lax.fori_loop(0, keys_t.shape[0], transpose_block, 0)

    def score_block(region, place_in, width, chunks, hidden):
        rows = pl.ds(pl.multiple_of(region * block, block), block)
        key_rows = keys[rows, :HEAD_WIDTH]
        for chunk in range(chunks):
            span = slice(chunk * width, (chunk + 1) * width)
            value = dot(key_rows, query[span], (1, 1)) * SCALE_LOG2
            if hidden is not None:
                value = jnp.where(hidden, NEGATIVE_FLOOR, value)
            scores[place_in, :, span] = value
            split = value.reshape(block // 8, 8, width)
            before = top[:, span]
            now = jnp.maximum(before, jnp.max(split, axis=0))
            top[:, span] = now
            mass[:, span] = mass[:, span] * jnp.exp2(before - now) + jnp.sum(
                jnp.exp2(split - now[None]), axis=0
            )

    def grad_block(region, place_in, width, chunks, log_mass):
        rows = pl.ds(pl.multiple_of(region * block, block), block)
        value_rows = keys[rows, HEAD_WIDTH:]
        turned = keys_t[region]
        value_sum = key_sum = None
        for chunk in range(chunks):
            span = slice(chunk * width, (chunk + 1) * width)
            p = jnp.exp2(scores[place_in, :, span] - log_mass[chunk])
            dp = dot(value_rows, gradient[span], (1, 1))
            half = (p * (dp - delta[0:1, span])).astype(BF16)
            by_value = dot(p.astype(BF16), gradient[span])
            by_key = dot(half, query[span])
            value_sum = by_value if chunk == 0 else value_sum + by_value
            key_sum = by_key if chunk == 0 else key_sum + by_key
            query_grad[:, span] += dot(turned, half)
        total[rows, HEAD_WIDTH:] += value_sum
        total[rows, :HEAD_WIDTH] += key_sum

    def begin(all_rows):
        top[:, :all_rows] = jnp.full((8, all_rows), NEGATIVE_FLOOR, F32)
        mass[:, :all_rows] = jnp.zeros((8, all_rows), F32)
        query_grad[:, :all_rows] = jnp.zeros((HEAD_WIDTH, all_rows), F32)

    def log_masses(width, chunks, live):
        found = []
        for chunk in range(chunks):
            span = slice(chunk * width, (chunk + 1) * width)
            peak = jnp.max(top[:, span], axis=0, keepdims=True)
            summed = jnp.sum(mass[:, span] * jnp.exp2(top[:, span] - peak), axis=0, keepdims=True)
            found.append(jnp.where(live, peak + jnp.log2(summed), DEAD))
        return found

    def absolute(index, half):
        return index + jnp.where(index < half, core * half, -core * half)

    def reply_tile(slot, carry):
        length = jnp.int32(0)
        for response in range(reply_len.shape[0]):
            mine = reply_slot[response] == group * RESP_DEV + slot
            length = length + jnp.where(mine, reply_len[response], 0)
        first = chip * positions
        source = pl.ds(pl.multiple_of(slot * own_positions, own_positions), own_positions)

        @pl.when(length > first)
        def _():
            for head in range(GROUP):
                for other in range(CORES):
                    at = head * positions + other * own_positions
                    to = slice(at, at + own_positions)
                    left = slice(head * HEAD_WIDTH, (head + 1) * HEAD_WIDTH)
                    right = slice(GROUP_WIDTH + head * HEAD_WIDTH, GROUP_WIDTH + (head + 1) * HEAD_WIDTH)
                    query[to] = rows_in[other][source, left]
                    gradient[to] = rows_in[other][source, right]
                    for which in range(RESP_DEV):
                        @pl.when(slot == which)
                        def _():
                            delta[0:1, to] = deltas[
                                other, head : head + 1, which * own_positions : (which + 1) * own_positions
                            ]
            begin(GROUP * positions)
            base = prompt_blocks + slot * chips
            past = prompt_blocks + chip

            def region_of(index):
                reply = base + ((index - prompt_blocks) ^ chip)
                return jnp.where(index < prompt_blocks, index, reply)

            def stats(index, carry):
                score_block(region_of(index), index, positions, GROUP, None)
                return carry

            def two_stats(index, carry):
                stats(2 * index, carry)
                return stats(2 * index + 1, carry)

            lax.fori_loop(0, past // 2, two_stats, 0)
            lax.fori_loop(past // 2 * 2, past, stats, 0)
            row_at = absolute(iota((1, positions), 1), own_positions)
            key_at = absolute(iota((block, 1), 0), own_positions)
            score_block(base, past, positions, GROUP, key_at > row_at)
            live = first + row_at < length
            log_mass = log_masses(positions, GROUP, live)

            def grads(index, carry):
                region = jnp.where(index == past, base, region_of(index))
                grad_block(region, index, positions, GROUP, log_mass)
                return carry

            def two_grads(index, carry):
                grads(2 * index, carry)
                return grads(2 * index + 1, carry)

            every = past + 1
            lax.fori_loop(0, every // 2, two_grads, 0)
            lax.fori_loop(every // 2 * 2, every, grads, 0)
            for head in range(GROUP):
                turned = (query_grad[:, head * positions : (head + 1) * positions].T * SCALE).astype(BF16)
                for other in range(CORES):
                    query_out[other][source, head * HEAD_WIDTH : (head + 1) * HEAD_WIDTH] = turned[
                        other * own_positions : (other + 1) * own_positions
                    ]

        @pl.when(length <= first)
        def _():
            for other in range(CORES):
                query_out[other][source, :] = jnp.zeros((own_positions, GROUP_WIDTH), BF16)

        return carry

    lax.fori_loop(0, RESP_DEV, reply_tile, 0)

    head_rows = CORES * prompt_own
    used = GROUP * head_rows
    all_rows = -(-used // 128) * 128
    if all_rows > used:
        query[used:all_rows] = jnp.zeros((all_rows - used, HEAD_WIDTH), BF16)
        gradient[used:all_rows] = jnp.zeros((all_rows - used, HEAD_WIDTH), BF16)
    delta[0:1, :all_rows] = jnp.zeros((1, all_rows), F32)
    for head in range(GROUP):
        for other in range(CORES):
            at = head * head_rows + other * prompt_own
            to = slice(at, at + prompt_own)
            left = slice(head * HEAD_WIDTH, (head + 1) * HEAD_WIDTH)
            right = slice(GROUP_WIDTH + head * HEAD_WIDTH, GROUP_WIDTH + (head + 1) * HEAD_WIDTH)
            query[to] = rows_in[other][reply_own:, left]
            gradient[to] = rows_in[other][reply_own:, right]
            delta[0:1, to] = deltas[other, head : head + 1, reply_own:]
    begin(all_rows)
    lane = iota((1, all_rows), 1)
    within = lane
    for head in range(1, GROUP):
        within = within - jnp.where(lane >= head * head_rows, head_rows, 0)
    offset = jnp.where(within < prompt_own, within, within - prompt_own)
    row_core = jnp.where(within < prompt_own, core, 1 - core)
    real = (lane < used) & (offset < prompt_rows)
    row_at = jnp.where(
        real, (chip * CORES + row_core) * prompt_keys + group * prompt_rows + offset, -1
    )
    seen = (chip + 1) * per_chip

    def prompt_region(index):
        return (index // per_chip ^ chip) * per_chip + index % per_chip

    def prompt_stats(index, carry):
        key_row = iota((block, 1), 0) + index % per_chip * block
        key_at = index // per_chip * chip_prompt + absolute(key_row, prompt_keys)
        score_block(prompt_region(index), index, all_rows, 1, key_at > row_at)
        return carry

    lax.fori_loop(0, seen, prompt_stats, 0)
    log_mass = log_masses(all_rows, 1, real)

    def prompt_grads(index, carry):
        grad_block(prompt_region(index), index, all_rows, 1, log_mass)
        return carry

    lax.fori_loop(0, seen, prompt_grads, 0)
    turned = (query_grad[:, :all_rows].T * SCALE).astype(BF16)
    for head in range(GROUP):
        for other in range(CORES):
            at = head * head_rows + other * prompt_own
            query_out[other][reply_own:, head * HEAD_WIDTH : (head + 1) * HEAD_WIDTH] = turned[
                at : at + prompt_own
            ]

    for index in range(chips * CORES):
        away, other = index // CORES, index % CORES
        out = keys_out[index] if joint_keys else keys_out[away].at[other]

        def put(to, at, count):
            out[to : to + count, :HEAD_WIDTH] = (total[at : at + count, :HEAD_WIDTH] * SCALE).astype(BF16)
            out[to : to + count, HEAD_WIDTH:] = total[at : at + count, HEAD_WIDTH:].astype(BF16)

        put(0, away * chip_prompt + other * prompt_keys, prompt_keys)
        for slot in range(RESP_DEV):
            at = prompt_blocks * block + (slot * chips + away) * positions + other * own_positions
            put(prompt_keys + slot * own_positions, at, own_positions)


def add(first, *rest):
    value = first.astype(F32)
    for part in rest:
        value = value + part.astype(F32)
    return value


def add_pairs(*refs):
    count = len(refs) // 3
    for index in range(count):
        refs[2 * count + index][...] = add(refs[index][...], refs[count + index][...]).astype(BF16)


def collect(*refs):
    parts, mine, theirs = refs[:-2], refs[-2], refs[-1]
    mine[...] = add(*(part[0] for part in parts))
    theirs[...] = add(*(part[1] for part in parts)).astype(BF16)


def spread_prompt(sizes, place, *refs):
    refs, outs, summed = refs[: sum(sizes)], refs[sum(sizes) : -1], refs[-1]
    groups, rows = len(outs), outs[0].shape[1]
    for index, size in enumerate(sizes):
        parts, refs = refs[:size], refs[size:]
        summed[index] = add(*(part[: groups * rows] for part in parts))
    for shift in range(groups):
        at = pl.ds(pl.multiple_of(lax.rem(place[2] + shift, groups) * rows, rows), rows)
        for index in range(len(sizes)):
            outs[shift][index] = summed[index, at].astype(BF16)


def finish_reply(sizes, place, *refs):
    parts_in, refs = refs[: sum(sizes)], refs[sum(sizes) :]
    queries, refs = refs[: len(sizes)], refs[len(sizes) :]
    prompt_dq, reply_dq, reply_dk, reply_dv = refs
    reply = reply_dq.shape[0]
    order = unsorting(reply)
    for index, size in enumerate(sizes):
        parts, parts_in = parts_in[:size], parts_in[size:]
        head = head_of(place[1], index % CORES, index // CORES)
        span = lanes(head, HEAD_WIDTH)
        value = add(*(part[part.shape[0] - reply :] for part in parts))
        value = dot(order, value.astype(BF16)).astype(BF16)
        reply_dk[:, span] = value[:, :HEAD_WIDTH]
        reply_dv[:, span] = value[:, HEAD_WIDTH:]
        span = lanes(head, GROUP_WIDTH)
        reply_dq[:, span] = dot(order, queries[index][:reply]).astype(BF16)
        prompt_dq[:, span] = queries[index][reply:]


def finish_prompt(place, *refs):
    parts, prompt_dk, prompt_dv = refs[:-2], refs[-2], refs[-1]
    for index in range(KEY_VALUE_HEADS):
        span = lanes(head_of(place[1], index % CORES, index // CORES), HEAD_WIDTH)
        value = add(*(part[index] for part in parts)).astype(BF16)
        prompt_dk[:, span] = value[:, :HEAD_WIDTH]
        prompt_dv[:, span] = value[:, HEAD_WIDTH:]


def on_device(
    prompt_query,
    prompt_k,
    prompt_value,
    prompt_output,
    prompt_output_gradient,
    reply_query,
    reply_key,
    reply_value,
    reply_output,
    reply_output_gradient,
    reply_len,
    reply_slot,
):
    devices = lax.axis_size("pre")
    groups = lax.axis_size("rsp")
    chips = devices // CORES
    prompt_rows = prompt_query.shape[0]
    prompt_own = -(-prompt_rows // 16) * 16
    prompt_keys = prompt_k.shape[0]
    reply_own = reply_query.shape[1]
    own_positions = reply_own // RESP_DEV
    positions = CORES * own_positions
    chip_prompt = CORES * prompt_keys
    assert chip_prompt % positions == 0 and chips & (chips - 1) == 0
    pre_index = lax.axis_index("pre")
    place = jnp.stack([lax.div(pre_index, CORES), lax.rem(pre_index, CORES), lax.axis_index("rsp")])

    def shape(*dims, dtype=BF16):
        return jax.ShapeDtypeStruct(dims, dtype)

    def move(array, away, cross=0):
        pairs = [(p, (p // CORES ^ away) * CORES + (p % CORES ^ cross)) for p in range(devices)]
        return lax.ppermute(array, "pre", pairs)

    def swap(array):
        return move(array, 0, 1)

    def call(kernel, name, mib, inputs, outs, scalars=1, spec=VMEM, **more):
        return pl.pallas_call(
            kernel,
            out_shape=outs,
            in_specs=[SMEM] * scalars + [spec] * (len(inputs) - scalars),
            out_specs=[VMEM] * len(outs),
            compiler_params=params(mib),
            name=name,
            **more,
        )(*inputs)

    relayed = chips == 4
    key_shape = (prompt_keys + reply_own, 2 * HEAD_WIDTH)
    mine0, theirs0, mine1, theirs, token = call(
        prepare_keys,
        "prepare_keys",
        LARGE_MIB,
        (place, prompt_k, prompt_value, reply_key[0], reply_value[0]),
        [shape(*key_shape)] * 3 + [shape(LOCAL_HEADS, *key_shape), shape(8, 128, dtype=F32)],
        spec=HBM,
        scratch_shapes=[
            pltpu.VMEM((rows, KEY_VALUE_HEADS * HEAD_WIDTH), BF16)
            for rows in (prompt_keys, prompt_keys, reply_own, reply_own)
        ]
        + [pltpu.SemaphoreType.DMA((4,))],
    )
    blocks0 = {(0, 0): mine0, (0, 1): swap(theirs)}
    for away in range(1, 3 if relayed else chips):
        blocks0[away, 0] = move(mine0, away)
        blocks0[away, 1] = move(theirs0, away, 1)
    if prompt_own > prompt_rows:
        room = ((0, prompt_own - prompt_rows), (0, 0))
        prompt_query, prompt_output, prompt_output_gradient = (
            jnp.pad(array, room)
            for array in (prompt_query, prompt_output, prompt_output_gradient)
        )
    own_rows = reply_own + prompt_own
    row_width = 2 * GROUP_WIDTH + HEAD_WIDTH

    rows = call(
        prepare_rows,
        "prepare_rows",
        LARGE_MIB,
        (
            place,
            token,
            prompt_query,
            prompt_output,
            prompt_output_gradient,
            reply_query[0],
            reply_output[0],
            reply_output_gradient[0],
        ),
        [shape(own_rows, row_width)] * KEY_VALUE_HEADS,
        spec=HBM,
        scratch_shapes=[
            pltpu.VMEM((KEY_VALUE_HEADS, rows, GROUP_WIDTH), BF16)
            for rows in [prompt_own] * 3 + [reply_own] * 3
        ]
        + [pltpu.SemaphoreType.DMA((KEY_VALUE_HEADS * 6,))],
        cost_estimate=pl.CostEstimate(
            flops=6 * reply_own * reply_own * QUERY_HEADS * HEAD_WIDTH,
            bytes_accessed=20 * reply_own * QUERY_HEADS * HEAD_WIDTH,
            transcendentals=0,
        ),
    )

    blocks0, rows, mine1 = lax.optimization_barrier((blocks0, rows, mine1))
    if relayed:
        blocks0[3, 0] = move(blocks0[1, 0], 2)
        blocks0[3, 1] = move(blocks0[2, 1], 1)
    chip1 = jnp.stack([mine1, blocks0[0, 1][1]])
    blocks1 = [chip1] + [move(chip1, away) for away in range(1, chips)]

    blocks = chips * (chip_prompt // positions) + RESP_DEV * chips
    slots = chips * (chip_prompt // positions) + chips
    all_rows = max(GROUP * positions, -(-GROUP * CORES * prompt_own // 128) * 128)
    sizes = (chips, reply_own, prompt_own, prompt_rows, prompt_keys)
    score_count = GROUP * (positions * RESP_DEV * slots * positions)

    def run_attend(local, key_blocks):
        joint_keys = local == 1
        sums = [shape(*key_shape)] * devices if joint_keys else [shape(CORES, *key_shape)] * chips
        query_mine, query_theirs, *sums = call(
            functools.partial(attend, sizes, joint_keys),
            "attend",
            VMEM_MIB,
            (
                place,
                reply_len,
                reply_slot,
                rows[CORES * local + 1],
                swap(rows[CORES * local]),
                *key_blocks,
            ),
            [shape(own_rows, GROUP_WIDTH)] * CORES + sums,
            scalars=3,
            scratch_shapes=[
                pltpu.VMEM((blocks * positions, 2 * HEAD_WIDTH), BF16),
                pltpu.VMEM((blocks, HEAD_WIDTH, positions), BF16),
                pltpu.VMEM((blocks * positions, 2 * HEAD_WIDTH), F32),
                pltpu.VMEM((all_rows, HEAD_WIDTH), BF16),
                pltpu.VMEM((all_rows, HEAD_WIDTH), BF16),
                pltpu.VMEM((CORES, 8, own_rows), F32),
                pltpu.VMEM((8, all_rows), F32),
                pltpu.VMEM((slots, positions, all_rows), F32),
                pltpu.VMEM((8, all_rows), F32),
                pltpu.VMEM((8, all_rows), F32),
                pltpu.VMEM((HEAD_WIDTH, all_rows), F32),
            ],
            cost_estimate=pl.CostEstimate(
                flops=score_count * 10 * HEAD_WIDTH,
                bytes_accessed=8 * 1024 * 1024,
                transcendentals=2 * score_count,
            ),
        )
        return query_mine, query_theirs, sums

    query_mine0, query_theirs0, sums0 = run_attend(
        0, [blocks0[away, other] for away in range(chips) for other in range(CORES)]
    )
    arrived0 = [sums0[0]] + [move(sums0[away], away) for away in range(1, chips)]
    query_theirs0 = swap(query_theirs0)
    query_mine1, query_theirs1, sums1 = run_attend(1, blocks1)
    arrived0, query_theirs0, query_theirs1, sums1 = lax.optimization_barrier(
        (arrived0, query_theirs0, query_theirs1, sums1)
    )
    sums1 = [sums1[CORES * away : CORES * away + CORES] for away in range(chips)]
    if relayed:
        through_y, through_x = move(sums1[3][0], 2), move(sums1[3][1], 1)
        for_x, for_y = call(
            add_pairs,
            "add_pairs",
            SMALL_MIB,
            (sums1[1][0], sums1[2][1], through_y, through_x),
            [shape(*key_shape)] * 2,
            scalars=0,
        )
        near = [sums1[0][0], move(sums1[1][1], 1, 1), move(sums1[2][0], 2)]
        for_x, for_y, sums1[0][1], query_theirs1 = lax.optimization_barrier(
            (for_x, for_y, sums1[0][1], query_theirs1)
        )
        lists1 = [[near[0], move(for_x, 1), near[2]], [swap(sums1[0][1]), near[1], move(for_y, 2, 1)]]
    else:
        lists1 = [
            [move(pair[other], away, other) if away or other else pair[other] for away, pair in enumerate(sums1)]
            for other in range(CORES)
        ]
    mine0, theirs0 = call(
        collect,
        "collect",
        SMALL_MIB,
        arrived0,
        [shape(*key_shape, dtype=F32), shape(*key_shape)],
        scalars=0,
    )
    lists = [[mine0], [swap(theirs0)]] + lists1
    queries = [query_mine0, query_theirs0, query_mine1, swap(query_theirs1)]
    counts = [len(parts) for parts in lists]
    parts = [part for one in lists for part in one]
    cut_rows = prompt_keys // groups
    cuts = call(
        functools.partial(spread_prompt, counts),
        "spread_prompt",
        SMALL_MIB,
        (place, *parts),
        [shape(KEY_VALUE_HEADS, cut_rows, 2 * HEAD_WIDTH)] * groups,
        scratch_shapes=[pltpu.VMEM((KEY_VALUE_HEADS, prompt_keys, 2 * HEAD_WIDTH), F32)],
    )
    slices = [cuts[0]] + [
        lax.ppermute(cuts[shift], "rsp", [(g, (g + shift) % groups) for g in range(groups)])
        for shift in range(1, groups)
    ]
    key_width = KEY_VALUE_HEADS * HEAD_WIDTH
    query_width = QUERY_HEADS * HEAD_WIDTH
    prompt_dq, reply_dq, reply_dk, reply_dv = call(
        functools.partial(finish_reply, counts),
        "finish_reply",
        SMALL_MIB,
        (place, *parts, *queries),
        [
            shape(prompt_own, query_width),
            shape(reply_own, query_width),
            shape(reply_own, key_width),
            shape(reply_own, key_width),
        ],
        cost_estimate=pl.CostEstimate(
            flops=2 * reply_own * reply_own * (query_width + 2 * key_width),
            bytes_accessed=16 * reply_own * query_width,
            transcendentals=0,
        ),
    )
    slices, prompt_dq = lax.optimization_barrier((slices, prompt_dq))
    prompt_dk, prompt_dv = call(
        finish_prompt,
        "finish_prompt",
        SMALL_MIB,
        (place, *slices),
        [shape(cut_rows, key_width)] * 2,
    )
    return (
        prompt_dq[:prompt_rows],
        prompt_dk,
        prompt_dv,
        reply_dq[None],
        reply_dk[None],
        reply_dv[None],
    )


def solution(mesh):
    return jax.shard_map(
        on_device,
        mesh=mesh,
        in_specs=(
            P(("pre", "rsp"), None),
            P("pre", None),
            P("pre", None),
            P(("pre", "rsp"), None),
            P(("pre", "rsp"), None),
            P("rsp", "pre", None),
            P("rsp", "pre", None),
            P("rsp", "pre", None),
            P("rsp", "pre", None),
            P("rsp", "pre", None),
            P(),
            P(),
        ),
        out_specs=(
            P(("pre", "rsp"), None),
            P(("pre", "rsp"), None),
            P(("pre", "rsp"), None),
            P("rsp", "pre", None),
            P("rsp", "pre", None),
            P("rsp", "pre", None),
        ),
        check_vma=False,
    )
```

```python
import functools
import math

import jax
import jax.numpy as jnp
from jax import lax
from jax.experimental import pallas as pl
from jax.experimental.pallas import tpu as pltpu
from jax.sharding import PartitionSpec as P

QUERY_HEADS = 20
KEY_VALUE_HEADS = 4
GROUP = QUERY_HEADS // KEY_VALUE_HEADS
HEAD_WIDTH = 128
RESP_DEV = 2
CORES = 2
LOCAL_HEADS = KEY_VALUE_HEADS // CORES
GROUP_WIDTH = GROUP * HEAD_WIDTH

SCALE = HEAD_WIDTH ** (-0.5)
SCALE_LOG2 = SCALE * math.log2(math.e)
NEGATIVE_FLOOR = -1e30
DEAD = 1e30
F32 = jnp.float32
BF16 = jnp.bfloat16
VMEM = pl.BlockSpec(memory_space=pltpu.VMEM)
SMEM = pl.BlockSpec(memory_space=pltpu.SMEM)
HBM = pl.BlockSpec(memory_space=pltpu.HBM)


VMEM_MIB = 40
SMALL_MIB = 24
LARGE_MIB = 58


def params(mib):
    return pltpu.CompilerParams(vmem_limit_bytes=mib * 1024 * 1024)


def dot(a, b, over=(1, 0)):
    return lax.dot_general(
        a, b, (((over[0],), (over[1],)), ((), ())), preferred_element_type=F32
    )


def iota(shape, axis):
    return lax.broadcasted_iota(jnp.int32, shape, axis)


def sorting(rows):
    half = rows // RESP_DEV
    out = iota((rows, rows), 0)
    source = jnp.where(out < half, RESP_DEV * out, RESP_DEV * (out - half) + 1)
    return (iota((rows, rows), 1) == source).astype(BF16)


def unsorting(rows):
    half = rows // RESP_DEV
    out = iota((rows, rows), 1)
    source = jnp.where(out < half, RESP_DEV * out, RESP_DEV * (out - half) + 1)
    return (iota((rows, rows), 0) == source).astype(BF16)


def lanes(index, width):
    return pl.ds(pl.multiple_of(index * width, width), width)


def head_of(core, cross, local):
    owner = (1 - core) if cross else core
    return owner * LOCAL_HEADS + local


def fetch(pairs, sems):
    copies = [pltpu.make_async_copy(src, dst, sems.at[i]) for i, (src, dst) in enumerate(pairs)]
    for copy in copies:
        copy.start()
    return copies


def prepare_keys(place, pk, pv, rk, rv, mine0, theirs0, mine1, theirs, token, *scratch):
    core = place[1]
    bufs, sems = scratch[:-1], scratch[-1]
    copies = fetch(zip((pk, pv, rk, rv), bufs), sems)
    prompt = pk.shape[0]
    order = sorting(rk.shape[0])
    for copy in copies:
        copy.wait()
    pk, pv, rk, rv = bufs
    for local, outs in enumerate(((mine0, theirs.at[0]), (mine1, theirs.at[1]))):
        for cross, out in enumerate(outs):
            span = lanes(head_of(core, cross, local), HEAD_WIDTH)
            for part, (p, r) in enumerate(((pk, rk), (pv, rv))):
                to = slice(part * HEAD_WIDTH, (part + 1) * HEAD_WIDTH)
                out[:prompt, to] = p[:, span]
                out[prompt:, to] = dot(order, r[:, span]).astype(BF16)
    theirs0[...] = theirs[0]
    token[...] = jnp.zeros_like(token)


def prepare_rows(place, token, pq, po, pg, rq, ro, rg, *refs):
    outs, bufs, sems = refs[:KEY_VALUE_HEADS], refs[KEY_VALUE_HEADS:-1], refs[-1]
    core = place[1]
    reply = rq.shape[0]
    sources = (pq, po, pg, rq, ro, rg)
    pairs = []
    for step in range(KEY_VALUE_HEADS):
        span = lanes(head_of(core, 1 - step % CORES, step // CORES), GROUP_WIDTH)
        pairs += [(source.at[:, span], buf.at[step]) for source, buf in zip(sources, bufs)]
    copies = fetch(pairs, sems)
    order = sorting(reply)
    column = iota((GROUP_WIDTH, HEAD_WIDTH), 1)
    pick = (column // 3 == iota((GROUP_WIDTH, HEAD_WIDTH), 0) // HEAD_WIDTH).astype(BF16)

    def delta(gradient, output):
        product = gradient.astype(F32) * output.astype(F32)
        high = product.astype(BF16)
        low = (product - high.astype(F32)).astype(BF16)
        value = dot(high, pick) + dot(low, pick)
        first = value.astype(BF16).astype(F32)
        second = (value - first).astype(BF16).astype(F32)
        part = iota(value.shape, 1) % 3
        return jnp.where(part == 0, first, jnp.where(part == 1, second, value - first - second)).astype(BF16)

    for step, out in enumerate(outs):
        for copy in copies[step * len(sources) : (step + 1) * len(sources)]:
            copy.wait()
        pq, po, pg, rq, ro, rg = (buf[step] for buf in bufs)
        out[reply:, :GROUP_WIDTH] = pq
        out[reply:, GROUP_WIDTH : 2 * GROUP_WIDTH] = pg
        out[reply:, 2 * GROUP_WIDTH :] = delta(pg, po)
        out[:reply, :GROUP_WIDTH] = dot(order, rq).astype(BF16)
        gradient = dot(order, rg).astype(BF16)
        out[:reply, GROUP_WIDTH : 2 * GROUP_WIDTH] = gradient
        out[:reply, 2 * GROUP_WIDTH :] = delta(gradient, dot(order, ro).astype(BF16))


def attend(sizes, joint_keys, place, reply_len, reply_slot, *refs):
    chips, reply_own, prompt_own, prompt_rows, prompt_keys = sizes
    own_positions = reply_own // RESP_DEV
    positions = CORES * own_positions
    chip_prompt = CORES * prompt_keys
    block = positions
    per_chip = chip_prompt // block
    prompt_blocks = chips * per_chip
    rows_in, refs = refs[:2], refs[2:]
    count = chips if joint_keys else chips * CORES
    keys_in, refs = refs[:count], refs[count:]
    query_out, refs = refs[:2], refs[2:]
    count = chips * CORES if joint_keys else chips
    keys_out, refs = refs[:count], refs[count:]
    keys, keys_t, total, query, gradient, query_t, gradient_t, deltas, delta, scores, top, mass, *refs = refs
    query_grad, stages = refs[0], (refs[1:3], refs[3:5])
    chip, core, group = place[0], place[1], place[2]

    pick = (iota((8, HEAD_WIDTH), 1) // 3 == iota((8, HEAD_WIDTH), 0)).astype(BF16)
    for other in range(CORES):
        deltas[other] = dot(pick, rows_in[other][:, 2 * GROUP_WIDTH :], (1, 1))

    for index in range(chips * CORES):
        away, other = index // CORES, index % CORES
        source = keys_in[away].at[other] if joint_keys else keys_in[index]
        source = source if len(source.shape) == 2 else source.at[0]
        at = away * chip_prompt + other * prompt_keys
        keys[at : at + prompt_keys] = source[:prompt_keys]
        for slot in range(RESP_DEV):
            at = prompt_blocks * block + (slot * chips + away) * positions + other * own_positions
            begin = prompt_keys + slot * own_positions
            keys[at : at + own_positions] = source[begin : begin + own_positions]
    total[...] = jnp.zeros_like(total)

    unit = (iota((HEAD_WIDTH, HEAD_WIDTH), 0) == iota((HEAD_WIDTH, HEAD_WIDTH), 1)).astype(BF16)

    def transpose_block(index, carry):
        rows = pl.ds(pl.multiple_of(index * block, block), block)
        keys_t[index] = dot(unit, keys[rows, :HEAD_WIDTH], (1, 1)).astype(BF16)
        return carry

    lax.fori_loop(0, keys_t.shape[0], transpose_block, 0)

    def score_block(region, place_in, width, chunks, hidden):
        rows = pl.ds(pl.multiple_of(region * block, block), block)
        key_rows = keys[rows, :HEAD_WIDTH]
        for chunk in range(chunks):
            span = slice(chunk * width, (chunk + 1) * width)
            value = dot(key_rows, query_t[:, span]) * SCALE_LOG2
            if hidden is not None:
                value = jnp.where(hidden, NEGATIVE_FLOOR, value)
            scores[place_in, :, span] = value
            split = value.reshape(block // 8, 8, width)
            before = top[:, span]
            now = jnp.maximum(before, jnp.max(split, axis=0))
            top[:, span] = now
            mass[:, span] = mass[:, span] * jnp.exp2(before - now) + jnp.sum(
                jnp.exp2(split - now[None]), axis=0
            )

    def weigh(region, place_in, width, chunks, log_mass, stage, earlier=None, earlier_stage=None):
        rows = pl.ds(pl.multiple_of(region * block, block), block)
        value_rows = keys[rows, HEAD_WIDTH:]
        for chunk in range(chunks):
            span = slice(chunk * width, (chunk + 1) * width)
            p = jnp.exp2(scores[place_in, :, span] - log_mass[chunk])
            dp = dot(value_rows, gradient_t[:, span])
            stage[0][:, span] = p.astype(BF16)
            stage[1][:, span] = (p * (dp - delta[0:1, span])).astype(BF16)
            if earlier is not None:
                multiply(earlier, width, chunks, earlier_stage, chunk)
        if earlier is not None:
            for chunk in range(chunks, 3):
                multiply(earlier, width, chunks, earlier_stage, chunk)

    def multiply(region, width, chunks, stage, part):
        rows = pl.ds(pl.multiple_of(region * block, block), block)
        used = width * chunks
        if part == 0:
            total[rows, HEAD_WIDTH:] += dot(stage[0][:, :used], gradient[:used])
        elif part == 1:
            total[rows, :HEAD_WIDTH] += dot(stage[1][:, :used], query[:used])
        elif part == 2:
            query_grad[:, :used] += dot(keys_t[region], stage[1][:, :used])

    def grad_blocks(count, region_of, width, chunks, log_mass):
        first, second = stages

        def later(index, stage, earlier_stage):
            weigh(
                region_of(index), index, width, chunks, log_mass, stage, region_of(index - 1), earlier_stage
            )

        def last(stage):
            for part in range(3):
                multiply(region_of(count - 1), width, chunks, stage, part)

        weigh(region_of(0), 0, width, chunks, log_mass, first)

        def two(index, carry):
            later(2 * index + 1, second, first)
            later(2 * index + 2, first, second)
            return carry

        lax.fori_loop(0, (count - 1) // 2, two, 0)

        @pl.when(count % 2 == 0)
        def _():
            later(count - 1, second, first)
            last(second)

        @pl.when(count % 2 == 1)
        def _():
            last(first)

    def turn(all_rows):
        query_t[:, :all_rows] = dot(unit, query[:all_rows], (1, 1)).astype(BF16)
        gradient_t[:, :all_rows] = dot(unit, gradient[:all_rows], (1, 1)).astype(BF16)

    def begin(all_rows):
        top[:, :all_rows] = jnp.full((8, all_rows), NEGATIVE_FLOOR, F32)
        mass[:, :all_rows] = jnp.zeros((8, all_rows), F32)
        query_grad[:, :all_rows] = jnp.zeros((HEAD_WIDTH, all_rows), F32)

    def log_masses(width, chunks, live):
        found = []
        for chunk in range(chunks):
            span = slice(chunk * width, (chunk + 1) * width)
            peak = jnp.max(top[:, span], axis=0, keepdims=True)
            summed = jnp.sum(mass[:, span] * jnp.exp2(top[:, span] - peak), axis=0, keepdims=True)
            found.append(jnp.where(live, peak + jnp.log2(summed), DEAD))
        return found

    def absolute(index, half):
        return index + jnp.where(index < half, core * half, -core * half)

    def reply_tile(slot, carry):
        length = jnp.int32(0)
        for response in range(reply_len.shape[0]):
            mine = reply_slot[response] == group * RESP_DEV + slot
            length = length + jnp.where(mine, reply_len[response], 0)
        first = chip * positions
        source = pl.ds(pl.multiple_of(slot * own_positions, own_positions), own_positions)

        @pl.when(length > first)
        def _():
            for head in range(GROUP):
                for other in range(CORES):
                    at = head * positions + other * own_positions
                    to = slice(at, at + own_positions)
                    left = slice(head * HEAD_WIDTH, (head + 1) * HEAD_WIDTH)
                    right = slice(GROUP_WIDTH + head * HEAD_WIDTH, GROUP_WIDTH + (head + 1) * HEAD_WIDTH)
                    query[to] = rows_in[other][source, left]
                    gradient[to] = rows_in[other][source, right]
                    for which in range(RESP_DEV):
                        @pl.when(slot == which)
                        def _():
                            delta[0:1, to] = deltas[
                                other, head : head + 1, which * own_positions : (which + 1) * own_positions
                            ]
            begin(GROUP * positions)
            turn(GROUP * positions)
            base = prompt_blocks + slot * chips
            past = prompt_blocks + chip

            def region_of(index):
                reply = base + ((index - prompt_blocks) ^ chip)
                return jnp.where(index < prompt_blocks, index, reply)

            def stats(index, carry):
                score_block(region_of(index), index, positions, GROUP, None)
                return carry

            lax.fori_loop(0, past, stats, 0)
            row_at = absolute(iota((1, positions), 1), own_positions)
            key_at = absolute(iota((block, 1), 0), own_positions)
            score_block(base, past, positions, GROUP, key_at > row_at)
            live = first + row_at < length
            log_mass = log_masses(positions, GROUP, live)

            grad_blocks(
                past + 1,
                lambda index: jnp.where(index == past, base, region_of(index)),
                positions,
                GROUP,
                log_mass,
            )
            for head in range(GROUP):
                turned = (query_grad[:, head * positions : (head + 1) * positions].T * SCALE).astype(BF16)
                for other in range(CORES):
                    query_out[other][source, head * HEAD_WIDTH : (head + 1) * HEAD_WIDTH] = turned[
                        other * own_positions : (other + 1) * own_positions
                    ]

        @pl.when(length <= first)
        def _():
            for other in range(CORES):
                query_out[other][source, :] = jnp.zeros((own_positions, GROUP_WIDTH), BF16)

        return carry

    lax.fori_loop(0, RESP_DEV, reply_tile, 0)

    head_rows = CORES * prompt_own
    used = GROUP * head_rows
    all_rows = -(-used // 128) * 128
    if all_rows > used:
        query[used:all_rows] = jnp.zeros((all_rows - used, HEAD_WIDTH), BF16)
        gradient[used:all_rows] = jnp.zeros((all_rows - used, HEAD_WIDTH), BF16)
    delta[0:1, :all_rows] = jnp.zeros((1, all_rows), F32)
    for head in range(GROUP):
        for other in range(CORES):
            at = head * head_rows + other * prompt_own
            to = slice(at, at + prompt_own)
            left = slice(head * HEAD_WIDTH, (head + 1) * HEAD_WIDTH)
            right = slice(GROUP_WIDTH + head * HEAD_WIDTH, GROUP_WIDTH + (head + 1) * HEAD_WIDTH)
            query[to] = rows_in[other][reply_own:, left]
            gradient[to] = rows_in[other][reply_own:, right]
            delta[0:1, to] = deltas[other, head : head + 1, reply_own:]
    begin(all_rows)
    turn(all_rows)
    lane = iota((1, all_rows), 1)
    within = lane
    for head in range(1, GROUP):
        within = within - jnp.where(lane >= head * head_rows, head_rows, 0)
    offset = jnp.where(within < prompt_own, within, within - prompt_own)
    row_core = jnp.where(within < prompt_own, core, 1 - core)
    real = (lane < used) & (offset < prompt_rows)
    row_at = jnp.where(
        real, (chip * CORES + row_core) * prompt_keys + group * prompt_rows + offset, -1
    )
    seen = (chip + 1) * per_chip

    def prompt_region(index):
        return (index // per_chip ^ chip) * per_chip + index % per_chip

    def prompt_stats(index, carry):
        key_row = iota((block, 1), 0) + index % per_chip * block
        key_at = index // per_chip * chip_prompt + absolute(key_row, prompt_keys)
        score_block(prompt_region(index), index, all_rows, 1, key_at > row_at)
        return carry

    lax.fori_loop(0, seen, prompt_stats, 0)
    log_mass = log_masses(all_rows, 1, real)

    grad_blocks(seen, prompt_region, all_rows, 1, log_mass)
    turned = (query_grad[:, :all_rows].T * SCALE).astype(BF16)
    for head in range(GROUP):
        for other in range(CORES):
            at = head * head_rows + other * prompt_own
            query_out[other][reply_own:, head * HEAD_WIDTH : (head + 1) * HEAD_WIDTH] = turned[
                at : at + prompt_own
            ]

    for index in range(chips * CORES):
        away, other = index // CORES, index % CORES
        out = keys_out[index] if joint_keys else keys_out[away].at[other]

        def put(to, at, count):
            out[to : to + count, :HEAD_WIDTH] = (total[at : at + count, :HEAD_WIDTH] * SCALE).astype(BF16)
            out[to : to + count, HEAD_WIDTH:] = total[at : at + count, HEAD_WIDTH:].astype(BF16)

        put(0, away * chip_prompt + other * prompt_keys, prompt_keys)
        for slot in range(RESP_DEV):
            at = prompt_blocks * block + (slot * chips + away) * positions + other * own_positions
            put(prompt_keys + slot * own_positions, at, own_positions)


def add(first, *rest):
    value = first.astype(F32)
    for part in rest:
        value = value + part.astype(F32)
    return value


def add_pairs(*refs):
    count = len(refs) // 3
    for index in range(count):
        refs[2 * count + index][...] = add(refs[index][...], refs[count + index][...]).astype(BF16)


def collect(*refs):
    parts, mine, theirs = refs[:-2], refs[-2], refs[-1]
    mine[...] = add(*(part[0] for part in parts))
    theirs[...] = add(*(part[1] for part in parts)).astype(BF16)


def spread_prompt(sizes, place, *refs):
    refs, outs, summed = refs[: sum(sizes)], refs[sum(sizes) : -1], refs[-1]
    groups, rows = len(outs), outs[0].shape[1]
    for index, size in enumerate(sizes):
        parts, refs = refs[:size], refs[size:]
        summed[index] = add(*(part[: groups * rows] for part in parts))
    for shift in range(groups):
        at = pl.ds(pl.multiple_of(lax.rem(place[2] + shift, groups) * rows, rows), rows)
        for index in range(len(sizes)):
            outs[shift][index] = summed[index, at].astype(BF16)


def finish_reply(sizes, place, *refs):
    parts_in, refs = refs[: sum(sizes)], refs[sum(sizes) :]
    queries, refs = refs[: len(sizes)], refs[len(sizes) :]
    prompt_dq, reply_dq, reply_dk, reply_dv = refs
    reply = reply_dq.shape[0]
    order = unsorting(reply)
    for index, size in enumerate(sizes):
        parts, parts_in = parts_in[:size], parts_in[size:]
        head = head_of(place[1], index % CORES, index // CORES)
        span = lanes(head, HEAD_WIDTH)
        value = add(*(part[part.shape[0] - reply :] for part in parts))
        value = dot(order, value.astype(BF16)).astype(BF16)
        reply_dk[:, span] = value[:, :HEAD_WIDTH]
        reply_dv[:, span] = value[:, HEAD_WIDTH:]
        span = lanes(head, GROUP_WIDTH)
        reply_dq[:, span] = dot(order, queries[index][:reply]).astype(BF16)
        prompt_dq[:, span] = queries[index][reply:]


def finish_prompt(place, *refs):
    parts, prompt_dk, prompt_dv = refs[:-2], refs[-2], refs[-1]
    for index in range(KEY_VALUE_HEADS):
        span = lanes(head_of(place[1], index % CORES, index // CORES), HEAD_WIDTH)
        value = add(*(part[index] for part in parts)).astype(BF16)
        prompt_dk[:, span] = value[:, :HEAD_WIDTH]
        prompt_dv[:, span] = value[:, HEAD_WIDTH:]


def on_device(
    prompt_query,
    prompt_k,
    prompt_value,
    prompt_output,
    prompt_output_gradient,
    reply_query,
    reply_key,
    reply_value,
    reply_output,
    reply_output_gradient,
    reply_len,
    reply_slot,
):
    devices = lax.axis_size("pre")
    groups = lax.axis_size("rsp")
    chips = devices // CORES
    prompt_rows = prompt_query.shape[0]
    prompt_own = -(-prompt_rows // 16) * 16
    prompt_keys = prompt_k.shape[0]
    reply_own = reply_query.shape[1]
    own_positions = reply_own // RESP_DEV
    positions = CORES * own_positions
    chip_prompt = CORES * prompt_keys
    assert chip_prompt % positions == 0 and chips & (chips - 1) == 0
    pre_index = lax.axis_index("pre")
    place = jnp.stack([lax.div(pre_index, CORES), lax.rem(pre_index, CORES), lax.axis_index("rsp")])

    def shape(*dims, dtype=BF16):
        return jax.ShapeDtypeStruct(dims, dtype)

    def move(array, away, cross=0):
        pairs = [(p, (p // CORES ^ away) * CORES + (p % CORES ^ cross)) for p in range(devices)]
        return lax.ppermute(array, "pre", pairs)

    def swap(array):
        return move(array, 0, 1)

    def call(kernel, name, mib, inputs, outs, scalars=1, spec=VMEM, **more):
        return pl.pallas_call(
            kernel,
            out_shape=outs,
            in_specs=[SMEM] * scalars + [spec] * (len(inputs) - scalars),
            out_specs=[VMEM] * len(outs),
            compiler_params=params(mib),
            name=name,
            **more,
        )(*inputs)

    relayed = chips == 4
    key_shape = (prompt_keys + reply_own, 2 * HEAD_WIDTH)
    mine0, theirs0, mine1, theirs, token = call(
        prepare_keys,
        "prepare_keys",
        LARGE_MIB,
        (place, prompt_k, prompt_value, reply_key[0], reply_value[0]),
        [shape(*key_shape)] * 3 + [shape(LOCAL_HEADS, *key_shape), shape(8, 128, dtype=F32)],
        spec=HBM,
        scratch_shapes=[
            pltpu.VMEM((rows, KEY_VALUE_HEADS * HEAD_WIDTH), BF16)
            for rows in (prompt_keys, prompt_keys, reply_own, reply_own)
        ]
        + [pltpu.SemaphoreType.DMA((4,))],
    )
    blocks0 = {(0, 0): mine0, (0, 1): swap(theirs)}
    for away in range(1, 3 if relayed else chips):
        blocks0[away, 0] = move(mine0, away)
        blocks0[away, 1] = move(theirs0, away, 1)
    if prompt_own > prompt_rows:
        room = ((0, prompt_own - prompt_rows), (0, 0))
        prompt_query, prompt_output, prompt_output_gradient = (
            jnp.pad(array, room)
            for array in (prompt_query, prompt_output, prompt_output_gradient)
        )
    own_rows = reply_own + prompt_own
    row_width = 2 * GROUP_WIDTH + HEAD_WIDTH

    rows = call(
        prepare_rows,
        "prepare_rows",
        LARGE_MIB,
        (
            place,
            token,
            prompt_query,
            prompt_output,
            prompt_output_gradient,
            reply_query[0],
            reply_output[0],
            reply_output_gradient[0],
        ),
        [shape(own_rows, row_width)] * KEY_VALUE_HEADS,
        spec=HBM,
        scratch_shapes=[
            pltpu.VMEM((KEY_VALUE_HEADS, rows, GROUP_WIDTH), BF16)
            for rows in [prompt_own] * 3 + [reply_own] * 3
        ]
        + [pltpu.SemaphoreType.DMA((KEY_VALUE_HEADS * 6,))],
        cost_estimate=pl.CostEstimate(
            flops=6 * reply_own * reply_own * QUERY_HEADS * HEAD_WIDTH,
            bytes_accessed=20 * reply_own * QUERY_HEADS * HEAD_WIDTH,
            transcendentals=0,
        ),
    )

    blocks0, rows, mine1 = lax.optimization_barrier((blocks0, rows, mine1))
    if relayed:
        blocks0[3, 0] = move(blocks0[1, 0], 2)
        blocks0[3, 1] = move(blocks0[2, 1], 1)
    chip1 = jnp.stack([mine1, blocks0[0, 1][1]])
    blocks1 = [chip1] + [move(chip1, away) for away in range(1, chips)]

    blocks = chips * (chip_prompt // positions) + RESP_DEV * chips
    slots = chips * (chip_prompt // positions) + chips
    all_rows = max(GROUP * positions, -(-GROUP * CORES * prompt_own // 128) * 128)
    sizes = (chips, reply_own, prompt_own, prompt_rows, prompt_keys)
    score_count = GROUP * (positions * RESP_DEV * slots * positions)

    def run_attend(local, key_blocks):
        joint_keys = local == 1
        sums = [shape(*key_shape)] * devices if joint_keys else [shape(CORES, *key_shape)] * chips
        query_mine, query_theirs, *sums = call(
            functools.partial(attend, sizes, joint_keys),
            "attend",
            VMEM_MIB,
            (
                place,
                reply_len,
                reply_slot,
                rows[CORES * local + 1],
                swap(rows[CORES * local]),
                *key_blocks,
            ),
            [shape(own_rows, GROUP_WIDTH)] * CORES + sums,
            scalars=3,
            scratch_shapes=[
                pltpu.VMEM((blocks * positions, 2 * HEAD_WIDTH), BF16),
                pltpu.VMEM((blocks, HEAD_WIDTH, positions), BF16),
                pltpu.VMEM((blocks * positions, 2 * HEAD_WIDTH), F32),
                pltpu.VMEM((all_rows, HEAD_WIDTH), BF16),
                pltpu.VMEM((all_rows, HEAD_WIDTH), BF16),
                pltpu.VMEM((HEAD_WIDTH, all_rows), BF16),
                pltpu.VMEM((HEAD_WIDTH, all_rows), BF16),
                pltpu.VMEM((CORES, 8, own_rows), F32),
                pltpu.VMEM((8, all_rows), F32),
                pltpu.VMEM((slots, positions, all_rows), F32),
                pltpu.VMEM((8, all_rows), F32),
                pltpu.VMEM((8, all_rows), F32),
                pltpu.VMEM((HEAD_WIDTH, all_rows), F32),
            ]
            + [pltpu.VMEM((positions, all_rows), BF16)] * 4,
            cost_estimate=pl.CostEstimate(
                flops=score_count * 10 * HEAD_WIDTH,
                bytes_accessed=8 * 1024 * 1024,
                transcendentals=2 * score_count,
            ),
        )
        return query_mine, query_theirs, sums

    query_mine0, query_theirs0, sums0 = run_attend(
        0, [blocks0[away, other] for away in range(chips) for other in range(CORES)]
    )
    arrived0 = [sums0[0]] + [move(sums0[away], away) for away in range(1, chips)]
    query_theirs0 = swap(query_theirs0)
    query_mine1, query_theirs1, sums1 = run_attend(1, blocks1)
    arrived0, query_theirs0, query_theirs1, sums1 = lax.optimization_barrier(
        (arrived0, query_theirs0, query_theirs1, sums1)
    )
    sums1 = [sums1[CORES * away : CORES * away + CORES] for away in range(chips)]
    if relayed:
        through_y, through_x = move(sums1[3][0], 2), move(sums1[3][1], 1)
        for_x, for_y = call(
            add_pairs,
            "add_pairs",
            SMALL_MIB,
            (sums1[1][0], sums1[2][1], through_y, through_x),
            [shape(*key_shape)] * 2,
            scalars=0,
        )
        near = [sums1[0][0], move(sums1[1][1], 1, 1), move(sums1[2][0], 2)]
        for_x, for_y, sums1[0][1], query_theirs1 = lax.optimization_barrier(
            (for_x, for_y, sums1[0][1], query_theirs1)
        )
        lists1 = [[near[0], move(for_x, 1), near[2]], [swap(sums1[0][1]), near[1], move(for_y, 2, 1)]]
    else:
        lists1 = [
            [move(pair[other], away, other) if away or other else pair[other] for away, pair in enumerate(sums1)]
            for other in range(CORES)
        ]
    mine0, theirs0 = call(
        collect,
        "collect",
        SMALL_MIB,
        arrived0,
        [shape(*key_shape, dtype=F32), shape(*key_shape)],
        scalars=0,
    )
    lists = [[mine0], [swap(theirs0)]] + lists1
    queries = [query_mine0, query_theirs0, query_mine1, swap(query_theirs1)]
    counts = [len(parts) for parts in lists]
    parts = [part for one in lists for part in one]
    cut_rows = prompt_keys // groups
    cuts = call(
        functools.partial(spread_prompt, counts),
        "spread_prompt",
        SMALL_MIB,
        (place, *parts),
        [shape(KEY_VALUE_HEADS, cut_rows, 2 * HEAD_WIDTH)] * groups,
        scratch_shapes=[pltpu.VMEM((KEY_VALUE_HEADS, prompt_keys, 2 * HEAD_WIDTH), F32)],
    )
    slices = [cuts[0]] + [
        lax.ppermute(cuts[shift], "rsp", [(g, (g + shift) % groups) for g in range(groups)])
        for shift in range(1, groups)
    ]
    key_width = KEY_VALUE_HEADS * HEAD_WIDTH
    query_width = QUERY_HEADS * HEAD_WIDTH
    prompt_dq, reply_dq, reply_dk, reply_dv = call(
        functools.partial(finish_reply, counts),
        "finish_reply",
        SMALL_MIB,
        (place, *parts, *queries),
        [
            shape(prompt_own, query_width),
            shape(reply_own, query_width),
            shape(reply_own, key_width),
            shape(reply_own, key_width),
        ],
        cost_estimate=pl.CostEstimate(
            flops=2 * reply_own * reply_own * (query_width + 2 * key_width),
            bytes_accessed=16 * reply_own * query_width,
            transcendentals=0,
        ),
    )
    slices, prompt_dq = lax.optimization_barrier((slices, prompt_dq))
    prompt_dk, prompt_dv = call(
        finish_prompt,
        "finish_prompt",
        SMALL_MIB,
        (place, *slices),
        [shape(cut_rows, key_width)] * 2,
    )
    return (
        prompt_dq[:prompt_rows],
        prompt_dk,
        prompt_dv,
        reply_dq[None],
        reply_dk[None],
        reply_dv[None],
    )


def solution(mesh):
    return jax.shard_map(
        on_device,
        mesh=mesh,
        in_specs=(
            P(("pre", "rsp"), None),
            P("pre", None),
            P("pre", None),
            P(("pre", "rsp"), None),
            P(("pre", "rsp"), None),
            P("rsp", "pre", None),
            P("rsp", "pre", None),
            P("rsp", "pre", None),
            P("rsp", "pre", None),
            P("rsp", "pre", None),
            P(),
            P(),
        ),
        out_specs=(
            P(("pre", "rsp"), None),
            P(("pre", "rsp"), None),
            P(("pre", "rsp"), None),
            P("rsp", "pre", None),
            P("rsp", "pre", None),
            P("rsp", "pre", None),
        ),
        check_vma=False,
    )
```

```python
import functools
import math

import jax
import jax.numpy as jnp
from jax import lax
from jax.experimental import pallas as pl
from jax.experimental.pallas import tpu as pltpu
from jax.sharding import PartitionSpec as P

QUERY_HEADS = 20
KEY_VALUE_HEADS = 4
GROUP = QUERY_HEADS // KEY_VALUE_HEADS
HEAD_WIDTH = 128
RESP_DEV = 2
CORES = 2
LOCAL_HEADS = KEY_VALUE_HEADS // CORES
GROUP_WIDTH = GROUP * HEAD_WIDTH

SCALE = HEAD_WIDTH ** (-0.5)
SCALE_LOG2 = SCALE * math.log2(math.e)
NEGATIVE_FLOOR = -1e30
DEAD = 1e30
F32 = jnp.float32
BF16 = jnp.bfloat16
VMEM = pl.BlockSpec(memory_space=pltpu.VMEM)
SMEM = pl.BlockSpec(memory_space=pltpu.SMEM)
HBM = pl.BlockSpec(memory_space=pltpu.HBM)


VMEM_MIB = 40
SMALL_MIB = 24
LARGE_MIB = 58


def params(mib):
    return pltpu.CompilerParams(vmem_limit_bytes=mib * 1024 * 1024)


def dot(a, b, over=(1, 0)):
    return lax.dot_general(
        a, b, (((over[0],), (over[1],)), ((), ())), preferred_element_type=F32
    )


def iota(shape, axis):
    return lax.broadcasted_iota(jnp.int32, shape, axis)


def sorting(rows):
    half = rows // RESP_DEV
    out = iota((rows, rows), 0)
    source = jnp.where(out < half, RESP_DEV * out, RESP_DEV * (out - half) + 1)
    return (iota((rows, rows), 1) == source).astype(BF16)


def unsorting(rows):
    half = rows // RESP_DEV
    out = iota((rows, rows), 1)
    source = jnp.where(out < half, RESP_DEV * out, RESP_DEV * (out - half) + 1)
    return (iota((rows, rows), 0) == source).astype(BF16)


def lanes(index, width):
    return pl.ds(pl.multiple_of(index * width, width), width)


def head_of(core, cross, local):
    owner = (1 - core) if cross else core
    return owner * LOCAL_HEADS + local


def fetch(pairs, sems):
    copies = [pltpu.make_async_copy(src, dst, sems.at[i]) for i, (src, dst) in enumerate(pairs)]
    for copy in copies:
        copy.start()
    return copies


def prepare_keys(place, pk, pv, rk, rv, mine0, theirs0, mine1, theirs, token, *scratch):
    core = place[1]
    bufs, sems = scratch[:-1], scratch[-1]
    copies = fetch(zip((pk, pv, rk, rv), bufs), sems)
    prompt = pk.shape[0]
    order = sorting(rk.shape[0])
    for copy in copies:
        copy.wait()
    pk, pv, rk, rv = bufs
    for local, outs in enumerate(((mine0, theirs.at[0]), (mine1, theirs.at[1]))):
        for cross, out in enumerate(outs):
            span = lanes(head_of(core, cross, local), HEAD_WIDTH)
            for part, (p, r) in enumerate(((pk, rk), (pv, rv))):
                to = slice(part * HEAD_WIDTH, (part + 1) * HEAD_WIDTH)
                out[:prompt, to] = p[:, span]
                out[prompt:, to] = dot(order, r[:, span]).astype(BF16)
    theirs0[...] = theirs[0]
    token[...] = jnp.zeros_like(token)


def prepare_rows(place, token, pq, po, pg, rq, ro, rg, *refs):
    outs, bufs, sems = refs[:KEY_VALUE_HEADS], refs[KEY_VALUE_HEADS:-1], refs[-1]
    core = place[1]
    reply = rq.shape[0]
    sources = (pq, po, pg, rq, ro, rg)
    pairs = []
    for step in range(KEY_VALUE_HEADS):
        span = lanes(head_of(core, 1 - step % CORES, step // CORES), GROUP_WIDTH)
        pairs += [(source.at[:, span], buf.at[step]) for source, buf in zip(sources, bufs)]
    copies = fetch(pairs, sems)
    order = sorting(reply)
    column = iota((GROUP_WIDTH, HEAD_WIDTH), 1)
    pick = (column // 3 == iota((GROUP_WIDTH, HEAD_WIDTH), 0) // HEAD_WIDTH).astype(BF16)

    def delta(gradient, output):
        product = gradient.astype(F32) * output.astype(F32)
        high = product.astype(BF16)
        low = (product - high.astype(F32)).astype(BF16)
        value = dot(high, pick) + dot(low, pick)
        first = value.astype(BF16).astype(F32)
        second = (value - first).astype(BF16).astype(F32)
        part = iota(value.shape, 1) % 3
        return jnp.where(part == 0, first, jnp.where(part == 1, second, value - first - second)).astype(BF16)

    for step, out in enumerate(outs):
        for copy in copies[step * len(sources) : (step + 1) * len(sources)]:
            copy.wait()
        pq, po, pg, rq, ro, rg = (buf[step] for buf in bufs)
        out[reply:, :GROUP_WIDTH] = pq
        out[reply:, GROUP_WIDTH : 2 * GROUP_WIDTH] = pg
        out[reply:, 2 * GROUP_WIDTH :] = delta(pg, po)
        out[:reply, :GROUP_WIDTH] = dot(order, rq).astype(BF16)
        gradient = dot(order, rg).astype(BF16)
        out[:reply, GROUP_WIDTH : 2 * GROUP_WIDTH] = gradient
        out[:reply, 2 * GROUP_WIDTH :] = delta(gradient, dot(order, ro).astype(BF16))


def attend(sizes, joint_keys, place, reply_len, reply_slot, *refs):
    chips, reply_own, prompt_own, prompt_rows, prompt_keys = sizes
    own_positions = reply_own // RESP_DEV
    positions = CORES * own_positions
    chip_prompt = CORES * prompt_keys
    block = 2 * positions
    prompt_blocks = chips * chip_prompt // block
    rows_in, refs = refs[:2], refs[2:]
    count = chips if joint_keys else chips * CORES
    keys_in, refs = refs[:count], refs[count:]
    query_out, refs = refs[:2], refs[2:]
    count = chips * CORES if joint_keys else chips
    keys_out, refs = refs[:count], refs[count:]
    keys, keys_t, total, query, gradient, query_t, gradient_t, deltas, delta, scores, top, mass, *refs = refs
    query_grad, stages = refs[0], (refs[1:3], refs[3:5])
    chip, core, group = place[0], place[1], place[2]

    pick = (iota((8, HEAD_WIDTH), 1) // 3 == iota((8, HEAD_WIDTH), 0)).astype(BF16)
    for other in range(CORES):
        deltas[other] = dot(pick, rows_in[other][:, 2 * GROUP_WIDTH :], (1, 1))

    for index in range(chips * CORES):
        away, other = index // CORES, index % CORES
        source = keys_in[away].at[other] if joint_keys else keys_in[index]
        source = source if len(source.shape) == 2 else source.at[0]
        at = away * chip_prompt + other * prompt_keys
        keys[at : at + prompt_keys] = source[:prompt_keys]
        for slot in range(RESP_DEV):
            at = chips * chip_prompt + (slot * chips + away) * positions + other * own_positions
            begin = prompt_keys + slot * own_positions
            keys[at : at + own_positions] = source[begin : begin + own_positions]
    total[...] = jnp.zeros_like(total)

    unit = (iota((HEAD_WIDTH, HEAD_WIDTH), 0) == iota((HEAD_WIDTH, HEAD_WIDTH), 1)).astype(BF16)

    def transpose_block(index, carry):
        rows = pl.ds(pl.multiple_of(index * block, block), block)
        keys_t[index] = dot(unit, keys[rows, :HEAD_WIDTH], (1, 1)).astype(BF16)
        return carry

    lax.fori_loop(0, keys_t.shape[0], transpose_block, 0)

    def score_block(region, place_in, width, chunks, hidden):
        rows = pl.ds(pl.multiple_of(region * block, block), block)
        key_rows = keys[rows, :HEAD_WIDTH]
        for chunk in range(chunks):
            span = slice(chunk * width, (chunk + 1) * width)
            value = dot(key_rows, query_t[:, span]) * SCALE_LOG2
            if hidden is not None:
                value = jnp.where(hidden, NEGATIVE_FLOOR, value)
            scores[place_in, :, span] = value
            split = value.reshape(block // 8, 8, width)
            before = top[:, span]
            now = jnp.maximum(before, jnp.max(split, axis=0))
            top[:, span] = now
            mass[:, span] = mass[:, span] * jnp.exp2(before - now) + jnp.sum(
                jnp.exp2(split - now[None]), axis=0
            )

    def weigh(region, place_in, width, chunks, log_mass, stage, earlier=None, earlier_stage=None):
        rows = pl.ds(pl.multiple_of(region * block, block), block)
        value_rows = keys[rows, HEAD_WIDTH:]
        for chunk in range(chunks):
            span = slice(chunk * width, (chunk + 1) * width)
            p = jnp.exp2(scores[place_in, :, span] - log_mass[chunk])
            dp = dot(value_rows, gradient_t[:, span])
            stage[0][:, span] = p.astype(BF16)
            stage[1][:, span] = (p * (dp - delta[0:1, span])).astype(BF16)
            if earlier is not None:
                multiply(earlier, width, chunks, earlier_stage, chunk)
        if earlier is not None:
            for chunk in range(chunks, 3):
                multiply(earlier, width, chunks, earlier_stage, chunk)

    def multiply(region, width, chunks, stage, part):
        rows = pl.ds(pl.multiple_of(region * block, block), block)
        used = width * chunks
        if part == 0:
            total[rows, HEAD_WIDTH:] += dot(stage[0][:, :used], gradient[:used])
        elif part == 1:
            total[rows, :HEAD_WIDTH] += dot(stage[1][:, :used], query[:used])
        elif part == 2:
            query_grad[:, :used] += dot(keys_t[region], stage[1][:, :used])

    def grad_blocks(count, region_of, width, chunks, log_mass):
        first, second = stages

        def later(index, stage, earlier_stage):
            weigh(
                region_of(index), index, width, chunks, log_mass, stage, region_of(index - 1), earlier_stage
            )

        def last(stage):
            for part in range(3):
                multiply(region_of(count - 1), width, chunks, stage, part)

        weigh(region_of(0), 0, width, chunks, log_mass, first)

        def two(index, carry):
            later(2 * index + 1, second, first)
            later(2 * index + 2, first, second)
            return carry

        lax.fori_loop(0, (count - 1) // 2, two, 0)

        @pl.when(count % 2 == 0)
        def _():
            later(count - 1, second, first)
            last(second)

        @pl.when(count % 2 == 1)
        def _():
            last(first)

    def turn(all_rows):
        query_t[:, :all_rows] = dot(unit, query[:all_rows], (1, 1)).astype(BF16)
        gradient_t[:, :all_rows] = dot(unit, gradient[:all_rows], (1, 1)).astype(BF16)

    def begin(all_rows):
        top[:, :all_rows] = jnp.full((8, all_rows), NEGATIVE_FLOOR, F32)
        mass[:, :all_rows] = jnp.zeros((8, all_rows), F32)
        query_grad[:, :all_rows] = jnp.zeros((HEAD_WIDTH, all_rows), F32)

    def log_masses(width, chunks, live):
        found = []
        for chunk in range(chunks):
            span = slice(chunk * width, (chunk + 1) * width)
            peak = jnp.max(top[:, span], axis=0, keepdims=True)
            summed = jnp.sum(mass[:, span] * jnp.exp2(top[:, span] - peak), axis=0, keepdims=True)
            found.append(jnp.where(live, peak + jnp.log2(summed), DEAD))
        return found

    def absolute(index, half):
        return index + jnp.where(index < half, core * half, -core * half)

    def reply_tile(slot, carry):
        length = jnp.int32(0)
        for response in range(reply_len.shape[0]):
            mine = reply_slot[response] == group * RESP_DEV + slot
            length = length + jnp.where(mine, reply_len[response], 0)
        first = chip * positions
        source = pl.ds(pl.multiple_of(slot * own_positions, own_positions), own_positions)

        @pl.when(length > first)
        def _():
            for head in range(GROUP):
                for other in range(CORES):
                    at = head * positions + other * own_positions
                    to = slice(at, at + own_positions)
                    left = slice(head * HEAD_WIDTH, (head + 1) * HEAD_WIDTH)
                    right = slice(GROUP_WIDTH + head * HEAD_WIDTH, GROUP_WIDTH + (head + 1) * HEAD_WIDTH)
                    query[to] = rows_in[other][source, left]
                    gradient[to] = rows_in[other][source, right]
                    for which in range(RESP_DEV):
                        @pl.when(slot == which)
                        def _():
                            delta[0:1, to] = deltas[
                                other, head : head + 1, which * own_positions : (which + 1) * own_positions
                            ]
            begin(GROUP * positions)
            turn(GROUP * positions)
            base = prompt_blocks + slot * (chips // 2)
            past = prompt_blocks + chip // 2

            def region_of(index):
                reply = base + ((index - prompt_blocks) ^ (chip // 2))
                return jnp.where(index < prompt_blocks, index, jnp.where(index == past, base, reply))

            def stats(index, carry):
                score_block(region_of(index), index, positions, GROUP, None)
                return carry

            lax.fori_loop(0, past, stats, 0)
            row_at = absolute(iota((1, positions), 1), own_positions)
            key = iota((block, 1), 0)
            key_at = jnp.where(key < positions, absolute(key, own_positions), lax.rem(chip + 1, 2) * block - 1)
            score_block(base, past, positions, GROUP, key_at > row_at)
            live = first + row_at < length
            log_mass = log_masses(positions, GROUP, live)

            grad_blocks(past + 1, region_of, positions, GROUP, log_mass)
            for head in range(GROUP):
                turned = (query_grad[:, head * positions : (head + 1) * positions].T * SCALE).astype(BF16)
                for other in range(CORES):
                    query_out[other][source, head * HEAD_WIDTH : (head + 1) * HEAD_WIDTH] = turned[
                        other * own_positions : (other + 1) * own_positions
                    ]

        @pl.when(length <= first)
        def _():
            for other in range(CORES):
                query_out[other][source, :] = jnp.zeros((own_positions, GROUP_WIDTH), BF16)

        return carry

    lax.fori_loop(0, RESP_DEV, reply_tile, 0)

    head_rows = CORES * prompt_own
    used = GROUP * head_rows
    all_rows = -(-used // 128) * 128
    if all_rows > used:
        query[used:all_rows] = jnp.zeros((all_rows - used, HEAD_WIDTH), BF16)
        gradient[used:all_rows] = jnp.zeros((all_rows - used, HEAD_WIDTH), BF16)
    delta[0:1, :all_rows] = jnp.zeros((1, all_rows), F32)
    for head in range(GROUP):
        for other in range(CORES):
            at = head * head_rows + other * prompt_own
            to = slice(at, at + prompt_own)
            left = slice(head * HEAD_WIDTH, (head + 1) * HEAD_WIDTH)
            right = slice(GROUP_WIDTH + head * HEAD_WIDTH, GROUP_WIDTH + (head + 1) * HEAD_WIDTH)
            query[to] = rows_in[other][reply_own:, left]
            gradient[to] = rows_in[other][reply_own:, right]
            delta[0:1, to] = deltas[other, head : head + 1, reply_own:]
    begin(all_rows)
    turn(all_rows)
    lane = iota((1, all_rows), 1)
    within = lane
    for head in range(1, GROUP):
        within = within - jnp.where(lane >= head * head_rows, head_rows, 0)
    offset = jnp.where(within < prompt_own, within, within - prompt_own)
    row_core = jnp.where(within < prompt_own, core, 1 - core)
    real = (lane < used) & (offset < prompt_rows)
    row_at = jnp.where(
        real, (chip * CORES + row_core) * prompt_keys + group * prompt_rows + offset, -1
    )
    per_block = max(block // chip_prompt, 1)
    block_parts = max(chip_prompt // block, 1)
    pair = chip // per_block
    seen = (pair + 1) * block_parts

    def prompt_region(index):
        return (index // block_parts ^ pair) * block_parts + index % block_parts

    def prompt_stats(index, carry):
        key = iota((block, 1), 0) + index % block_parts * block
        key_chip = ((index // block_parts ^ pair) * per_block + key // chip_prompt) ^ chip
        key_at = key_chip * chip_prompt + absolute(key % chip_prompt, prompt_keys)
        score_block(prompt_region(index), index, all_rows, 1, key_at > row_at)
        return carry

    lax.fori_loop(0, seen, prompt_stats, 0)
    log_mass = log_masses(all_rows, 1, real)

    grad_blocks(seen, prompt_region, all_rows, 1, log_mass)
    turned = (query_grad[:, :all_rows].T * SCALE).astype(BF16)
    for head in range(GROUP):
        for other in range(CORES):
            at = head * head_rows + other * prompt_own
            query_out[other][reply_own:, head * HEAD_WIDTH : (head + 1) * HEAD_WIDTH] = turned[
                at : at + prompt_own
            ]

    for index in range(chips * CORES):
        away, other = index // CORES, index % CORES
        out = keys_out[index] if joint_keys else keys_out[away].at[other]

        def put(to, at, count):
            out[to : to + count, :HEAD_WIDTH] = (total[at : at + count, :HEAD_WIDTH] * SCALE).astype(BF16)
            out[to : to + count, HEAD_WIDTH:] = total[at : at + count, HEAD_WIDTH:].astype(BF16)

        put(0, away * chip_prompt + other * prompt_keys, prompt_keys)
        for slot in range(RESP_DEV):
            at = chips * chip_prompt + (slot * chips + away) * positions + other * own_positions
            put(prompt_keys + slot * own_positions, at, own_positions)


def add(first, *rest):
    value = first.astype(F32)
    for part in rest:
        value = value + part.astype(F32)
    return value


def add_pairs(*refs):
    count = len(refs) // 3
    for index in range(count):
        refs[2 * count + index][...] = add(refs[index][...], refs[count + index][...]).astype(BF16)


def collect(*refs):
    parts, mine, theirs = refs[:-2], refs[-2], refs[-1]
    mine[...] = add(*(part[0] for part in parts))
    theirs[...] = add(*(part[1] for part in parts)).astype(BF16)


def spread_prompt(sizes, place, *refs):
    refs, outs, summed = refs[: sum(sizes)], refs[sum(sizes) : -1], refs[-1]
    groups, rows = len(outs), outs[0].shape[1]
    for index, size in enumerate(sizes):
        parts, refs = refs[:size], refs[size:]
        summed[index] = add(*(part[: groups * rows] for part in parts))
    for shift in range(groups):
        at = pl.ds(pl.multiple_of(lax.rem(place[2] + shift, groups) * rows, rows), rows)
        for index in range(len(sizes)):
            outs[shift][index] = summed[index, at].astype(BF16)


def finish_reply(sizes, place, *refs):
    parts_in, refs = refs[: sum(sizes)], refs[sum(sizes) :]
    queries, refs = refs[: len(sizes)], refs[len(sizes) :]
    prompt_dq, reply_dq, reply_dk, reply_dv = refs
    reply = reply_dq.shape[0]
    order = unsorting(reply)
    for index, size in enumerate(sizes):
        parts, parts_in = parts_in[:size], parts_in[size:]
        head = head_of(place[1], index % CORES, index // CORES)
        span = lanes(head, HEAD_WIDTH)
        value = add(*(part[part.shape[0] - reply :] for part in parts))
        value = dot(order, value.astype(BF16)).astype(BF16)
        reply_dk[:, span] = value[:, :HEAD_WIDTH]
        reply_dv[:, span] = value[:, HEAD_WIDTH:]
        span = lanes(head, GROUP_WIDTH)
        reply_dq[:, span] = dot(order, queries[index][:reply]).astype(BF16)
        prompt_dq[:, span] = queries[index][reply:]


def finish_prompt(place, *refs):
    parts, prompt_dk, prompt_dv = refs[:-2], refs[-2], refs[-1]
    for index in range(KEY_VALUE_HEADS):
        span = lanes(head_of(place[1], index % CORES, index // CORES), HEAD_WIDTH)
        value = add(*(part[index] for part in parts)).astype(BF16)
        prompt_dk[:, span] = value[:, :HEAD_WIDTH]
        prompt_dv[:, span] = value[:, HEAD_WIDTH:]


def on_device(
    prompt_query,
    prompt_k,
    prompt_value,
    prompt_output,
    prompt_output_gradient,
    reply_query,
    reply_key,
    reply_value,
    reply_output,
    reply_output_gradient,
    reply_len,
    reply_slot,
):
    devices = lax.axis_size("pre")
    groups = lax.axis_size("rsp")
    chips = devices // CORES
    prompt_rows = prompt_query.shape[0]
    prompt_own = -(-prompt_rows // 16) * 16
    prompt_keys = prompt_k.shape[0]
    reply_own = reply_query.shape[1]
    own_positions = reply_own // RESP_DEV
    positions = CORES * own_positions
    chip_prompt = CORES * prompt_keys
    block = 2 * positions
    assert (chip_prompt % block == 0 or block % chip_prompt == 0) and chips > 1 and chips & (chips - 1) == 0
    pre_index = lax.axis_index("pre")
    place = jnp.stack([lax.div(pre_index, CORES), lax.rem(pre_index, CORES), lax.axis_index("rsp")])

    def shape(*dims, dtype=BF16):
        return jax.ShapeDtypeStruct(dims, dtype)

    def move(array, away, cross=0):
        pairs = [(p, (p // CORES ^ away) * CORES + (p % CORES ^ cross)) for p in range(devices)]
        return lax.ppermute(array, "pre", pairs)

    def swap(array):
        return move(array, 0, 1)

    def call(kernel, name, mib, inputs, outs, scalars=1, spec=VMEM, **more):
        return pl.pallas_call(
            kernel,
            out_shape=outs,
            in_specs=[SMEM] * scalars + [spec] * (len(inputs) - scalars),
            out_specs=[VMEM] * len(outs),
            compiler_params=params(mib),
            name=name,
            **more,
        )(*inputs)

    relayed = chips == 4
    key_shape = (prompt_keys + reply_own, 2 * HEAD_WIDTH)
    mine0, theirs0, mine1, theirs, token = call(
        prepare_keys,
        "prepare_keys",
        LARGE_MIB,
        (place, prompt_k, prompt_value, reply_key[0], reply_value[0]),
        [shape(*key_shape)] * 3 + [shape(LOCAL_HEADS, *key_shape), shape(8, 128, dtype=F32)],
        spec=HBM,
        scratch_shapes=[
            pltpu.VMEM((rows, KEY_VALUE_HEADS * HEAD_WIDTH), BF16)
            for rows in (prompt_keys, prompt_keys, reply_own, reply_own)
        ]
        + [pltpu.SemaphoreType.DMA((4,))],
    )
    blocks0 = {(0, 0): mine0, (0, 1): swap(theirs)}
    for away in range(1, 3 if relayed else chips):
        blocks0[away, 0] = move(mine0, away)
        blocks0[away, 1] = move(theirs0, away, 1)
    if prompt_own > prompt_rows:
        room = ((0, prompt_own - prompt_rows), (0, 0))
        prompt_query, prompt_output, prompt_output_gradient = (
            jnp.pad(array, room)
            for array in (prompt_query, prompt_output, prompt_output_gradient)
        )
    own_rows = reply_own + prompt_own
    row_width = 2 * GROUP_WIDTH + HEAD_WIDTH

    rows = call(
        prepare_rows,
        "prepare_rows",
        LARGE_MIB,
        (
            place,
            token,
            prompt_query,
            prompt_output,
            prompt_output_gradient,
            reply_query[0],
            reply_output[0],
            reply_output_gradient[0],
        ),
        [shape(own_rows, row_width)] * KEY_VALUE_HEADS,
        spec=HBM,
        scratch_shapes=[
            pltpu.VMEM((KEY_VALUE_HEADS, rows, GROUP_WIDTH), BF16)
            for rows in [prompt_own] * 3 + [reply_own] * 3
        ]
        + [pltpu.SemaphoreType.DMA((KEY_VALUE_HEADS * 6,))],
        cost_estimate=pl.CostEstimate(
            flops=6 * reply_own * reply_own * QUERY_HEADS * HEAD_WIDTH,
            bytes_accessed=20 * reply_own * QUERY_HEADS * HEAD_WIDTH,
            transcendentals=0,
        ),
    )

    blocks0, rows, mine1 = lax.optimization_barrier((blocks0, rows, mine1))
    if relayed:
        blocks0[3, 0] = move(blocks0[1, 0], 2)
        blocks0[3, 1] = move(blocks0[2, 1], 1)
    chip1 = jnp.stack([mine1, blocks0[0, 1][1]])
    blocks1 = [chip1] + [move(chip1, away) for away in range(1, chips)]

    blocks = (chips * chip_prompt + RESP_DEV * chips * positions) // block
    slots = (chips * chip_prompt + chips * positions) // block
    all_rows = max(GROUP * positions, -(-GROUP * CORES * prompt_own // 128) * 128)
    sizes = (chips, reply_own, prompt_own, prompt_rows, prompt_keys)
    score_count = GROUP * (positions * RESP_DEV * slots * block)

    def run_attend(local, key_blocks):
        joint_keys = local == 1
        sums = [shape(*key_shape)] * devices if joint_keys else [shape(CORES, *key_shape)] * chips
        query_mine, query_theirs, *sums = call(
            functools.partial(attend, sizes, joint_keys),
            "attend",
            VMEM_MIB,
            (
                place,
                reply_len,
                reply_slot,
                rows[CORES * local + 1],
                swap(rows[CORES * local]),
                *key_blocks,
            ),
            [shape(own_rows, GROUP_WIDTH)] * CORES + sums,
            scalars=3,
            scratch_shapes=[
                pltpu.VMEM((blocks * block, 2 * HEAD_WIDTH), BF16),
                pltpu.VMEM((blocks, HEAD_WIDTH, block), BF16),
                pltpu.VMEM((blocks * block, 2 * HEAD_WIDTH), F32),
                pltpu.VMEM((all_rows, HEAD_WIDTH), BF16),
                pltpu.VMEM((all_rows, HEAD_WIDTH), BF16),
                pltpu.VMEM((HEAD_WIDTH, all_rows), BF16),
                pltpu.VMEM((HEAD_WIDTH, all_rows), BF16),
                pltpu.VMEM((CORES, 8, own_rows), F32),
                pltpu.VMEM((8, all_rows), F32),
                pltpu.VMEM((slots, block, all_rows), F32),
                pltpu.VMEM((8, all_rows), F32),
                pltpu.VMEM((8, all_rows), F32),
                pltpu.VMEM((HEAD_WIDTH, all_rows), F32),
            ]
            + [pltpu.VMEM((block, all_rows), BF16)] * 4,
            cost_estimate=pl.CostEstimate(
                flops=score_count * 10 * HEAD_WIDTH,
                bytes_accessed=8 * 1024 * 1024,
                transcendentals=2 * score_count,
            ),
        )
        return query_mine, query_theirs, sums

    query_mine0, query_theirs0, sums0 = run_attend(
        0, [blocks0[away, other] for away in range(chips) for other in range(CORES)]
    )
    arrived0 = [sums0[0]] + [move(sums0[away], away) for away in range(1, chips)]
    query_theirs0 = swap(query_theirs0)
    query_mine1, query_theirs1, sums1 = run_attend(1, blocks1)
    arrived0, query_theirs0, query_theirs1, sums1 = lax.optimization_barrier(
        (arrived0, query_theirs0, query_theirs1, sums1)
    )
    sums1 = [sums1[CORES * away : CORES * away + CORES] for away in range(chips)]
    if relayed:
        through_y, through_x = move(sums1[3][0], 2), move(sums1[3][1], 1)
        for_x, for_y = call(
            add_pairs,
            "add_pairs",
            SMALL_MIB,
            (sums1[1][0], sums1[2][1], through_y, through_x),
            [shape(*key_shape)] * 2,
            scalars=0,
        )
        near = [sums1[0][0], move(sums1[1][1], 1, 1), move(sums1[2][0], 2)]
        for_x, for_y, sums1[0][1], query_theirs1 = lax.optimization_barrier(
            (for_x, for_y, sums1[0][1], query_theirs1)
        )
        lists1 = [[near[0], move(for_x, 1), near[2]], [swap(sums1[0][1]), near[1], move(for_y, 2, 1)]]
    else:
        lists1 = [
            [move(pair[other], away, other) if away or other else pair[other] for away, pair in enumerate(sums1)]
            for other in range(CORES)
        ]
    mine0, theirs0 = call(
        collect,
        "collect",
        SMALL_MIB,
        arrived0,
        [shape(*key_shape, dtype=F32), shape(*key_shape)],
        scalars=0,
    )
    lists = [[mine0], [swap(theirs0)]] + lists1
    queries = [query_mine0, query_theirs0, query_mine1, swap(query_theirs1)]
    counts = [len(parts) for parts in lists]
    parts = [part for one in lists for part in one]
    cut_rows = prompt_keys // groups
    cuts = call(
        functools.partial(spread_prompt, counts),
        "spread_prompt",
        SMALL_MIB,
        (place, *parts),
        [shape(KEY_VALUE_HEADS, cut_rows, 2 * HEAD_WIDTH)] * groups,
        scratch_shapes=[pltpu.VMEM((KEY_VALUE_HEADS, prompt_keys, 2 * HEAD_WIDTH), F32)],
    )
    slices = [cuts[0]] + [
        lax.ppermute(cuts[shift], "rsp", [(g, (g + shift) % groups) for g in range(groups)])
        for shift in range(1, groups)
    ]
    key_width = KEY_VALUE_HEADS * HEAD_WIDTH
    query_width = QUERY_HEADS * HEAD_WIDTH
    prompt_dq, reply_dq, reply_dk, reply_dv = call(
        functools.partial(finish_reply, counts),
        "finish_reply",
        SMALL_MIB,
        (place, *parts, *queries),
        [
            shape(prompt_own, query_width),
            shape(reply_own, query_width),
            shape(reply_own, key_width),
            shape(reply_own, key_width),
        ],
        cost_estimate=pl.CostEstimate(
            flops=2 * reply_own * reply_own * (query_width + 2 * key_width),
            bytes_accessed=16 * reply_own * query_width,
            transcendentals=0,
        ),
    )
    slices, prompt_dq = lax.optimization_barrier((slices, prompt_dq))
    prompt_dk, prompt_dv = call(
        finish_prompt,
        "finish_prompt",
        SMALL_MIB,
        (place, *slices),
        [shape(cut_rows, key_width)] * 2,
    )
    return (
        prompt_dq[:prompt_rows],
        prompt_dk,
        prompt_dv,
        reply_dq[None],
        reply_dk[None],
        reply_dv[None],
    )


def solution(mesh):
    return jax.shard_map(
        on_device,
        mesh=mesh,
        in_specs=(
            P(("pre", "rsp"), None),
            P("pre", None),
            P("pre", None),
            P(("pre", "rsp"), None),
            P(("pre", "rsp"), None),
            P("rsp", "pre", None),
            P("rsp", "pre", None),
            P("rsp", "pre", None),
            P("rsp", "pre", None),
            P("rsp", "pre", None),
            P(),
            P(),
        ),
        out_specs=(
            P(("pre", "rsp"), None),
            P(("pre", "rsp"), None),
            P(("pre", "rsp"), None),
            P("rsp", "pre", None),
            P("rsp", "pre", None),
            P("rsp", "pre", None),
        ),
        check_vma=False,
    )
```

```python
import functools
import math

import jax
import jax.numpy as jnp
from jax import lax
from jax.experimental import pallas as pl
from jax.experimental.pallas import tpu as pltpu
from jax.sharding import PartitionSpec as P

QUERY_HEADS = 20
KEY_VALUE_HEADS = 4
GROUP = QUERY_HEADS // KEY_VALUE_HEADS
HEAD_WIDTH = 128
RESP_DEV = 2
CORES = 2
LOCAL_HEADS = KEY_VALUE_HEADS // CORES
GROUP_WIDTH = GROUP * HEAD_WIDTH

SCALE = HEAD_WIDTH ** (-0.5)
SCALE_LOG2 = SCALE * math.log2(math.e)
PART = 128
NEGATIVE_FLOOR = -1e30
DEAD = 1e30
F32 = jnp.float32
BF16 = jnp.bfloat16
VMEM = pl.BlockSpec(memory_space=pltpu.VMEM)
SMEM = pl.BlockSpec(memory_space=pltpu.SMEM)
HBM = pl.BlockSpec(memory_space=pltpu.HBM)


VMEM_MIB = 40
SMALL_MIB = 24
LARGE_MIB = 58


def params(mib):
    return pltpu.CompilerParams(vmem_limit_bytes=mib * 1024 * 1024)


def dot(a, b, over=(1, 0)):
    return lax.dot_general(
        a, b, (((over[0],), (over[1],)), ((), ())), preferred_element_type=F32
    )


def iota(shape, axis):
    return lax.broadcasted_iota(jnp.int32, shape, axis)


def sorting(rows):
    half = rows // RESP_DEV
    out = iota((rows, rows), 0)
    source = jnp.where(out < half, RESP_DEV * out, RESP_DEV * (out - half) + 1)
    return (iota((rows, rows), 1) == source).astype(BF16)


def unsorting(rows):
    half = rows // RESP_DEV
    out = iota((rows, rows), 1)
    source = jnp.where(out < half, RESP_DEV * out, RESP_DEV * (out - half) + 1)
    return (iota((rows, rows), 0) == source).astype(BF16)


def lanes(index, width):
    return pl.ds(pl.multiple_of(index * width, width), width)


def head_of(core, cross, local):
    owner = (1 - core) if cross else core
    return owner * LOCAL_HEADS + local


def fetch(pairs, sems):
    copies = [pltpu.make_async_copy(src, dst, sems.at[i]) for i, (src, dst) in enumerate(pairs)]
    for copy in copies:
        copy.start()
    return copies


def prepare_keys(place, pk, pv, rk, rv, mine0, theirs0, mine1, theirs, token, *scratch):
    core = place[1]
    bufs, sems = scratch[:-1], scratch[-1]
    copies = fetch(zip((pk, pv, rk, rv), bufs), sems)
    prompt = pk.shape[0]
    order = sorting(rk.shape[0])
    for copy in copies:
        copy.wait()
    pk, pv, rk, rv = bufs
    for local, outs in enumerate(((mine0, theirs.at[0]), (mine1, theirs.at[1]))):
        for cross, out in enumerate(outs):
            span = lanes(head_of(core, cross, local), HEAD_WIDTH)
            for part, (p, r) in enumerate(((pk, rk), (pv, rv))):
                to = slice(part * HEAD_WIDTH, (part + 1) * HEAD_WIDTH)
                out[:prompt, to] = p[:, span]
                out[prompt:, to] = dot(order, r[:, span]).astype(BF16)
    theirs0[...] = theirs[0]
    token[...] = jnp.zeros_like(token)


def prepare_rows(place, token, pq, po, pg, rq, ro, rg, *refs):
    (theirs, *mine), bufs, sems = refs[: 1 + LOCAL_HEADS], refs[1 + LOCAL_HEADS : -1], refs[-1]
    outs = [out for local in range(LOCAL_HEADS) for out in (theirs.at[local], mine[local])]
    core = place[1]
    reply = rq.shape[0]
    sources = (pq, po, pg, rq, ro, rg)
    pairs = []
    for step in range(KEY_VALUE_HEADS):
        span = lanes(head_of(core, 1 - step % CORES, step // CORES), GROUP_WIDTH)
        pairs += [(source.at[:, span], buf.at[step]) for source, buf in zip(sources, bufs)]
    copies = fetch(pairs, sems)
    order = sorting(reply)
    column = iota((GROUP_WIDTH, HEAD_WIDTH), 1)
    pick = (column // 3 == iota((GROUP_WIDTH, HEAD_WIDTH), 0) // HEAD_WIDTH).astype(BF16)

    def delta(gradient, output):
        product = gradient.astype(F32) * output.astype(F32)
        high = product.astype(BF16)
        low = (product - high.astype(F32)).astype(BF16)
        value = dot(high, pick) + dot(low, pick)
        first = value.astype(BF16).astype(F32)
        second = (value - first).astype(BF16).astype(F32)
        part = iota(value.shape, 1) % 3
        return jnp.where(part == 0, first, jnp.where(part == 1, second, value - first - second)).astype(BF16)

    for step, out in enumerate(outs):
        for copy in copies[step * len(sources) : (step + 1) * len(sources)]:
            copy.wait()
        pq, po, pg, rq, ro, rg = (buf[step] for buf in bufs)
        out[reply:, :GROUP_WIDTH] = pq
        out[reply:, GROUP_WIDTH : 2 * GROUP_WIDTH] = pg
        out[reply:, 2 * GROUP_WIDTH :] = delta(pg, po)
        out[:reply, :GROUP_WIDTH] = dot(order, rq).astype(BF16)
        gradient = dot(order, rg).astype(BF16)
        out[:reply, GROUP_WIDTH : 2 * GROUP_WIDTH] = gradient
        out[:reply, 2 * GROUP_WIDTH :] = delta(gradient, dot(order, ro).astype(BF16))


def attend(sizes, joint_keys, place, reply_len, reply_slot, *refs):
    chips, reply_own, prompt_own, prompt_rows, prompt_keys = sizes
    own_positions = reply_own // RESP_DEV
    positions = CORES * own_positions
    chip_prompt = CORES * prompt_keys
    block = 2 * positions
    prompt_blocks = chips * chip_prompt // block
    rows_in, refs = (refs[0], refs[1].at[int(joint_keys)]), refs[2:]
    count = chips if joint_keys else chips * CORES
    keys_in, refs = refs[:count], refs[count:]
    query_out, refs = refs[:2], refs[2:]
    count = chips * CORES if joint_keys else chips
    keys_out, refs = refs[:count], refs[count:]
    keys, keys_t, total, query, gradient, query_t, gradient_t, deltas, delta, scores, peaks, top, mass, *refs = refs
    query_grad, stages = refs[0], (refs[1:3], refs[3:5])
    chip, core, group = place[0], place[1], place[2]

    pick = (iota((8, HEAD_WIDTH), 1) // 3 == iota((8, HEAD_WIDTH), 0)).astype(BF16)
    for other in range(CORES):
        deltas[other] = dot(pick, rows_in[other][:, 2 * GROUP_WIDTH :], (1, 1))

    for index in range(chips * CORES):
        away, other = index // CORES, index % CORES
        source = keys_in[away].at[other] if joint_keys else keys_in[index]
        source = source if len(source.shape) == 2 else source.at[0]
        at = away * chip_prompt + other * prompt_keys
        keys[at : at + prompt_keys] = source[:prompt_keys]
        for slot in range(RESP_DEV):
            at = chips * chip_prompt + (slot * chips + away) * positions + other * own_positions
            begin = prompt_keys + slot * own_positions
            keys[at : at + own_positions] = source[begin : begin + own_positions]
    total[...] = jnp.zeros_like(total)

    unit = (iota((HEAD_WIDTH, HEAD_WIDTH), 0) == iota((HEAD_WIDTH, HEAD_WIDTH), 1)).astype(BF16)

    def transpose_block(index, carry):
        rows = pl.ds(pl.multiple_of(index * block, block), block)
        keys_t[index] = dot(unit, keys[rows, :HEAD_WIDTH], (1, 1)).astype(BF16)
        return carry

    lax.fori_loop(0, keys_t.shape[0], transpose_block, 0)

    def score_block(region, place_in, width, chunks, hidden):
        rows = pl.ds(pl.multiple_of(region * block, block), block)
        key_rows = keys[rows, :HEAD_WIDTH]
        for chunk in range(chunks):
            span = slice(chunk * width, (chunk + 1) * width)
            value = dot(key_rows, query_t[:, span]) * SCALE_LOG2
            if hidden is not None:
                value = jnp.where(hidden, NEGATIVE_FLOOR, value)
            split = value.reshape(block // 8, 8, width)
            peak, summed = top[:, span], mass[:, span]
            for part in range(block // PART):
                piece = split[part * PART // 8 : (part + 1) * PART // 8]
                now = jnp.maximum(peak, jnp.max(piece, axis=0))
                shifted = jnp.exp2(piece - now[None])
                scores[place_in, part * PART : (part + 1) * PART, span] = shifted.reshape(PART, width)
                peaks[place_in, part, :, span] = now
                summed = summed * jnp.exp2(peak - now) + jnp.sum(shifted, axis=0)
                peak = now
            top[:, span], mass[:, span] = peak, summed

    def weigh(region, place_in, width, chunks, log_mass, stage, earlier=None, earlier_stage=None):
        rows = pl.ds(pl.multiple_of(region * block, block), block)
        value_rows = keys[rows, HEAD_WIDTH:]
        for chunk in range(chunks):
            span = slice(chunk * width, (chunk + 1) * width)
            dp = dot(value_rows, gradient_t[:, span])
            for part in range(block // PART):
                at = slice(part * PART, (part + 1) * PART)
                factor = jnp.exp2(peaks[place_in, part, :, span] - log_mass[chunk])
                p = scores[place_in, at, span].reshape(PART // 8, 8, width) * factor[None]
                p = p.reshape(PART, width)
                stage[0][at, span] = p.astype(BF16)
                stage[1][at, span] = (p * (dp[at] - delta[0:1, span])).astype(BF16)
            if earlier is not None:
                multiply(earlier, width, chunks, earlier_stage, chunk)
        if earlier is not None:
            for chunk in range(chunks, 3):
                multiply(earlier, width, chunks, earlier_stage, chunk)

    def multiply(region, width, chunks, stage, part):
        rows = pl.ds(pl.multiple_of(region * block, block), block)
        used = width * chunks
        if part == 0:
            total[rows, HEAD_WIDTH:] += dot(stage[0][:, :used], gradient[:used])
        elif part == 1:
            total[rows, :HEAD_WIDTH] += dot(stage[1][:, :used], query[:used])
        elif part == 2:
            query_grad[:, :used] += dot(keys_t[region], stage[1][:, :used])

    def grad_blocks(count, region_of, width, chunks, log_mass):
        first, second = stages

        def later(index, stage, earlier_stage):
            weigh(
                region_of(index), index, width, chunks, log_mass, stage, region_of(index - 1), earlier_stage
            )

        def last(stage):
            for part in range(3):
                multiply(region_of(count - 1), width, chunks, stage, part)

        weigh(region_of(0), 0, width, chunks, log_mass, first)

        def two(index, carry):
            later(2 * index + 1, second, first)
            later(2 * index + 2, first, second)
            return carry

        lax.fori_loop(0, (count - 1) // 2, two, 0)

        @pl.when(count % 2 == 0)
        def _():
            later(count - 1, second, first)
            last(second)

        @pl.when(count % 2 == 1)
        def _():
            last(first)

    def turn(all_rows):
        query_t[:, :all_rows] = dot(unit, query[:all_rows], (1, 1)).astype(BF16)
        gradient_t[:, :all_rows] = dot(unit, gradient[:all_rows], (1, 1)).astype(BF16)

    def begin(all_rows):
        top[:, :all_rows] = jnp.full((8, all_rows), NEGATIVE_FLOOR, F32)
        mass[:, :all_rows] = jnp.zeros((8, all_rows), F32)
        query_grad[:, :all_rows] = jnp.zeros((HEAD_WIDTH, all_rows), F32)

    def log_masses(width, chunks, live):
        found = []
        for chunk in range(chunks):
            span = slice(chunk * width, (chunk + 1) * width)
            peak = jnp.max(top[:, span], axis=0, keepdims=True)
            summed = jnp.sum(mass[:, span] * jnp.exp2(top[:, span] - peak), axis=0, keepdims=True)
            found.append(jnp.where(live, peak + jnp.log2(summed), DEAD))
        return found

    def absolute(index, half):
        return index + jnp.where(index < half, core * half, -core * half)

    def reply_tile(slot, carry):
        length = jnp.int32(0)
        for response in range(reply_len.shape[0]):
            mine = reply_slot[response] == group * RESP_DEV + slot
            length = length + jnp.where(mine, reply_len[response], 0)
        first = chip * positions
        source = pl.ds(pl.multiple_of(slot * own_positions, own_positions), own_positions)

        @pl.when(length > first)
        def _():
            for head in range(GROUP):
                for other in range(CORES):
                    at = head * positions + other * own_positions
                    to = slice(at, at + own_positions)
                    left = slice(head * HEAD_WIDTH, (head + 1) * HEAD_WIDTH)
                    right = slice(GROUP_WIDTH + head * HEAD_WIDTH, GROUP_WIDTH + (head + 1) * HEAD_WIDTH)
                    query[to] = rows_in[other][source, left]
                    gradient[to] = rows_in[other][source, right]
                    for which in range(RESP_DEV):
                        @pl.when(slot == which)
                        def _():
                            delta[0:1, to] = deltas[
                                other, head : head + 1, which * own_positions : (which + 1) * own_positions
                            ]
            begin(GROUP * positions)
            turn(GROUP * positions)
            base = prompt_blocks + slot * (chips // 2)
            past = prompt_blocks + chip // 2

            def region_of(index):
                reply = base + ((index - prompt_blocks) ^ (chip // 2))
                return jnp.where(index < prompt_blocks, index, jnp.where(index == past, base, reply))

            def stats(index, carry):
                score_block(region_of(index), index, positions, GROUP, None)
                return carry

            lax.fori_loop(0, past, stats, 0)
            row_at = absolute(iota((1, positions), 1), own_positions)
            key = iota((block, 1), 0)
            key_at = jnp.where(key < positions, absolute(key, own_positions), lax.rem(chip + 1, 2) * block - 1)
            score_block(base, past, positions, GROUP, key_at > row_at)
            live = first + row_at < length
            log_mass = log_masses(positions, GROUP, live)

            grad_blocks(past + 1, region_of, positions, GROUP, log_mass)
            for head in range(GROUP):
                turned = (query_grad[:, head * positions : (head + 1) * positions].T * SCALE).astype(BF16)
                for other in range(CORES):
                    query_out[other][source, head * HEAD_WIDTH : (head + 1) * HEAD_WIDTH] = turned[
                        other * own_positions : (other + 1) * own_positions
                    ]

        @pl.when(length <= first)
        def _():
            for other in range(CORES):
                query_out[other][source, :] = jnp.zeros((own_positions, GROUP_WIDTH), BF16)

        return carry

    lax.fori_loop(0, RESP_DEV, reply_tile, 0)

    head_rows = CORES * prompt_own
    used = GROUP * head_rows
    all_rows = -(-used // 128) * 128
    if all_rows > used:
        query[used:all_rows] = jnp.zeros((all_rows - used, HEAD_WIDTH), BF16)
        gradient[used:all_rows] = jnp.zeros((all_rows - used, HEAD_WIDTH), BF16)
    delta[0:1, :all_rows] = jnp.zeros((1, all_rows), F32)
    for head in range(GROUP):
        for other in range(CORES):
            at = head * head_rows + other * prompt_own
            to = slice(at, at + prompt_own)
            left = slice(head * HEAD_WIDTH, (head + 1) * HEAD_WIDTH)
            right = slice(GROUP_WIDTH + head * HEAD_WIDTH, GROUP_WIDTH + (head + 1) * HEAD_WIDTH)
            query[to] = rows_in[other][reply_own:, left]
            gradient[to] = rows_in[other][reply_own:, right]
            delta[0:1, to] = deltas[other, head : head + 1, reply_own:]
    begin(all_rows)
    turn(all_rows)
    lane = iota((1, all_rows), 1)
    within = lane
    for head in range(1, GROUP):
        within = within - jnp.where(lane >= head * head_rows, head_rows, 0)
    offset = jnp.where(within < prompt_own, within, within - prompt_own)
    row_core = jnp.where(within < prompt_own, core, 1 - core)
    real = (lane < used) & (offset < prompt_rows)
    row_at = jnp.where(
        real, (chip * CORES + row_core) * prompt_keys + group * prompt_rows + offset, -1
    )
    per_block = max(block // chip_prompt, 1)
    block_parts = max(chip_prompt // block, 1)
    pair = chip // per_block
    seen = (pair + 1) * block_parts

    def prompt_region(index):
        return (index // block_parts ^ pair) * block_parts + index % block_parts

    def prompt_stats(index, carry):
        key = iota((block, 1), 0) + index % block_parts * block
        key_chip = ((index // block_parts ^ pair) * per_block + key // chip_prompt) ^ chip
        key_at = key_chip * chip_prompt + absolute(key % chip_prompt, prompt_keys)
        score_block(prompt_region(index), index, all_rows, 1, key_at > row_at)
        return carry

    lax.fori_loop(0, seen, prompt_stats, 0)
    log_mass = log_masses(all_rows, 1, real)

    grad_blocks(seen, prompt_region, all_rows, 1, log_mass)
    turned = (query_grad[:, :all_rows].T * SCALE).astype(BF16)
    for head in range(GROUP):
        for other in range(CORES):
            at = head * head_rows + other * prompt_own
            query_out[other][reply_own:, head * HEAD_WIDTH : (head + 1) * HEAD_WIDTH] = turned[
                at : at + prompt_own
            ]

    for index in range(chips * CORES):
        away, other = index // CORES, index % CORES
        out = keys_out[index] if joint_keys else keys_out[away].at[other]

        def put(to, at, count):
            out[to : to + count, :HEAD_WIDTH] = (total[at : at + count, :HEAD_WIDTH] * SCALE).astype(BF16)
            out[to : to + count, HEAD_WIDTH:] = total[at : at + count, HEAD_WIDTH:].astype(BF16)

        put(0, away * chip_prompt + other * prompt_keys, prompt_keys)
        for slot in range(RESP_DEV):
            at = chips * chip_prompt + (slot * chips + away) * positions + other * own_positions
            put(prompt_keys + slot * own_positions, at, own_positions)


def add(first, *rest):
    value = first.astype(F32)
    for part in rest:
        value = value + part.astype(F32)
    return value


def add_pairs(*refs):
    count = len(refs) // 3
    for index in range(count):
        refs[2 * count + index][...] = add(refs[index][...], refs[count + index][...]).astype(BF16)


def collect(*refs):
    parts, mine, theirs = refs[:-2], refs[-2], refs[-1]
    mine[...] = add(*(part[0] for part in parts))
    theirs[...] = add(*(part[1] for part in parts)).astype(BF16)


def spread_prompt(sizes, place, *refs):
    refs, outs, summed = refs[: sum(sizes)], refs[sum(sizes) : -1], refs[-1]
    groups, rows = len(outs), outs[0].shape[1]
    for index, size in enumerate(sizes):
        parts, refs = refs[:size], refs[size:]
        summed[index] = add(*(part[: groups * rows] for part in parts))
    for shift in range(groups):
        at = pl.ds(pl.multiple_of(lax.rem(place[2] + shift, groups) * rows, rows), rows)
        for index in range(len(sizes)):
            outs[shift][index] = summed[index, at].astype(BF16)


def finish_reply(sizes, place, *refs):
    parts_in, refs = refs[: sum(sizes)], refs[sum(sizes) :]
    queries, refs = refs[: len(sizes)], refs[len(sizes) :]
    prompt_dq, reply_dq, reply_dk, reply_dv = refs
    reply = reply_dq.shape[0]
    order = unsorting(reply)
    for index, size in enumerate(sizes):
        parts, parts_in = parts_in[:size], parts_in[size:]
        head = head_of(place[1], index % CORES, index // CORES)
        span = lanes(head, HEAD_WIDTH)
        value = add(*(part[part.shape[0] - reply :] for part in parts))
        value = dot(order, value.astype(BF16)).astype(BF16)
        reply_dk[:, span] = value[:, :HEAD_WIDTH]
        reply_dv[:, span] = value[:, HEAD_WIDTH:]
        span = lanes(head, GROUP_WIDTH)
        reply_dq[:, span] = dot(order, queries[index][:reply]).astype(BF16)
        prompt_dq[:, span] = queries[index][reply:]


def finish_prompt(place, *refs):
    parts, prompt_dk, prompt_dv = refs[:-2], refs[-2], refs[-1]
    for index in range(KEY_VALUE_HEADS):
        span = lanes(head_of(place[1], index % CORES, index // CORES), HEAD_WIDTH)
        value = add(*(part[index] for part in parts)).astype(BF16)
        prompt_dk[:, span] = value[:, :HEAD_WIDTH]
        prompt_dv[:, span] = value[:, HEAD_WIDTH:]


def on_device(
    prompt_query,
    prompt_k,
    prompt_value,
    prompt_output,
    prompt_output_gradient,
    reply_query,
    reply_key,
    reply_value,
    reply_output,
    reply_output_gradient,
    reply_len,
    reply_slot,
):
    devices = lax.axis_size("pre")
    groups = lax.axis_size("rsp")
    chips = devices // CORES
    prompt_rows = prompt_query.shape[0]
    prompt_own = -(-prompt_rows // 16) * 16
    prompt_keys = prompt_k.shape[0]
    reply_own = reply_query.shape[1]
    own_positions = reply_own // RESP_DEV
    positions = CORES * own_positions
    chip_prompt = CORES * prompt_keys
    block = 2 * positions
    assert (chip_prompt % block == 0 or block % chip_prompt == 0) and chips > 1 and chips & (chips - 1) == 0
    pre_index = lax.axis_index("pre")
    place = jnp.stack([lax.div(pre_index, CORES), lax.rem(pre_index, CORES), lax.axis_index("rsp")])

    def shape(*dims, dtype=BF16):
        return jax.ShapeDtypeStruct(dims, dtype)

    def move(array, away, cross=0):
        pairs = [(p, (p // CORES ^ away) * CORES + (p % CORES ^ cross)) for p in range(devices)]
        return lax.ppermute(array, "pre", pairs)

    def swap(array):
        return move(array, 0, 1)

    def call(kernel, name, mib, inputs, outs, scalars=1, spec=VMEM, **more):
        return pl.pallas_call(
            kernel,
            out_shape=outs,
            in_specs=[SMEM] * scalars + [spec] * (len(inputs) - scalars),
            out_specs=[VMEM] * len(outs),
            compiler_params=params(mib),
            name=name,
            **more,
        )(*inputs)

    relayed = chips == 4
    key_shape = (prompt_keys + reply_own, 2 * HEAD_WIDTH)
    mine0, theirs0, mine1, theirs, token = call(
        prepare_keys,
        "prepare_keys",
        LARGE_MIB,
        (place, prompt_k, prompt_value, reply_key[0], reply_value[0]),
        [shape(*key_shape)] * 3 + [shape(LOCAL_HEADS, *key_shape), shape(8, 128, dtype=F32)],
        spec=HBM,
        scratch_shapes=[
            pltpu.VMEM((rows, KEY_VALUE_HEADS * HEAD_WIDTH), BF16)
            for rows in (prompt_keys, prompt_keys, reply_own, reply_own)
        ]
        + [pltpu.SemaphoreType.DMA((4,))],
    )
    blocks0 = {(0, 0): mine0, (0, 1): swap(theirs)}
    for away in range(1, 3 if relayed else chips):
        blocks0[away, 0] = move(mine0, away)
        blocks0[away, 1] = move(theirs0, away, 1)
    if prompt_own > prompt_rows:
        room = ((0, prompt_own - prompt_rows), (0, 0))
        prompt_query, prompt_output, prompt_output_gradient = (
            jnp.pad(array, room)
            for array in (prompt_query, prompt_output, prompt_output_gradient)
        )
    own_rows = reply_own + prompt_own
    row_width = 2 * GROUP_WIDTH + HEAD_WIDTH

    rows = call(
        prepare_rows,
        "prepare_rows",
        LARGE_MIB,
        (
            place,
            token,
            prompt_query,
            prompt_output,
            prompt_output_gradient,
            reply_query[0],
            reply_output[0],
            reply_output_gradient[0],
        ),
        [shape(LOCAL_HEADS, own_rows, row_width)] + [shape(own_rows, row_width)] * LOCAL_HEADS,
        spec=HBM,
        scratch_shapes=[
            pltpu.VMEM((KEY_VALUE_HEADS, rows, GROUP_WIDTH), BF16)
            for rows in [prompt_own] * 3 + [reply_own] * 3
        ]
        + [pltpu.SemaphoreType.DMA((KEY_VALUE_HEADS * 6,))],
        cost_estimate=pl.CostEstimate(
            flops=6 * reply_own * reply_own * QUERY_HEADS * HEAD_WIDTH,
            bytes_accessed=20 * reply_own * QUERY_HEADS * HEAD_WIDTH,
            transcendentals=0,
        ),
    )

    blocks0, rows, mine1 = lax.optimization_barrier((blocks0, rows, mine1))
    if relayed:
        blocks0[3, 0] = move(blocks0[1, 0], 2)
        blocks0[3, 1] = move(blocks0[2, 1], 1)
    chip1 = jnp.stack([mine1, blocks0[0, 1][1]])
    blocks1 = [chip1] + [move(chip1, away) for away in range(1, chips)]

    blocks = (chips * chip_prompt + RESP_DEV * chips * positions) // block
    slots = (chips * chip_prompt + chips * positions) // block
    all_rows = max(GROUP * positions, -(-GROUP * CORES * prompt_own // 128) * 128)
    sizes = (chips, reply_own, prompt_own, prompt_rows, prompt_keys)
    score_count = GROUP * (positions * RESP_DEV * slots * block)

    rows_theirs, *rows_mine = rows
    rows_theirs = swap(rows_theirs)

    def run_attend(local, key_blocks):
        joint_keys = local == 1
        sums = [shape(*key_shape)] * devices if joint_keys else [shape(CORES, *key_shape)] * chips
        query_mine, query_theirs, *sums = call(
            functools.partial(attend, sizes, joint_keys),
            "attend",
            VMEM_MIB,
            (
                place,
                reply_len,
                reply_slot,
                rows_mine[local],
                rows_theirs,
                *key_blocks,
            ),
            [shape(own_rows, GROUP_WIDTH)] * CORES + sums,
            scalars=3,
            scratch_shapes=[
                pltpu.VMEM((blocks * block, 2 * HEAD_WIDTH), BF16),
                pltpu.VMEM((blocks, HEAD_WIDTH, block), BF16),
                pltpu.VMEM((blocks * block, 2 * HEAD_WIDTH), F32),
                pltpu.VMEM((all_rows, HEAD_WIDTH), BF16),
                pltpu.VMEM((all_rows, HEAD_WIDTH), BF16),
                pltpu.VMEM((HEAD_WIDTH, all_rows), BF16),
                pltpu.VMEM((HEAD_WIDTH, all_rows), BF16),
                pltpu.VMEM((CORES, 8, own_rows), F32),
                pltpu.VMEM((8, all_rows), F32),
                pltpu.VMEM((slots, block, all_rows), F32),
                pltpu.VMEM((slots, block // PART, 8, all_rows), F32),
                pltpu.VMEM((8, all_rows), F32),
                pltpu.VMEM((8, all_rows), F32),
                pltpu.VMEM((HEAD_WIDTH, all_rows), F32),
            ]
            + [pltpu.VMEM((block, all_rows), BF16)] * 4,
            cost_estimate=pl.CostEstimate(
                flops=score_count * 10 * HEAD_WIDTH,
                bytes_accessed=8 * 1024 * 1024,
                transcendentals=2 * score_count,
            ),
        )
        return query_mine, query_theirs, sums

    query_mine0, query_theirs0, sums0 = run_attend(
        0, [blocks0[away, other] for away in range(chips) for other in range(CORES)]
    )
    arrived0 = [sums0[0]] + [move(sums0[away], away) for away in range(1, chips)]
    query_theirs0 = swap(query_theirs0)
    query_mine1, query_theirs1, sums1 = run_attend(1, blocks1)
    arrived0, query_theirs0, query_theirs1, sums1 = lax.optimization_barrier(
        (arrived0, query_theirs0, query_theirs1, sums1)
    )
    sums1 = [sums1[CORES * away : CORES * away + CORES] for away in range(chips)]
    mine0, theirs0 = call(
        collect,
        "collect",
        SMALL_MIB,
        arrived0,
        [shape(*key_shape, dtype=F32), shape(*key_shape)],
        scalars=0,
    )
    if relayed:
        through_y, through_x = move(sums1[3][0], 2), move(sums1[3][1], 1)
        for_x, for_y = call(
            add_pairs,
            "add_pairs",
            SMALL_MIB,
            (sums1[1][0], sums1[2][1], through_y, through_x),
            [shape(*key_shape)] * 2,
            scalars=0,
        )
        near = [sums1[0][0], move(sums1[1][1], 1, 1), move(sums1[2][0], 2)]
        for_x, for_y, near, sums1[0][1], query_theirs1, theirs0 = lax.optimization_barrier(
            (for_x, for_y, near, sums1[0][1], query_theirs1, theirs0)
        )
        lists1 = [[near[0], move(for_x, 1), near[2]], [swap(sums1[0][1]), near[1], move(for_y, 2, 1)]]
    else:
        lists1 = [
            [move(pair[other], away, other) if away or other else pair[other] for away, pair in enumerate(sums1)]
            for other in range(CORES)
        ]
    lists = [[mine0], [swap(theirs0)]] + lists1
    queries = [query_mine0, query_theirs0, query_mine1, swap(query_theirs1)]
    counts = [len(parts) for parts in lists]
    parts = [part for one in lists for part in one]
    cut_rows = prompt_keys // groups
    cuts = call(
        functools.partial(spread_prompt, counts),
        "spread_prompt",
        SMALL_MIB,
        (place, *parts),
        [shape(KEY_VALUE_HEADS, cut_rows, 2 * HEAD_WIDTH)] * groups,
        scratch_shapes=[pltpu.VMEM((KEY_VALUE_HEADS, prompt_keys, 2 * HEAD_WIDTH), F32)],
    )
    slices = [cuts[0]] + [
        lax.ppermute(cuts[shift], "rsp", [(g, (g + shift) % groups) for g in range(groups)])
        for shift in range(1, groups)
    ]
    key_width = KEY_VALUE_HEADS * HEAD_WIDTH
    query_width = QUERY_HEADS * HEAD_WIDTH
    prompt_dq, reply_dq, reply_dk, reply_dv = call(
        functools.partial(finish_reply, counts),
        "finish_reply",
        SMALL_MIB,
        (place, *parts, *queries),
        [
            shape(prompt_own, query_width),
            shape(reply_own, query_width),
            shape(reply_own, key_width),
            shape(reply_own, key_width),
        ],
        cost_estimate=pl.CostEstimate(
            flops=2 * reply_own * reply_own * (query_width + 2 * key_width),
            bytes_accessed=16 * reply_own * query_width,
            transcendentals=0,
        ),
    )
    slices, prompt_dq = lax.optimization_barrier((slices, prompt_dq))
    prompt_dk, prompt_dv = call(
        finish_prompt,
        "finish_prompt",
        SMALL_MIB,
        (place, *slices),
        [shape(cut_rows, key_width)] * 2,
    )
    return (
        prompt_dq[:prompt_rows],
        prompt_dk,
        prompt_dv,
        reply_dq[None],
        reply_dk[None],
        reply_dv[None],
    )


def solution(mesh):
    return jax.shard_map(
        on_device,
        mesh=mesh,
        in_specs=(
            P(("pre", "rsp"), None),
            P("pre", None),
            P("pre", None),
            P(("pre", "rsp"), None),
            P(("pre", "rsp"), None),
            P("rsp", "pre", None),
            P("rsp", "pre", None),
            P("rsp", "pre", None),
            P("rsp", "pre", None),
            P("rsp", "pre", None),
            P(),
            P(),
        ),
        out_specs=(
            P(("pre", "rsp"), None),
            P(("pre", "rsp"), None),
            P(("pre", "rsp"), None),
            P("rsp", "pre", None),
            P("rsp", "pre", None),
            P("rsp", "pre", None),
        ),
        check_vma=False,
    )
```

```python
import functools
import math

import jax
import jax.numpy as jnp
from jax import lax
from jax.experimental import pallas as pl
from jax.experimental.pallas import tpu as pltpu
from jax.sharding import PartitionSpec as P

QUERY_HEADS = 20
KEY_VALUE_HEADS = 4
GROUP = QUERY_HEADS // KEY_VALUE_HEADS
HEAD_WIDTH = 128
RESP_DEV = 2
CORES = 2
LOCAL_HEADS = KEY_VALUE_HEADS // CORES
GROUP_WIDTH = GROUP * HEAD_WIDTH

SCALE = HEAD_WIDTH ** (-0.5)
SCALE_LOG2 = SCALE * math.log2(math.e)
PART = 128
NEGATIVE_FLOOR = -1e30
DEAD = 1e30
F32 = jnp.float32
BF16 = jnp.bfloat16
VMEM = pl.BlockSpec(memory_space=pltpu.VMEM)
SMEM = pl.BlockSpec(memory_space=pltpu.SMEM)
HBM = pl.BlockSpec(memory_space=pltpu.HBM)


VMEM_MIB = 40
SMALL_MIB = 24
LARGE_MIB = 58


def params(mib):
    return pltpu.CompilerParams(vmem_limit_bytes=mib * 1024 * 1024)


def dot(a, b, over=(1, 0)):
    return lax.dot_general(
        a, b, (((over[0],), (over[1],)), ((), ())), preferred_element_type=F32
    )


def iota(shape, axis):
    return lax.broadcasted_iota(jnp.int32, shape, axis)


def sorting(rows):
    half = rows // RESP_DEV
    out = iota((rows, rows), 0)
    source = jnp.where(out < half, RESP_DEV * out, RESP_DEV * (out - half) + 1)
    return (iota((rows, rows), 1) == source).astype(BF16)


def unsorting(rows):
    half = rows // RESP_DEV
    out = iota((rows, rows), 1)
    source = jnp.where(out < half, RESP_DEV * out, RESP_DEV * (out - half) + 1)
    return (iota((rows, rows), 0) == source).astype(BF16)


def lanes(index, width):
    return pl.ds(pl.multiple_of(index * width, width), width)


def head_of(core, cross, local):
    owner = (1 - core) if cross else core
    return owner * LOCAL_HEADS + local


def fetch(pairs, sems):
    copies = [pltpu.make_async_copy(src, dst, sems.at[i]) for i, (src, dst) in enumerate(pairs)]
    for copy in copies:
        copy.start()
    return copies


def prepare_keys(place, pk, pv, rk, rv, mine0, theirs0, mine1, theirs, token, *scratch):
    core = place[1]
    bufs, sems = scratch[:-1], scratch[-1]
    copies = fetch(zip((pk, pv, rk, rv), bufs), sems)
    prompt = pk.shape[0]
    order = sorting(rk.shape[0])
    for copy in copies:
        copy.wait()
    pk, pv, rk, rv = bufs
    for local, outs in enumerate(((mine0, theirs.at[0]), (mine1, theirs.at[1]))):
        for cross, out in enumerate(outs):
            span = lanes(head_of(core, cross, local), HEAD_WIDTH)
            for part, (p, r) in enumerate(((pk, rk), (pv, rv))):
                to = slice(part * HEAD_WIDTH, (part + 1) * HEAD_WIDTH)
                out[:prompt, to] = p[:, span]
                out[prompt:, to] = dot(order, r[:, span]).astype(BF16)
    theirs0[...] = theirs[0]
    token[...] = jnp.zeros_like(token)


def prepare_rows(place, token, pq, po, pg, rq, ro, rg, *refs):
    (theirs, *mine), bufs, sems = refs[: 1 + LOCAL_HEADS], refs[1 + LOCAL_HEADS : -1], refs[-1]
    outs = [out for local in range(LOCAL_HEADS) for out in (theirs.at[local], mine[local])]
    core = place[1]
    reply = rq.shape[0]
    sources = (pq, po, pg, rq, ro, rg)
    pairs = []
    for step in range(KEY_VALUE_HEADS):
        span = lanes(head_of(core, 1 - step % CORES, step // CORES), GROUP_WIDTH)
        pairs += [(source.at[:, span], buf.at[step]) for source, buf in zip(sources, bufs)]
    copies = fetch(pairs, sems)
    order = sorting(reply)
    column = iota((GROUP_WIDTH, HEAD_WIDTH), 1)
    pick = (column // 3 == iota((GROUP_WIDTH, HEAD_WIDTH), 0) // HEAD_WIDTH).astype(BF16)

    def delta(gradient, output):
        product = gradient.astype(F32) * output.astype(F32)
        high = product.astype(BF16)
        low = (product - high.astype(F32)).astype(BF16)
        value = dot(high, pick) + dot(low, pick)
        first = value.astype(BF16).astype(F32)
        second = (value - first).astype(BF16).astype(F32)
        part = iota(value.shape, 1) % 3
        return jnp.where(part == 0, first, jnp.where(part == 1, second, value - first - second)).astype(BF16)

    for step, out in enumerate(outs):
        for copy in copies[step * len(sources) : (step + 1) * len(sources)]:
            copy.wait()
        pq, po, pg, rq, ro, rg = (buf[step] for buf in bufs)
        out[reply:, :GROUP_WIDTH] = pq
        out[reply:, GROUP_WIDTH : 2 * GROUP_WIDTH] = pg
        out[reply:, 2 * GROUP_WIDTH :] = delta(pg, po)
        out[:reply, :GROUP_WIDTH] = dot(order, rq).astype(BF16)
        gradient = dot(order, rg).astype(BF16)
        out[:reply, GROUP_WIDTH : 2 * GROUP_WIDTH] = gradient
        out[:reply, 2 * GROUP_WIDTH :] = delta(gradient, dot(order, ro).astype(BF16))


def attend(sizes, joint_keys, place, reply_len, reply_slot, *refs):
    chips, reply_own, prompt_own, prompt_rows, prompt_keys = sizes
    own_positions = reply_own // RESP_DEV
    positions = CORES * own_positions
    chip_prompt = CORES * prompt_keys
    block = 2 * positions
    prompt_blocks = chips * chip_prompt // block
    rows_in, refs = (refs[0], refs[1].at[int(joint_keys)]), refs[2:]
    count = chips if joint_keys else chips * CORES
    keys_in, refs = refs[:count], refs[count:]
    query_out, refs = refs[:2], refs[2:]
    keys_out, refs = refs[:chips], refs[chips:]
    groups = prompt_keys // prompt_rows
    cuts_out, refs = (refs[:groups], refs[groups:]) if joint_keys else ((), refs)
    keys, keys_t, total, query, gradient, query_t, gradient_t, deltas, delta, scores, peaks, top, mass, *refs = refs
    query_grad, stages = refs[0], (refs[1:3], refs[3:5])
    chip, core, group = place[0], place[1], place[2]

    pick = (iota((8, HEAD_WIDTH), 1) // 3 == iota((8, HEAD_WIDTH), 0)).astype(BF16)
    for other in range(CORES):
        deltas[other] = dot(pick, rows_in[other][:, 2 * GROUP_WIDTH :], (1, 1))

    for index in range(chips * CORES):
        away, other = index // CORES, index % CORES
        source = keys_in[away].at[other] if joint_keys else keys_in[index]
        source = source if len(source.shape) == 2 else source.at[0]
        at = away * chip_prompt + other * prompt_keys
        keys[at : at + prompt_keys] = source[:prompt_keys]
        for slot in range(RESP_DEV):
            at = chips * chip_prompt + (slot * chips + away) * positions + other * own_positions
            begin = prompt_keys + slot * own_positions
            keys[at : at + own_positions] = source[begin : begin + own_positions]
    total[...] = jnp.zeros_like(total)

    unit = (iota((HEAD_WIDTH, HEAD_WIDTH), 0) == iota((HEAD_WIDTH, HEAD_WIDTH), 1)).astype(BF16)

    def transpose_block(index, carry):
        rows = pl.ds(pl.multiple_of(index * block, block), block)
        keys_t[index] = dot(unit, keys[rows, :HEAD_WIDTH], (1, 1)).astype(BF16)
        return carry

    lax.fori_loop(0, keys_t.shape[0], transpose_block, 0)

    def score_block(region, place_in, width, chunks, hidden):
        rows = pl.ds(pl.multiple_of(region * block, block), block)
        key_rows = keys[rows, :HEAD_WIDTH]
        for chunk in range(chunks):
            span = slice(chunk * width, (chunk + 1) * width)
            value = dot(key_rows, query_t[:, span]) * SCALE_LOG2
            if hidden is not None:
                value = jnp.where(hidden, NEGATIVE_FLOOR, value)
            split = value.reshape(block // 8, 8, width)
            peak, summed = top[:, span], mass[:, span]
            for part in range(block // PART):
                piece = split[part * PART // 8 : (part + 1) * PART // 8]
                now = jnp.maximum(peak, jnp.max(piece, axis=0))
                shifted = jnp.exp2(piece - now[None])
                scores[place_in, part * PART : (part + 1) * PART, span] = shifted.reshape(PART, width)
                peaks[place_in, part, :, span] = now
                summed = summed * jnp.exp2(peak - now) + jnp.sum(shifted, axis=0)
                peak = now
            top[:, span], mass[:, span] = peak, summed

    def weigh(region, place_in, width, chunks, log_mass, stage, earlier=None, earlier_stage=None):
        rows = pl.ds(pl.multiple_of(region * block, block), block)
        value_rows = keys[rows, HEAD_WIDTH:]
        for chunk in range(chunks):
            span = slice(chunk * width, (chunk + 1) * width)
            dp = dot(value_rows, gradient_t[:, span])
            for part in range(block // PART):
                at = slice(part * PART, (part + 1) * PART)
                factor = jnp.exp2(peaks[place_in, part, :, span] - log_mass[chunk])
                p = scores[place_in, at, span].reshape(PART // 8, 8, width) * factor[None]
                p = p.reshape(PART, width)
                stage[0][at, span] = p.astype(BF16)
                stage[1][at, span] = (p * (dp[at] - delta[0:1, span])).astype(BF16)
            if earlier is not None:
                multiply(earlier, width, chunks, earlier_stage, chunk)
        if earlier is not None:
            for chunk in range(chunks, 3):
                multiply(earlier, width, chunks, earlier_stage, chunk)

    def multiply(region, width, chunks, stage, part):
        rows = pl.ds(pl.multiple_of(region * block, block), block)
        used = width * chunks
        if part == 0:
            total[rows, HEAD_WIDTH:] += dot(stage[0][:, :used], gradient[:used])
        elif part == 1:
            total[rows, :HEAD_WIDTH] += dot(stage[1][:, :used], query[:used])
        elif part == 2:
            query_grad[:, :used] += dot(keys_t[region], stage[1][:, :used])

    def grad_blocks(count, region_of, width, chunks, log_mass):
        first, second = stages

        def later(index, stage, earlier_stage):
            weigh(
                region_of(index), index, width, chunks, log_mass, stage, region_of(index - 1), earlier_stage
            )

        def last(stage):
            for part in range(3):
                multiply(region_of(count - 1), width, chunks, stage, part)

        weigh(region_of(0), 0, width, chunks, log_mass, first)

        def two(index, carry):
            later(2 * index + 1, second, first)
            later(2 * index + 2, first, second)
            return carry

        lax.fori_loop(0, (count - 1) // 2, two, 0)

        @pl.when(count % 2 == 0)
        def _():
            later(count - 1, second, first)
            last(second)

        @pl.when(count % 2 == 1)
        def _():
            last(first)

    def turn(all_rows):
        query_t[:, :all_rows] = dot(unit, query[:all_rows], (1, 1)).astype(BF16)
        gradient_t[:, :all_rows] = dot(unit, gradient[:all_rows], (1, 1)).astype(BF16)

    def begin(all_rows):
        top[:, :all_rows] = jnp.full((8, all_rows), NEGATIVE_FLOOR, F32)
        mass[:, :all_rows] = jnp.zeros((8, all_rows), F32)
        query_grad[:, :all_rows] = jnp.zeros((HEAD_WIDTH, all_rows), F32)

    def log_masses(width, chunks, live):
        found = []
        for chunk in range(chunks):
            span = slice(chunk * width, (chunk + 1) * width)
            peak = jnp.max(top[:, span], axis=0, keepdims=True)
            summed = jnp.sum(mass[:, span] * jnp.exp2(top[:, span] - peak), axis=0, keepdims=True)
            found.append(jnp.where(live, peak + jnp.log2(summed), DEAD))
        return found

    def absolute(index, half):
        return index + jnp.where(index < half, core * half, -core * half)

    def reply_tile(slot, carry):
        length = jnp.int32(0)
        for response in range(reply_len.shape[0]):
            mine = reply_slot[response] == group * RESP_DEV + slot
            length = length + jnp.where(mine, reply_len[response], 0)
        first = chip * positions
        source = pl.ds(pl.multiple_of(slot * own_positions, own_positions), own_positions)

        @pl.when(length > first)
        def _():
            for head in range(GROUP):
                for other in range(CORES):
                    at = head * positions + other * own_positions
                    to = slice(at, at + own_positions)
                    left = slice(head * HEAD_WIDTH, (head + 1) * HEAD_WIDTH)
                    right = slice(GROUP_WIDTH + head * HEAD_WIDTH, GROUP_WIDTH + (head + 1) * HEAD_WIDTH)
                    query[to] = rows_in[other][source, left]
                    gradient[to] = rows_in[other][source, right]
                    for which in range(RESP_DEV):
                        @pl.when(slot == which)
                        def _():
                            delta[0:1, to] = deltas[
                                other, head : head + 1, which * own_positions : (which + 1) * own_positions
                            ]
            begin(GROUP * positions)
            turn(GROUP * positions)
            base = prompt_blocks + slot * (chips // 2)
            past = prompt_blocks + chip // 2

            def region_of(index):
                reply = base + ((index - prompt_blocks) ^ (chip // 2))
                return jnp.where(index < prompt_blocks, index, jnp.where(index == past, base, reply))

            def stats(index, carry):
                score_block(region_of(index), index, positions, GROUP, None)
                return carry

            lax.fori_loop(0, past, stats, 0)
            row_at = absolute(iota((1, positions), 1), own_positions)
            key = iota((block, 1), 0)
            key_at = jnp.where(key < positions, absolute(key, own_positions), lax.rem(chip + 1, 2) * block - 1)
            score_block(base, past, positions, GROUP, key_at > row_at)
            live = first + row_at < length
            log_mass = log_masses(positions, GROUP, live)

            grad_blocks(past + 1, region_of, positions, GROUP, log_mass)
            for head in range(GROUP):
                turned = (query_grad[:, head * positions : (head + 1) * positions].T * SCALE).astype(BF16)
                for other in range(CORES):
                    query_out[other][source, head * HEAD_WIDTH : (head + 1) * HEAD_WIDTH] = turned[
                        other * own_positions : (other + 1) * own_positions
                    ]

        @pl.when(length <= first)
        def _():
            for other in range(CORES):
                query_out[other][source, :] = jnp.zeros((own_positions, GROUP_WIDTH), BF16)

        return carry

    lax.fori_loop(0, RESP_DEV, reply_tile, 0)

    head_rows = CORES * prompt_own
    used = GROUP * head_rows
    all_rows = -(-used // 128) * 128
    if all_rows > used:
        query[used:all_rows] = jnp.zeros((all_rows - used, HEAD_WIDTH), BF16)
        gradient[used:all_rows] = jnp.zeros((all_rows - used, HEAD_WIDTH), BF16)
    delta[0:1, :all_rows] = jnp.zeros((1, all_rows), F32)
    for head in range(GROUP):
        for other in range(CORES):
            at = head * head_rows + other * prompt_own
            to = slice(at, at + prompt_own)
            left = slice(head * HEAD_WIDTH, (head + 1) * HEAD_WIDTH)
            right = slice(GROUP_WIDTH + head * HEAD_WIDTH, GROUP_WIDTH + (head + 1) * HEAD_WIDTH)
            query[to] = rows_in[other][reply_own:, left]
            gradient[to] = rows_in[other][reply_own:, right]
            delta[0:1, to] = deltas[other, head : head + 1, reply_own:]
    begin(all_rows)
    turn(all_rows)
    lane = iota((1, all_rows), 1)
    within = lane
    for head in range(1, GROUP):
        within = within - jnp.where(lane >= head * head_rows, head_rows, 0)
    offset = jnp.where(within < prompt_own, within, within - prompt_own)
    row_core = jnp.where(within < prompt_own, core, 1 - core)
    real = (lane < used) & (offset < prompt_rows)
    row_at = jnp.where(
        real, (chip * CORES + row_core) * prompt_keys + group * prompt_rows + offset, -1
    )
    per_block = max(block // chip_prompt, 1)
    block_parts = max(chip_prompt // block, 1)
    pair = chip // per_block
    seen = (pair + 1) * block_parts

    def prompt_region(index):
        return (index // block_parts ^ pair) * block_parts + index % block_parts

    def prompt_stats(index, carry):
        key = iota((block, 1), 0) + index % block_parts * block
        key_chip = ((index // block_parts ^ pair) * per_block + key // chip_prompt) ^ chip
        key_at = key_chip * chip_prompt + absolute(key % chip_prompt, prompt_keys)
        score_block(prompt_region(index), index, all_rows, 1, key_at > row_at)
        return carry

    lax.fori_loop(0, seen, prompt_stats, 0)
    log_mass = log_masses(all_rows, 1, real)

    grad_blocks(seen, prompt_region, all_rows, 1, log_mass)
    turned = (query_grad[:, :all_rows].T * SCALE).astype(BF16)
    for head in range(GROUP):
        for other in range(CORES):
            at = head * head_rows + other * prompt_own
            query_out[other][reply_own:, head * HEAD_WIDTH : (head + 1) * HEAD_WIDTH] = turned[
                at : at + prompt_own
            ]

    def put(out, at, count):
        out[:, :HEAD_WIDTH] = (total[pl.ds(at, count), :HEAD_WIDTH] * SCALE).astype(BF16)
        out[:, HEAD_WIDTH:] = total[pl.ds(at, count), HEAD_WIDTH:].astype(BF16)

    for index in range(chips * CORES):
        away, other = index // CORES, index % CORES
        out = keys_out[away].at[other]
        prompt_at = away * chip_prompt + other * prompt_keys
        if not joint_keys:
            put(out.at[:prompt_keys], prompt_at, prompt_keys)
        for shift, cut in enumerate(cuts_out):
            part = lax.rem(group + shift, groups) * prompt_rows
            put(cut.at[index], pl.multiple_of(prompt_at + part, prompt_rows), prompt_rows)
        for slot in range(RESP_DEV):
            at = chips * chip_prompt + (slot * chips + away) * positions + other * own_positions
            to = slot * own_positions + (0 if joint_keys else prompt_keys)
            put(out.at[to : to + own_positions], at, own_positions)


def add(first, *rest):
    value = first.astype(F32)
    for part in rest:
        value = value + part.astype(F32)
    return value


def collect_first(chips, prompt_keys, place, *refs):
    parts, refs = refs[:chips], refs[chips:]
    groups = (len(refs) - 3) // 2
    cuts, mine, theirs, outs, summed = refs[:groups], refs[groups], refs[groups + 1], refs[groups + 2 : -1], refs[-1]
    rows = prompt_keys // groups
    for other in range(CORES):
        value = add(*(part[other, prompt_keys:] for part in parts))
        if other == 0:
            mine[...] = value
        else:
            theirs[...] = value.astype(BF16)
        summed[other] = add(*(part[other, :prompt_keys] for part in parts))
    for shift in range(groups):
        at = pl.ds(pl.multiple_of(lax.rem(place[2] + shift, groups) * rows, rows), rows)
        for other in range(CORES):
            outs[shift][other] = summed[other, at].astype(BF16)
        outs[shift][CORES:] = cuts[shift][...]


def add_groups(groups, *refs):
    parts, first, outs = refs[:groups], refs[groups], refs[groups + 1 :]
    value = add(*(part[...] for part in parts)).astype(BF16)
    first[...] = value[:CORES]
    for away, out in enumerate(outs):
        out[...] = value[CORES * (away + 1) : CORES * (away + 2)]


def collect_second(chips, *refs):
    reply_parts, refs = refs[:chips], refs[chips:]
    prompt_parts, refs = refs[:chips], refs[chips:]
    prompt0, theirs0, reply1, prompt1, theirs = refs
    reply, rows = theirs0.shape[0], prompt0.shape[1]
    step = max(rows, 16)
    reply1[...] = add(*(part[0] for part in reply_parts))
    prompt1[...] = add(*(part[0] for part in prompt_parts))
    theirs[:reply] = theirs0[...]
    theirs[reply : 2 * reply] = add(*(part[1] for part in reply_parts)).astype(BF16)
    theirs[2 * reply : 2 * reply + rows] = prompt0[1]
    theirs[2 * reply + step : 2 * reply + step + rows] = add(*(part[1] for part in prompt_parts)).astype(BF16)


def finish_queries(place, *refs):
    queries, prompt_dq, reply_dq = refs[:-2], refs[-2], refs[-1]
    reply = reply_dq.shape[0]
    order = unsorting(reply)
    for index, query in enumerate(queries):
        span = lanes(head_of(place[1], index % CORES, index // CORES), GROUP_WIDTH)
        reply_dq[:, span] = dot(order, query[:reply]).astype(BF16)
        prompt_dq[:, span] = query[reply:]


def finish_keys(place, reply0, reply1, prompt0, prompt1, theirs, prompt_dk, prompt_dv, reply_dk, reply_dv):
    reply, rows = reply_dk.shape[0], prompt_dk.shape[0]
    step = max(rows, 16)
    order = unsorting(reply)
    for local in range(LOCAL_HEADS):
        for other in range(CORES):
            span = lanes(head_of(place[1], other, local), HEAD_WIDTH)
            if other:
                value = theirs[local * reply : (local + 1) * reply]
                prompt = theirs[2 * reply + local * step : 2 * reply + local * step + rows]
            else:
                value = (reply1 if local else reply0)[...].astype(BF16)
                prompt = prompt1[...].astype(BF16) if local else prompt0[0]
            value = dot(order, value).astype(BF16)
            reply_dk[:, span] = value[:, :HEAD_WIDTH]
            reply_dv[:, span] = value[:, HEAD_WIDTH:]
            prompt_dk[:, span] = prompt[:, :HEAD_WIDTH]
            prompt_dv[:, span] = prompt[:, HEAD_WIDTH:]


def on_device(
    prompt_query,
    prompt_k,
    prompt_value,
    prompt_output,
    prompt_output_gradient,
    reply_query,
    reply_key,
    reply_value,
    reply_output,
    reply_output_gradient,
    reply_len,
    reply_slot,
):
    devices = lax.axis_size("pre")
    groups = lax.axis_size("rsp")
    chips = devices // CORES
    prompt_rows = prompt_query.shape[0]
    prompt_own = -(-prompt_rows // 16) * 16
    prompt_keys = prompt_k.shape[0]
    reply_own = reply_query.shape[1]
    own_positions = reply_own // RESP_DEV
    positions = CORES * own_positions
    chip_prompt = CORES * prompt_keys
    block = 2 * positions
    assert (chip_prompt % block == 0 or block % chip_prompt == 0) and chips > 1 and chips & (chips - 1) == 0
    pre_index = lax.axis_index("pre")
    place = jnp.stack([lax.div(pre_index, CORES), lax.rem(pre_index, CORES), lax.axis_index("rsp")])

    def shape(*dims, dtype=BF16):
        return jax.ShapeDtypeStruct(dims, dtype)

    def move(array, away, cross=0):
        pairs = [(p, (p // CORES ^ away) * CORES + (p % CORES ^ cross)) for p in range(devices)]
        return lax.ppermute(array, "pre", pairs)

    def swap(array):
        return move(array, 0, 1)

    def call(kernel, name, mib, inputs, outs, scalars=1, spec=VMEM, **more):
        return pl.pallas_call(
            kernel,
            out_shape=outs,
            in_specs=[SMEM] * scalars + [spec] * (len(inputs) - scalars),
            out_specs=[VMEM] * len(outs),
            compiler_params=params(mib),
            name=name,
            **more,
        )(*inputs)

    relayed = chips == 4
    key_shape = (prompt_keys + reply_own, 2 * HEAD_WIDTH)
    mine0, theirs0, mine1, theirs, token = call(
        prepare_keys,
        "prepare_keys",
        LARGE_MIB,
        (place, prompt_k, prompt_value, reply_key[0], reply_value[0]),
        [shape(*key_shape)] * 3 + [shape(LOCAL_HEADS, *key_shape), shape(8, 128, dtype=F32)],
        spec=HBM,
        scratch_shapes=[
            pltpu.VMEM((rows, KEY_VALUE_HEADS * HEAD_WIDTH), BF16)
            for rows in (prompt_keys, prompt_keys, reply_own, reply_own)
        ]
        + [pltpu.SemaphoreType.DMA((4,))],
    )
    blocks0 = {(0, 0): mine0, (0, 1): swap(theirs)}
    for away in range(1, 3 if relayed else chips):
        blocks0[away, 0] = move(mine0, away)
        blocks0[away, 1] = move(theirs0, away, 1)
    if prompt_own > prompt_rows:
        room = ((0, prompt_own - prompt_rows), (0, 0))
        prompt_query, prompt_output, prompt_output_gradient = (
            jnp.pad(array, room)
            for array in (prompt_query, prompt_output, prompt_output_gradient)
        )
    own_rows = reply_own + prompt_own
    row_width = 2 * GROUP_WIDTH + HEAD_WIDTH

    rows = call(
        prepare_rows,
        "prepare_rows",
        LARGE_MIB,
        (
            place,
            token,
            prompt_query,
            prompt_output,
            prompt_output_gradient,
            reply_query[0],
            reply_output[0],
            reply_output_gradient[0],
        ),
        [shape(LOCAL_HEADS, own_rows, row_width)] + [shape(own_rows, row_width)] * LOCAL_HEADS,
        spec=HBM,
        scratch_shapes=[
            pltpu.VMEM((KEY_VALUE_HEADS, rows, GROUP_WIDTH), BF16)
            for rows in [prompt_own] * 3 + [reply_own] * 3
        ]
        + [pltpu.SemaphoreType.DMA((KEY_VALUE_HEADS * 6,))],
        cost_estimate=pl.CostEstimate(
            flops=6 * reply_own * reply_own * QUERY_HEADS * HEAD_WIDTH,
            bytes_accessed=20 * reply_own * QUERY_HEADS * HEAD_WIDTH,
            transcendentals=0,
        ),
    )

    blocks0, rows, mine1 = lax.optimization_barrier((blocks0, rows, mine1))
    if relayed:
        blocks0[3, 0] = move(blocks0[1, 0], 2)
        blocks0[3, 1] = move(blocks0[2, 1], 1)
    chip1 = jnp.stack([mine1, blocks0[0, 1][1]])
    blocks1 = [chip1] + [move(chip1, away) for away in range(1, chips)]

    blocks = (chips * chip_prompt + RESP_DEV * chips * positions) // block
    slots = (chips * chip_prompt + chips * positions) // block
    all_rows = max(GROUP * positions, -(-GROUP * CORES * prompt_own // 128) * 128)
    sizes = (chips, reply_own, prompt_own, prompt_rows, prompt_keys)
    score_count = GROUP * (positions * RESP_DEV * slots * block)

    cut_rows = prompt_keys // groups
    rows_theirs, *rows_mine = rows
    rows_theirs = swap(rows_theirs)

    def run_attend(local, key_blocks):
        joint_keys = local == 1
        cut = [shape(devices, cut_rows, 2 * HEAD_WIDTH)] * groups
        sums = [shape(CORES, reply_own, 2 * HEAD_WIDTH)] * chips + cut if joint_keys else [shape(CORES, *key_shape)] * chips
        query_mine, query_theirs, *sums = call(
            functools.partial(attend, sizes, joint_keys),
            "attend",
            VMEM_MIB,
            (
                place,
                reply_len,
                reply_slot,
                rows_mine[local],
                rows_theirs,
                *key_blocks,
            ),
            [shape(own_rows, GROUP_WIDTH)] * CORES + sums,
            scalars=3,
            scratch_shapes=[
                pltpu.VMEM((blocks * block, 2 * HEAD_WIDTH), BF16),
                pltpu.VMEM((blocks, HEAD_WIDTH, block), BF16),
                pltpu.VMEM((blocks * block, 2 * HEAD_WIDTH), F32),
                pltpu.VMEM((all_rows, HEAD_WIDTH), BF16),
                pltpu.VMEM((all_rows, HEAD_WIDTH), BF16),
                pltpu.VMEM((HEAD_WIDTH, all_rows), BF16),
                pltpu.VMEM((HEAD_WIDTH, all_rows), BF16),
                pltpu.VMEM((CORES, 8, own_rows), F32),
                pltpu.VMEM((8, all_rows), F32),
                pltpu.VMEM((slots, block, all_rows), F32),
                pltpu.VMEM((slots, block // PART, 8, all_rows), F32),
                pltpu.VMEM((8, all_rows), F32),
                pltpu.VMEM((8, all_rows), F32),
                pltpu.VMEM((HEAD_WIDTH, all_rows), F32),
            ]
            + [pltpu.VMEM((block, all_rows), BF16)] * 4,
            cost_estimate=pl.CostEstimate(
                flops=score_count * 10 * HEAD_WIDTH,
                bytes_accessed=8 * 1024 * 1024,
                transcendentals=2 * score_count,
            ),
        )
        return query_mine, query_theirs, sums

    query_mine0, query_theirs0, sums0 = run_attend(
        0, [blocks0[away, other] for away in range(chips) for other in range(CORES)]
    )
    arrived0 = [sums0[0]] + [move(sums0[away], away) for away in range(1, chips)]
    query_theirs0 = swap(query_theirs0)
    query_mine1, query_theirs1, sums1 = run_attend(1, blocks1)
    arrived0, query_theirs0, query_theirs1, sums1 = lax.optimization_barrier(
        (arrived0, query_theirs0, query_theirs1, sums1)
    )
    sums1, cuts1 = sums1[:chips], sums1[chips:]
    key_width = KEY_VALUE_HEADS * HEAD_WIDTH
    query_width = QUERY_HEADS * HEAD_WIDTH
    reply0, theirs0, *cuts = call(
        functools.partial(collect_first, chips, prompt_keys),
        "collect_first",
        SMALL_MIB,
        (place, *arrived0, *cuts1),
        [shape(reply_own, 2 * HEAD_WIDTH, dtype=F32), shape(reply_own, 2 * HEAD_WIDTH)]
        + [shape(CORES + devices, cut_rows, 2 * HEAD_WIDTH)] * groups,
        scratch_shapes=[pltpu.VMEM((CORES, prompt_keys, 2 * HEAD_WIDTH), F32)],
    )
    slices = [cuts[0]] + [
        lax.ppermute(cuts[shift], "rsp", [(g, (g + shift) % groups) for g in range(groups)])
        for shift in range(1, groups)
    ]
    slices[1], sums1[chips - 1], query_theirs1 = lax.optimization_barrier(
        (slices[1], sums1[chips - 1], query_theirs1)
    )
    arrived1 = [sums1[0]] + [move(sums1[away], away) for away in range(1, chips)]
    prompt_dq, reply_dq = call(
        finish_queries,
        "finish_queries",
        SMALL_MIB,
        (place, query_mine0, query_theirs0, query_mine1, swap(query_theirs1)),
        [shape(prompt_own, query_width), shape(reply_own, query_width)],
        cost_estimate=pl.CostEstimate(
            flops=2 * reply_own * reply_own * query_width,
            bytes_accessed=8 * reply_own * query_width,
            transcendentals=0,
        ),
    )
    slices, prompt_dq, reply_dq = lax.optimization_barrier((slices, prompt_dq, reply_dq))
    prompt0, *prompt_parts = call(
        functools.partial(add_groups, groups),
        "add_groups",
        SMALL_MIB,
        slices,
        [shape(CORES, cut_rows, 2 * HEAD_WIDTH)] * (1 + chips),
        scalars=0,
    )
    prompt_parts = [prompt_parts[0]] + [move(prompt_parts[away], away) for away in range(1, chips)]
    reply1, prompt1, theirs = call(
        functools.partial(collect_second, chips),
        "collect_second",
        SMALL_MIB,
        (*arrived1, *prompt_parts, prompt0, theirs0),
        [
            shape(reply_own, 2 * HEAD_WIDTH, dtype=F32),
            shape(cut_rows, 2 * HEAD_WIDTH, dtype=F32),
            shape(2 * reply_own + 2 * max(cut_rows, 16), 2 * HEAD_WIDTH),
        ],
        scalars=0,
    )
    prompt_dk, prompt_dv, reply_dk, reply_dv = call(
        finish_keys,
        "finish_keys",
        SMALL_MIB,
        (place, reply0, reply1, prompt0, prompt1, swap(theirs)),
        [shape(cut_rows, key_width)] * 2 + [shape(reply_own, key_width)] * 2,
    )
    return (
        prompt_dq[:prompt_rows],
        prompt_dk,
        prompt_dv,
        reply_dq[None],
        reply_dk[None],
        reply_dv[None],
    )


def solution(mesh):
    return jax.shard_map(
        on_device,
        mesh=mesh,
        in_specs=(
            P(("pre", "rsp"), None),
            P("pre", None),
            P("pre", None),
            P(("pre", "rsp"), None),
            P(("pre", "rsp"), None),
            P("rsp", "pre", None),
            P("rsp", "pre", None),
            P("rsp", "pre", None),
            P("rsp", "pre", None),
            P("rsp", "pre", None),
            P(),
            P(),
        ),
        out_specs=(
            P(("pre", "rsp"), None),
            P(("pre", "rsp"), None),
            P(("pre", "rsp"), None),
            P("rsp", "pre", None),
            P("rsp", "pre", None),
            P("rsp", "pre", None),
        ),
        check_vma=False,
    )
```

```python
import functools
import math

import jax
import jax.numpy as jnp
from jax import lax
from jax.experimental import pallas as pl
from jax.experimental.pallas import tpu as pltpu
from jax.sharding import PartitionSpec as P

QUERY_HEADS = 20
KEY_VALUE_HEADS = 4
GROUP = QUERY_HEADS // KEY_VALUE_HEADS
HEAD_WIDTH = 128
RESP_DEV = 2
CORES = 2
LOCAL_HEADS = KEY_VALUE_HEADS // CORES
GROUP_WIDTH = GROUP * HEAD_WIDTH

SCALE = HEAD_WIDTH ** (-0.5)
SCALE_LOG2 = SCALE * math.log2(math.e)
PART = 128
NEGATIVE_FLOOR = -1e30
DEAD = 1e30
F32 = jnp.float32
BF16 = jnp.bfloat16
VMEM = pl.BlockSpec(memory_space=pltpu.VMEM)
SMEM = pl.BlockSpec(memory_space=pltpu.SMEM)
HBM = pl.BlockSpec(memory_space=pltpu.HBM)


VMEM_MIB = 40
SMALL_MIB = 24
LARGE_MIB = 58


def params(mib):
    return pltpu.CompilerParams(vmem_limit_bytes=mib * 1024 * 1024)


def dot(a, b, over=(1, 0)):
    return lax.dot_general(
        a, b, (((over[0],), (over[1],)), ((), ())), preferred_element_type=F32
    )


def iota(shape, axis):
    return lax.broadcasted_iota(jnp.int32, shape, axis)


def sorting(rows):
    half = rows // RESP_DEV
    out = iota((rows, rows), 0)
    source = jnp.where(out < half, RESP_DEV * out, RESP_DEV * (out - half) + 1)
    return (iota((rows, rows), 1) == source).astype(BF16)


def unsorting(rows):
    half = rows // RESP_DEV
    out = iota((rows, rows), 1)
    source = jnp.where(out < half, RESP_DEV * out, RESP_DEV * (out - half) + 1)
    return (iota((rows, rows), 0) == source).astype(BF16)


def lanes(index, width):
    return pl.ds(pl.multiple_of(index * width, width), width)


def head_of(core, cross, local):
    owner = (1 - core) if cross else core
    return owner * LOCAL_HEADS + local


def fetch(pairs, sems):
    copies = [pltpu.make_async_copy(src, dst, sems.at[i]) for i, (src, dst) in enumerate(pairs)]
    for copy in copies:
        copy.start()
    return copies


def prepare_keys(place, pk, pv, rk, rv, mine0, theirs0, mine1, theirs, token, *scratch):
    core = place[1]
    bufs, sems = scratch[:-1], scratch[-1]
    copies = fetch(zip((pk, pv, rk, rv), bufs), sems)
    prompt = pk.shape[0]
    order = sorting(rk.shape[0])
    for copy in copies:
        copy.wait()
    pk, pv, rk, rv = bufs
    for local, outs in enumerate(((mine0, theirs.at[0]), (mine1, theirs.at[1]))):
        for cross, out in enumerate(outs):
            span = lanes(head_of(core, cross, local), HEAD_WIDTH)
            for part, (p, r) in enumerate(((pk, rk), (pv, rv))):
                to = slice(part * HEAD_WIDTH, (part + 1) * HEAD_WIDTH)
                out[:prompt, to] = p[:, span]
                out[prompt:, to] = dot(order, r[:, span]).astype(BF16)
    theirs0[...] = theirs[0]
    token[...] = jnp.zeros_like(token)


def prepare_rows(place, token, pq, po, pg, rq, ro, rg, *refs):
    (theirs, *mine), bufs, sems = refs[: 1 + LOCAL_HEADS], refs[1 + LOCAL_HEADS : -1], refs[-1]
    outs = [out for local in range(LOCAL_HEADS) for out in (theirs.at[local], mine[local])]
    core = place[1]
    reply = rq.shape[0]
    sources = (pq, po, pg, rq, ro, rg)
    pairs = []
    for step in range(KEY_VALUE_HEADS):
        span = lanes(head_of(core, 1 - step % CORES, step // CORES), GROUP_WIDTH)
        pairs += [(source.at[:, span], buf.at[step]) for source, buf in zip(sources, bufs)]
    copies = fetch(pairs, sems)
    order = sorting(reply)
    column = iota((GROUP_WIDTH, HEAD_WIDTH), 1)
    pick = (column // 3 == iota((GROUP_WIDTH, HEAD_WIDTH), 0) // HEAD_WIDTH).astype(BF16)

    def delta(gradient, output):
        product = gradient.astype(F32) * output.astype(F32)
        high = product.astype(BF16)
        low = (product - high.astype(F32)).astype(BF16)
        value = dot(high, pick) + dot(low, pick)
        first = value.astype(BF16).astype(F32)
        second = (value - first).astype(BF16).astype(F32)
        part = iota(value.shape, 1) % 3
        return jnp.where(part == 0, first, jnp.where(part == 1, second, value - first - second)).astype(BF16)

    for step, out in enumerate(outs):
        for copy in copies[step * len(sources) : (step + 1) * len(sources)]:
            copy.wait()
        pq, po, pg, rq, ro, rg = (buf[step] for buf in bufs)
        out[reply:, :GROUP_WIDTH] = pq
        out[reply:, GROUP_WIDTH : 2 * GROUP_WIDTH] = pg
        out[reply:, 2 * GROUP_WIDTH :] = delta(pg, po)
        out[:reply, :GROUP_WIDTH] = dot(order, rq).astype(BF16)
        gradient = dot(order, rg).astype(BF16)
        out[:reply, GROUP_WIDTH : 2 * GROUP_WIDTH] = gradient
        out[:reply, 2 * GROUP_WIDTH :] = delta(gradient, dot(order, ro).astype(BF16))


def attend(sizes, joint_keys, place, reply_len, reply_slot, *refs):
    chips, reply_own, prompt_own, prompt_rows, prompt_keys = sizes
    own_positions = reply_own // RESP_DEV
    positions = CORES * own_positions
    chip_prompt = CORES * prompt_keys
    block = 2 * positions
    prompt_blocks = chips * chip_prompt // block
    rows_in, refs = (refs[0], refs[1].at[int(joint_keys)]), refs[2:]
    count = chips if joint_keys else chips * CORES
    keys_in, refs = refs[:count], refs[count:]
    query_out, refs = refs[:2], refs[2:]
    keys_out, refs = refs[:chips], refs[chips:]
    prompt_out, refs = (refs[:chips], refs[chips:]) if joint_keys else (keys_out, refs)
    keys, keys_t, total, query, gradient, query_t, gradient_t, deltas, delta, scores, peaks, top, mass, *refs = refs
    query_grad, stages = refs[0], (refs[1:3], refs[3:5])
    chip, core, group = place[0], place[1], place[2]

    pick = (iota((8, HEAD_WIDTH), 1) // 3 == iota((8, HEAD_WIDTH), 0)).astype(BF16)
    for other in range(CORES):
        deltas[other] = dot(pick, rows_in[other][:, 2 * GROUP_WIDTH :], (1, 1))

    for index in range(chips * CORES):
        away, other = index // CORES, index % CORES
        source = keys_in[away].at[other] if joint_keys else keys_in[index]
        source = source if len(source.shape) == 2 else source.at[0]
        at = away * chip_prompt + other * prompt_keys
        keys[at : at + prompt_keys] = source[:prompt_keys]
        for slot in range(RESP_DEV):
            at = chips * chip_prompt + (slot * chips + away) * positions + other * own_positions
            begin = prompt_keys + slot * own_positions
            keys[at : at + own_positions] = source[begin : begin + own_positions]
    total[...] = jnp.zeros_like(total)

    unit = (iota((HEAD_WIDTH, HEAD_WIDTH), 0) == iota((HEAD_WIDTH, HEAD_WIDTH), 1)).astype(BF16)

    def transpose_block(index, carry):
        rows = pl.ds(pl.multiple_of(index * block, block), block)
        keys_t[index] = dot(unit, keys[rows, :HEAD_WIDTH], (1, 1)).astype(BF16)
        return carry

    lax.fori_loop(0, keys_t.shape[0], transpose_block, 0)

    def score_block(region, place_in, width, chunks, hidden):
        rows = pl.ds(pl.multiple_of(region * block, block), block)
        key_rows = keys[rows, :HEAD_WIDTH]
        for chunk in range(chunks):
            span = slice(chunk * width, (chunk + 1) * width)
            value = dot(key_rows, query_t[:, span]) * SCALE_LOG2
            if hidden is not None:
                value = jnp.where(hidden, NEGATIVE_FLOOR, value)
            split = value.reshape(block // 8, 8, width)
            peak, summed = top[:, span], mass[:, span]
            for part in range(block // PART):
                piece = split[part * PART // 8 : (part + 1) * PART // 8]
                now = jnp.maximum(peak, jnp.max(piece, axis=0))
                shifted = jnp.exp2(piece - now[None])
                scores[place_in, part * PART : (part + 1) * PART, span] = shifted.reshape(PART, width)
                peaks[place_in, part, :, span] = now
                summed = summed * jnp.exp2(peak - now) + jnp.sum(shifted, axis=0)
                peak = now
            top[:, span], mass[:, span] = peak, summed

    def weigh(region, place_in, width, chunks, log_mass, stage, earlier=None, earlier_stage=None):
        rows = pl.ds(pl.multiple_of(region * block, block), block)
        value_rows = keys[rows, HEAD_WIDTH:]
        for chunk in range(chunks):
            span = slice(chunk * width, (chunk + 1) * width)
            dp = dot(value_rows, gradient_t[:, span])
            for part in range(block // PART):
                at = slice(part * PART, (part + 1) * PART)
                factor = jnp.exp2(peaks[place_in, part, :, span] - log_mass[chunk])
                p = scores[place_in, at, span].reshape(PART // 8, 8, width) * factor[None]
                p = p.reshape(PART, width)
                stage[0][at, span] = p.astype(BF16)
                stage[1][at, span] = (p * (dp[at] - delta[0:1, span])).astype(BF16)
            if earlier is not None:
                multiply(earlier, width, chunks, earlier_stage, chunk)
        if earlier is not None:
            for chunk in range(chunks, 3):
                multiply(earlier, width, chunks, earlier_stage, chunk)

    def multiply(region, width, chunks, stage, part):
        rows = pl.ds(pl.multiple_of(region * block, block), block)
        used = width * chunks
        if part == 0:
            total[rows, HEAD_WIDTH:] += dot(stage[0][:, :used], gradient[:used])
        elif part == 1:
            total[rows, :HEAD_WIDTH] += dot(stage[1][:, :used], query[:used])
        elif part == 2:
            query_grad[:, :used] += dot(keys_t[region], stage[1][:, :used])

    def grad_blocks(count, region_of, width, chunks, log_mass):
        first, second = stages

        def later(index, stage, earlier_stage):
            weigh(
                region_of(index), index, width, chunks, log_mass, stage, region_of(index - 1), earlier_stage
            )

        def last(stage):
            for part in range(3):
                multiply(region_of(count - 1), width, chunks, stage, part)

        weigh(region_of(0), 0, width, chunks, log_mass, first)

        def two(index, carry):
            later(2 * index + 1, second, first)
            later(2 * index + 2, first, second)
            return carry

        lax.fori_loop(0, (count - 1) // 2, two, 0)

        @pl.when(count % 2 == 0)
        def _():
            later(count - 1, second, first)
            last(second)

        @pl.when(count % 2 == 1)
        def _():
            last(first)

    def turn(all_rows):
        query_t[:, :all_rows] = dot(unit, query[:all_rows], (1, 1)).astype(BF16)
        gradient_t[:, :all_rows] = dot(unit, gradient[:all_rows], (1, 1)).astype(BF16)

    def begin(all_rows):
        top[:, :all_rows] = jnp.full((8, all_rows), NEGATIVE_FLOOR, F32)
        mass[:, :all_rows] = jnp.zeros((8, all_rows), F32)
        query_grad[:, :all_rows] = jnp.zeros((HEAD_WIDTH, all_rows), F32)

    def log_masses(width, chunks, live):
        found = []
        for chunk in range(chunks):
            span = slice(chunk * width, (chunk + 1) * width)
            peak = jnp.max(top[:, span], axis=0, keepdims=True)
            summed = jnp.sum(mass[:, span] * jnp.exp2(top[:, span] - peak), axis=0, keepdims=True)
            found.append(jnp.where(live, peak + jnp.log2(summed), DEAD))
        return found

    def absolute(index, half):
        return index + jnp.where(index < half, core * half, -core * half)

    def reply_tile(slot, carry):
        length = jnp.int32(0)
        for response in range(reply_len.shape[0]):
            mine = reply_slot[response] == group * RESP_DEV + slot
            length = length + jnp.where(mine, reply_len[response], 0)
        first = chip * positions
        source = pl.ds(pl.multiple_of(slot * own_positions, own_positions), own_positions)

        @pl.when(length > first)
        def _():
            for head in range(GROUP):
                for other in range(CORES):
                    at = head * positions + other * own_positions
                    to = slice(at, at + own_positions)
                    left = slice(head * HEAD_WIDTH, (head + 1) * HEAD_WIDTH)
                    right = slice(GROUP_WIDTH + head * HEAD_WIDTH, GROUP_WIDTH + (head + 1) * HEAD_WIDTH)
                    query[to] = rows_in[other][source, left]
                    gradient[to] = rows_in[other][source, right]
                    for which in range(RESP_DEV):
                        @pl.when(slot == which)
                        def _():
                            delta[0:1, to] = deltas[
                                other, head : head + 1, which * own_positions : (which + 1) * own_positions
                            ]
            begin(GROUP * positions)
            turn(GROUP * positions)
            base = prompt_blocks + slot * (chips // 2)
            past = prompt_blocks + chip // 2

            def region_of(index):
                reply = base + ((index - prompt_blocks) ^ (chip // 2))
                return jnp.where(index < prompt_blocks, index, jnp.where(index == past, base, reply))

            def stats(index, carry):
                score_block(region_of(index), index, positions, GROUP, None)
                return carry

            lax.fori_loop(0, past, stats, 0)
            row_at = absolute(iota((1, positions), 1), own_positions)
            key = iota((block, 1), 0)
            key_at = jnp.where(key < positions, absolute(key, own_positions), lax.rem(chip + 1, 2) * block - 1)
            score_block(base, past, positions, GROUP, key_at > row_at)
            live = first + row_at < length
            log_mass = log_masses(positions, GROUP, live)

            grad_blocks(past + 1, region_of, positions, GROUP, log_mass)
            for head in range(GROUP):
                turned = (query_grad[:, head * positions : (head + 1) * positions].T * SCALE).astype(BF16)
                for other in range(CORES):
                    query_out[other][source, head * HEAD_WIDTH : (head + 1) * HEAD_WIDTH] = turned[
                        other * own_positions : (other + 1) * own_positions
                    ]

        @pl.when(length <= first)
        def _():
            for other in range(CORES):
                query_out[other][source, :] = jnp.zeros((own_positions, GROUP_WIDTH), BF16)

        return carry

    lax.fori_loop(0, RESP_DEV, reply_tile, 0)

    head_rows = CORES * prompt_own
    used = GROUP * head_rows
    all_rows = -(-used // 128) * 128
    if all_rows > used:
        query[used:all_rows] = jnp.zeros((all_rows - used, HEAD_WIDTH), BF16)
        gradient[used:all_rows] = jnp.zeros((all_rows - used, HEAD_WIDTH), BF16)
    delta[0:1, :all_rows] = jnp.zeros((1, all_rows), F32)
    for head in range(GROUP):
        for other in range(CORES):
            at = head * head_rows + other * prompt_own
            to = slice(at, at + prompt_own)
            left = slice(head * HEAD_WIDTH, (head + 1) * HEAD_WIDTH)
            right = slice(GROUP_WIDTH + head * HEAD_WIDTH, GROUP_WIDTH + (head + 1) * HEAD_WIDTH)
            query[to] = rows_in[other][reply_own:, left]
            gradient[to] = rows_in[other][reply_own:, right]
            delta[0:1, to] = deltas[other, head : head + 1, reply_own:]
    begin(all_rows)
    turn(all_rows)
    lane = iota((1, all_rows), 1)
    within = lane
    for head in range(1, GROUP):
        within = within - jnp.where(lane >= head * head_rows, head_rows, 0)
    offset = jnp.where(within < prompt_own, within, within - prompt_own)
    row_core = jnp.where(within < prompt_own, core, 1 - core)
    real = (lane < used) & (offset < prompt_rows)
    row_at = jnp.where(
        real, (chip * CORES + row_core) * prompt_keys + group * prompt_rows + offset, -1
    )
    per_block = max(block // chip_prompt, 1)
    block_parts = max(chip_prompt // block, 1)
    pair = chip // per_block
    seen = (pair + 1) * block_parts

    def prompt_region(index):
        return (index // block_parts ^ pair) * block_parts + index % block_parts

    def prompt_stats(index, carry):
        key = iota((block, 1), 0) + index % block_parts * block
        key_chip = ((index // block_parts ^ pair) * per_block + key // chip_prompt) ^ chip
        key_at = key_chip * chip_prompt + absolute(key % chip_prompt, prompt_keys)
        score_block(prompt_region(index), index, all_rows, 1, key_at > row_at)
        return carry

    lax.fori_loop(0, seen, prompt_stats, 0)
    log_mass = log_masses(all_rows, 1, real)

    grad_blocks(seen, prompt_region, all_rows, 1, log_mass)
    turned = (query_grad[:, :all_rows].T * SCALE).astype(BF16)
    for head in range(GROUP):
        for other in range(CORES):
            at = head * head_rows + other * prompt_own
            query_out[other][reply_own:, head * HEAD_WIDTH : (head + 1) * HEAD_WIDTH] = turned[
                at : at + prompt_own
            ]

    def put(out, at, count):
        out[:, :HEAD_WIDTH] = (total[at : at + count, :HEAD_WIDTH] * SCALE).astype(BF16)
        out[:, HEAD_WIDTH:] = total[at : at + count, HEAD_WIDTH:].astype(BF16)

    for index in range(chips * CORES):
        away, other = index // CORES, index % CORES
        put(prompt_out[away].at[other, :prompt_keys], away * chip_prompt + other * prompt_keys, prompt_keys)
        for slot in range(RESP_DEV):
            at = chips * chip_prompt + (slot * chips + away) * positions + other * own_positions
            to = slot * own_positions + (0 if joint_keys else prompt_keys)
            put(keys_out[away].at[other, to : to + own_positions], at, own_positions)


def add(first, *rest):
    value = first.astype(F32)
    for part in rest:
        value = value + part.astype(F32)
    return value


def collect_first(chips, place, *refs):
    parts, prompt_parts, refs = refs[:chips], refs[chips : 2 * chips], refs[2 * chips :]
    mine, theirs, outs, summed = refs[0], refs[1], refs[2:-1], refs[-1]
    groups, rows = len(outs), outs[0].shape[1]
    prompt_keys = groups * rows
    mine[...] = add(*(part[0, prompt_keys:] for part in parts))
    theirs[...] = add(*(part[1, prompt_keys:] for part in parts)).astype(BF16)
    for other in range(CORES):
        summed[other] = add(*(part[other, :prompt_keys] for part in parts))
        summed[CORES + other] = add(*(part[other] for part in prompt_parts))
    for shift in range(groups):
        at = pl.ds(pl.multiple_of(lax.rem(place[2] + shift, groups) * rows, rows), rows)
        for index in range(summed.shape[0]):
            outs[shift][index] = summed[index, at].astype(BF16)


def collect_second(chips, *refs):
    parts, slices, (theirs0, mine, prompt, theirs) = refs[:chips], refs[chips:-4], refs[-4:]
    reply, rows = theirs0.shape[0], prompt.shape[1]
    step = max(rows, 16)
    mine[...] = add(*(part[0] for part in parts))
    theirs[:reply] = theirs0[...]
    theirs[reply : 2 * reply] = add(*(part[1] for part in parts)).astype(BF16)
    for local in range(LOCAL_HEADS):
        prompt[local] = add(*(part[CORES * local] for part in slices))
        at = 2 * reply + local * step
        theirs[at : at + rows] = add(*(part[CORES * local + 1] for part in slices)).astype(BF16)


def finish_queries(place, *refs):
    queries, prompt_dq, reply_dq = refs[:-2], refs[-2], refs[-1]
    reply = reply_dq.shape[0]
    order = unsorting(reply)
    for index, query in enumerate(queries):
        span = lanes(head_of(place[1], index % CORES, index // CORES), GROUP_WIDTH)
        reply_dq[:, span] = dot(order, query[:reply]).astype(BF16)
        prompt_dq[:, span] = query[reply:]


def finish_keys(place, reply0, reply1, prompts, theirs, prompt_dk, prompt_dv, reply_dk, reply_dv):
    reply, rows = reply_dk.shape[0], prompt_dk.shape[0]
    step = max(rows, 16)
    order = unsorting(reply)
    for local in range(LOCAL_HEADS):
        for other in range(CORES):
            span = lanes(head_of(place[1], other, local), HEAD_WIDTH)
            if other:
                value = theirs[local * reply : (local + 1) * reply]
                prompt = theirs[2 * reply + local * step : 2 * reply + local * step + rows]
            else:
                value = (reply1 if local else reply0)[...].astype(BF16)
                prompt = prompts[local].astype(BF16)
            value = dot(order, value).astype(BF16)
            reply_dk[:, span] = value[:, :HEAD_WIDTH]
            reply_dv[:, span] = value[:, HEAD_WIDTH:]
            prompt_dk[:, span] = prompt[:, :HEAD_WIDTH]
            prompt_dv[:, span] = prompt[:, HEAD_WIDTH:]


def on_device(
    prompt_query,
    prompt_k,
    prompt_value,
    prompt_output,
    prompt_output_gradient,
    reply_query,
    reply_key,
    reply_value,
    reply_output,
    reply_output_gradient,
    reply_len,
    reply_slot,
):
    devices = lax.axis_size("pre")
    groups = lax.axis_size("rsp")
    chips = devices // CORES
    prompt_rows = prompt_query.shape[0]
    prompt_own = -(-prompt_rows // 16) * 16
    prompt_keys = prompt_k.shape[0]
    reply_own = reply_query.shape[1]
    own_positions = reply_own // RESP_DEV
    positions = CORES * own_positions
    chip_prompt = CORES * prompt_keys
    block = 2 * positions
    assert (chip_prompt % block == 0 or block % chip_prompt == 0) and chips > 1 and chips & (chips - 1) == 0
    pre_index = lax.axis_index("pre")
    place = jnp.stack([lax.div(pre_index, CORES), lax.rem(pre_index, CORES), lax.axis_index("rsp")])

    def shape(*dims, dtype=BF16):
        return jax.ShapeDtypeStruct(dims, dtype)

    def move(array, away, cross=0):
        pairs = [(p, (p // CORES ^ away) * CORES + (p % CORES ^ cross)) for p in range(devices)]
        return lax.ppermute(array, "pre", pairs)

    def swap(array):
        return move(array, 0, 1)

    def call(kernel, name, mib, inputs, outs, scalars=1, spec=VMEM, **more):
        return pl.pallas_call(
            kernel,
            out_shape=outs,
            in_specs=[SMEM] * scalars + [spec] * (len(inputs) - scalars),
            out_specs=[VMEM] * len(outs),
            compiler_params=params(mib),
            name=name,
            **more,
        )(*inputs)

    relayed = chips == 4
    key_shape = (prompt_keys + reply_own, 2 * HEAD_WIDTH)
    mine0, theirs0, mine1, theirs, token = call(
        prepare_keys,
        "prepare_keys",
        LARGE_MIB,
        (place, prompt_k, prompt_value, reply_key[0], reply_value[0]),
        [shape(*key_shape)] * 3 + [shape(LOCAL_HEADS, *key_shape), shape(8, 128, dtype=F32)],
        spec=HBM,
        scratch_shapes=[
            pltpu.VMEM((rows, KEY_VALUE_HEADS * HEAD_WIDTH), BF16)
            for rows in (prompt_keys, prompt_keys, reply_own, reply_own)
        ]
        + [pltpu.SemaphoreType.DMA((4,))],
    )
    blocks0 = {(0, 0): mine0, (0, 1): swap(theirs)}
    for away in range(1, 3 if relayed else chips):
        blocks0[away, 0] = move(mine0, away)
        blocks0[away, 1] = move(theirs0, away, 1)
    if prompt_own > prompt_rows:
        room = ((0, prompt_own - prompt_rows), (0, 0))
        prompt_query, prompt_output, prompt_output_gradient = (
            jnp.pad(array, room)
            for array in (prompt_query, prompt_output, prompt_output_gradient)
        )
    own_rows = reply_own + prompt_own
    row_width = 2 * GROUP_WIDTH + HEAD_WIDTH

    rows = call(
        prepare_rows,
        "prepare_rows",
        LARGE_MIB,
        (
            place,
            token,
            prompt_query,
            prompt_output,
            prompt_output_gradient,
            reply_query[0],
            reply_output[0],
            reply_output_gradient[0],
        ),
        [shape(LOCAL_HEADS, own_rows, row_width)] + [shape(own_rows, row_width)] * LOCAL_HEADS,
        spec=HBM,
        scratch_shapes=[
            pltpu.VMEM((KEY_VALUE_HEADS, rows, GROUP_WIDTH), BF16)
            for rows in [prompt_own] * 3 + [reply_own] * 3
        ]
        + [pltpu.SemaphoreType.DMA((KEY_VALUE_HEADS * 6,))],
        cost_estimate=pl.CostEstimate(
            flops=6 * reply_own * reply_own * QUERY_HEADS * HEAD_WIDTH,
            bytes_accessed=20 * reply_own * QUERY_HEADS * HEAD_WIDTH,
            transcendentals=0,
        ),
    )

    blocks0, rows, mine1 = lax.optimization_barrier((blocks0, rows, mine1))
    if relayed:
        blocks0[3, 0] = move(blocks0[1, 0], 2)
        blocks0[3, 1] = move(blocks0[2, 1], 1)
    chip1 = jnp.stack([mine1, blocks0[0, 1][1]])
    blocks1 = [chip1] + [move(chip1, away) for away in range(1, chips)]

    blocks = (chips * chip_prompt + RESP_DEV * chips * positions) // block
    slots = (chips * chip_prompt + chips * positions) // block
    all_rows = max(GROUP * positions, -(-GROUP * CORES * prompt_own // 128) * 128)
    sizes = (chips, reply_own, prompt_own, prompt_rows, prompt_keys)
    score_count = GROUP * (positions * RESP_DEV * slots * block)

    cut_rows = prompt_keys // groups
    rows_theirs, *rows_mine = rows
    rows_theirs = swap(rows_theirs)

    def run_attend(local, key_blocks):
        joint_keys = local == 1
        sums = [shape(CORES, *key_shape)] * chips
        if joint_keys:
            sums = [shape(CORES, n, 2 * HEAD_WIDTH) for n in [reply_own] * chips + [prompt_keys] * chips]
        query_mine, query_theirs, *sums = call(
            functools.partial(attend, sizes, joint_keys),
            "attend",
            VMEM_MIB,
            (
                place,
                reply_len,
                reply_slot,
                rows_mine[local],
                rows_theirs,
                *key_blocks,
            ),
            [shape(own_rows, GROUP_WIDTH)] * CORES + sums,
            scalars=3,
            scratch_shapes=[
                pltpu.VMEM((blocks * block, 2 * HEAD_WIDTH), BF16),
                pltpu.VMEM((blocks, HEAD_WIDTH, block), BF16),
                pltpu.VMEM((blocks * block, 2 * HEAD_WIDTH), F32),
                pltpu.VMEM((all_rows, HEAD_WIDTH), BF16),
                pltpu.VMEM((all_rows, HEAD_WIDTH), BF16),
                pltpu.VMEM((HEAD_WIDTH, all_rows), BF16),
                pltpu.VMEM((HEAD_WIDTH, all_rows), BF16),
                pltpu.VMEM((CORES, 8, own_rows), F32),
                pltpu.VMEM((8, all_rows), F32),
                pltpu.VMEM((slots, block, all_rows), F32),
                pltpu.VMEM((slots, block // PART, 8, all_rows), F32),
                pltpu.VMEM((8, all_rows), F32),
                pltpu.VMEM((8, all_rows), F32),
                pltpu.VMEM((HEAD_WIDTH, all_rows), F32),
            ]
            + [pltpu.VMEM((block, all_rows), BF16)] * 4,
            cost_estimate=pl.CostEstimate(
                flops=score_count * 10 * HEAD_WIDTH,
                bytes_accessed=8 * 1024 * 1024,
                transcendentals=2 * score_count,
            ),
        )
        return query_mine, query_theirs, sums

    query_mine0, query_theirs0, sums0 = run_attend(
        0, [blocks0[away, other] for away in range(chips) for other in range(CORES)]
    )
    arrived0 = [sums0[0]] + [move(sums0[away], away) for away in range(1, chips)]
    query_theirs0 = swap(query_theirs0)
    query_mine1, query_theirs1, sums1 = run_attend(1, blocks1)
    arrived0, query_theirs0, query_theirs1, sums1 = lax.optimization_barrier(
        (arrived0, query_theirs0, query_theirs1, sums1)
    )
    prompt1 = [sums1[chips]] + [move(sums1[chips + away], away) for away in range(1, chips)]
    arrived1 = [sums1[0]] + [move(sums1[away], away) for away in range(1, chips)]
    key_width = KEY_VALUE_HEADS * HEAD_WIDTH
    query_width = QUERY_HEADS * HEAD_WIDTH
    reply0, theirs0, *cuts = call(
        functools.partial(collect_first, chips),
        "collect_first",
        SMALL_MIB,
        (place, *arrived0, *prompt1),
        [shape(reply_own, 2 * HEAD_WIDTH, dtype=F32), shape(reply_own, 2 * HEAD_WIDTH)]
        + [shape(KEY_VALUE_HEADS, cut_rows, 2 * HEAD_WIDTH)] * groups,
        scratch_shapes=[pltpu.VMEM((KEY_VALUE_HEADS, prompt_keys, 2 * HEAD_WIDTH), F32)],
    )
    slices = [cuts[0]] + [
        lax.ppermute(cuts[shift], "rsp", [(g, (g + shift) % groups) for g in range(groups)])
        for shift in range(1, groups)
    ]
    prompt_dq, reply_dq = call(
        finish_queries,
        "finish_queries",
        SMALL_MIB,
        (place, query_mine0, query_theirs0, query_mine1, swap(query_theirs1)),
        [shape(prompt_own, query_width), shape(reply_own, query_width)],
        cost_estimate=pl.CostEstimate(
            flops=2 * reply_own * reply_own * query_width,
            bytes_accessed=8 * reply_own * query_width,
            transcendentals=0,
        ),
    )
    slices, prompt_dq, reply_dq = lax.optimization_barrier((slices, prompt_dq, reply_dq))
    reply1, prompts, theirs = call(
        functools.partial(collect_second, chips),
        "collect_second",
        SMALL_MIB,
        (*arrived1, *slices, theirs0),
        [
            shape(reply_own, 2 * HEAD_WIDTH, dtype=F32),
            shape(LOCAL_HEADS, cut_rows, 2 * HEAD_WIDTH, dtype=F32),
            shape(2 * reply_own + 2 * max(cut_rows, 16), 2 * HEAD_WIDTH),
        ],
        scalars=0,
    )
    prompt_dk, prompt_dv, reply_dk, reply_dv = call(
        finish_keys,
        "finish_keys",
        SMALL_MIB,
        (place, reply0, reply1, prompts, swap(theirs)),
        [shape(cut_rows, key_width)] * 2 + [shape(reply_own, key_width)] * 2,
    )
    return (
        prompt_dq[:prompt_rows],
        prompt_dk,
        prompt_dv,
        reply_dq[None],
        reply_dk[None],
        reply_dv[None],
    )


def solution(mesh):
    return jax.shard_map(
        on_device,
        mesh=mesh,
        in_specs=(
            P(("pre", "rsp"), None),
            P("pre", None),
            P("pre", None),
            P(("pre", "rsp"), None),
            P(("pre", "rsp"), None),
            P("rsp", "pre", None),
            P("rsp", "pre", None),
            P("rsp", "pre", None),
            P("rsp", "pre", None),
            P("rsp", "pre", None),
            P(),
            P(),
        ),
        out_specs=(
            P(("pre", "rsp"), None),
            P(("pre", "rsp"), None),
            P(("pre", "rsp"), None),
            P("rsp", "pre", None),
            P("rsp", "pre", None),
            P("rsp", "pre", None),
        ),
        check_vma=False,
    )
```

```python
import functools
import math

import jax
import jax.numpy as jnp
from jax import lax
from jax.experimental import pallas as pl
from jax.experimental.pallas import tpu as pltpu
from jax.sharding import PartitionSpec as P

QUERY_HEADS = 20
KEY_VALUE_HEADS = 4
GROUP = QUERY_HEADS // KEY_VALUE_HEADS
HEAD_WIDTH = 128
RESP_DEV = 2
CORES = 2
LOCAL_HEADS = KEY_VALUE_HEADS // CORES
GROUP_WIDTH = GROUP * HEAD_WIDTH

SCALE = HEAD_WIDTH ** (-0.5)
SCALE_LOG2 = SCALE * math.log2(math.e)
PART = 128
NEGATIVE_FLOOR = -1e30
DEAD = 1e30
F32 = jnp.float32
BF16 = jnp.bfloat16
VMEM = pl.BlockSpec(memory_space=pltpu.VMEM)
SMEM = pl.BlockSpec(memory_space=pltpu.SMEM)
HBM = pl.BlockSpec(memory_space=pltpu.HBM)


VMEM_MIB = 40
SMALL_MIB = 24
LARGE_MIB = 58


def params(mib):
    return pltpu.CompilerParams(vmem_limit_bytes=mib * 1024 * 1024)


def dot(a, b, over=(1, 0)):
    return lax.dot_general(
        a, b, (((over[0],), (over[1],)), ((), ())), preferred_element_type=F32
    )


def iota(shape, axis):
    return lax.broadcasted_iota(jnp.int32, shape, axis)


def sorting(rows):
    half = rows // RESP_DEV
    out = iota((rows, rows), 0)
    source = jnp.where(out < half, RESP_DEV * out, RESP_DEV * (out - half) + 1)
    return (iota((rows, rows), 1) == source).astype(BF16)


def unsorting(rows):
    half = rows // RESP_DEV
    out = iota((rows, rows), 1)
    source = jnp.where(out < half, RESP_DEV * out, RESP_DEV * (out - half) + 1)
    return (iota((rows, rows), 0) == source).astype(BF16)


def lanes(index, width):
    return pl.ds(pl.multiple_of(index * width, width), width)


def head_of(core, cross, local):
    owner = (1 - core) if cross else core
    return owner * LOCAL_HEADS + local


def fetch(pairs, sems):
    copies = [pltpu.make_async_copy(src, dst, sems.at[i]) for i, (src, dst) in enumerate(pairs)]
    for copy in copies:
        copy.start()
    return copies


def prepare_keys(pk, pv, rk, rv, mine0, theirs0, mine1, theirs, token, *scratch):
    core = lax.rem(lax.axis_index("pre"), CORES)
    bufs, sems = scratch[:-1], scratch[-1]
    copies = fetch(zip((pk, pv, rk, rv), bufs), sems)
    prompt = pk.shape[0]
    order = sorting(rk.shape[0])
    for copy in copies:
        copy.wait()
    pk, pv, rk, rv = bufs
    for local, outs in enumerate(((mine0, theirs.at[0]), (mine1, theirs.at[1]))):
        for cross, out in enumerate(outs):
            span = lanes(head_of(core, cross, local), HEAD_WIDTH)
            for part, (p, r) in enumerate(((pk, rk), (pv, rv))):
                to = slice(part * HEAD_WIDTH, (part + 1) * HEAD_WIDTH)
                out[:prompt, to] = p[:, span]
                out[prompt:, to] = dot(order, r[:, span]).astype(BF16)
    theirs0[...] = theirs[0]
    token[...] = jnp.zeros_like(token)


def prepare_rows(place, token, pq, po, pg, rq, ro, rg, *refs):
    (theirs, *mine), bufs, sems = refs[: 1 + LOCAL_HEADS], refs[1 + LOCAL_HEADS : -1], refs[-1]
    outs = [out for local in range(LOCAL_HEADS) for out in (theirs.at[local], mine[local])]
    core = place[1]
    reply = rq.shape[0]
    sources = (pq, po, pg, rq, ro, rg)
    pairs = []
    for step in range(KEY_VALUE_HEADS):
        span = lanes(head_of(core, 1 - step % CORES, step // CORES), GROUP_WIDTH)
        pairs += [(source.at[:, span], buf.at[step]) for source, buf in zip(sources, bufs)]
    copies = fetch(pairs, sems)
    order = sorting(reply)
    column = iota((GROUP_WIDTH, HEAD_WIDTH), 1)
    pick = (column // 3 == iota((GROUP_WIDTH, HEAD_WIDTH), 0) // HEAD_WIDTH).astype(BF16)

    def delta(gradient, output):
        product = gradient.astype(F32) * output.astype(F32)
        high = product.astype(BF16)
        low = (product - high.astype(F32)).astype(BF16)
        value = dot(high, pick) + dot(low, pick)
        first = value.astype(BF16).astype(F32)
        second = (value - first).astype(BF16).astype(F32)
        part = iota(value.shape, 1) % 3
        return jnp.where(part == 0, first, jnp.where(part == 1, second, value - first - second)).astype(BF16)

    for step, out in enumerate(outs):
        for copy in copies[step * len(sources) : (step + 1) * len(sources)]:
            copy.wait()
        pq, po, pg, rq, ro, rg = (buf[step] for buf in bufs)
        out[reply:, :GROUP_WIDTH] = pq
        out[reply:, GROUP_WIDTH : 2 * GROUP_WIDTH] = pg
        out[reply:, 2 * GROUP_WIDTH :] = delta(pg, po)
        out[:reply, :GROUP_WIDTH] = dot(order, rq).astype(BF16)
        gradient = dot(order, rg).astype(BF16)
        out[:reply, GROUP_WIDTH : 2 * GROUP_WIDTH] = gradient
        out[:reply, 2 * GROUP_WIDTH :] = delta(gradient, dot(order, ro).astype(BF16))


def attend(sizes, joint_keys, place, reply_len, reply_slot, *refs):
    chips, reply_own, prompt_own, prompt_rows, prompt_keys = sizes
    own_positions = reply_own // RESP_DEV
    positions = CORES * own_positions
    chip_prompt = CORES * prompt_keys
    block = 2 * positions
    prompt_blocks = chips * chip_prompt // block
    rows_in, refs = (refs[0], refs[1].at[int(joint_keys)]), refs[2:]
    count = chips if joint_keys else chips * CORES
    keys_in, refs = refs[:count], refs[count:]
    query_out, refs = refs[:2], refs[2:]
    keys_out, refs = refs[:chips], refs[chips:]
    prompt_out, refs = (refs[:chips], refs[chips:]) if joint_keys else (keys_out, refs)
    keys, keys_t, total, query, gradient, query_t, gradient_t, deltas, delta, scores, peaks, top, mass, *refs = refs
    query_grad, stages = refs[0], (refs[1:3], refs[3:5])
    chip, core, group = place[0], place[1], place[2]

    pick = (iota((8, HEAD_WIDTH), 1) // 3 == iota((8, HEAD_WIDTH), 0)).astype(BF16)
    for other in range(CORES):
        deltas[other] = dot(pick, rows_in[other][:, 2 * GROUP_WIDTH :], (1, 1))

    for index in range(chips * CORES):
        away, other = index // CORES, index % CORES
        source = keys_in[away].at[other] if joint_keys else keys_in[index]
        source = source if len(source.shape) == 2 else source.at[0]
        at = away * chip_prompt + other * prompt_keys
        keys[at : at + prompt_keys] = source[:prompt_keys]
        for slot in range(RESP_DEV):
            at = chips * chip_prompt + (slot * chips + away) * positions + other * own_positions
            begin = prompt_keys + slot * own_positions
            keys[at : at + own_positions] = source[begin : begin + own_positions]
    total[...] = jnp.zeros_like(total)

    unit = (iota((HEAD_WIDTH, HEAD_WIDTH), 0) == iota((HEAD_WIDTH, HEAD_WIDTH), 1)).astype(BF16)

    def transpose_block(index, carry):
        rows = pl.ds(pl.multiple_of(index * block, block), block)
        keys_t[index] = dot(unit, keys[rows, :HEAD_WIDTH], (1, 1)).astype(BF16)
        return carry

    lax.fori_loop(0, keys_t.shape[0], transpose_block, 0)

    def score_block(region, place_in, width, chunks, hidden, count=block):
        rows = pl.ds(pl.multiple_of(region * block, block), count)
        key_rows = keys[rows, :HEAD_WIDTH]
        for chunk in range(chunks):
            span = slice(chunk * width, (chunk + 1) * width)
            value = dot(key_rows, query_t[:, span]) * SCALE_LOG2
            if hidden is not None:
                value = jnp.where(hidden, NEGATIVE_FLOOR, value)
            split = value.reshape(count // 8, 8, width)
            peak, summed = top[:, span], mass[:, span]
            for part in range(count // PART):
                piece = split[part * PART // 8 : (part + 1) * PART // 8]
                now = jnp.maximum(peak, jnp.max(piece, axis=0))
                shifted = jnp.exp2(piece - now[None])
                scores[place_in, part * PART : (part + 1) * PART, span] = shifted.reshape(PART, width)
                peaks[place_in, part, :, span] = now
                summed = summed * jnp.exp2(peak - now) + jnp.sum(shifted, axis=0)
                peak = now
            top[:, span], mass[:, span] = peak, summed

    def weigh(region, place_in, width, chunks, log_mass, stage, count=block, earlier=None):
        rows = pl.ds(pl.multiple_of(region * block, block), count)
        value_rows = keys[rows, HEAD_WIDTH:]
        for chunk in range(chunks):
            span = slice(chunk * width, (chunk + 1) * width)
            dp = dot(value_rows, gradient_t[:, span])
            for part in range(count // PART):
                at = slice(part * PART, (part + 1) * PART)
                factor = jnp.exp2(peaks[place_in, part, :, span] - log_mass[chunk])
                p = scores[place_in, at, span].reshape(PART // 8, 8, width) * factor[None]
                p = p.reshape(PART, width)
                stage[0][at, span] = p.astype(BF16)
                stage[1][at, span] = (p * (dp[at] - delta[0:1, span])).astype(BF16)
            if earlier is not None:
                multiply(*earlier, width, chunks, chunk)
        if earlier is not None:
            for chunk in range(chunks, 3):
                multiply(*earlier, width, chunks, chunk)

    def multiply(region, stage, count, width, chunks, part):
        rows = pl.ds(pl.multiple_of(region * block, block), count)
        used = width * chunks
        if part == 0:
            total[rows, HEAD_WIDTH:] += dot(stage[0][:count, :used], gradient[:used])
        elif part == 1:
            total[rows, :HEAD_WIDTH] += dot(stage[1][:count, :used], query[:used])
        elif part == 2:
            query_grad[:, :used] += dot(keys_t[region, :, :count], stage[1][:count, :used])

    def grad_blocks(blocks, region_of, width, chunks, log_mass, begin_with):
        first, second = stages

        def later(index, stage, earlier_stage):
            earlier = region_of(index - 1), earlier_stage, block
            weigh(region_of(index), index, width, chunks, log_mass, stage, earlier=earlier)

        def last(stage):
            for part in range(3):
                multiply(region_of(blocks - 1), stage, block, width, chunks, part)

        begin_with(first, second)

        def two(index, carry):
            later(2 * index + 1, first, second)
            later(2 * index + 2, second, first)
            return carry

        lax.fori_loop(0, (blocks - 1) // 2, two, 0)

        @pl.when(blocks % 2 == 0)
        def _():
            later(blocks - 1, first, second)
            last(first)

        @pl.when(blocks % 2 == 1)
        def _():
            last(second)

    def turn(all_rows):
        query_t[:, :all_rows] = dot(unit, query[:all_rows], (1, 1)).astype(BF16)
        gradient_t[:, :all_rows] = dot(unit, gradient[:all_rows], (1, 1)).astype(BF16)

    def begin(all_rows):
        top[:, :all_rows] = jnp.full((8, all_rows), NEGATIVE_FLOOR, F32)
        mass[:, :all_rows] = jnp.zeros((8, all_rows), F32)
        query_grad[:, :all_rows] = jnp.zeros((HEAD_WIDTH, all_rows), F32)

    def log_masses(width, chunks, live):
        found = []
        for chunk in range(chunks):
            span = slice(chunk * width, (chunk + 1) * width)
            peak = jnp.max(top[:, span], axis=0, keepdims=True)
            summed = jnp.sum(mass[:, span] * jnp.exp2(top[:, span] - peak), axis=0, keepdims=True)
            found.append(jnp.where(live, peak + jnp.log2(summed), DEAD))
        return found

    def absolute(index, half):
        return index + jnp.where(index < half, core * half, -core * half)

    def reply_tile(slot, carry):
        length = jnp.int32(0)
        for response in range(reply_len.shape[0]):
            mine = reply_slot[response] == group * RESP_DEV + slot
            length = length + jnp.where(mine, reply_len[response], 0)
        first = chip * positions
        source = pl.ds(pl.multiple_of(slot * own_positions, own_positions), own_positions)

        @pl.when(length > first)
        def _():
            for head in range(GROUP):
                for other in range(CORES):
                    at = head * positions + other * own_positions
                    to = slice(at, at + own_positions)
                    left = slice(head * HEAD_WIDTH, (head + 1) * HEAD_WIDTH)
                    right = slice(GROUP_WIDTH + head * HEAD_WIDTH, GROUP_WIDTH + (head + 1) * HEAD_WIDTH)
                    query[to] = rows_in[other][source, left]
                    gradient[to] = rows_in[other][source, right]
                    for which in range(RESP_DEV):
                        @pl.when(slot == which)
                        def _():
                            delta[0:1, to] = deltas[
                                other, head : head + 1, which * own_positions : (which + 1) * own_positions
                            ]
            begin(GROUP * positions)
            turn(GROUP * positions)
            base = prompt_blocks + slot * (chips // 2)
            past = prompt_blocks + chip // 2

            def region_of(index):
                reply = base + ((index - prompt_blocks) ^ (chip // 2))
                return jnp.where(index < prompt_blocks, index, reply)

            def stats(index, carry):
                score_block(region_of(index), index, positions, GROUP, None)
                return carry

            lax.fori_loop(0, past, stats, 0)
            row_at = absolute(iota((1, positions), 1), own_positions)
            odd = chip % 2 == 1

            def own_stats(count):
                key = iota((count, 1), 0)
                key_at = jnp.where(key < positions, absolute(key, own_positions), -1)
                score_block(base, past, positions, GROUP, key_at > row_at, count)

            @pl.when(odd)
            def _():
                own_stats(block)

            @pl.when(jnp.logical_not(odd))
            def _():
                own_stats(positions)

            live = first + row_at < length
            log_mass = log_masses(positions, GROUP, live)


            def own_grads(stage, next_stage):
                def run(count):
                    weigh(base, past, positions, GROUP, log_mass, stage, count)
                    earlier = base, stage, count
                    weigh(region_of(0), 0, positions, GROUP, log_mass, next_stage, earlier=earlier)

                @pl.when(odd)
                def _():
                    run(block)

                @pl.when(jnp.logical_not(odd))
                def _():
                    run(positions)

            grad_blocks(past, region_of, positions, GROUP, log_mass, own_grads)
            for head in range(GROUP):
                turned = (query_grad[:, head * positions : (head + 1) * positions].T * SCALE).astype(BF16)
                for other in range(CORES):
                    query_out[other][source, head * HEAD_WIDTH : (head + 1) * HEAD_WIDTH] = turned[
                        other * own_positions : (other + 1) * own_positions
                    ]

        @pl.when(length <= first)
        def _():
            for other in range(CORES):
                query_out[other][source, :] = jnp.zeros((own_positions, GROUP_WIDTH), BF16)

        return carry

    lax.fori_loop(0, RESP_DEV, reply_tile, 0)

    head_rows = CORES * prompt_own
    used = GROUP * head_rows
    all_rows = -(-used // 128) * 128
    if all_rows > used:
        query[used:all_rows] = jnp.zeros((all_rows - used, HEAD_WIDTH), BF16)
        gradient[used:all_rows] = jnp.zeros((all_rows - used, HEAD_WIDTH), BF16)
    delta[0:1, :all_rows] = jnp.zeros((1, all_rows), F32)
    for head in range(GROUP):
        for other in range(CORES):
            at = head * head_rows + other * prompt_own
            to = slice(at, at + prompt_own)
            left = slice(head * HEAD_WIDTH, (head + 1) * HEAD_WIDTH)
            right = slice(GROUP_WIDTH + head * HEAD_WIDTH, GROUP_WIDTH + (head + 1) * HEAD_WIDTH)
            query[to] = rows_in[other][reply_own:, left]
            gradient[to] = rows_in[other][reply_own:, right]
            delta[0:1, to] = deltas[other, head : head + 1, reply_own:]
    begin(all_rows)
    turn(all_rows)
    lane = iota((1, all_rows), 1)
    within = lane
    for head in range(1, GROUP):
        within = within - jnp.where(lane >= head * head_rows, head_rows, 0)
    offset = jnp.where(within < prompt_own, within, within - prompt_own)
    row_core = jnp.where(within < prompt_own, core, 1 - core)
    real = (lane < used) & (offset < prompt_rows)
    row_at = jnp.where(
        real, (chip * CORES + row_core) * prompt_keys + group * prompt_rows + offset, -1
    )
    per_block = max(block // chip_prompt, 1)
    block_parts = max(chip_prompt // block, 1)
    pair = chip // per_block
    seen = (pair + 1) * block_parts

    def prompt_region(index):
        return (index // block_parts ^ pair) * block_parts + index % block_parts

    def prompt_stats(index, carry):
        key = iota((block, 1), 0) + index % block_parts * block
        key_chip = ((index // block_parts ^ pair) * per_block + key // chip_prompt) ^ chip
        key_at = key_chip * chip_prompt + absolute(key % chip_prompt, prompt_keys)
        score_block(prompt_region(index), index, all_rows, 1, key_at > row_at)
        return carry

    lax.fori_loop(0, seen, prompt_stats, 0)
    log_mass = log_masses(all_rows, 1, real)


    def first_grads(stage, next_stage):
        weigh(prompt_region(0), 0, all_rows, 1, log_mass, next_stage)

    grad_blocks(seen, prompt_region, all_rows, 1, log_mass, first_grads)
    turned = (query_grad[:, :all_rows].T * SCALE).astype(BF16)
    for head in range(GROUP):
        for other in range(CORES):
            at = head * head_rows + other * prompt_own
            query_out[other][reply_own:, head * HEAD_WIDTH : (head + 1) * HEAD_WIDTH] = turned[
                at : at + prompt_own
            ]

    def put(out, at, count):
        out[:, :HEAD_WIDTH] = (total[at : at + count, :HEAD_WIDTH] * SCALE).astype(BF16)
        out[:, HEAD_WIDTH:] = total[at : at + count, HEAD_WIDTH:].astype(BF16)

    for index in range(chips * CORES):
        away, other = index // CORES, index % CORES
        put(prompt_out[away].at[other, :prompt_keys], away * chip_prompt + other * prompt_keys, prompt_keys)
        for slot in range(RESP_DEV):
            at = chips * chip_prompt + (slot * chips + away) * positions + other * own_positions
            to = slot * own_positions + (0 if joint_keys else prompt_keys)
            put(keys_out[away].at[other, to : to + own_positions], at, own_positions)


def add(first, *rest):
    value = first.astype(F32)
    for part in rest:
        value = value + part.astype(F32)
    return value


def collect_first(chips, place, *refs):
    parts, prompt_parts, refs = refs[:chips], refs[chips : 2 * chips], refs[2 * chips :]
    mine, theirs, outs, summed = refs[0], refs[1], refs[2:-1], refs[-1]
    groups, rows = len(outs), outs[0].shape[1]
    prompt_keys = groups * rows
    mine[...] = add(*(part[0, prompt_keys:] for part in parts))
    theirs[...] = add(*(part[1, prompt_keys:] for part in parts)).astype(BF16)
    for other in range(CORES):
        summed[other] = add(*(part[other, :prompt_keys] for part in parts))
        summed[CORES + other] = add(*(part[other] for part in prompt_parts))
    for shift in range(groups):
        at = pl.ds(pl.multiple_of(lax.rem(place[2] + shift, groups) * rows, rows), rows)
        for index in range(summed.shape[0]):
            outs[shift][index] = summed[index, at].astype(BF16)


def collect_second(chips, *refs):
    parts, slices, (theirs0, mine, prompt, theirs) = refs[:chips], refs[chips:-4], refs[-4:]
    reply, rows = theirs0.shape[0], prompt.shape[1]
    step = max(rows, 16)
    mine[...] = add(*(part[0] for part in parts))
    theirs[:reply] = theirs0[...]
    theirs[reply : 2 * reply] = add(*(part[1] for part in parts)).astype(BF16)
    for local in range(LOCAL_HEADS):
        prompt[local] = add(*(part[CORES * local] for part in slices))
        at = 2 * reply + local * step
        theirs[at : at + rows] = add(*(part[CORES * local + 1] for part in slices)).astype(BF16)


def finish_queries(place, *refs):
    queries, prompt_dq, reply_dq = refs[:-2], refs[-2], refs[-1]
    reply = reply_dq.shape[0]
    order = unsorting(reply)
    for index, query in enumerate(queries):
        span = lanes(head_of(place[1], index % CORES, index // CORES), GROUP_WIDTH)
        reply_dq[:, span] = dot(order, query[:reply]).astype(BF16)
        prompt_dq[:, span] = query[reply:]


def finish_keys(place, reply0, reply1, prompts, theirs, prompt_dk, prompt_dv, reply_dk, reply_dv):
    reply, rows = reply_dk.shape[0], prompt_dk.shape[0]
    step = max(rows, 16)
    order = unsorting(reply)
    for local in range(LOCAL_HEADS):
        for other in range(CORES):
            span = lanes(head_of(place[1], other, local), HEAD_WIDTH)
            if other:
                value = theirs[local * reply : (local + 1) * reply]
                prompt = theirs[2 * reply + local * step : 2 * reply + local * step + rows]
            else:
                value = (reply1 if local else reply0)[...].astype(BF16)
                prompt = prompts[local].astype(BF16)
            value = dot(order, value).astype(BF16)
            reply_dk[:, span] = value[:, :HEAD_WIDTH]
            reply_dv[:, span] = value[:, HEAD_WIDTH:]
            prompt_dk[:, span] = prompt[:, :HEAD_WIDTH]
            prompt_dv[:, span] = prompt[:, HEAD_WIDTH:]


def on_device(
    prompt_query,
    prompt_k,
    prompt_value,
    prompt_output,
    prompt_output_gradient,
    reply_query,
    reply_key,
    reply_value,
    reply_output,
    reply_output_gradient,
    reply_len,
    reply_slot,
):
    devices = lax.axis_size("pre")
    groups = lax.axis_size("rsp")
    chips = devices // CORES
    prompt_rows = prompt_query.shape[0]
    prompt_own = -(-prompt_rows // 16) * 16
    prompt_keys = prompt_k.shape[0]
    reply_own = reply_query.shape[1]
    own_positions = reply_own // RESP_DEV
    positions = CORES * own_positions
    chip_prompt = CORES * prompt_keys
    block = 2 * positions
    assert (chip_prompt % block == 0 or block % chip_prompt == 0) and chips > 1 and chips & (chips - 1) == 0
    pre_index = lax.axis_index("pre")
    place = jnp.stack([lax.div(pre_index, CORES), lax.rem(pre_index, CORES), lax.axis_index("rsp")])

    def shape(*dims, dtype=BF16):
        return jax.ShapeDtypeStruct(dims, dtype)

    def move(array, away, cross=0):
        pairs = [(p, (p // CORES ^ away) * CORES + (p % CORES ^ cross)) for p in range(devices)]
        return lax.ppermute(array, "pre", pairs)

    def swap(array):
        return move(array, 0, 1)

    def call(kernel, name, mib, inputs, outs, scalars=1, spec=VMEM, **more):
        return pl.pallas_call(
            kernel,
            out_shape=outs,
            in_specs=[SMEM] * scalars + [spec] * (len(inputs) - scalars),
            out_specs=[VMEM] * len(outs),
            compiler_params=params(mib),
            name=name,
            **more,
        )(*inputs)

    relayed = chips == 4
    key_shape = (prompt_keys + reply_own, 2 * HEAD_WIDTH)
    mine0, theirs0, mine1, theirs, token = call(
        prepare_keys,
        "prepare_keys",
        LARGE_MIB,
        (prompt_k, prompt_value, reply_key[0], reply_value[0]),
        [shape(*key_shape)] * 3 + [shape(LOCAL_HEADS, *key_shape), shape(8, 128, dtype=F32)],
        scalars=0,
        spec=HBM,
        scratch_shapes=[
            pltpu.VMEM((rows, KEY_VALUE_HEADS * HEAD_WIDTH), BF16)
            for rows in (prompt_keys, prompt_keys, reply_own, reply_own)
        ]
        + [pltpu.SemaphoreType.DMA((4,))],
    )
    blocks0 = {(0, 0): mine0, (0, 1): swap(theirs)}
    for away in range(1, 3 if relayed else chips):
        blocks0[away, 0] = move(mine0, away)
        blocks0[away, 1] = move(theirs0, away, 1)
    if prompt_own > prompt_rows:
        room = ((0, prompt_own - prompt_rows), (0, 0))
        prompt_query, prompt_output, prompt_output_gradient = (
            jnp.pad(array, room)
            for array in (prompt_query, prompt_output, prompt_output_gradient)
        )
    own_rows = reply_own + prompt_own
    row_width = 2 * GROUP_WIDTH + HEAD_WIDTH

    rows = call(
        prepare_rows,
        "prepare_rows",
        LARGE_MIB,
        (
            place,
            token,
            prompt_query,
            prompt_output,
            prompt_output_gradient,
            reply_query[0],
            reply_output[0],
            reply_output_gradient[0],
        ),
        [shape(LOCAL_HEADS, own_rows, row_width)] + [shape(own_rows, row_width)] * LOCAL_HEADS,
        spec=HBM,
        scratch_shapes=[
            pltpu.VMEM((KEY_VALUE_HEADS, rows, GROUP_WIDTH), BF16)
            for rows in [prompt_own] * 3 + [reply_own] * 3
        ]
        + [pltpu.SemaphoreType.DMA((KEY_VALUE_HEADS * 6,))],
        cost_estimate=pl.CostEstimate(
            flops=6 * reply_own * reply_own * QUERY_HEADS * HEAD_WIDTH,
            bytes_accessed=20 * reply_own * QUERY_HEADS * HEAD_WIDTH,
            transcendentals=0,
        ),
    )

    blocks0, rows, mine1 = lax.optimization_barrier((blocks0, rows, mine1))
    if relayed:
        blocks0[3, 0] = move(blocks0[1, 0], 2)
        blocks0[3, 1] = move(blocks0[2, 1], 1)
    chip1 = jnp.stack([mine1, blocks0[0, 1][1]])
    blocks1 = [chip1] + [move(chip1, away) for away in range(1, chips)]

    blocks = (chips * chip_prompt + RESP_DEV * chips * positions) // block
    slots = (chips * chip_prompt + chips * positions) // block
    all_rows = max(GROUP * positions, -(-GROUP * CORES * prompt_own // 128) * 128)
    sizes = (chips, reply_own, prompt_own, prompt_rows, prompt_keys)
    score_count = GROUP * (positions * RESP_DEV * slots * block)

    cut_rows = prompt_keys // groups
    rows_theirs, *rows_mine = rows
    rows_theirs = swap(rows_theirs)

    def run_attend(local, key_blocks):
        joint_keys = local == 1
        sums = [shape(CORES, *key_shape)] * chips
        if joint_keys:
            sums = [shape(CORES, n, 2 * HEAD_WIDTH) for n in [reply_own] * chips + [prompt_keys] * chips]
        query_mine, query_theirs, *sums = call(
            functools.partial(attend, sizes, joint_keys),
            "attend",
            VMEM_MIB,
            (
                place,
                reply_len,
                reply_slot,
                rows_mine[local],
                rows_theirs,
                *key_blocks,
            ),
            [shape(own_rows, GROUP_WIDTH)] * CORES + sums,
            scalars=3,
            scratch_shapes=[
                pltpu.VMEM((blocks * block, 2 * HEAD_WIDTH), BF16),
                pltpu.VMEM((blocks, HEAD_WIDTH, block), BF16),
                pltpu.VMEM((blocks * block, 2 * HEAD_WIDTH), F32),
                pltpu.VMEM((all_rows, HEAD_WIDTH), BF16),
                pltpu.VMEM((all_rows, HEAD_WIDTH), BF16),
                pltpu.VMEM((HEAD_WIDTH, all_rows), BF16),
                pltpu.VMEM((HEAD_WIDTH, all_rows), BF16),
                pltpu.VMEM((CORES, 8, own_rows), F32),
                pltpu.VMEM((8, all_rows), F32),
                pltpu.VMEM((slots, block, all_rows), F32),
                pltpu.VMEM((slots, block // PART, 8, all_rows), F32),
                pltpu.VMEM((8, all_rows), F32),
                pltpu.VMEM((8, all_rows), F32),
                pltpu.VMEM((HEAD_WIDTH, all_rows), F32),
            ]
            + [pltpu.VMEM((block, all_rows), BF16)] * 4,
            cost_estimate=pl.CostEstimate(
                flops=score_count * 10 * HEAD_WIDTH,
                bytes_accessed=8 * 1024 * 1024,
                transcendentals=2 * score_count,
            ),
        )
        return query_mine, query_theirs, sums

    query_mine0, query_theirs0, sums0 = run_attend(
        0, [blocks0[away, other] for away in range(chips) for other in range(CORES)]
    )
    arrived0 = [sums0[0]] + [move(sums0[away], away) for away in range(1, chips)]
    query_theirs0 = swap(query_theirs0)
    query_mine1, query_theirs1, sums1 = run_attend(1, blocks1)
    arrived0, query_theirs0, query_theirs1, sums1 = lax.optimization_barrier(
        (arrived0, query_theirs0, query_theirs1, sums1)
    )
    prompt1 = [sums1[chips]] + [move(sums1[chips + away], away) for away in range(1, chips)]
    arrived1 = [sums1[0], move(sums1[1], 1)]
    key_width = KEY_VALUE_HEADS * HEAD_WIDTH
    query_width = QUERY_HEADS * HEAD_WIDTH
    query_theirs1 = swap(query_theirs1)
    prompt1, query_theirs1, sums1[2:chips] = lax.optimization_barrier(
        (prompt1, query_theirs1, sums1[2:chips])
    )
    arrived1 += [move(sums1[away], away) for away in range(2, chips)]
    reply0, theirs0, *cuts = call(
        functools.partial(collect_first, chips),
        "collect_first",
        SMALL_MIB,
        (place, *arrived0, *prompt1),
        [shape(reply_own, 2 * HEAD_WIDTH, dtype=F32), shape(reply_own, 2 * HEAD_WIDTH)]
        + [shape(KEY_VALUE_HEADS, cut_rows, 2 * HEAD_WIDTH)] * groups,
        scratch_shapes=[pltpu.VMEM((KEY_VALUE_HEADS, prompt_keys, 2 * HEAD_WIDTH), F32)],
    )
    slices = [cuts[0]] + [
        lax.ppermute(cuts[shift], "rsp", [(g, (g + shift) % groups) for g in range(groups)])
        for shift in range(1, groups)
    ]
    prompt_dq, reply_dq = call(
        finish_queries,
        "finish_queries",
        SMALL_MIB,
        (place, query_mine0, query_theirs0, query_mine1, query_theirs1),
        [shape(prompt_own, query_width), shape(reply_own, query_width)],
        cost_estimate=pl.CostEstimate(
            flops=2 * reply_own * reply_own * query_width,
            bytes_accessed=8 * reply_own * query_width,
            transcendentals=0,
        ),
    )
    slices, prompt_dq, reply_dq = lax.optimization_barrier((slices, prompt_dq, reply_dq))
    reply1, prompts, theirs = call(
        functools.partial(collect_second, chips),
        "collect_second",
        SMALL_MIB,
        (*arrived1, *slices, theirs0),
        [
            shape(reply_own, 2 * HEAD_WIDTH, dtype=F32),
            shape(LOCAL_HEADS, cut_rows, 2 * HEAD_WIDTH, dtype=F32),
            shape(2 * reply_own + 2 * max(cut_rows, 16), 2 * HEAD_WIDTH),
        ],
        scalars=0,
    )
    prompt_dk, prompt_dv, reply_dk, reply_dv = call(
        finish_keys,
        "finish_keys",
        SMALL_MIB,
        (place, reply0, reply1, prompts, swap(theirs)),
        [shape(cut_rows, key_width)] * 2 + [shape(reply_own, key_width)] * 2,
    )
    return (
        prompt_dq[:prompt_rows],
        prompt_dk,
        prompt_dv,
        reply_dq[None],
        reply_dk[None],
        reply_dv[None],
    )


def solution(mesh):
    return jax.shard_map(
        on_device,
        mesh=mesh,
        in_specs=(
            P(("pre", "rsp"), None),
            P("pre", None),
            P("pre", None),
            P(("pre", "rsp"), None),
            P(("pre", "rsp"), None),
            P("rsp", "pre", None),
            P("rsp", "pre", None),
            P("rsp", "pre", None),
            P("rsp", "pre", None),
            P("rsp", "pre", None),
            P(),
            P(),
        ),
        out_specs=(
            P(("pre", "rsp"), None),
            P(("pre", "rsp"), None),
            P(("pre", "rsp"), None),
            P("rsp", "pre", None),
            P("rsp", "pre", None),
            P("rsp", "pre", None),
        ),
        check_vma=False,
    )
```

```python
import functools
import math

import jax
import jax.numpy as jnp
from jax import lax
from jax.experimental import pallas as pl
from jax.experimental.pallas import tpu as pltpu
from jax.sharding import PartitionSpec as P

QUERY_HEADS = 20
KEY_VALUE_HEADS = 4
GROUP = QUERY_HEADS // KEY_VALUE_HEADS
HEAD_WIDTH = 128
RESP_DEV = 2
CORES = 2
LOCAL_HEADS = KEY_VALUE_HEADS // CORES
GROUP_WIDTH = GROUP * HEAD_WIDTH

SCALE = HEAD_WIDTH ** (-0.5)
SCALE_LOG2 = SCALE * math.log2(math.e)
PART = 128
NEGATIVE_FLOOR = -1e30
DEAD = 1e30
F32 = jnp.float32
BF16 = jnp.bfloat16
VMEM = pl.BlockSpec(memory_space=pltpu.VMEM)
SMEM = pl.BlockSpec(memory_space=pltpu.SMEM)
HBM = pl.BlockSpec(memory_space=pltpu.HBM)


VMEM_MIB = 40
SMALL_MIB = 24
LARGE_MIB = 58


def params(mib):
    return pltpu.CompilerParams(vmem_limit_bytes=mib * 1024 * 1024)


def dot(a, b, over=(1, 0)):
    return lax.dot_general(
        a, b, (((over[0],), (over[1],)), ((), ())), preferred_element_type=F32
    )


def iota(shape, axis):
    return lax.broadcasted_iota(jnp.int32, shape, axis)


def sorting(rows):
    half = rows // RESP_DEV
    out = iota((rows, rows), 0)
    source = jnp.where(out < half, RESP_DEV * out, RESP_DEV * (out - half) + 1)
    return (iota((rows, rows), 1) == source).astype(BF16)


def unsorting(rows):
    half = rows // RESP_DEV
    out = iota((rows, rows), 1)
    source = jnp.where(out < half, RESP_DEV * out, RESP_DEV * (out - half) + 1)
    return (iota((rows, rows), 0) == source).astype(BF16)


def lanes(index, width):
    return pl.ds(pl.multiple_of(index * width, width), width)


def head_of(core, cross, local):
    owner = (1 - core) if cross else core
    return owner * LOCAL_HEADS + local


def fetch(pairs, sems):
    copies = [pltpu.make_async_copy(src, dst, sems.at[i]) for i, (src, dst) in enumerate(pairs)]
    for copy in copies:
        copy.start()
    return copies


def prepare_keys(pk, pv, rk, rv, mine0, theirs0, mine1, theirs, token, *scratch):
    core = lax.rem(lax.axis_index("pre"), CORES)
    bufs, sems = scratch[:-1], scratch[-1]
    copies = fetch(zip((pk, pv, rk, rv), bufs), sems)
    prompt = pk.shape[0]
    order = sorting(rk.shape[0])
    for copy in copies:
        copy.wait()
    pk, pv, rk, rv = bufs
    for local, outs in enumerate(((mine0, theirs.at[0]), (mine1, theirs.at[1]))):
        for cross, out in enumerate(outs):
            span = lanes(head_of(core, cross, local), HEAD_WIDTH)
            for part, (p, r) in enumerate(((pk, rk), (pv, rv))):
                to = slice(part * HEAD_WIDTH, (part + 1) * HEAD_WIDTH)
                out[:prompt, to] = p[:, span]
                out[prompt:, to] = dot(order, r[:, span]).astype(BF16)
    theirs0[...] = theirs[0]
    token[...] = jnp.zeros_like(token)


def prepare_rows(place, token, pq, po, pg, rq, ro, rg, *refs):
    (theirs, *mine), bufs, sems = refs[: 1 + LOCAL_HEADS], refs[1 + LOCAL_HEADS : -1], refs[-1]
    outs = [out for local in range(LOCAL_HEADS) for out in (theirs.at[local], mine[local])]
    core = place[1]
    reply = rq.shape[0]
    sources = (pq, po, pg, rq, ro, rg)
    pairs = []
    for step in range(KEY_VALUE_HEADS):
        span = lanes(head_of(core, 1 - step % CORES, step // CORES), GROUP_WIDTH)
        pairs += [(source.at[:, span], buf.at[step]) for source, buf in zip(sources, bufs)]
    copies = fetch(pairs, sems)
    order = sorting(reply)
    column = iota((GROUP_WIDTH, HEAD_WIDTH), 1)
    pick = (column // 3 == iota((GROUP_WIDTH, HEAD_WIDTH), 0) // HEAD_WIDTH).astype(BF16)

    def delta(gradient, output):
        product = gradient.astype(F32) * output.astype(F32)
        high = product.astype(BF16)
        low = (product - high.astype(F32)).astype(BF16)
        value = dot(high, pick) + dot(low, pick)
        first = value.astype(BF16).astype(F32)
        second = (value - first).astype(BF16).astype(F32)
        part = iota(value.shape, 1) % 3
        return jnp.where(part == 0, first, jnp.where(part == 1, second, value - first - second)).astype(BF16)

    for step, out in enumerate(outs):
        for copy in copies[step * len(sources) : (step + 1) * len(sources)]:
            copy.wait()
        pq, po, pg, rq, ro, rg = (buf[step] for buf in bufs)
        out[reply:, :GROUP_WIDTH] = pq
        out[reply:, GROUP_WIDTH : 2 * GROUP_WIDTH] = pg
        out[reply:, 2 * GROUP_WIDTH :] = delta(pg, po)
        out[:reply, :GROUP_WIDTH] = dot(order, rq).astype(BF16)
        gradient = dot(order, rg).astype(BF16)
        out[:reply, GROUP_WIDTH : 2 * GROUP_WIDTH] = gradient
        out[:reply, 2 * GROUP_WIDTH :] = delta(gradient, dot(order, ro).astype(BF16))


def attend(sizes, joint_keys, place, reply_len, reply_slot, *refs):
    chips, reply_own, prompt_own, prompt_rows, prompt_keys = sizes
    own_positions = reply_own // RESP_DEV
    positions = CORES * own_positions
    chip_prompt = CORES * prompt_keys
    block = 2 * positions
    prompt_blocks = chips * chip_prompt // block
    rows_in, refs = (refs[0], refs[1].at[int(joint_keys)]), refs[2:]
    count = chips if joint_keys else chips * CORES
    keys_in, refs = refs[:count], refs[count:]
    query_out, refs = refs[:2], refs[2:]
    keys_out, refs = refs[:chips], refs[chips:]
    prompt_out, refs = (refs[:chips], refs[chips:]) if joint_keys else (keys_out, refs)
    keys, keys_t, total, query, gradient, query_t, gradient_t, deltas, delta, scores, peaks, top, mass, *refs = refs
    query_grad, stages = refs[0], (refs[1:3], refs[3:5])
    chip, core, group = place[0], place[1], place[2]

    pick = (iota((8, HEAD_WIDTH), 1) // 3 == iota((8, HEAD_WIDTH), 0)).astype(BF16)
    for other in range(CORES):
        deltas[other] = dot(pick, rows_in[other][:, 2 * GROUP_WIDTH :], (1, 1))

    for index in range(chips * CORES):
        away, other = index // CORES, index % CORES
        source = keys_in[away].at[other] if joint_keys else keys_in[index]
        source = source if len(source.shape) == 2 else source.at[0]
        at = away * chip_prompt + other * prompt_keys
        keys[at : at + prompt_keys] = source[:prompt_keys]
        for slot in range(RESP_DEV):
            at = chips * chip_prompt + (slot * chips + away) * positions + other * own_positions
            begin = prompt_keys + slot * own_positions
            keys[at : at + own_positions] = source[begin : begin + own_positions]
    total[...] = jnp.zeros_like(total)

    unit = (iota((HEAD_WIDTH, HEAD_WIDTH), 0) == iota((HEAD_WIDTH, HEAD_WIDTH), 1)).astype(BF16)

    def transpose_block(index, carry):
        rows = pl.ds(pl.multiple_of(index * block, block), block)
        keys_t[index] = dot(unit, keys[rows, :HEAD_WIDTH], (1, 1)).astype(BF16)
        return carry

    lax.fori_loop(0, keys_t.shape[0], transpose_block, 0)

    def score_block(region, place_in, width, chunks, hidden, count=block):
        rows = pl.ds(pl.multiple_of(region * block, block), count)
        key_rows = keys[rows, :HEAD_WIDTH]
        for chunk in range(chunks):
            span = slice(chunk * width, (chunk + 1) * width)
            value = dot(key_rows, query_t[:, span]) * SCALE_LOG2
            if hidden is not None:
                value = jnp.where(hidden, NEGATIVE_FLOOR, value)
            split = value.reshape(count // 8, 8, width)
            peak, summed = top[:, span], mass[:, span]
            for part in range(count // PART):
                piece = split[part * PART // 8 : (part + 1) * PART // 8]
                now = jnp.maximum(peak, jnp.max(piece, axis=0))
                shifted = jnp.exp2(piece - now[None])
                scores[place_in, part * PART : (part + 1) * PART, span] = shifted.reshape(PART, width)
                peaks[place_in, part, :, span] = now
                summed = summed * jnp.exp2(peak - now) + jnp.sum(shifted, axis=0)
                peak = now
            top[:, span], mass[:, span] = peak, summed

    def weigh(region, place_in, width, chunks, log_mass, stage, count=block, earlier=None):
        rows = pl.ds(pl.multiple_of(region * block, block), count)
        value_rows = keys[rows, HEAD_WIDTH:]
        for chunk in range(chunks):
            span = slice(chunk * width, (chunk + 1) * width)
            dp = dot(value_rows, gradient_t[:, span])
            for part in range(count // PART):
                at = slice(part * PART, (part + 1) * PART)
                factor = jnp.exp2(peaks[place_in, part, :, span] - log_mass[chunk])
                p = scores[place_in, at, span].reshape(PART // 8, 8, width) * factor[None]
                p = p.reshape(PART, width)
                stage[0][at, span] = p.astype(BF16)
                stage[1][at, span] = (p * (dp[at] - delta[0:1, span])).astype(BF16)
            if earlier is not None:
                multiply(*earlier, width, chunks, chunk)
        if earlier is not None:
            for chunk in range(chunks, 3):
                multiply(*earlier, width, chunks, chunk)

    def multiply(region, stage, count, width, chunks, part):
        rows = pl.ds(pl.multiple_of(region * block, block), count)
        used = width * chunks
        if part == 0:
            total[rows, HEAD_WIDTH:] += dot(stage[0][:count, :used], gradient[:used])
        elif part == 1:
            total[rows, :HEAD_WIDTH] += dot(stage[1][:count, :used], query[:used])
        elif part == 2:
            query_grad[:, :used] += dot(keys_t[region, :, :count], stage[1][:count, :used])

    def grad_blocks(blocks, region_of, width, chunks, log_mass, begin_with):
        first, second = stages

        def later(index, stage, earlier_stage):
            earlier = region_of(index - 1), earlier_stage, block
            weigh(region_of(index), index, width, chunks, log_mass, stage, earlier=earlier)

        def last(stage):
            for part in range(3):
                multiply(region_of(blocks - 1), stage, block, width, chunks, part)

        begin_with(first, second)

        def two(index, carry):
            later(2 * index + 1, first, second)

            @pl.when(2 * index + 2 < blocks)
            def _():
                later(2 * index + 2, second, first)

            return carry

        lax.fori_loop(0, blocks // 2, two, 0)

        @pl.when(blocks % 2 == 0)
        def _():
            last(first)

        @pl.when(blocks % 2 == 1)
        def _():
            last(second)

    def turn(all_rows):
        query_t[:, :all_rows] = dot(unit, query[:all_rows], (1, 1)).astype(BF16)
        gradient_t[:, :all_rows] = dot(unit, gradient[:all_rows], (1, 1)).astype(BF16)

    def begin(all_rows):
        top[:, :all_rows] = jnp.full((8, all_rows), NEGATIVE_FLOOR, F32)
        mass[:, :all_rows] = jnp.zeros((8, all_rows), F32)
        query_grad[:, :all_rows] = jnp.zeros((HEAD_WIDTH, all_rows), F32)

    def log_masses(width, chunks, live):
        found = []
        for chunk in range(chunks):
            span = slice(chunk * width, (chunk + 1) * width)
            peak = jnp.max(top[:, span], axis=0, keepdims=True)
            summed = jnp.sum(mass[:, span] * jnp.exp2(top[:, span] - peak), axis=0, keepdims=True)
            found.append(jnp.where(live, peak + jnp.log2(summed), DEAD))
        return found

    def absolute(index, half):
        return index + jnp.where(index < half, core * half, -core * half)

    def reply_tile(slot, carry):
        length = jnp.int32(0)
        for response in range(reply_len.shape[0]):
            mine = reply_slot[response] == group * RESP_DEV + slot
            length = length + jnp.where(mine, reply_len[response], 0)
        first = chip * positions
        source = pl.ds(pl.multiple_of(slot * own_positions, own_positions), own_positions)

        @pl.when(length > first)
        def _():
            for head in range(GROUP):
                for other in range(CORES):
                    at = head * positions + other * own_positions
                    to = slice(at, at + own_positions)
                    left = slice(head * HEAD_WIDTH, (head + 1) * HEAD_WIDTH)
                    right = slice(GROUP_WIDTH + head * HEAD_WIDTH, GROUP_WIDTH + (head + 1) * HEAD_WIDTH)
                    query[to] = rows_in[other][source, left]
                    gradient[to] = rows_in[other][source, right]
                    for which in range(RESP_DEV):
                        @pl.when(slot == which)
                        def _():
                            delta[0:1, to] = deltas[
                                other, head : head + 1, which * own_positions : (which + 1) * own_positions
                            ]
            begin(GROUP * positions)
            turn(GROUP * positions)
            base = prompt_blocks + slot * (chips // 2)
            past = prompt_blocks + chip // 2

            def region_of(index):
                reply = base + ((index - prompt_blocks) ^ (chip // 2))
                return jnp.where(index < prompt_blocks, index, reply)

            def stats(index, carry):
                score_block(region_of(index), index, positions, GROUP, None)
                return carry

            lax.fori_loop(0, past, stats, 0)
            row_at = absolute(iota((1, positions), 1), own_positions)
            odd = chip % 2 == 1

            def own_stats(count):
                key = iota((count, 1), 0)
                key_at = jnp.where(key < positions, absolute(key, own_positions), -1)
                score_block(base, past, positions, GROUP, key_at > row_at, count)

            @pl.when(odd)
            def _():
                own_stats(block)

            @pl.when(jnp.logical_not(odd))
            def _():
                own_stats(positions)

            live = first + row_at < length
            log_mass = log_masses(positions, GROUP, live)


            def own_grads(stage, next_stage):
                def run(count):
                    weigh(base, past, positions, GROUP, log_mass, stage, count)
                    earlier = base, stage, count
                    weigh(region_of(0), 0, positions, GROUP, log_mass, next_stage, earlier=earlier)

                @pl.when(odd)
                def _():
                    run(block)

                @pl.when(jnp.logical_not(odd))
                def _():
                    run(positions)

            grad_blocks(past, region_of, positions, GROUP, log_mass, own_grads)
            for head in range(GROUP):
                turned = (query_grad[:, head * positions : (head + 1) * positions].T * SCALE).astype(BF16)
                for other in range(CORES):
                    query_out[other][source, head * HEAD_WIDTH : (head + 1) * HEAD_WIDTH] = turned[
                        other * own_positions : (other + 1) * own_positions
                    ]

        @pl.when(length <= first)
        def _():
            for other in range(CORES):
                query_out[other][source, :] = jnp.zeros((own_positions, GROUP_WIDTH), BF16)

        return carry

    lax.fori_loop(0, RESP_DEV, reply_tile, 0)

    head_rows = CORES * prompt_own
    used = GROUP * head_rows
    all_rows = -(-used // 128) * 128
    if all_rows > used:
        query[used:all_rows] = jnp.zeros((all_rows - used, HEAD_WIDTH), BF16)
        gradient[used:all_rows] = jnp.zeros((all_rows - used, HEAD_WIDTH), BF16)
    delta[0:1, :all_rows] = jnp.zeros((1, all_rows), F32)
    for head in range(GROUP):
        for other in range(CORES):
            at = head * head_rows + other * prompt_own
            to = slice(at, at + prompt_own)
            left = slice(head * HEAD_WIDTH, (head + 1) * HEAD_WIDTH)
            right = slice(GROUP_WIDTH + head * HEAD_WIDTH, GROUP_WIDTH + (head + 1) * HEAD_WIDTH)
            query[to] = rows_in[other][reply_own:, left]
            gradient[to] = rows_in[other][reply_own:, right]
            delta[0:1, to] = deltas[other, head : head + 1, reply_own:]
    begin(all_rows)
    turn(all_rows)
    lane = iota((1, all_rows), 1)
    within = lane
    for head in range(1, GROUP):
        within = within - jnp.where(lane >= head * head_rows, head_rows, 0)
    offset = jnp.where(within < prompt_own, within, within - prompt_own)
    row_core = jnp.where(within < prompt_own, core, 1 - core)
    real = (lane < used) & (offset < prompt_rows)
    row_at = jnp.where(
        real, (chip * CORES + row_core) * prompt_keys + group * prompt_rows + offset, -1
    )
    per_block = max(block // chip_prompt, 1)
    block_parts = max(chip_prompt // block, 1)
    pair = chip // per_block
    seen = (pair + 1) * block_parts

    def prompt_region(index):
        return (index // block_parts ^ pair) * block_parts + index % block_parts

    def prompt_stats(index, carry):
        key = iota((block, 1), 0) + index % block_parts * block
        key_chip = ((index // block_parts ^ pair) * per_block + key // chip_prompt) ^ chip
        key_at = key_chip * chip_prompt + absolute(key % chip_prompt, prompt_keys)
        score_block(prompt_region(index), index, all_rows, 1, key_at > row_at)
        return carry

    lax.fori_loop(0, seen, prompt_stats, 0)
    log_mass = log_masses(all_rows, 1, real)


    def prompt_grads(index, carry):
        weigh(prompt_region(index), index, all_rows, 1, log_mass, stages[0])
        for part in range(3):
            multiply(prompt_region(index), stages[0], block, all_rows, 1, part)
        return carry

    lax.fori_loop(0, seen, prompt_grads, 0)
    turned = (query_grad[:, :all_rows].T * SCALE).astype(BF16)
    for head in range(GROUP):
        for other in range(CORES):
            at = head * head_rows + other * prompt_own
            query_out[other][reply_own:, head * HEAD_WIDTH : (head + 1) * HEAD_WIDTH] = turned[
                at : at + prompt_own
            ]

    def put(out, at, count):
        out[:, :HEAD_WIDTH] = (total[at : at + count, :HEAD_WIDTH] * SCALE).astype(BF16)
        out[:, HEAD_WIDTH:] = total[at : at + count, HEAD_WIDTH:].astype(BF16)

    for index in range(chips * CORES):
        away, other = index // CORES, index % CORES
        put(prompt_out[away].at[other, :prompt_keys], away * chip_prompt + other * prompt_keys, prompt_keys)
        for slot in range(RESP_DEV):
            at = chips * chip_prompt + (slot * chips + away) * positions + other * own_positions
            to = slot * own_positions + (0 if joint_keys else prompt_keys)
            put(keys_out[away].at[other, to : to + own_positions], at, own_positions)


def add(first, *rest):
    value = first.astype(F32)
    for part in rest:
        value = value + part.astype(F32)
    return value


def collect_first(chips, place, *refs):
    parts, prompt_parts, refs = refs[:chips], refs[chips : 2 * chips], refs[2 * chips :]
    mine, theirs, outs, summed = refs[0], refs[1], refs[2:-1], refs[-1]
    groups, rows = len(outs), outs[0].shape[1]
    prompt_keys = groups * rows
    mine[...] = add(*(part[0, prompt_keys:] for part in parts))
    theirs[...] = add(*(part[1, prompt_keys:] for part in parts)).astype(BF16)
    for other in range(CORES):
        summed[other] = add(*(part[other, :prompt_keys] for part in parts))
        summed[CORES + other] = add(*(part[other] for part in prompt_parts))
    for shift in range(groups):
        at = pl.ds(pl.multiple_of(lax.rem(place[2] + shift, groups) * rows, rows), rows)
        for index in range(summed.shape[0]):
            outs[shift][index] = summed[index, at].astype(BF16)


def collect_second(chips, *refs):
    parts, slices, (theirs0, mine, prompt, theirs) = refs[:chips], refs[chips:-4], refs[-4:]
    reply, rows = theirs0.shape[0], prompt.shape[1]
    step = max(rows, 16)
    mine[...] = add(*(part[0] for part in parts))
    theirs[:reply] = theirs0[...]
    theirs[reply : 2 * reply] = add(*(part[1] for part in parts)).astype(BF16)
    for local in range(LOCAL_HEADS):
        prompt[local] = add(*(part[CORES * local] for part in slices))
        at = 2 * reply + local * step
        theirs[at : at + rows] = add(*(part[CORES * local + 1] for part in slices)).astype(BF16)


def finish_queries(place, *refs):
    queries, prompt_dq, reply_dq = refs[:-2], refs[-2], refs[-1]
    reply = reply_dq.shape[0]
    order = unsorting(reply)
    for index, query in enumerate(queries):
        span = lanes(head_of(place[1], index % CORES, index // CORES), GROUP_WIDTH)
        reply_dq[:, span] = dot(order, query[:reply]).astype(BF16)
        prompt_dq[:, span] = query[reply:]


def finish_keys(place, reply0, reply1, prompts, theirs, prompt_dk, prompt_dv, reply_dk, reply_dv):
    reply, rows = reply_dk.shape[0], prompt_dk.shape[0]
    step = max(rows, 16)
    order = unsorting(reply)
    for local in range(LOCAL_HEADS):
        for other in range(CORES):
            span = lanes(head_of(place[1], other, local), HEAD_WIDTH)
            if other:
                value = theirs[local * reply : (local + 1) * reply]
                prompt = theirs[2 * reply + local * step : 2 * reply + local * step + rows]
            else:
                value = (reply1 if local else reply0)[...].astype(BF16)
                prompt = prompts[local].astype(BF16)
            value = dot(order, value).astype(BF16)
            reply_dk[:, span] = value[:, :HEAD_WIDTH]
            reply_dv[:, span] = value[:, HEAD_WIDTH:]
            prompt_dk[:, span] = prompt[:, :HEAD_WIDTH]
            prompt_dv[:, span] = prompt[:, HEAD_WIDTH:]


def on_device(
    prompt_query,
    prompt_k,
    prompt_value,
    prompt_output,
    prompt_output_gradient,
    reply_query,
    reply_key,
    reply_value,
    reply_output,
    reply_output_gradient,
    reply_len,
    reply_slot,
):
    devices = lax.axis_size("pre")
    groups = lax.axis_size("rsp")
    chips = devices // CORES
    prompt_rows = prompt_query.shape[0]
    prompt_own = -(-prompt_rows // 16) * 16
    prompt_keys = prompt_k.shape[0]
    reply_own = reply_query.shape[1]
    own_positions = reply_own // RESP_DEV
    positions = CORES * own_positions
    chip_prompt = CORES * prompt_keys
    block = 2 * positions
    assert (chip_prompt % block == 0 or block % chip_prompt == 0) and chips > 1 and chips & (chips - 1) == 0
    pre_index = lax.axis_index("pre")
    place = jnp.stack([lax.div(pre_index, CORES), lax.rem(pre_index, CORES), lax.axis_index("rsp")])

    def shape(*dims, dtype=BF16):
        return jax.ShapeDtypeStruct(dims, dtype)

    def move(array, away, cross=0):
        pairs = [(p, (p // CORES ^ away) * CORES + (p % CORES ^ cross)) for p in range(devices)]
        return lax.ppermute(array, "pre", pairs)

    def swap(array):
        return move(array, 0, 1)

    def call(kernel, name, mib, inputs, outs, scalars=1, spec=VMEM, **more):
        return pl.pallas_call(
            kernel,
            out_shape=outs,
            in_specs=[SMEM] * scalars + [spec] * (len(inputs) - scalars),
            out_specs=[VMEM] * len(outs),
            compiler_params=params(mib),
            name=name,
            **more,
        )(*inputs)

    relayed = chips == 4
    key_shape = (prompt_keys + reply_own, 2 * HEAD_WIDTH)
    mine0, theirs0, mine1, theirs, token = call(
        prepare_keys,
        "prepare_keys",
        LARGE_MIB,
        (prompt_k, prompt_value, reply_key[0], reply_value[0]),
        [shape(*key_shape)] * 3 + [shape(LOCAL_HEADS, *key_shape), shape(8, 128, dtype=F32)],
        scalars=0,
        spec=HBM,
        scratch_shapes=[
            pltpu.VMEM((rows, KEY_VALUE_HEADS * HEAD_WIDTH), BF16)
            for rows in (prompt_keys, prompt_keys, reply_own, reply_own)
        ]
        + [pltpu.SemaphoreType.DMA((4,))],
    )
    blocks0 = {(0, 0): mine0, (0, 1): swap(theirs)}
    for away in range(1, 3 if relayed else chips):
        blocks0[away, 0] = move(mine0, away)
        blocks0[away, 1] = move(theirs0, away, 1)
    if prompt_own > prompt_rows:
        room = ((0, prompt_own - prompt_rows), (0, 0))
        prompt_query, prompt_output, prompt_output_gradient = (
            jnp.pad(array, room)
            for array in (prompt_query, prompt_output, prompt_output_gradient)
        )
    own_rows = reply_own + prompt_own
    row_width = 2 * GROUP_WIDTH + HEAD_WIDTH

    rows = call(
        prepare_rows,
        "prepare_rows",
        LARGE_MIB,
        (
            place,
            token,
            prompt_query,
            prompt_output,
            prompt_output_gradient,
            reply_query[0],
            reply_output[0],
            reply_output_gradient[0],
        ),
        [shape(LOCAL_HEADS, own_rows, row_width)] + [shape(own_rows, row_width)] * LOCAL_HEADS,
        spec=HBM,
        scratch_shapes=[
            pltpu.VMEM((KEY_VALUE_HEADS, rows, GROUP_WIDTH), BF16)
            for rows in [prompt_own] * 3 + [reply_own] * 3
        ]
        + [pltpu.SemaphoreType.DMA((KEY_VALUE_HEADS * 6,))],
        cost_estimate=pl.CostEstimate(
            flops=6 * reply_own * reply_own * QUERY_HEADS * HEAD_WIDTH,
            bytes_accessed=20 * reply_own * QUERY_HEADS * HEAD_WIDTH,
            transcendentals=0,
        ),
    )

    blocks0, rows, mine1 = lax.optimization_barrier((blocks0, rows, mine1))
    if relayed:
        blocks0[3, 0] = move(blocks0[1, 0], 2)
        blocks0[3, 1] = move(blocks0[2, 1], 1)
    chip1 = jnp.stack([mine1, blocks0[0, 1][1]])
    blocks1 = [chip1] + [move(chip1, away) for away in range(1, chips)]

    blocks = (chips * chip_prompt + RESP_DEV * chips * positions) // block
    slots = (chips * chip_prompt + chips * positions) // block
    all_rows = max(GROUP * positions, -(-GROUP * CORES * prompt_own // 128) * 128)
    sizes = (chips, reply_own, prompt_own, prompt_rows, prompt_keys)
    score_count = GROUP * (positions * RESP_DEV * slots * block)

    cut_rows = prompt_keys // groups
    rows_theirs, *rows_mine = rows
    rows_theirs = swap(rows_theirs)

    def run_attend(local, key_blocks):
        joint_keys = local == 1
        sums = [shape(CORES, *key_shape)] * chips
        if joint_keys:
            sums = [shape(CORES, n, 2 * HEAD_WIDTH) for n in [reply_own] * chips + [prompt_keys] * chips]
        query_mine, query_theirs, *sums = call(
            functools.partial(attend, sizes, joint_keys),
            "attend",
            VMEM_MIB,
            (
                place,
                reply_len,
                reply_slot,
                rows_mine[local],
                rows_theirs,
                *key_blocks,
            ),
            [shape(own_rows, GROUP_WIDTH)] * CORES + sums,
            scalars=3,
            scratch_shapes=[
                pltpu.VMEM((blocks * block, 2 * HEAD_WIDTH), BF16),
                pltpu.VMEM((blocks, HEAD_WIDTH, block), BF16),
                pltpu.VMEM((blocks * block, 2 * HEAD_WIDTH), F32),
                pltpu.VMEM((all_rows, HEAD_WIDTH), BF16),
                pltpu.VMEM((all_rows, HEAD_WIDTH), BF16),
                pltpu.VMEM((HEAD_WIDTH, all_rows), BF16),
                pltpu.VMEM((HEAD_WIDTH, all_rows), BF16),
                pltpu.VMEM((CORES, 8, own_rows), F32),
                pltpu.VMEM((8, all_rows), F32),
                pltpu.VMEM((slots, block, all_rows), F32),
                pltpu.VMEM((slots, block // PART, 8, all_rows), F32),
                pltpu.VMEM((8, all_rows), F32),
                pltpu.VMEM((8, all_rows), F32),
                pltpu.VMEM((HEAD_WIDTH, all_rows), F32),
            ]
            + [pltpu.VMEM((block, all_rows), BF16)] * 4,
            cost_estimate=pl.CostEstimate(
                flops=score_count * 10 * HEAD_WIDTH,
                bytes_accessed=8 * 1024 * 1024,
                transcendentals=2 * score_count,
            ),
        )
        return query_mine, query_theirs, sums

    query_mine0, query_theirs0, sums0 = run_attend(
        0, [blocks0[away, other] for away in range(chips) for other in range(CORES)]
    )
    arrived0 = [sums0[0]] + [move(sums0[away], away) for away in range(1, chips)]
    query_theirs0 = swap(query_theirs0)
    query_mine1, query_theirs1, sums1 = run_attend(1, blocks1)
    arrived0, query_theirs0, query_theirs1, sums1 = lax.optimization_barrier(
        (arrived0, query_theirs0, query_theirs1, sums1)
    )
    prompt1 = [sums1[chips]] + [move(sums1[chips + away], away) for away in range(1, chips)]
    arrived1 = [sums1[0], move(sums1[1], 1)]
    key_width = KEY_VALUE_HEADS * HEAD_WIDTH
    query_width = QUERY_HEADS * HEAD_WIDTH
    query_theirs1 = swap(query_theirs1)
    prompt1, query_theirs1, sums1[2:chips] = lax.optimization_barrier(
        (prompt1, query_theirs1, sums1[2:chips])
    )
    arrived1 += [move(sums1[away], away) for away in range(2, chips)]
    reply0, theirs0, *cuts = call(
        functools.partial(collect_first, chips),
        "collect_first",
        SMALL_MIB,
        (place, *arrived0, *prompt1),
        [shape(reply_own, 2 * HEAD_WIDTH, dtype=F32), shape(reply_own, 2 * HEAD_WIDTH)]
        + [shape(KEY_VALUE_HEADS, cut_rows, 2 * HEAD_WIDTH)] * groups,
        scratch_shapes=[pltpu.VMEM((KEY_VALUE_HEADS, prompt_keys, 2 * HEAD_WIDTH), F32)],
    )
    slices = [cuts[0]] + [
        lax.ppermute(cuts[shift], "rsp", [(g, (g + shift) % groups) for g in range(groups)])
        for shift in range(1, groups)
    ]
    prompt_dq, reply_dq = call(
        finish_queries,
        "finish_queries",
        SMALL_MIB,
        (place, query_mine0, query_theirs0, query_mine1, query_theirs1),
        [shape(prompt_own, query_width), shape(reply_own, query_width)],
        cost_estimate=pl.CostEstimate(
            flops=2 * reply_own * reply_own * query_width,
            bytes_accessed=8 * reply_own * query_width,
            transcendentals=0,
        ),
    )
    slices, prompt_dq, reply_dq = lax.optimization_barrier((slices, prompt_dq, reply_dq))
    reply1, prompts, theirs = call(
        functools.partial(collect_second, chips),
        "collect_second",
        SMALL_MIB,
        (*arrived1, *slices, theirs0),
        [
            shape(reply_own, 2 * HEAD_WIDTH, dtype=F32),
            shape(LOCAL_HEADS, cut_rows, 2 * HEAD_WIDTH, dtype=F32),
            shape(2 * reply_own + 2 * max(cut_rows, 16), 2 * HEAD_WIDTH),
        ],
        scalars=0,
    )
    prompt_dk, prompt_dv, reply_dk, reply_dv = call(
        finish_keys,
        "finish_keys",
        SMALL_MIB,
        (place, reply0, reply1, prompts, swap(theirs)),
        [shape(cut_rows, key_width)] * 2 + [shape(reply_own, key_width)] * 2,
    )
    return (
        prompt_dq[:prompt_rows],
        prompt_dk,
        prompt_dv,
        reply_dq[None],
        reply_dk[None],
        reply_dv[None],
    )


def solution(mesh):
    return jax.shard_map(
        on_device,
        mesh=mesh,
        in_specs=(
            P(("pre", "rsp"), None),
            P("pre", None),
            P("pre", None),
            P(("pre", "rsp"), None),
            P(("pre", "rsp"), None),
            P("rsp", "pre", None),
            P("rsp", "pre", None),
            P("rsp", "pre", None),
            P("rsp", "pre", None),
            P("rsp", "pre", None),
            P(),
            P(),
        ),
        out_specs=(
            P(("pre", "rsp"), None),
            P(("pre", "rsp"), None),
            P(("pre", "rsp"), None),
            P("rsp", "pre", None),
            P("rsp", "pre", None),
            P("rsp", "pre", None),
        ),
        check_vma=False,
    )
```

```python
import functools
import math

import jax
import jax.numpy as jnp
from jax import lax
from jax.experimental import pallas as pl
from jax.experimental.pallas import tpu as pltpu
from jax.sharding import PartitionSpec as P

QUERY_HEADS = 20
KEY_VALUE_HEADS = 4
GROUP = QUERY_HEADS // KEY_VALUE_HEADS
HEAD_WIDTH = 128
RESP_DEV = 2
CORES = 2
LOCAL_HEADS = KEY_VALUE_HEADS // CORES
GROUP_WIDTH = GROUP * HEAD_WIDTH

SCALE = HEAD_WIDTH ** (-0.5)
SCALE_LOG2 = SCALE * math.log2(math.e)
PART = 128
NEGATIVE_FLOOR = -1e30
DEAD = 1e30
F32 = jnp.float32
BF16 = jnp.bfloat16
VMEM = pl.BlockSpec(memory_space=pltpu.VMEM)
SMEM = pl.BlockSpec(memory_space=pltpu.SMEM)
HBM = pl.BlockSpec(memory_space=pltpu.HBM)


VMEM_MIB = 40
SMALL_MIB = 24
LARGE_MIB = 58


def params(mib):
    return pltpu.CompilerParams(vmem_limit_bytes=mib * 1024 * 1024)


def dot(a, b, over=(1, 0)):
    return lax.dot_general(
        a, b, (((over[0],), (over[1],)), ((), ())), preferred_element_type=F32
    )


def iota(shape, axis):
    return lax.broadcasted_iota(jnp.int32, shape, axis)


def sorting(rows):
    half = rows // RESP_DEV
    out = iota((rows, rows), 0)
    source = jnp.where(out < half, RESP_DEV * out, RESP_DEV * (out - half) + 1)
    return (iota((rows, rows), 1) == source).astype(BF16)


def unsorting(rows):
    half = rows // RESP_DEV
    out = iota((rows, rows), 1)
    source = jnp.where(out < half, RESP_DEV * out, RESP_DEV * (out - half) + 1)
    return (iota((rows, rows), 0) == source).astype(BF16)


def lanes(index, width):
    return pl.ds(pl.multiple_of(index * width, width), width)


def head_of(core, cross, local):
    owner = (1 - core) if cross else core
    return owner * LOCAL_HEADS + local


def fetch(pairs, sems):
    copies = [pltpu.make_async_copy(src, dst, sems.at[i]) for i, (src, dst) in enumerate(pairs)]
    for copy in copies:
        copy.start()
    return copies


def prepare_keys(pk, pv, rk, rv, mine0, theirs0, mine1, theirs, token, *scratch):
    core = lax.rem(lax.axis_index("pre"), CORES)
    bufs, sems = scratch[:-1], scratch[-1]
    copies = fetch(zip((pk, pv, rk, rv), bufs), sems)
    prompt = pk.shape[0]
    order = sorting(rk.shape[0])
    for copy in copies:
        copy.wait()
    pk, pv, rk, rv = bufs
    for local, outs in enumerate(((mine0, theirs.at[0]), (mine1, theirs.at[1]))):
        for cross, out in enumerate(outs):
            span = lanes(head_of(core, cross, local), HEAD_WIDTH)
            for part, (p, r) in enumerate(((pk, rk), (pv, rv))):
                to = slice(part * HEAD_WIDTH, (part + 1) * HEAD_WIDTH)
                out[:prompt, to] = p[:, span]
                out[prompt:, to] = dot(order, r[:, span]).astype(BF16)
    theirs0[...] = theirs[0]
    token[...] = jnp.zeros_like(token)


def prepare_rows(place, token, pq, po, pg, rq, ro, rg, *refs):
    (theirs, *mine), bufs, sems = refs[: 1 + LOCAL_HEADS], refs[1 + LOCAL_HEADS : -1], refs[-1]
    outs = [out for local in range(LOCAL_HEADS) for out in (theirs.at[local], mine[local])]
    core = place[1]
    reply = rq.shape[0]
    sources = (pq, po, pg, rq, ro, rg)
    pairs = []
    for step in range(KEY_VALUE_HEADS):
        span = lanes(head_of(core, 1 - step % CORES, step // CORES), GROUP_WIDTH)
        pairs += [(source.at[:, span], buf.at[step]) for source, buf in zip(sources, bufs)]
    copies = fetch(pairs, sems)
    order = sorting(reply)
    column = iota((GROUP_WIDTH, HEAD_WIDTH), 1)
    pick = (column // 3 == iota((GROUP_WIDTH, HEAD_WIDTH), 0) // HEAD_WIDTH).astype(BF16)

    def delta(gradient, output):
        product = gradient.astype(F32) * output.astype(F32)
        high = product.astype(BF16)
        low = (product - high.astype(F32)).astype(BF16)
        value = dot(high, pick) + dot(low, pick)
        first = value.astype(BF16).astype(F32)
        second = (value - first).astype(BF16).astype(F32)
        part = iota(value.shape, 1) % 3
        return jnp.where(part == 0, first, jnp.where(part == 1, second, value - first - second)).astype(BF16)

    for step, out in enumerate(outs):
        for copy in copies[step * len(sources) : (step + 1) * len(sources)]:
            copy.wait()
        pq, po, pg, rq, ro, rg = (buf[step] for buf in bufs)
        out[reply:, :GROUP_WIDTH] = pq
        out[reply:, GROUP_WIDTH : 2 * GROUP_WIDTH] = pg
        out[reply:, 2 * GROUP_WIDTH :] = delta(pg, po)
        out[:reply, :GROUP_WIDTH] = dot(order, rq).astype(BF16)
        gradient = dot(order, rg).astype(BF16)
        out[:reply, GROUP_WIDTH : 2 * GROUP_WIDTH] = gradient
        out[:reply, 2 * GROUP_WIDTH :] = delta(gradient, dot(order, ro).astype(BF16))


def attend(sizes, joint_keys, place, reply_len, reply_slot, *refs):
    chips, reply_own, prompt_own, prompt_rows, prompt_keys = sizes
    own_positions = reply_own // RESP_DEV
    positions = CORES * own_positions
    chip_prompt = CORES * prompt_keys
    block = 2 * positions
    prompt_blocks = chips * chip_prompt // block
    rows_in, refs = (refs[0], refs[1].at[int(joint_keys)]), refs[2:]
    count = chips if joint_keys else chips * CORES
    keys_in, refs = refs[:count], refs[count:]
    query_out, refs = refs[:2], refs[2:]
    keys_out, refs = refs[:chips], refs[chips:]
    prompt_out, refs = (refs[:chips], refs[chips:]) if joint_keys else (keys_out, refs)
    keys, keys_t, total, query, gradient, query_t, gradient_t, deltas, delta, scores, peaks, top, mass, *refs = refs
    query_grad, stages = refs[0], (refs[1:3], refs[3:5])
    chip, core, group = place[0], place[1], place[2]

    pick = (iota((8, HEAD_WIDTH), 1) // 3 == iota((8, HEAD_WIDTH), 0)).astype(BF16)
    for other in range(CORES):
        deltas[other] = dot(pick, rows_in[other][:, 2 * GROUP_WIDTH :], (1, 1))

    for index in range(chips * CORES):
        away, other = index // CORES, index % CORES
        source = keys_in[away].at[other] if joint_keys else keys_in[index]
        source = source if len(source.shape) == 2 else source.at[0]
        at = away * chip_prompt + other * prompt_keys
        keys[at : at + prompt_keys] = source[:prompt_keys]
        for slot in range(RESP_DEV):
            at = chips * chip_prompt + (slot * chips + away) * positions + other * own_positions
            begin = prompt_keys + slot * own_positions
            keys[at : at + own_positions] = source[begin : begin + own_positions]
    total[...] = jnp.zeros_like(total)

    unit = (iota((HEAD_WIDTH, HEAD_WIDTH), 0) == iota((HEAD_WIDTH, HEAD_WIDTH), 1)).astype(BF16)

    def transpose_block(index, carry):
        rows = pl.ds(pl.multiple_of(index * block, block), block)
        keys_t[index] = dot(unit, keys[rows, :HEAD_WIDTH], (1, 1)).astype(BF16)
        return carry

    lax.fori_loop(0, keys_t.shape[0], transpose_block, 0)

    def score_block(region, place_in, width, chunks, hidden, count=block):
        rows = pl.ds(pl.multiple_of(region * block, block), count)
        key_rows = keys[rows, :HEAD_WIDTH]
        for chunk in range(chunks):
            span = slice(chunk * width, (chunk + 1) * width)
            value = dot(key_rows, query_t[:, span]) * SCALE_LOG2
            if hidden is not None:
                value = jnp.where(hidden, NEGATIVE_FLOOR, value)
            split = value.reshape(count // 8, 8, width)
            peak, summed = top[:, span], mass[:, span]
            for part in range(count // PART):
                piece = split[part * PART // 8 : (part + 1) * PART // 8]
                now = jnp.maximum(peak, jnp.max(piece, axis=0))
                shifted = jnp.exp2(piece - now[None])
                scores[place_in, part * PART : (part + 1) * PART, span] = shifted.reshape(PART, width)
                peaks[place_in, part, :, span] = now
                summed = summed * jnp.exp2(peak - now) + jnp.sum(shifted, axis=0)
                peak = now
            top[:, span], mass[:, span] = peak, summed

    def weigh(region, place_in, width, chunks, log_mass, stage, count=block, earlier=None):
        rows = pl.ds(pl.multiple_of(region * block, block), count)
        value_rows = keys[rows, HEAD_WIDTH:]
        for chunk in range(chunks):
            span = slice(chunk * width, (chunk + 1) * width)
            dp = dot(value_rows, gradient_t[:, span])
            for part in range(count // PART):
                at = slice(part * PART, (part + 1) * PART)
                factor = jnp.exp2(peaks[place_in, part, :, span] - log_mass[chunk])
                p = scores[place_in, at, span].reshape(PART // 8, 8, width) * factor[None]
                p = p.reshape(PART, width)
                stage[0][at, span] = p.astype(BF16)
                stage[1][at, span] = (p * (dp[at] - delta[0:1, span])).astype(BF16)
            if earlier is not None:
                multiply(*earlier, width, chunks, chunk)
        if earlier is not None:
            for chunk in range(chunks, 3):
                multiply(*earlier, width, chunks, chunk)

    def multiply(region, stage, count, width, chunks, part):
        rows = pl.ds(pl.multiple_of(region * block, block), count)
        used = width * chunks
        if part == 0:
            total[rows, HEAD_WIDTH:] += dot(stage[0][:count, :used], gradient[:used])
        elif part == 1:
            total[rows, :HEAD_WIDTH] += dot(stage[1][:count, :used], query[:used])
        elif part == 2:
            query_grad[:, :used] += dot(keys_t[region, :, :count], stage[1][:count, :used])

    def grad_blocks(blocks, region_of, width, chunks, log_mass, begin_with):
        first, second = stages

        def later(index, stage, earlier_stage):
            earlier = region_of(index - 1), earlier_stage, block
            weigh(region_of(index), index, width, chunks, log_mass, stage, earlier=earlier)

        def last(stage):
            for part in range(3):
                multiply(region_of(blocks - 1), stage, block, width, chunks, part)

        begin_with(first, second)

        def two(index, carry):
            later(2 * index + 1, first, second)

            @pl.when(2 * index + 2 < blocks)
            def _():
                later(2 * index + 2, second, first)

            return carry

        lax.fori_loop(0, blocks // 2, two, 0)

        @pl.when(blocks % 2 == 0)
        def _():
            last(first)

        @pl.when(blocks % 2 == 1)
        def _():
            last(second)

    def turn(all_rows):
        query_t[:, :all_rows] = dot(unit, query[:all_rows], (1, 1)).astype(BF16)
        gradient_t[:, :all_rows] = dot(unit, gradient[:all_rows], (1, 1)).astype(BF16)

    def begin(all_rows):
        top[:, :all_rows] = jnp.full((8, all_rows), NEGATIVE_FLOOR, F32)
        mass[:, :all_rows] = jnp.zeros((8, all_rows), F32)
        query_grad[:, :all_rows] = jnp.zeros((HEAD_WIDTH, all_rows), F32)

    def log_masses(width, chunks, live):
        found = []
        for chunk in range(chunks):
            span = slice(chunk * width, (chunk + 1) * width)
            peak = jnp.max(top[:, span], axis=0, keepdims=True)
            summed = jnp.sum(mass[:, span] * jnp.exp2(top[:, span] - peak), axis=0, keepdims=True)
            found.append(jnp.where(live, peak + jnp.log2(summed), DEAD))
        return found

    def absolute(index, half):
        return index + jnp.where(index < half, core * half, -core * half)

    def reply_tile(slot, carry):
        length = jnp.int32(0)
        for response in range(reply_len.shape[0]):
            mine = reply_slot[response] == group * RESP_DEV + slot
            length = length + jnp.where(mine, reply_len[response], 0)
        first = chip * positions
        source = pl.ds(pl.multiple_of(slot * own_positions, own_positions), own_positions)

        @pl.when(length > first)
        def _():
            for head in range(GROUP):
                for other in range(CORES):
                    at = head * positions + other * own_positions
                    to = slice(at, at + own_positions)
                    left = slice(head * HEAD_WIDTH, (head + 1) * HEAD_WIDTH)
                    right = slice(GROUP_WIDTH + head * HEAD_WIDTH, GROUP_WIDTH + (head + 1) * HEAD_WIDTH)
                    query[to] = rows_in[other][source, left]
                    gradient[to] = rows_in[other][source, right]
                    for which in range(RESP_DEV):
                        @pl.when(slot == which)
                        def _():
                            delta[0:1, to] = deltas[
                                other, head : head + 1, which * own_positions : (which + 1) * own_positions
                            ]
            begin(GROUP * positions)
            turn(GROUP * positions)
            base = prompt_blocks + slot * (chips // 2)
            past = prompt_blocks + chip // 2

            def region_of(index):
                reply = base + ((index - prompt_blocks) ^ (chip // 2))
                return jnp.where(index < prompt_blocks, index, reply)

            def stats(index, carry):
                score_block(region_of(index), index, positions, GROUP, None)
                return carry

            lax.fori_loop(0, past, stats, 0)
            row_at = absolute(iota((1, positions), 1), own_positions)
            odd = chip % 2 == 1

            def own_stats(count):
                key = iota((count, 1), 0)
                key_at = jnp.where(key < positions, absolute(key, own_positions), -1)
                score_block(base, past, positions, GROUP, key_at > row_at, count)

            @pl.when(odd)
            def _():
                own_stats(block)

            @pl.when(jnp.logical_not(odd))
            def _():
                own_stats(positions)

            live = first + row_at < length
            log_mass = log_masses(positions, GROUP, live)


            def own_grads(stage, next_stage):
                def run(count):
                    weigh(base, past, positions, GROUP, log_mass, stage, count)
                    earlier = base, stage, count
                    weigh(region_of(0), 0, positions, GROUP, log_mass, next_stage, earlier=earlier)

                @pl.when(odd)
                def _():
                    run(block)

                @pl.when(jnp.logical_not(odd))
                def _():
                    run(positions)

            grad_blocks(past, region_of, positions, GROUP, log_mass, own_grads)
            for head in range(GROUP):
                turned = (query_grad[:, head * positions : (head + 1) * positions].T * SCALE).astype(BF16)
                for other in range(CORES):
                    query_out[other][source, head * HEAD_WIDTH : (head + 1) * HEAD_WIDTH] = turned[
                        other * own_positions : (other + 1) * own_positions
                    ]

        @pl.when(length <= first)
        def _():
            for other in range(CORES):
                query_out[other][source, :] = jnp.zeros((own_positions, GROUP_WIDTH), BF16)

        return carry

    lax.fori_loop(0, RESP_DEV, reply_tile, 0)

    head_rows = CORES * prompt_own
    used = GROUP * head_rows
    all_rows = -(-used // 128) * 128
    if all_rows > used:
        query[used:all_rows] = jnp.zeros((all_rows - used, HEAD_WIDTH), BF16)
        gradient[used:all_rows] = jnp.zeros((all_rows - used, HEAD_WIDTH), BF16)
    delta[0:1, :all_rows] = jnp.zeros((1, all_rows), F32)
    for head in range(GROUP):
        for other in range(CORES):
            at = head * head_rows + other * prompt_own
            to = slice(at, at + prompt_own)
            left = slice(head * HEAD_WIDTH, (head + 1) * HEAD_WIDTH)
            right = slice(GROUP_WIDTH + head * HEAD_WIDTH, GROUP_WIDTH + (head + 1) * HEAD_WIDTH)
            query[to] = rows_in[other][reply_own:, left]
            gradient[to] = rows_in[other][reply_own:, right]
            delta[0:1, to] = deltas[other, head : head + 1, reply_own:]
    begin(all_rows)
    turn(all_rows)
    lane = iota((1, all_rows), 1)
    within = lane
    for head in range(1, GROUP):
        within = within - jnp.where(lane >= head * head_rows, head_rows, 0)
    offset = jnp.where(within < prompt_own, within, within - prompt_own)
    row_core = jnp.where(within < prompt_own, core, 1 - core)
    real = (lane < used) & (offset < prompt_rows)
    row_at = jnp.where(
        real, (chip * CORES + row_core) * prompt_keys + group * prompt_rows + offset, -1
    )
    per_block = max(block // chip_prompt, 1)
    block_parts = max(chip_prompt // block, 1)
    pair = chip // per_block
    seen = (pair + 1) * block_parts

    def prompt_region(index):
        return (index // block_parts ^ pair) * block_parts + index % block_parts

    def prompt_stats(index, carry):
        key = iota((block, 1), 0) + index % block_parts * block
        key_chip = ((index // block_parts ^ pair) * per_block + key // chip_prompt) ^ chip
        key_at = key_chip * chip_prompt + absolute(key % chip_prompt, prompt_keys)
        score_block(prompt_region(index), index, all_rows, 1, key_at > row_at)
        return carry

    lax.fori_loop(0, seen, prompt_stats, 0)
    log_mass = log_masses(all_rows, 1, real)


    def prompt_grads(index, carry):
        weigh(prompt_region(index), index, all_rows, 1, log_mass, stages[0])
        for part in range(3):
            multiply(prompt_region(index), stages[0], block, all_rows, 1, part)
        return carry

    lax.fori_loop(0, seen, prompt_grads, 0)
    turned = (query_grad[:, :all_rows].T * SCALE).astype(BF16)
    for head in range(GROUP):
        for other in range(CORES):
            at = head * head_rows + other * prompt_own
            query_out[other][reply_own:, head * HEAD_WIDTH : (head + 1) * HEAD_WIDTH] = turned[
                at : at + prompt_own
            ]

    def put(out, at, count):
        out[:, :HEAD_WIDTH] = (total[at : at + count, :HEAD_WIDTH] * SCALE).astype(BF16)
        out[:, HEAD_WIDTH:] = total[at : at + count, HEAD_WIDTH:].astype(BF16)

    for index in range(chips * CORES):
        away, other = index // CORES, index % CORES
        put(prompt_out[away].at[other, :prompt_keys], away * chip_prompt + other * prompt_keys, prompt_keys)
        for slot in range(RESP_DEV):
            at = chips * chip_prompt + (slot * chips + away) * positions + other * own_positions
            to = slot * own_positions + (0 if joint_keys else prompt_keys)
            put(keys_out[away].at[other, to : to + own_positions], at, own_positions)


def add(first, *rest):
    value = first.astype(F32)
    for part in rest:
        value = value + part.astype(F32)
    return value


def collect_first(chips, place, *refs):
    parts, prompt_parts, refs = refs[:chips], refs[chips : 2 * chips], refs[2 * chips :]
    mine, theirs, outs, summed = refs[0], refs[1], refs[2:-1], refs[-1]
    groups, rows = len(outs), outs[0].shape[1]
    prompt_keys = groups * rows
    mine[...] = add(*(part[0, prompt_keys:] for part in parts))
    theirs[...] = add(*(part[1, prompt_keys:] for part in parts)).astype(BF16)
    for other in range(CORES):
        summed[other] = add(*(part[other, :prompt_keys] for part in parts))
        summed[CORES + other] = add(*(part[other] for part in prompt_parts))
    for shift in range(groups):
        at = pl.ds(pl.multiple_of(lax.rem(place[2] + shift, groups) * rows, rows), rows)
        for index in range(summed.shape[0]):
            outs[shift][index] = summed[index, at].astype(BF16)


def collect_second(chips, *refs):
    parts, slices, (theirs0, mine, prompt, theirs) = refs[:chips], refs[chips:-4], refs[-4:]
    reply, rows = theirs0.shape[0], prompt.shape[1]
    step = max(rows, 16)
    mine[...] = add(*(part[0] for part in parts))
    theirs[:reply] = theirs0[...]
    theirs[reply : 2 * reply] = add(*(part[1] for part in parts)).astype(BF16)
    for local in range(LOCAL_HEADS):
        prompt[local] = add(*(part[CORES * local] for part in slices))
        at = 2 * reply + local * step
        theirs[at : at + rows] = add(*(part[CORES * local + 1] for part in slices)).astype(BF16)


def finish_queries(place, *refs):
    queries, prompt_dq, reply_dq = refs[:-2], refs[-2], refs[-1]
    reply = reply_dq.shape[0]
    order = unsorting(reply)
    for index, query in enumerate(queries):
        span = lanes(head_of(place[1], index % CORES, index // CORES), GROUP_WIDTH)
        reply_dq[:, span] = dot(order, query[:reply]).astype(BF16)
        prompt_dq[:, span] = query[reply:]


def finish_keys(place, reply0, reply1, prompts, theirs, prompt_dk, prompt_dv, reply_dk, reply_dv):
    reply, rows = reply_dk.shape[0], prompt_dk.shape[0]
    step = max(rows, 16)
    order = unsorting(reply)
    for local in range(LOCAL_HEADS):
        for other in range(CORES):
            span = lanes(head_of(place[1], other, local), HEAD_WIDTH)
            if other:
                value = theirs[local * reply : (local + 1) * reply]
                prompt = theirs[2 * reply + local * step : 2 * reply + local * step + rows]
            else:
                value = (reply1 if local else reply0)[...].astype(BF16)
                prompt = prompts[local].astype(BF16)
            value = dot(order, value).astype(BF16)
            reply_dk[:, span] = value[:, :HEAD_WIDTH]
            reply_dv[:, span] = value[:, HEAD_WIDTH:]
            prompt_dk[:, span] = prompt[:, :HEAD_WIDTH]
            prompt_dv[:, span] = prompt[:, HEAD_WIDTH:]


def on_device(
    prompt_query,
    prompt_k,
    prompt_value,
    prompt_output,
    prompt_output_gradient,
    reply_query,
    reply_key,
    reply_value,
    reply_output,
    reply_output_gradient,
    reply_len,
    reply_slot,
):
    devices = lax.axis_size("pre")
    groups = lax.axis_size("rsp")
    chips = devices // CORES
    prompt_rows = prompt_query.shape[0]
    prompt_own = -(-prompt_rows // 16) * 16
    prompt_keys = prompt_k.shape[0]
    reply_own = reply_query.shape[1]
    own_positions = reply_own // RESP_DEV
    positions = CORES * own_positions
    chip_prompt = CORES * prompt_keys
    block = 2 * positions
    assert (chip_prompt % block == 0 or block % chip_prompt == 0) and chips > 1 and chips & (chips - 1) == 0
    pre_index = lax.axis_index("pre")
    place = jnp.stack([lax.div(pre_index, CORES), lax.rem(pre_index, CORES), lax.axis_index("rsp")])

    def shape(*dims, dtype=BF16):
        return jax.ShapeDtypeStruct(dims, dtype)

    def move(array, away, cross=0):
        pairs = [(p, (p // CORES ^ away) * CORES + (p % CORES ^ cross)) for p in range(devices)]
        return lax.ppermute(array, "pre", pairs)

    def swap(array):
        return move(array, 0, 1)

    def call(kernel, name, mib, inputs, outs, scalars=1, spec=VMEM, **more):
        return pl.pallas_call(
            kernel,
            out_shape=outs,
            in_specs=[SMEM] * scalars + [spec] * (len(inputs) - scalars),
            out_specs=[VMEM] * len(outs),
            compiler_params=params(mib),
            name=name,
            **more,
        )(*inputs)

    relayed = chips == 4
    key_shape = (prompt_keys + reply_own, 2 * HEAD_WIDTH)
    mine0, theirs0, mine1, theirs, token = call(
        prepare_keys,
        "prepare_keys",
        LARGE_MIB,
        (prompt_k, prompt_value, reply_key[0], reply_value[0]),
        [shape(*key_shape)] * 3 + [shape(LOCAL_HEADS, *key_shape), shape(8, 128, dtype=F32)],
        scalars=0,
        spec=HBM,
        scratch_shapes=[
            pltpu.VMEM((rows, KEY_VALUE_HEADS * HEAD_WIDTH), BF16)
            for rows in (prompt_keys, prompt_keys, reply_own, reply_own)
        ]
        + [pltpu.SemaphoreType.DMA((4,))],
    )
    blocks0 = {(0, 0): mine0, (0, 1): swap(theirs)}
    for away in range(1, 3 if relayed else chips):
        blocks0[away, 0] = move(mine0, away)
        blocks0[away, 1] = move(theirs0, away, 1)
    if prompt_own > prompt_rows:
        room = ((0, prompt_own - prompt_rows), (0, 0))
        prompt_query, prompt_output, prompt_output_gradient = (
            jnp.pad(array, room)
            for array in (prompt_query, prompt_output, prompt_output_gradient)
        )
    own_rows = reply_own + prompt_own
    row_width = 2 * GROUP_WIDTH + HEAD_WIDTH

    rows = call(
        prepare_rows,
        "prepare_rows",
        LARGE_MIB,
        (
            place,
            token,
            prompt_query,
            prompt_output,
            prompt_output_gradient,
            reply_query[0],
            reply_output[0],
            reply_output_gradient[0],
        ),
        [shape(LOCAL_HEADS, own_rows, row_width)] + [shape(own_rows, row_width)] * LOCAL_HEADS,
        spec=HBM,
        scratch_shapes=[
            pltpu.VMEM((KEY_VALUE_HEADS, rows, GROUP_WIDTH), BF16)
            for rows in [prompt_own] * 3 + [reply_own] * 3
        ]
        + [pltpu.SemaphoreType.DMA((KEY_VALUE_HEADS * 6,))],
        cost_estimate=pl.CostEstimate(
            flops=6 * reply_own * reply_own * QUERY_HEADS * HEAD_WIDTH,
            bytes_accessed=20 * reply_own * QUERY_HEADS * HEAD_WIDTH,
            transcendentals=0,
        ),
    )

    blocks0, rows, mine1 = lax.optimization_barrier((blocks0, rows, mine1))
    if relayed:
        blocks0[3, 0] = move(blocks0[1, 0], 2)
        blocks0[3, 1] = move(blocks0[2, 1], 1)
    rows_theirs, *rows_mine = rows
    rows_theirs, mine1 = lax.optimization_barrier((swap(rows_theirs), mine1))
    chip1 = jnp.stack([mine1, blocks0[0, 1][1]])
    blocks1 = [chip1] + [move(chip1, away) for away in range(1, chips)]

    blocks = (chips * chip_prompt + RESP_DEV * chips * positions) // block
    slots = (chips * chip_prompt + chips * positions) // block
    all_rows = max(GROUP * positions, -(-GROUP * CORES * prompt_own // 128) * 128)
    sizes = (chips, reply_own, prompt_own, prompt_rows, prompt_keys)
    score_count = GROUP * (positions * RESP_DEV * slots * block)

    cut_rows = prompt_keys // groups
    def run_attend(local, key_blocks):
        joint_keys = local == 1
        sums = [shape(CORES, *key_shape)] * chips
        if joint_keys:
            sums = [shape(CORES, n, 2 * HEAD_WIDTH) for n in [reply_own] * chips + [prompt_keys] * chips]
        query_mine, query_theirs, *sums = call(
            functools.partial(attend, sizes, joint_keys),
            "attend",
            VMEM_MIB,
            (
                place,
                reply_len,
                reply_slot,
                rows_mine[local],
                rows_theirs,
                *key_blocks,
            ),
            [shape(own_rows, GROUP_WIDTH)] * CORES + sums,
            scalars=3,
            scratch_shapes=[
                pltpu.VMEM((blocks * block, 2 * HEAD_WIDTH), BF16),
                pltpu.VMEM((blocks, HEAD_WIDTH, block), BF16),
                pltpu.VMEM((blocks * block, 2 * HEAD_WIDTH), F32),
                pltpu.VMEM((all_rows, HEAD_WIDTH), BF16),
                pltpu.VMEM((all_rows, HEAD_WIDTH), BF16),
                pltpu.VMEM((HEAD_WIDTH, all_rows), BF16),
                pltpu.VMEM((HEAD_WIDTH, all_rows), BF16),
                pltpu.VMEM((CORES, 8, own_rows), F32),
                pltpu.VMEM((8, all_rows), F32),
                pltpu.VMEM((slots, block, all_rows), F32),
                pltpu.VMEM((slots, block // PART, 8, all_rows), F32),
                pltpu.VMEM((8, all_rows), F32),
                pltpu.VMEM((8, all_rows), F32),
                pltpu.VMEM((HEAD_WIDTH, all_rows), F32),
            ]
            + [pltpu.VMEM((block, all_rows), BF16)] * 4,
            cost_estimate=pl.CostEstimate(
                flops=score_count * 10 * HEAD_WIDTH,
                bytes_accessed=8 * 1024 * 1024,
                transcendentals=2 * score_count,
            ),
        )
        return query_mine, query_theirs, sums

    query_mine0, query_theirs0, sums0 = run_attend(
        0, [blocks0[away, other] for away in range(chips) for other in range(CORES)]
    )
    arrived0 = [sums0[0]] + [move(sums0[away], away) for away in range(1, chips)]
    query_theirs0 = swap(query_theirs0)
    query_mine1, query_theirs1, sums1 = run_attend(1, blocks1)
    arrived0, query_theirs0, query_theirs1, sums1 = lax.optimization_barrier(
        (arrived0, query_theirs0, query_theirs1, sums1)
    )
    prompt1 = [sums1[chips]] + [move(sums1[chips + away], away) for away in range(1, chips)]
    key_width = KEY_VALUE_HEADS * HEAD_WIDTH
    query_width = QUERY_HEADS * HEAD_WIDTH
    query_theirs1 = swap(query_theirs1)
    prompt1, query_theirs1, sums1 = lax.optimization_barrier((prompt1, query_theirs1, sums1[:chips]))
    arrived1 = [sums1[0]] + [move(sums1[away], away) for away in range(1, chips)]
    reply0, theirs0, *cuts = call(
        functools.partial(collect_first, chips),
        "collect_first",
        SMALL_MIB,
        (place, *arrived0, *prompt1),
        [shape(reply_own, 2 * HEAD_WIDTH, dtype=F32), shape(reply_own, 2 * HEAD_WIDTH)]
        + [shape(KEY_VALUE_HEADS, cut_rows, 2 * HEAD_WIDTH)] * groups,
        scratch_shapes=[pltpu.VMEM((KEY_VALUE_HEADS, prompt_keys, 2 * HEAD_WIDTH), F32)],
    )
    slices = [cuts[0]] + [
        lax.ppermute(cuts[shift], "rsp", [(g, (g + shift) % groups) for g in range(groups)])
        for shift in range(1, groups)
    ]
    prompt_dq, reply_dq = call(
        finish_queries,
        "finish_queries",
        SMALL_MIB,
        (place, query_mine0, query_theirs0, query_mine1, query_theirs1),
        [shape(prompt_own, query_width), shape(reply_own, query_width)],
        cost_estimate=pl.CostEstimate(
            flops=2 * reply_own * reply_own * query_width,
            bytes_accessed=8 * reply_own * query_width,
            transcendentals=0,
        ),
    )
    slices, prompt_dq, reply_dq = lax.optimization_barrier((slices, prompt_dq, reply_dq))
    reply1, prompts, theirs = call(
        functools.partial(collect_second, chips),
        "collect_second",
        SMALL_MIB,
        (*arrived1, *slices, theirs0),
        [
            shape(reply_own, 2 * HEAD_WIDTH, dtype=F32),
            shape(LOCAL_HEADS, cut_rows, 2 * HEAD_WIDTH, dtype=F32),
            shape(2 * reply_own + 2 * max(cut_rows, 16), 2 * HEAD_WIDTH),
        ],
        scalars=0,
    )
    prompt_dk, prompt_dv, reply_dk, reply_dv = call(
        finish_keys,
        "finish_keys",
        SMALL_MIB,
        (place, reply0, reply1, prompts, swap(theirs)),
        [shape(cut_rows, key_width)] * 2 + [shape(reply_own, key_width)] * 2,
    )
    return (
        prompt_dq[:prompt_rows],
        prompt_dk,
        prompt_dv,
        reply_dq[None],
        reply_dk[None],
        reply_dv[None],
    )


def solution(mesh):
    return jax.shard_map(
        on_device,
        mesh=mesh,
        in_specs=(
            P(("pre", "rsp"), None),
            P("pre", None),
            P("pre", None),
            P(("pre", "rsp"), None),
            P(("pre", "rsp"), None),
            P("rsp", "pre", None),
            P("rsp", "pre", None),
            P("rsp", "pre", None),
            P("rsp", "pre", None),
            P("rsp", "pre", None),
            P(),
            P(),
        ),
        out_specs=(
            P(("pre", "rsp"), None),
            P(("pre", "rsp"), None),
            P(("pre", "rsp"), None),
            P("rsp", "pre", None),
            P("rsp", "pre", None),
            P("rsp", "pre", None),
        ),
        check_vma=False,
    )
```

```python
import functools
import math

import jax
import jax.numpy as jnp
from jax import lax
from jax.experimental import pallas as pl
from jax.experimental.pallas import tpu as pltpu
from jax.sharding import PartitionSpec as P

QUERY_HEADS = 20
KEY_VALUE_HEADS = 4
GROUP = QUERY_HEADS // KEY_VALUE_HEADS
HEAD_WIDTH = 128
RESP_DEV = 2
CORES = 2
LOCAL_HEADS = KEY_VALUE_HEADS // CORES
GROUP_WIDTH = GROUP * HEAD_WIDTH

SCALE = HEAD_WIDTH ** (-0.5)
SCALE_LOG2 = SCALE * math.log2(math.e)
PART = 128
NEGATIVE_FLOOR = -1e30
DEAD = 1e30
F32 = jnp.float32
BF16 = jnp.bfloat16
VMEM = pl.BlockSpec(memory_space=pltpu.VMEM)
SMEM = pl.BlockSpec(memory_space=pltpu.SMEM)
HBM = pl.BlockSpec(memory_space=pltpu.HBM)


VMEM_MIB = 40
SMALL_MIB = 24
LARGE_MIB = 58


def params(mib):
    return pltpu.CompilerParams(vmem_limit_bytes=mib * 1024 * 1024)


def dot(a, b, over=(1, 0)):
    return lax.dot_general(
        a, b, (((over[0],), (over[1],)), ((), ())), preferred_element_type=F32
    )


def iota(shape, axis):
    return lax.broadcasted_iota(jnp.int32, shape, axis)


def sorting(rows):
    half = rows // RESP_DEV
    out = iota((rows, rows), 0)
    source = jnp.where(out < half, RESP_DEV * out, RESP_DEV * (out - half) + 1)
    return (iota((rows, rows), 1) == source).astype(BF16)


def unsorting(rows):
    half = rows // RESP_DEV
    out = iota((rows, rows), 1)
    source = jnp.where(out < half, RESP_DEV * out, RESP_DEV * (out - half) + 1)
    return (iota((rows, rows), 0) == source).astype(BF16)


def lanes(index, width):
    return pl.ds(pl.multiple_of(index * width, width), width)


def head_of(core, cross, local):
    owner = (1 - core) if cross else core
    return owner * LOCAL_HEADS + local


def fetch(pairs, sems):
    copies = [pltpu.make_async_copy(src, dst, sems.at[i]) for i, (src, dst) in enumerate(pairs)]
    for copy in copies:
        copy.start()
    return copies


def prepare_keys(pk, pv, rk, rv, mine0, theirs0, mine1, theirs, token, *scratch):
    core = lax.rem(lax.axis_index("pre"), CORES)
    bufs, sems = scratch[:-1], scratch[-1]
    copies = fetch(zip((pk, pv, rk, rv), bufs), sems)
    prompt = pk.shape[0]
    order = sorting(rk.shape[0])
    for copy in copies:
        copy.wait()
    pk, pv, rk, rv = bufs
    for local, outs in enumerate(((mine0, theirs.at[0]), (mine1, theirs.at[1]))):
        for cross, out in enumerate(outs):
            span = lanes(head_of(core, cross, local), HEAD_WIDTH)
            for part, (p, r) in enumerate(((pk, rk), (pv, rv))):
                to = slice(part * HEAD_WIDTH, (part + 1) * HEAD_WIDTH)
                out[:prompt, to] = p[:, span]
                out[prompt:, to] = dot(order, r[:, span]).astype(BF16)
    theirs0[...] = theirs[0]
    token[...] = jnp.zeros_like(token)


def prepare_rows(local, place, token, pq, po, pg, rq, ro, rg, *refs):
    outs, bufs, sems = refs[:CORES], refs[CORES:-1], refs[-1]
    core = place[1]
    reply = rq.shape[0]
    sources = (pq, po, pg, rq, ro, rg)
    pairs = []
    for step in range(CORES):
        span = lanes(head_of(core, 1 - step, local), GROUP_WIDTH)
        pairs += [(source.at[:, span], buf.at[step]) for source, buf in zip(sources, bufs)]
    copies = fetch(pairs, sems)
    order = sorting(reply)
    column = iota((GROUP_WIDTH, HEAD_WIDTH), 1)
    pick = (column // 3 == iota((GROUP_WIDTH, HEAD_WIDTH), 0) // HEAD_WIDTH).astype(BF16)

    def delta(gradient, output):
        product = gradient.astype(F32) * output.astype(F32)
        high = product.astype(BF16)
        low = (product - high.astype(F32)).astype(BF16)
        value = dot(high, pick) + dot(low, pick)
        first = value.astype(BF16).astype(F32)
        second = (value - first).astype(BF16).astype(F32)
        part = iota(value.shape, 1) % 3
        return jnp.where(part == 0, first, jnp.where(part == 1, second, value - first - second)).astype(BF16)

    for step, out in enumerate(outs):
        for copy in copies[step * len(sources) : (step + 1) * len(sources)]:
            copy.wait()
        pq, po, pg, rq, ro, rg = (buf[step] for buf in bufs)
        out[reply:, :GROUP_WIDTH] = pq
        out[reply:, GROUP_WIDTH : 2 * GROUP_WIDTH] = pg
        out[reply:, 2 * GROUP_WIDTH :] = delta(pg, po)
        out[:reply, :GROUP_WIDTH] = dot(order, rq).astype(BF16)
        gradient = dot(order, rg).astype(BF16)
        out[:reply, GROUP_WIDTH : 2 * GROUP_WIDTH] = gradient
        out[:reply, 2 * GROUP_WIDTH :] = delta(gradient, dot(order, ro).astype(BF16))


def attend(sizes, joint_keys, place, reply_len, reply_slot, *refs):
    chips, reply_own, prompt_own, prompt_rows, prompt_keys = sizes
    own_positions = reply_own // RESP_DEV
    positions = CORES * own_positions
    chip_prompt = CORES * prompt_keys
    block = 2 * positions
    prompt_blocks = chips * chip_prompt // block
    rows_in, refs = refs[:2], refs[2:]
    count = chips if joint_keys else chips * CORES
    keys_in, refs = refs[:count], refs[count:]
    query_out, refs = refs[:2], refs[2:]
    keys_out, refs = refs[:chips], refs[chips:]
    prompt_out, refs = (refs[:chips], refs[chips:]) if joint_keys else (keys_out, refs)
    keys, keys_t, total, query, gradient, query_t, gradient_t, deltas, delta, scores, peaks, top, mass, *refs = refs
    query_grad, stages = refs[0], (refs[1:3], refs[3:5])
    chip, core, group = place[0], place[1], place[2]

    pick = (iota((8, HEAD_WIDTH), 1) // 3 == iota((8, HEAD_WIDTH), 0)).astype(BF16)
    for other in range(CORES):
        deltas[other] = dot(pick, rows_in[other][:, 2 * GROUP_WIDTH :], (1, 1))

    for index in range(chips * CORES):
        away, other = index // CORES, index % CORES
        source = keys_in[away].at[other] if joint_keys else keys_in[index]
        source = source if len(source.shape) == 2 else source.at[0]
        at = away * chip_prompt + other * prompt_keys
        keys[at : at + prompt_keys] = source[:prompt_keys]
        for slot in range(RESP_DEV):
            at = chips * chip_prompt + (slot * chips + away) * positions + other * own_positions
            begin = prompt_keys + slot * own_positions
            keys[at : at + own_positions] = source[begin : begin + own_positions]
    total[...] = jnp.zeros_like(total)

    unit = (iota((HEAD_WIDTH, HEAD_WIDTH), 0) == iota((HEAD_WIDTH, HEAD_WIDTH), 1)).astype(BF16)

    def transpose_block(index, carry):
        rows = pl.ds(pl.multiple_of(index * block, block), block)
        keys_t[index] = dot(unit, keys[rows, :HEAD_WIDTH], (1, 1)).astype(BF16)
        return carry

    lax.fori_loop(0, keys_t.shape[0], transpose_block, 0)

    def score_block(region, place_in, width, chunks, hidden, count=block):
        rows = pl.ds(pl.multiple_of(region * block, block), count)
        key_rows = keys[rows, :HEAD_WIDTH]
        for chunk in range(chunks):
            span = slice(chunk * width, (chunk + 1) * width)
            value = dot(key_rows, query_t[:, span]) * SCALE_LOG2
            if hidden is not None:
                value = jnp.where(hidden, NEGATIVE_FLOOR, value)
            split = value.reshape(count // 8, 8, width)
            peak, summed = top[:, span], mass[:, span]
            for part in range(count // PART):
                piece = split[part * PART // 8 : (part + 1) * PART // 8]
                now = jnp.maximum(peak, jnp.max(piece, axis=0))
                shifted = jnp.exp2(piece - now[None])
                scores[place_in, part * PART : (part + 1) * PART, span] = shifted.reshape(PART, width)
                peaks[place_in, part, :, span] = now
                summed = summed * jnp.exp2(peak - now) + jnp.sum(shifted, axis=0)
                peak = now
            top[:, span], mass[:, span] = peak, summed

    def weigh(region, place_in, width, chunks, log_mass, stage, count=block, earlier=None):
        rows = pl.ds(pl.multiple_of(region * block, block), count)
        value_rows = keys[rows, HEAD_WIDTH:]
        for chunk in range(chunks):
            span = slice(chunk * width, (chunk + 1) * width)
            dp = dot(value_rows, gradient_t[:, span])
            for part in range(count // PART):
                at = slice(part * PART, (part + 1) * PART)
                factor = jnp.exp2(peaks[place_in, part, :, span] - log_mass[chunk])
                p = scores[place_in, at, span].reshape(PART // 8, 8, width) * factor[None]
                p = p.reshape(PART, width)
                stage[0][at, span] = p.astype(BF16)
                stage[1][at, span] = (p * (dp[at] - delta[0:1, span])).astype(BF16)
            if earlier is not None:
                multiply(*earlier, width, chunks, chunk)
        if earlier is not None:
            for chunk in range(chunks, 3):
                multiply(*earlier, width, chunks, chunk)

    def multiply(region, stage, count, width, chunks, part):
        rows = pl.ds(pl.multiple_of(region * block, block), count)
        used = width * chunks
        if part == 0:
            total[rows, HEAD_WIDTH:] += dot(stage[0][:count, :used], gradient[:used])
        elif part == 1:
            total[rows, :HEAD_WIDTH] += dot(stage[1][:count, :used], query[:used])
        elif part == 2:
            query_grad[:, :used] += dot(keys_t[region, :, :count], stage[1][:count, :used])

    def grad_blocks(blocks, region_of, width, chunks, log_mass, begin_with):
        first, second = stages

        def later(index, stage, earlier_stage):
            earlier = region_of(index - 1), earlier_stage, block
            weigh(region_of(index), index, width, chunks, log_mass, stage, earlier=earlier)

        def last(stage):
            for part in range(3):
                multiply(region_of(blocks - 1), stage, block, width, chunks, part)

        begin_with(first, second)

        def two(index, carry):
            later(2 * index + 1, first, second)

            @pl.when(2 * index + 2 < blocks)
            def _():
                later(2 * index + 2, second, first)

            return carry

        lax.fori_loop(0, blocks // 2, two, 0)

        @pl.when(blocks % 2 == 0)
        def _():
            last(first)

        @pl.when(blocks % 2 == 1)
        def _():
            last(second)

    def turn(all_rows):
        query_t[:, :all_rows] = dot(unit, query[:all_rows], (1, 1)).astype(BF16)
        gradient_t[:, :all_rows] = dot(unit, gradient[:all_rows], (1, 1)).astype(BF16)

    def begin(all_rows):
        top[:, :all_rows] = jnp.full((8, all_rows), NEGATIVE_FLOOR, F32)
        mass[:, :all_rows] = jnp.zeros((8, all_rows), F32)
        query_grad[:, :all_rows] = jnp.zeros((HEAD_WIDTH, all_rows), F32)

    def log_masses(width, chunks, live):
        found = []
        for chunk in range(chunks):
            span = slice(chunk * width, (chunk + 1) * width)
            peak = jnp.max(top[:, span], axis=0, keepdims=True)
            summed = jnp.sum(mass[:, span] * jnp.exp2(top[:, span] - peak), axis=0, keepdims=True)
            found.append(jnp.where(live, peak + jnp.log2(summed), DEAD))
        return found

    def absolute(index, half):
        return index + jnp.where(index < half, core * half, -core * half)

    def reply_tile(slot, carry):
        length = jnp.int32(0)
        for response in range(reply_len.shape[0]):
            mine = reply_slot[response] == group * RESP_DEV + slot
            length = length + jnp.where(mine, reply_len[response], 0)
        first = chip * positions
        source = pl.ds(pl.multiple_of(slot * own_positions, own_positions), own_positions)

        @pl.when(length > first)
        def _():
            for head in range(GROUP):
                for other in range(CORES):
                    at = head * positions + other * own_positions
                    to = slice(at, at + own_positions)
                    left = slice(head * HEAD_WIDTH, (head + 1) * HEAD_WIDTH)
                    right = slice(GROUP_WIDTH + head * HEAD_WIDTH, GROUP_WIDTH + (head + 1) * HEAD_WIDTH)
                    query[to] = rows_in[other][source, left]
                    gradient[to] = rows_in[other][source, right]
                    for which in range(RESP_DEV):
                        @pl.when(slot == which)
                        def _():
                            delta[0:1, to] = deltas[
                                other, head : head + 1, which * own_positions : (which + 1) * own_positions
                            ]
            begin(GROUP * positions)
            turn(GROUP * positions)
            base = prompt_blocks + slot * (chips // 2)
            past = prompt_blocks + chip // 2

            def region_of(index):
                reply = base + ((index - prompt_blocks) ^ (chip // 2))
                return jnp.where(index < prompt_blocks, index, reply)

            def stats(index, carry):
                score_block(region_of(index), index, positions, GROUP, None)
                return carry

            lax.fori_loop(0, past, stats, 0)
            row_at = absolute(iota((1, positions), 1), own_positions)
            odd = chip % 2 == 1

            def own_stats(count):
                key = iota((count, 1), 0)
                key_at = jnp.where(key < positions, absolute(key, own_positions), -1)
                score_block(base, past, positions, GROUP, key_at > row_at, count)

            @pl.when(odd)
            def _():
                own_stats(block)

            @pl.when(jnp.logical_not(odd))
            def _():
                own_stats(positions)

            live = first + row_at < length
            log_mass = log_masses(positions, GROUP, live)


            def own_grads(stage, next_stage):
                def run(count):
                    weigh(base, past, positions, GROUP, log_mass, stage, count)
                    earlier = base, stage, count
                    weigh(region_of(0), 0, positions, GROUP, log_mass, next_stage, earlier=earlier)

                @pl.when(odd)
                def _():
                    run(block)

                @pl.when(jnp.logical_not(odd))
                def _():
                    run(positions)

            grad_blocks(past, region_of, positions, GROUP, log_mass, own_grads)
            for head in range(GROUP):
                turned = (query_grad[:, head * positions : (head + 1) * positions].T * SCALE).astype(BF16)
                for other in range(CORES):
                    query_out[other][source, head * HEAD_WIDTH : (head + 1) * HEAD_WIDTH] = turned[
                        other * own_positions : (other + 1) * own_positions
                    ]

        @pl.when(length <= first)
        def _():
            for other in range(CORES):
                query_out[other][source, :] = jnp.zeros((own_positions, GROUP_WIDTH), BF16)

        return carry

    lax.fori_loop(0, RESP_DEV, reply_tile, 0)

    head_rows = CORES * prompt_own
    used = GROUP * head_rows
    all_rows = -(-used // 128) * 128
    if all_rows > used:
        query[used:all_rows] = jnp.zeros((all_rows - used, HEAD_WIDTH), BF16)
        gradient[used:all_rows] = jnp.zeros((all_rows - used, HEAD_WIDTH), BF16)
    delta[0:1, :all_rows] = jnp.zeros((1, all_rows), F32)
    for head in range(GROUP):
        for other in range(CORES):
            at = head * head_rows + other * prompt_own
            to = slice(at, at + prompt_own)
            left = slice(head * HEAD_WIDTH, (head + 1) * HEAD_WIDTH)
            right = slice(GROUP_WIDTH + head * HEAD_WIDTH, GROUP_WIDTH + (head + 1) * HEAD_WIDTH)
            query[to] = rows_in[other][reply_own:, left]
            gradient[to] = rows_in[other][reply_own:, right]
            delta[0:1, to] = deltas[other, head : head + 1, reply_own:]
    begin(all_rows)
    turn(all_rows)
    lane = iota((1, all_rows), 1)
    within = lane
    for head in range(1, GROUP):
        within = within - jnp.where(lane >= head * head_rows, head_rows, 0)
    offset = jnp.where(within < prompt_own, within, within - prompt_own)
    row_core = jnp.where(within < prompt_own, core, 1 - core)
    real = (lane < used) & (offset < prompt_rows)
    row_at = jnp.where(
        real, (chip * CORES + row_core) * prompt_keys + group * prompt_rows + offset, -1
    )
    per_block = max(block // chip_prompt, 1)
    block_parts = max(chip_prompt // block, 1)
    pair = chip // per_block
    seen = (pair + 1) * block_parts

    def prompt_region(index):
        return (index // block_parts ^ pair) * block_parts + index % block_parts

    def prompt_stats(index, carry):
        key = iota((block, 1), 0) + index % block_parts * block
        key_chip = ((index // block_parts ^ pair) * per_block + key // chip_prompt) ^ chip
        key_at = key_chip * chip_prompt + absolute(key % chip_prompt, prompt_keys)
        score_block(prompt_region(index), index, all_rows, 1, key_at > row_at)
        return carry

    lax.fori_loop(0, seen, prompt_stats, 0)
    log_mass = log_masses(all_rows, 1, real)


    def prompt_grads(index, carry):
        weigh(prompt_region(index), index, all_rows, 1, log_mass, stages[0])
        for part in range(3):
            multiply(prompt_region(index), stages[0], block, all_rows, 1, part)
        return carry

    lax.fori_loop(0, seen, prompt_grads, 0)
    turned = (query_grad[:, :all_rows].T * SCALE).astype(BF16)
    for head in range(GROUP):
        for other in range(CORES):
            at = head * head_rows + other * prompt_own
            query_out[other][reply_own:, head * HEAD_WIDTH : (head + 1) * HEAD_WIDTH] = turned[
                at : at + prompt_own
            ]

    def put(out, at, count):
        out[:, :HEAD_WIDTH] = (total[at : at + count, :HEAD_WIDTH] * SCALE).astype(BF16)
        out[:, HEAD_WIDTH:] = total[at : at + count, HEAD_WIDTH:].astype(BF16)

    for index in range(chips * CORES):
        away, other = index // CORES, index % CORES
        put(prompt_out[away].at[other, :prompt_keys], away * chip_prompt + other * prompt_keys, prompt_keys)
        for slot in range(RESP_DEV):
            at = chips * chip_prompt + (slot * chips + away) * positions + other * own_positions
            to = slot * own_positions + (0 if joint_keys else prompt_keys)
            put(keys_out[away].at[other, to : to + own_positions], at, own_positions)


def add(first, *rest):
    value = first.astype(F32)
    for part in rest:
        value = value + part.astype(F32)
    return value


def collect_first(chips, place, *refs):
    parts, prompt_parts, refs = refs[:chips], refs[chips : 2 * chips], refs[2 * chips :]
    mine, theirs, outs, summed = refs[0], refs[1], refs[2:-1], refs[-1]
    groups, rows = len(outs), outs[0].shape[1]
    prompt_keys = groups * rows
    mine[...] = add(*(part[0, prompt_keys:] for part in parts))
    theirs[...] = add(*(part[1, prompt_keys:] for part in parts)).astype(BF16)
    for other in range(CORES):
        summed[other] = add(*(part[other, :prompt_keys] for part in parts))
        summed[CORES + other] = add(*(part[other] for part in prompt_parts))
    for shift in range(groups):
        at = pl.ds(pl.multiple_of(lax.rem(place[2] + shift, groups) * rows, rows), rows)
        for index in range(summed.shape[0]):
            outs[shift][index] = summed[index, at].astype(BF16)


def collect_second(chips, *refs):
    parts, slices, (theirs0, mine, prompt, theirs) = refs[:chips], refs[chips:-4], refs[-4:]
    reply, rows = theirs0.shape[0], prompt.shape[1]
    step = max(rows, 16)
    mine[...] = add(*(part[0] for part in parts))
    theirs[:reply] = theirs0[...]
    theirs[reply : 2 * reply] = add(*(part[1] for part in parts)).astype(BF16)
    for local in range(LOCAL_HEADS):
        prompt[local] = add(*(part[CORES * local] for part in slices))
        at = 2 * reply + local * step
        theirs[at : at + rows] = add(*(part[CORES * local + 1] for part in slices)).astype(BF16)


def finish_queries(place, *refs):
    queries, prompt_dq, reply_dq = refs[:-2], refs[-2], refs[-1]
    reply = reply_dq.shape[0]
    order = unsorting(reply)
    for index, query in enumerate(queries):
        span = lanes(head_of(place[1], index % CORES, index // CORES), GROUP_WIDTH)
        reply_dq[:, span] = dot(order, query[:reply]).astype(BF16)
        prompt_dq[:, span] = query[reply:]


def finish_keys(place, reply0, reply1, prompts, theirs, prompt_dk, prompt_dv, reply_dk, reply_dv):
    reply, rows = reply_dk.shape[0], prompt_dk.shape[0]
    step = max(rows, 16)
    order = unsorting(reply)
    for local in range(LOCAL_HEADS):
        for other in range(CORES):
            span = lanes(head_of(place[1], other, local), HEAD_WIDTH)
            if other:
                value = theirs[local * reply : (local + 1) * reply]
                prompt = theirs[2 * reply + local * step : 2 * reply + local * step + rows]
            else:
                value = (reply1 if local else reply0)[...].astype(BF16)
                prompt = prompts[local].astype(BF16)
            value = dot(order, value).astype(BF16)
            reply_dk[:, span] = value[:, :HEAD_WIDTH]
            reply_dv[:, span] = value[:, HEAD_WIDTH:]
            prompt_dk[:, span] = prompt[:, :HEAD_WIDTH]
            prompt_dv[:, span] = prompt[:, HEAD_WIDTH:]


def on_device(
    prompt_query,
    prompt_k,
    prompt_value,
    prompt_output,
    prompt_output_gradient,
    reply_query,
    reply_key,
    reply_value,
    reply_output,
    reply_output_gradient,
    reply_len,
    reply_slot,
):
    devices = lax.axis_size("pre")
    groups = lax.axis_size("rsp")
    chips = devices // CORES
    prompt_rows = prompt_query.shape[0]
    prompt_own = -(-prompt_rows // 16) * 16
    prompt_keys = prompt_k.shape[0]
    reply_own = reply_query.shape[1]
    own_positions = reply_own // RESP_DEV
    positions = CORES * own_positions
    chip_prompt = CORES * prompt_keys
    block = 2 * positions
    assert (chip_prompt % block == 0 or block % chip_prompt == 0) and chips > 1 and chips & (chips - 1) == 0
    pre_index = lax.axis_index("pre")
    place = jnp.stack([lax.div(pre_index, CORES), lax.rem(pre_index, CORES), lax.axis_index("rsp")])

    def shape(*dims, dtype=BF16):
        return jax.ShapeDtypeStruct(dims, dtype)

    def move(array, away, cross=0):
        pairs = [(p, (p // CORES ^ away) * CORES + (p % CORES ^ cross)) for p in range(devices)]
        return lax.ppermute(array, "pre", pairs)

    def swap(array):
        return move(array, 0, 1)

    def call(kernel, name, mib, inputs, outs, scalars=1, spec=VMEM, **more):
        return pl.pallas_call(
            kernel,
            out_shape=outs,
            in_specs=[SMEM] * scalars + [spec] * (len(inputs) - scalars),
            out_specs=[VMEM] * len(outs),
            compiler_params=params(mib),
            name=name,
            **more,
        )(*inputs)

    relayed = chips == 4
    key_shape = (prompt_keys + reply_own, 2 * HEAD_WIDTH)
    mine0, theirs0, mine1, theirs, token = call(
        prepare_keys,
        "prepare_keys",
        LARGE_MIB,
        (prompt_k, prompt_value, reply_key[0], reply_value[0]),
        [shape(*key_shape)] * 3 + [shape(LOCAL_HEADS, *key_shape), shape(8, 128, dtype=F32)],
        scalars=0,
        spec=HBM,
        scratch_shapes=[
            pltpu.VMEM((rows, KEY_VALUE_HEADS * HEAD_WIDTH), BF16)
            for rows in (prompt_keys, prompt_keys, reply_own, reply_own)
        ]
        + [pltpu.SemaphoreType.DMA((4,))],
    )
    blocks0 = {(0, 0): mine0, (0, 1): swap(theirs)}
    for away in range(1, 3 if relayed else chips):
        blocks0[away, 0] = move(mine0, away)
        blocks0[away, 1] = move(theirs0, away, 1)
    if prompt_own > prompt_rows:
        room = ((0, prompt_own - prompt_rows), (0, 0))
        prompt_query, prompt_output, prompt_output_gradient = (
            jnp.pad(array, room)
            for array in (prompt_query, prompt_output, prompt_output_gradient)
        )
    own_rows = reply_own + prompt_own
    row_width = 2 * GROUP_WIDTH + HEAD_WIDTH

    arrays = (
        prompt_query,
        prompt_output,
        prompt_output_gradient,
        reply_query[0],
        reply_output[0],
        reply_output_gradient[0],
    )

    def prepare(local, token):
        return call(
            functools.partial(prepare_rows, local),
            "prepare_rows",
            LARGE_MIB,
            (place, token, *arrays),
            [shape(own_rows, row_width)] * CORES,
            spec=HBM,
            scratch_shapes=[
                pltpu.VMEM((CORES, rows, GROUP_WIDTH), BF16) for rows in [prompt_own] * 3 + [reply_own] * 3
            ]
            + [pltpu.SemaphoreType.DMA((CORES * 6,))],
            cost_estimate=pl.CostEstimate(
                flops=3 * reply_own * reply_own * QUERY_HEADS * HEAD_WIDTH,
                bytes_accessed=10 * reply_own * QUERY_HEADS * HEAD_WIDTH,
                transcendentals=0,
            ),
        )

    theirs_rows0, mine_rows0 = prepare(0, token)
    blocks0, theirs_rows0, mine1, token = lax.optimization_barrier((blocks0, theirs_rows0, mine1, token))
    if relayed:
        blocks0[3, 0] = move(blocks0[1, 0], 2)
        blocks0[3, 1] = move(blocks0[2, 1], 1)
    chip1 = jnp.stack([mine1, blocks0[0, 1][1]])
    blocks1 = [chip1] + [move(chip1, away) for away in range(1, chips)]

    blocks = (chips * chip_prompt + RESP_DEV * chips * positions) // block
    slots = (chips * chip_prompt + chips * positions) // block
    all_rows = max(GROUP * positions, -(-GROUP * CORES * prompt_own // 128) * 128)
    sizes = (chips, reply_own, prompt_own, prompt_rows, prompt_keys)
    score_count = GROUP * (positions * RESP_DEV * slots * block)

    cut_rows = prompt_keys // groups
    theirs_rows0 = swap(theirs_rows0)
    theirs_rows1, mine_rows1 = prepare(1, token)
    rows_mine, rows_theirs = (mine_rows0, mine_rows1), (theirs_rows0, swap(theirs_rows1))

    def run_attend(local, key_blocks):
        joint_keys = local == 1
        sums = [shape(CORES, *key_shape)] * chips
        if joint_keys:
            sums = [shape(CORES, n, 2 * HEAD_WIDTH) for n in [reply_own] * chips + [prompt_keys] * chips]
        query_mine, query_theirs, *sums = call(
            functools.partial(attend, sizes, joint_keys),
            "attend",
            VMEM_MIB,
            (
                place,
                reply_len,
                reply_slot,
                rows_mine[local],
                rows_theirs[local],
                *key_blocks,
            ),
            [shape(own_rows, GROUP_WIDTH)] * CORES + sums,
            scalars=3,
            scratch_shapes=[
                pltpu.VMEM((blocks * block, 2 * HEAD_WIDTH), BF16),
                pltpu.VMEM((blocks, HEAD_WIDTH, block), BF16),
                pltpu.VMEM((blocks * block, 2 * HEAD_WIDTH), F32),
                pltpu.VMEM((all_rows, HEAD_WIDTH), BF16),
                pltpu.VMEM((all_rows, HEAD_WIDTH), BF16),
                pltpu.VMEM((HEAD_WIDTH, all_rows), BF16),
                pltpu.VMEM((HEAD_WIDTH, all_rows), BF16),
                pltpu.VMEM((CORES, 8, own_rows), F32),
                pltpu.VMEM((8, all_rows), F32),
                pltpu.VMEM((slots, block, all_rows), F32),
                pltpu.VMEM((slots, block // PART, 8, all_rows), F32),
                pltpu.VMEM((8, all_rows), F32),
                pltpu.VMEM((8, all_rows), F32),
                pltpu.VMEM((HEAD_WIDTH, all_rows), F32),
            ]
            + [pltpu.VMEM((block, all_rows), BF16)] * 4,
            cost_estimate=pl.CostEstimate(
                flops=score_count * 10 * HEAD_WIDTH,
                bytes_accessed=8 * 1024 * 1024,
                transcendentals=2 * score_count,
            ),
        )
        return query_mine, query_theirs, sums

    query_mine0, query_theirs0, sums0 = run_attend(
        0, [blocks0[away, other] for away in range(chips) for other in range(CORES)]
    )
    arrived0 = [sums0[0]] + [move(sums0[away], away) for away in range(1, chips)]
    query_theirs0 = swap(query_theirs0)
    query_mine1, query_theirs1, sums1 = run_attend(1, blocks1)
    arrived0, query_theirs0, query_theirs1, sums1 = lax.optimization_barrier(
        (arrived0, query_theirs0, query_theirs1, sums1)
    )
    prompt1 = [sums1[chips]] + [move(sums1[chips + away], away) for away in range(1, chips)]
    arrived1 = [sums1[0], move(sums1[1], 1)]
    key_width = KEY_VALUE_HEADS * HEAD_WIDTH
    query_width = QUERY_HEADS * HEAD_WIDTH
    query_theirs1 = swap(query_theirs1)
    prompt1, query_theirs1, sums1[2:chips] = lax.optimization_barrier(
        (prompt1, query_theirs1, sums1[2:chips])
    )
    arrived1 += [move(sums1[away], away) for away in range(2, chips)]
    reply0, theirs0, *cuts = call(
        functools.partial(collect_first, chips),
        "collect_first",
        SMALL_MIB,
        (place, *arrived0, *prompt1),
        [shape(reply_own, 2 * HEAD_WIDTH, dtype=F32), shape(reply_own, 2 * HEAD_WIDTH)]
        + [shape(KEY_VALUE_HEADS, cut_rows, 2 * HEAD_WIDTH)] * groups,
        scratch_shapes=[pltpu.VMEM((KEY_VALUE_HEADS, prompt_keys, 2 * HEAD_WIDTH), F32)],
    )
    slices = [cuts[0]] + [
        lax.ppermute(cuts[shift], "rsp", [(g, (g + shift) % groups) for g in range(groups)])
        for shift in range(1, groups)
    ]
    prompt_dq, reply_dq = call(
        finish_queries,
        "finish_queries",
        SMALL_MIB,
        (place, query_mine0, query_theirs0, query_mine1, query_theirs1),
        [shape(prompt_own, query_width), shape(reply_own, query_width)],
        cost_estimate=pl.CostEstimate(
            flops=2 * reply_own * reply_own * query_width,
            bytes_accessed=8 * reply_own * query_width,
            transcendentals=0,
        ),
    )
    slices, prompt_dq, reply_dq = lax.optimization_barrier((slices, prompt_dq, reply_dq))
    reply1, prompts, theirs = call(
        functools.partial(collect_second, chips),
        "collect_second",
        SMALL_MIB,
        (*arrived1, *slices, theirs0),
        [
            shape(reply_own, 2 * HEAD_WIDTH, dtype=F32),
            shape(LOCAL_HEADS, cut_rows, 2 * HEAD_WIDTH, dtype=F32),
            shape(2 * reply_own + 2 * max(cut_rows, 16), 2 * HEAD_WIDTH),
        ],
        scalars=0,
    )
    prompt_dk, prompt_dv, reply_dk, reply_dv = call(
        finish_keys,
        "finish_keys",
        SMALL_MIB,
        (place, reply0, reply1, prompts, swap(theirs)),
        [shape(cut_rows, key_width)] * 2 + [shape(reply_own, key_width)] * 2,
    )
    return (
        prompt_dq[:prompt_rows],
        prompt_dk,
        prompt_dv,
        reply_dq[None],
        reply_dk[None],
        reply_dv[None],
    )


def solution(mesh):
    return jax.shard_map(
        on_device,
        mesh=mesh,
        in_specs=(
            P(("pre", "rsp"), None),
            P("pre", None),
            P("pre", None),
            P(("pre", "rsp"), None),
            P(("pre", "rsp"), None),
            P("rsp", "pre", None),
            P("rsp", "pre", None),
            P("rsp", "pre", None),
            P("rsp", "pre", None),
            P("rsp", "pre", None),
            P(),
            P(),
        ),
        out_specs=(
            P(("pre", "rsp"), None),
            P(("pre", "rsp"), None),
            P(("pre", "rsp"), None),
            P("rsp", "pre", None),
            P("rsp", "pre", None),
            P("rsp", "pre", None),
        ),
        check_vma=False,
    )
```

```python
import functools
import math

import jax
import jax.numpy as jnp
from jax import lax
from jax.experimental import pallas as pl
from jax.experimental.pallas import tpu as pltpu
from jax.sharding import PartitionSpec as P

QUERY_HEADS = 20
KEY_VALUE_HEADS = 4
GROUP = QUERY_HEADS // KEY_VALUE_HEADS
HEAD_WIDTH = 128
RESP_DEV = 2
CORES = 2
LOCAL_HEADS = KEY_VALUE_HEADS // CORES
GROUP_WIDTH = GROUP * HEAD_WIDTH

SCALE = HEAD_WIDTH ** (-0.5)
SCALE_LOG2 = SCALE * math.log2(math.e)
PART = 128
NEGATIVE_FLOOR = -1e30
DEAD = 1e30
F32 = jnp.float32
BF16 = jnp.bfloat16
VMEM = pl.BlockSpec(memory_space=pltpu.VMEM)
SMEM = pl.BlockSpec(memory_space=pltpu.SMEM)
HBM = pl.BlockSpec(memory_space=pltpu.HBM)


VMEM_MIB = 40
SMALL_MIB = 24
LARGE_MIB = 58


def params(mib):
    return pltpu.CompilerParams(vmem_limit_bytes=mib * 1024 * 1024)


def dot(a, b, over=(1, 0)):
    return lax.dot_general(
        a, b, (((over[0],), (over[1],)), ((), ())), preferred_element_type=F32
    )


def iota(shape, axis):
    return lax.broadcasted_iota(jnp.int32, shape, axis)


def sorting(rows):
    half = rows // RESP_DEV
    out = iota((rows, rows), 0)
    source = jnp.where(out < half, RESP_DEV * out, RESP_DEV * (out - half) + 1)
    return (iota((rows, rows), 1) == source).astype(BF16)


def unsorting(rows):
    half = rows // RESP_DEV
    out = iota((rows, rows), 1)
    source = jnp.where(out < half, RESP_DEV * out, RESP_DEV * (out - half) + 1)
    return (iota((rows, rows), 0) == source).astype(BF16)


def lanes(index, width):
    return pl.ds(pl.multiple_of(index * width, width), width)


def head_of(core, cross, local):
    owner = (1 - core) if cross else core
    return owner * LOCAL_HEADS + local


def fetch(pairs, sems):
    copies = [pltpu.make_async_copy(src, dst, sems.at[i]) for i, (src, dst) in enumerate(pairs)]
    for copy in copies:
        copy.start()
    return copies


def prepare_keys(pk, pv, rk, rv, mine0, theirs0, mine1, theirs, token, *scratch):
    core = lax.rem(lax.axis_index("pre"), CORES)
    bufs, sems = scratch[:-1], scratch[-1]
    copies = fetch(zip((pk, pv, rk, rv), bufs), sems)
    prompt = pk.shape[0]
    order = sorting(rk.shape[0])
    for copy in copies:
        copy.wait()
    pk, pv, rk, rv = bufs
    for local, outs in enumerate(((mine0, theirs.at[0]), (mine1, theirs.at[1]))):
        for cross, out in enumerate(outs):
            span = lanes(head_of(core, cross, local), HEAD_WIDTH)
            for part, (p, r) in enumerate(((pk, rk), (pv, rv))):
                to = slice(part * HEAD_WIDTH, (part + 1) * HEAD_WIDTH)
                out[:prompt, to] = p[:, span]
                out[prompt:, to] = dot(order, r[:, span]).astype(BF16)
    theirs0[...] = theirs[0]
    token[...] = jnp.zeros_like(token)


def prepare_rows(token, pq, po, pg, rq, ro, rg, *refs):
    (theirs, *mine), bufs, sems = refs[: 1 + LOCAL_HEADS], refs[1 + LOCAL_HEADS : -1], refs[-1]
    outs = [out for local in range(LOCAL_HEADS) for out in (theirs.at[local], mine[local])]
    core = lax.rem(lax.axis_index("pre"), CORES)
    reply = rq.shape[0]
    sources = (pq, po, pg, rq, ro, rg)
    pairs = []
    for step in range(KEY_VALUE_HEADS):
        span = lanes(head_of(core, 1 - step % CORES, step // CORES), GROUP_WIDTH)
        pairs += [(source.at[:, span], buf.at[step]) for source, buf in zip(sources, bufs)]
    copies = fetch(pairs, sems)
    order = sorting(reply)
    column = iota((GROUP_WIDTH, HEAD_WIDTH), 1)
    pick = (column // 3 == iota((GROUP_WIDTH, HEAD_WIDTH), 0) // HEAD_WIDTH).astype(BF16)

    def delta(gradient, output):
        product = gradient.astype(F32) * output.astype(F32)
        high = product.astype(BF16)
        low = (product - high.astype(F32)).astype(BF16)
        value = dot(high, pick) + dot(low, pick)
        first = value.astype(BF16).astype(F32)
        second = (value - first).astype(BF16).astype(F32)
        part = iota(value.shape, 1) % 3
        return jnp.where(part == 0, first, jnp.where(part == 1, second, value - first - second)).astype(BF16)

    for step, out in enumerate(outs):
        for copy in copies[step * len(sources) : (step + 1) * len(sources)]:
            copy.wait()
        pq, po, pg, rq, ro, rg = (buf[step] for buf in bufs)
        out[reply:, :GROUP_WIDTH] = pq
        out[reply:, GROUP_WIDTH : 2 * GROUP_WIDTH] = pg
        out[reply:, 2 * GROUP_WIDTH :] = delta(pg, po)
        out[:reply, :GROUP_WIDTH] = dot(order, rq).astype(BF16)
        gradient = dot(order, rg).astype(BF16)
        out[:reply, GROUP_WIDTH : 2 * GROUP_WIDTH] = gradient
        out[:reply, 2 * GROUP_WIDTH :] = delta(gradient, dot(order, ro).astype(BF16))


def attend(sizes, joint_keys, place, reply_len, reply_slot, *refs):
    chips, reply_own, prompt_own, prompt_rows, prompt_keys = sizes
    own_positions = reply_own // RESP_DEV
    positions = CORES * own_positions
    chip_prompt = CORES * prompt_keys
    block = 2 * positions
    prompt_blocks = chips * chip_prompt // block
    rows_in, refs = (refs[0], refs[1].at[int(joint_keys)]), refs[2:]
    count = chips if joint_keys else chips * CORES
    keys_in, refs = refs[:count], refs[count:]
    query_out, refs = refs[:2], refs[2:]
    keys_out, refs = refs[:chips], refs[chips:]
    prompt_out, refs = (refs[:chips], refs[chips:]) if joint_keys else (keys_out, refs)
    keys, keys_t, total, query, gradient, query_t, gradient_t, deltas, delta, scores, peaks, top, mass, *refs = refs
    query_grad, stages = refs[0], (refs[1:3], refs[3:5])
    chip, core, group = place[0], place[1], place[2]

    pick = (iota((8, HEAD_WIDTH), 1) // 3 == iota((8, HEAD_WIDTH), 0)).astype(BF16)
    for other in range(CORES):
        deltas[other] = dot(pick, rows_in[other][:, 2 * GROUP_WIDTH :], (1, 1))

    for index in range(chips * CORES):
        away, other = index // CORES, index % CORES
        source = keys_in[away].at[other] if joint_keys else keys_in[index]
        source = source if len(source.shape) == 2 else source.at[0]
        at = away * chip_prompt + other * prompt_keys
        keys[at : at + prompt_keys] = source[:prompt_keys]
        for slot in range(RESP_DEV):
            at = chips * chip_prompt + (slot * chips + away) * positions + other * own_positions
            begin = prompt_keys + slot * own_positions
            keys[at : at + own_positions] = source[begin : begin + own_positions]
    total[...] = jnp.zeros_like(total)

    unit = (iota((HEAD_WIDTH, HEAD_WIDTH), 0) == iota((HEAD_WIDTH, HEAD_WIDTH), 1)).astype(BF16)

    def transpose_block(index, carry):
        rows = pl.ds(pl.multiple_of(index * block, block), block)
        keys_t[index] = dot(unit, keys[rows, :HEAD_WIDTH], (1, 1)).astype(BF16)
        return carry

    lax.fori_loop(0, keys_t.shape[0], transpose_block, 0)

    def score_block(region, place_in, width, chunks, hidden, count=block):
        rows = pl.ds(pl.multiple_of(region * block, block), count)
        key_rows = keys[rows, :HEAD_WIDTH]
        for chunk in range(chunks):
            span = slice(chunk * width, (chunk + 1) * width)
            value = dot(key_rows, query_t[:, span]) * SCALE_LOG2
            if hidden is not None:
                value = jnp.where(hidden, NEGATIVE_FLOOR, value)
            split = value.reshape(count // 8, 8, width)
            peak, summed = top[:, span], mass[:, span]
            for part in range(count // PART):
                piece = split[part * PART // 8 : (part + 1) * PART // 8]
                now = jnp.maximum(peak, jnp.max(piece, axis=0))
                shifted = jnp.exp2(piece - now[None])
                scores[place_in, part * PART : (part + 1) * PART, span] = shifted.reshape(PART, width)
                peaks[place_in, part, :, span] = now
                summed = summed * jnp.exp2(peak - now) + jnp.sum(shifted, axis=0)
                peak = now
            top[:, span], mass[:, span] = peak, summed

    def weigh(region, place_in, width, chunks, log_mass, stage, count=block, earlier=None):
        rows = pl.ds(pl.multiple_of(region * block, block), count)
        value_rows = keys[rows, HEAD_WIDTH:]
        for chunk in range(chunks):
            span = slice(chunk * width, (chunk + 1) * width)
            dp = dot(value_rows, gradient_t[:, span])
            for part in range(count // PART):
                at = slice(part * PART, (part + 1) * PART)
                factor = jnp.exp2(peaks[place_in, part, :, span] - log_mass[chunk])
                p = scores[place_in, at, span].reshape(PART // 8, 8, width) * factor[None]
                p = p.reshape(PART, width)
                stage[0][at, span] = p.astype(BF16)
                stage[1][at, span] = (p * (dp[at] - delta[0:1, span])).astype(BF16)
            if earlier is not None:
                multiply(*earlier, width, chunks, chunk)
        if earlier is not None:
            for chunk in range(chunks, 3):
                multiply(*earlier, width, chunks, chunk)

    def multiply(region, stage, count, width, chunks, part):
        rows = pl.ds(pl.multiple_of(region * block, block), count)
        used = width * chunks
        if part == 0:
            total[rows, HEAD_WIDTH:] += dot(stage[0][:count, :used], gradient[:used])
        elif part == 1:
            total[rows, :HEAD_WIDTH] += dot(stage[1][:count, :used], query[:used])
        elif part == 2:
            query_grad[:, :used] += dot(keys_t[region, :, :count], stage[1][:count, :used])

    def grad_blocks(blocks, region_of, width, chunks, log_mass, begin_with):
        first, second = stages

        def later(index, stage, earlier_stage):
            earlier = region_of(index - 1), earlier_stage, block
            weigh(region_of(index), index, width, chunks, log_mass, stage, earlier=earlier)

        def last(stage):
            for part in range(3):
                multiply(region_of(blocks - 1), stage, block, width, chunks, part)

        begin_with(first, second)

        def two(index, carry):
            later(2 * index + 1, first, second)

            @pl.when(2 * index + 2 < blocks)
            def _():
                later(2 * index + 2, second, first)

            return carry

        lax.fori_loop(0, blocks // 2, two, 0)

        @pl.when(blocks % 2 == 0)
        def _():
            last(first)

        @pl.when(blocks % 2 == 1)
        def _():
            last(second)

    def turn(all_rows):
        query_t[:, :all_rows] = dot(unit, query[:all_rows], (1, 1)).astype(BF16)
        gradient_t[:, :all_rows] = dot(unit, gradient[:all_rows], (1, 1)).astype(BF16)

    def begin(all_rows):
        top[:, :all_rows] = jnp.full((8, all_rows), NEGATIVE_FLOOR, F32)
        mass[:, :all_rows] = jnp.zeros((8, all_rows), F32)
        query_grad[:, :all_rows] = jnp.zeros((HEAD_WIDTH, all_rows), F32)

    def log_masses(width, chunks, live):
        found = []
        for chunk in range(chunks):
            span = slice(chunk * width, (chunk + 1) * width)
            peak = jnp.max(top[:, span], axis=0, keepdims=True)
            summed = jnp.sum(mass[:, span] * jnp.exp2(top[:, span] - peak), axis=0, keepdims=True)
            found.append(jnp.where(live, peak + jnp.log2(summed), DEAD))
        return found

    def absolute(index, half):
        return index + jnp.where(index < half, core * half, -core * half)

    def reply_tile(slot, carry):
        length = jnp.int32(0)
        for response in range(reply_len.shape[0]):
            mine = reply_slot[response] == group * RESP_DEV + slot
            length = length + jnp.where(mine, reply_len[response], 0)
        first = chip * positions
        source = pl.ds(pl.multiple_of(slot * own_positions, own_positions), own_positions)

        @pl.when(length > first)
        def _():
            for head in range(GROUP):
                for other in range(CORES):
                    at = head * positions + other * own_positions
                    to = slice(at, at + own_positions)
                    left = slice(head * HEAD_WIDTH, (head + 1) * HEAD_WIDTH)
                    right = slice(GROUP_WIDTH + head * HEAD_WIDTH, GROUP_WIDTH + (head + 1) * HEAD_WIDTH)
                    query[to] = rows_in[other][source, left]
                    gradient[to] = rows_in[other][source, right]
                    for which in range(RESP_DEV):
                        @pl.when(slot == which)
                        def _():
                            delta[0:1, to] = deltas[
                                other, head : head + 1, which * own_positions : (which + 1) * own_positions
                            ]
            begin(GROUP * positions)
            turn(GROUP * positions)
            base = prompt_blocks + slot * (chips // 2)
            past = prompt_blocks + chip // 2

            def region_of(index):
                reply = base + ((index - prompt_blocks) ^ (chip // 2))
                return jnp.where(index < prompt_blocks, index, reply)

            def stats(index, carry):
                score_block(region_of(index), index, positions, GROUP, None)
                return carry

            lax.fori_loop(0, past, stats, 0)
            row_at = absolute(iota((1, positions), 1), own_positions)
            odd = chip % 2 == 1

            def own_stats(count):
                key = iota((count, 1), 0)
                key_at = jnp.where(key < positions, absolute(key, own_positions), -1)
                score_block(base, past, positions, GROUP, key_at > row_at, count)

            @pl.when(odd)
            def _():
                own_stats(block)

            @pl.when(jnp.logical_not(odd))
            def _():
                own_stats(positions)

            live = first + row_at < length
            log_mass = log_masses(positions, GROUP, live)


            def own_grads(stage, next_stage):
                def run(count):
                    weigh(base, past, positions, GROUP, log_mass, stage, count)
                    earlier = base, stage, count
                    weigh(region_of(0), 0, positions, GROUP, log_mass, next_stage, earlier=earlier)

                @pl.when(odd)
                def _():
                    run(block)

                @pl.when(jnp.logical_not(odd))
                def _():
                    run(positions)

            grad_blocks(past, region_of, positions, GROUP, log_mass, own_grads)
            for head in range(GROUP):
                turned = (query_grad[:, head * positions : (head + 1) * positions].T * SCALE).astype(BF16)
                for other in range(CORES):
                    query_out[other][source, head * HEAD_WIDTH : (head + 1) * HEAD_WIDTH] = turned[
                        other * own_positions : (other + 1) * own_positions
                    ]

        @pl.when(length <= first)
        def _():
            for other in range(CORES):
                query_out[other][source, :] = jnp.zeros((own_positions, GROUP_WIDTH), BF16)

        return carry

    lax.fori_loop(0, RESP_DEV, reply_tile, 0)

    head_rows = CORES * prompt_own
    used = GROUP * head_rows
    all_rows = -(-used // 128) * 128
    if all_rows > used:
        query[used:all_rows] = jnp.zeros((all_rows - used, HEAD_WIDTH), BF16)
        gradient[used:all_rows] = jnp.zeros((all_rows - used, HEAD_WIDTH), BF16)
    delta[0:1, :all_rows] = jnp.zeros((1, all_rows), F32)
    for head in range(GROUP):
        for other in range(CORES):
            at = head * head_rows + other * prompt_own
            to = slice(at, at + prompt_own)
            left = slice(head * HEAD_WIDTH, (head + 1) * HEAD_WIDTH)
            right = slice(GROUP_WIDTH + head * HEAD_WIDTH, GROUP_WIDTH + (head + 1) * HEAD_WIDTH)
            query[to] = rows_in[other][reply_own:, left]
            gradient[to] = rows_in[other][reply_own:, right]
            delta[0:1, to] = deltas[other, head : head + 1, reply_own:]
    begin(all_rows)
    turn(all_rows)
    lane = iota((1, all_rows), 1)
    within = lane
    for head in range(1, GROUP):
        within = within - jnp.where(lane >= head * head_rows, head_rows, 0)
    offset = jnp.where(within < prompt_own, within, within - prompt_own)
    row_core = jnp.where(within < prompt_own, core, 1 - core)
    real = (lane < used) & (offset < prompt_rows)
    row_at = jnp.where(
        real, (chip * CORES + row_core) * prompt_keys + group * prompt_rows + offset, -1
    )
    per_block = max(block // chip_prompt, 1)
    block_parts = max(chip_prompt // block, 1)
    pair = chip // per_block
    seen = (pair + 1) * block_parts

    def prompt_region(index):
        return (index // block_parts ^ pair) * block_parts + index % block_parts

    def prompt_stats(index, carry):
        key = iota((block, 1), 0) + index % block_parts * block
        key_chip = ((index // block_parts ^ pair) * per_block + key // chip_prompt) ^ chip
        key_at = key_chip * chip_prompt + absolute(key % chip_prompt, prompt_keys)
        score_block(prompt_region(index), index, all_rows, 1, key_at > row_at)
        return carry

    lax.fori_loop(0, seen, prompt_stats, 0)
    log_mass = log_masses(all_rows, 1, real)


    def prompt_grads(index, carry):
        weigh(prompt_region(index), index, all_rows, 1, log_mass, stages[0])
        for part in range(3):
            multiply(prompt_region(index), stages[0], block, all_rows, 1, part)
        return carry

    lax.fori_loop(0, seen, prompt_grads, 0)
    turned = (query_grad[:, :all_rows].T * SCALE).astype(BF16)
    for head in range(GROUP):
        for other in range(CORES):
            at = head * head_rows + other * prompt_own
            query_out[other][reply_own:, head * HEAD_WIDTH : (head + 1) * HEAD_WIDTH] = turned[
                at : at + prompt_own
            ]

    def put(out, at, count):
        out[:, :HEAD_WIDTH] = (total[at : at + count, :HEAD_WIDTH] * SCALE).astype(BF16)
        out[:, HEAD_WIDTH:] = total[at : at + count, HEAD_WIDTH:].astype(BF16)

    for index in range(chips * CORES):
        away, other = index // CORES, index % CORES
        put(prompt_out[away].at[other, :prompt_keys], away * chip_prompt + other * prompt_keys, prompt_keys)
        for slot in range(RESP_DEV):
            at = chips * chip_prompt + (slot * chips + away) * positions + other * own_positions
            to = slot * own_positions + (0 if joint_keys else prompt_keys)
            put(keys_out[away].at[other, to : to + own_positions], at, own_positions)


def add(first, *rest):
    value = first.astype(F32)
    for part in rest:
        value = value + part.astype(F32)
    return value


def collect_first(chips, place, *refs):
    parts, prompt_parts, refs = refs[:chips], refs[chips : 2 * chips], refs[2 * chips :]
    outs, summed = refs[:-1], refs[-1]
    groups, rows = len(outs), outs[0].shape[1]
    prompt_keys = groups * rows
    for other in range(CORES):
        summed[other] = add(*(part[other, :prompt_keys] for part in parts))
        summed[CORES + other] = add(*(part[other] for part in prompt_parts))
    for shift in range(groups):
        at = pl.ds(pl.multiple_of(lax.rem(place[2] + shift, groups) * rows, rows), rows)
        for index in range(summed.shape[0]):
            outs[shift][index] = summed[index, at].astype(BF16)


def collect_replies(*refs):
    parts, mine, theirs = refs[:-2], refs[-2], refs[-1]
    begin = parts[0].shape[1] - mine.shape[0]
    mine[...] = add(*(part[0, begin:] for part in parts))
    theirs[...] = add(*(part[1, begin:] for part in parts)).astype(BF16)


def collect_second(chips, *refs):
    parts, slices, (theirs0, mine, prompt, theirs) = refs[:chips], refs[chips:-4], refs[-4:]
    reply, rows = theirs0.shape[0], prompt.shape[1]
    step = max(rows, 16)
    mine[...] = add(*(part[0] for part in parts))
    theirs[:reply] = theirs0[...]
    theirs[reply : 2 * reply] = add(*(part[1] for part in parts)).astype(BF16)
    for local in range(LOCAL_HEADS):
        prompt[local] = add(*(part[CORES * local] for part in slices))
        at = 2 * reply + local * step
        theirs[at : at + rows] = add(*(part[CORES * local + 1] for part in slices)).astype(BF16)


def finish_queries(place, *refs):
    queries, prompt_dq, reply_dq = refs[:-2], refs[-2], refs[-1]
    reply = reply_dq.shape[0]
    order = unsorting(reply)
    for index, query in enumerate(queries):
        span = lanes(head_of(place[1], index % CORES, index // CORES), GROUP_WIDTH)
        reply_dq[:, span] = dot(order, query[:reply]).astype(BF16)
        prompt_dq[:, span] = query[reply:]


def finish_keys(place, reply0, reply1, prompts, theirs, prompt_dk, prompt_dv, reply_dk, reply_dv):
    reply, rows = reply_dk.shape[0], prompt_dk.shape[0]
    step = max(rows, 16)
    order = unsorting(reply)
    for local in range(LOCAL_HEADS):
        for other in range(CORES):
            span = lanes(head_of(place[1], other, local), HEAD_WIDTH)
            if other:
                value = theirs[local * reply : (local + 1) * reply]
                prompt = theirs[2 * reply + local * step : 2 * reply + local * step + rows]
            else:
                value = (reply1 if local else reply0)[...].astype(BF16)
                prompt = prompts[local].astype(BF16)
            value = dot(order, value).astype(BF16)
            reply_dk[:, span] = value[:, :HEAD_WIDTH]
            reply_dv[:, span] = value[:, HEAD_WIDTH:]
            prompt_dk[:, span] = prompt[:, :HEAD_WIDTH]
            prompt_dv[:, span] = prompt[:, HEAD_WIDTH:]


def on_device(
    prompt_query,
    prompt_k,
    prompt_value,
    prompt_output,
    prompt_output_gradient,
    reply_query,
    reply_key,
    reply_value,
    reply_output,
    reply_output_gradient,
    reply_len,
    reply_slot,
):
    devices = lax.axis_size("pre")
    groups = lax.axis_size("rsp")
    chips = devices // CORES
    prompt_rows = prompt_query.shape[0]
    prompt_own = -(-prompt_rows // 16) * 16
    prompt_keys = prompt_k.shape[0]
    reply_own = reply_query.shape[1]
    own_positions = reply_own // RESP_DEV
    positions = CORES * own_positions
    chip_prompt = CORES * prompt_keys
    block = 2 * positions
    assert (chip_prompt % block == 0 or block % chip_prompt == 0) and chips > 1 and chips & (chips - 1) == 0
    pre_index = lax.axis_index("pre")
    place = jnp.stack([lax.div(pre_index, CORES), lax.rem(pre_index, CORES), lax.axis_index("rsp")])

    def shape(*dims, dtype=BF16):
        return jax.ShapeDtypeStruct(dims, dtype)

    def move(array, away, cross=0):
        pairs = [(p, (p // CORES ^ away) * CORES + (p % CORES ^ cross)) for p in range(devices)]
        return lax.ppermute(array, "pre", pairs)

    def swap(array):
        return move(array, 0, 1)

    def call(kernel, name, mib, inputs, outs, scalars=1, spec=VMEM, **more):
        return pl.pallas_call(
            kernel,
            out_shape=outs,
            in_specs=[SMEM] * scalars + [spec] * (len(inputs) - scalars),
            out_specs=[VMEM] * len(outs),
            compiler_params=params(mib),
            name=name,
            **more,
        )(*inputs)

    relayed = chips == 4
    key_shape = (prompt_keys + reply_own, 2 * HEAD_WIDTH)
    mine0, theirs0, mine1, theirs, token = call(
        prepare_keys,
        "prepare_keys",
        LARGE_MIB,
        (prompt_k, prompt_value, reply_key[0], reply_value[0]),
        [shape(*key_shape)] * 3 + [shape(LOCAL_HEADS, *key_shape), shape(8, 128, dtype=F32)],
        scalars=0,
        spec=HBM,
        scratch_shapes=[
            pltpu.VMEM((rows, KEY_VALUE_HEADS * HEAD_WIDTH), BF16)
            for rows in (prompt_keys, prompt_keys, reply_own, reply_own)
        ]
        + [pltpu.SemaphoreType.DMA((4,))],
    )
    blocks0 = {(0, 0): mine0, (0, 1): swap(theirs)}
    for away in range(1, 3 if relayed else chips):
        blocks0[away, 0] = move(mine0, away)
        blocks0[away, 1] = move(theirs0, away, 1)
    if prompt_own > prompt_rows:
        room = ((0, prompt_own - prompt_rows), (0, 0))
        prompt_query, prompt_output, prompt_output_gradient = (
            jnp.pad(array, room)
            for array in (prompt_query, prompt_output, prompt_output_gradient)
        )
    own_rows = reply_own + prompt_own
    row_width = 2 * GROUP_WIDTH + HEAD_WIDTH

    rows = call(
        prepare_rows,
        "prepare_rows",
        LARGE_MIB,
        (
            token,
            prompt_query,
            prompt_output,
            prompt_output_gradient,
            reply_query[0],
            reply_output[0],
            reply_output_gradient[0],
        ),
        [shape(LOCAL_HEADS, own_rows, row_width)] + [shape(own_rows, row_width)] * LOCAL_HEADS,
        scalars=0,
        spec=HBM,
        scratch_shapes=[
            pltpu.VMEM((KEY_VALUE_HEADS, rows, GROUP_WIDTH), BF16)
            for rows in [prompt_own] * 3 + [reply_own] * 3
        ]
        + [pltpu.SemaphoreType.DMA((KEY_VALUE_HEADS * 6,))],
        cost_estimate=pl.CostEstimate(
            flops=6 * reply_own * reply_own * QUERY_HEADS * HEAD_WIDTH,
            bytes_accessed=20 * reply_own * QUERY_HEADS * HEAD_WIDTH,
            transcendentals=0,
        ),
    )

    blocks0, rows, mine1 = lax.optimization_barrier((blocks0, rows, mine1))
    if relayed:
        blocks0[3, 0] = move(blocks0[1, 0], 2)
        blocks0[3, 1] = move(blocks0[2, 1], 1)
    chip1 = jnp.stack([mine1, blocks0[0, 1][1]])
    blocks1 = [chip1] + [move(chip1, away) for away in range(1, chips)]

    blocks = (chips * chip_prompt + RESP_DEV * chips * positions) // block
    slots = (chips * chip_prompt + chips * positions) // block
    all_rows = max(GROUP * positions, -(-GROUP * CORES * prompt_own // 128) * 128)
    sizes = (chips, reply_own, prompt_own, prompt_rows, prompt_keys)
    score_count = GROUP * (positions * RESP_DEV * slots * block)

    cut_rows = prompt_keys // groups
    rows_theirs, *rows_mine = rows
    rows_theirs = swap(rows_theirs)

    def run_attend(local, key_blocks):
        joint_keys = local == 1
        sums = [shape(CORES, *key_shape)] * chips
        if joint_keys:
            sums = [shape(CORES, n, 2 * HEAD_WIDTH) for n in [reply_own] * chips + [prompt_keys] * chips]
        query_mine, query_theirs, *sums = call(
            functools.partial(attend, sizes, joint_keys),
            "attend",
            VMEM_MIB,
            (
                place,
                reply_len,
                reply_slot,
                rows_mine[local],
                rows_theirs,
                *key_blocks,
            ),
            [shape(own_rows, GROUP_WIDTH)] * CORES + sums,
            scalars=3,
            scratch_shapes=[
                pltpu.VMEM((blocks * block, 2 * HEAD_WIDTH), BF16),
                pltpu.VMEM((blocks, HEAD_WIDTH, block), BF16),
                pltpu.VMEM((blocks * block, 2 * HEAD_WIDTH), F32),
                pltpu.VMEM((all_rows, HEAD_WIDTH), BF16),
                pltpu.VMEM((all_rows, HEAD_WIDTH), BF16),
                pltpu.VMEM((HEAD_WIDTH, all_rows), BF16),
                pltpu.VMEM((HEAD_WIDTH, all_rows), BF16),
                pltpu.VMEM((CORES, 8, own_rows), F32),
                pltpu.VMEM((8, all_rows), F32),
                pltpu.VMEM((slots, block, all_rows), F32),
                pltpu.VMEM((slots, block // PART, 8, all_rows), F32),
                pltpu.VMEM((8, all_rows), F32),
                pltpu.VMEM((8, all_rows), F32),
                pltpu.VMEM((HEAD_WIDTH, all_rows), F32),
            ]
            + [pltpu.VMEM((block, all_rows), BF16)] * 4,
            cost_estimate=pl.CostEstimate(
                flops=score_count * 10 * HEAD_WIDTH,
                bytes_accessed=8 * 1024 * 1024,
                transcendentals=2 * score_count,
            ),
        )
        return query_mine, query_theirs, sums

    query_mine0, query_theirs0, sums0 = run_attend(
        0, [blocks0[away, other] for away in range(chips) for other in range(CORES)]
    )
    arrived0 = [sums0[0]] + [move(sums0[away], away) for away in range(1, chips)]
    query_theirs0 = swap(query_theirs0)
    query_mine1, query_theirs1, sums1 = run_attend(1, blocks1)
    arrived0, query_theirs0, query_theirs1, sums1 = lax.optimization_barrier(
        (arrived0, query_theirs0, query_theirs1, sums1)
    )
    prompt1 = [sums1[chips]] + [move(sums1[chips + away], away) for away in range(1, chips)]
    arrived1 = [sums1[0], move(sums1[1], 1)]
    key_width = KEY_VALUE_HEADS * HEAD_WIDTH
    query_width = QUERY_HEADS * HEAD_WIDTH
    query_theirs1 = swap(query_theirs1)
    prompt1, query_theirs1, sums1[2:chips] = lax.optimization_barrier(
        (prompt1, query_theirs1, sums1[2:chips])
    )
    arrived1 += [move(sums1[away], away) for away in range(2, chips)]
    cuts = call(
        functools.partial(collect_first, chips),
        "collect_first",
        SMALL_MIB,
        (place, *arrived0, *prompt1),
        [shape(KEY_VALUE_HEADS, cut_rows, 2 * HEAD_WIDTH)] * groups,
        scratch_shapes=[pltpu.VMEM((KEY_VALUE_HEADS, prompt_keys, 2 * HEAD_WIDTH), F32)],
    )
    slices = [cuts[0]] + [
        lax.ppermute(cuts[shift], "rsp", [(g, (g + shift) % groups) for g in range(groups)])
        for shift in range(1, groups)
    ]
    prompt_dq, reply_dq = call(
        finish_queries,
        "finish_queries",
        SMALL_MIB,
        (place, query_mine0, query_theirs0, query_mine1, query_theirs1),
        [shape(prompt_own, query_width), shape(reply_own, query_width)],
        cost_estimate=pl.CostEstimate(
            flops=2 * reply_own * reply_own * query_width,
            bytes_accessed=8 * reply_own * query_width,
            transcendentals=0,
        ),
    )
    reply0, theirs0 = call(
        collect_replies,
        "collect_replies",
        SMALL_MIB,
        arrived0,
        [shape(reply_own, 2 * HEAD_WIDTH, dtype=F32), shape(reply_own, 2 * HEAD_WIDTH)],
        scalars=0,
    )
    slices, prompt_dq, reply_dq, theirs0 = lax.optimization_barrier((slices, prompt_dq, reply_dq, theirs0))
    reply1, prompts, theirs = call(
        functools.partial(collect_second, chips),
        "collect_second",
        SMALL_MIB,
        (*arrived1, *slices, theirs0),
        [
            shape(reply_own, 2 * HEAD_WIDTH, dtype=F32),
            shape(LOCAL_HEADS, cut_rows, 2 * HEAD_WIDTH, dtype=F32),
            shape(2 * reply_own + 2 * max(cut_rows, 16), 2 * HEAD_WIDTH),
        ],
        scalars=0,
    )
    prompt_dk, prompt_dv, reply_dk, reply_dv = call(
        finish_keys,
        "finish_keys",
        SMALL_MIB,
        (place, reply0, reply1, prompts, swap(theirs)),
        [shape(cut_rows, key_width)] * 2 + [shape(reply_own, key_width)] * 2,
    )
    return (
        prompt_dq[:prompt_rows],
        prompt_dk,
        prompt_dv,
        reply_dq[None],
        reply_dk[None],
        reply_dv[None],
    )


def solution(mesh):
    return jax.shard_map(
        on_device,
        mesh=mesh,
        in_specs=(
            P(("pre", "rsp"), None),
            P("pre", None),
            P("pre", None),
            P(("pre", "rsp"), None),
            P(("pre", "rsp"), None),
            P("rsp", "pre", None),
            P("rsp", "pre", None),
            P("rsp", "pre", None),
            P("rsp", "pre", None),
            P("rsp", "pre", None),
            P(),
            P(),
        ),
        out_specs=(
            P(("pre", "rsp"), None),
            P(("pre", "rsp"), None),
            P(("pre", "rsp"), None),
            P("rsp", "pre", None),
            P("rsp", "pre", None),
            P("rsp", "pre", None),
        ),
        check_vma=False,
    )
```
